32 devices in a mesh: dp: 32 (over z, y, x, core).
Axes of the slice: x: 2, y: 2, z: 4, core: 2. Of those that a mesh axis runs over, the one named last changes fastest.
Arguments:
- tokens: bfloat16 [2560, 37, 384], P('dp'), may hold values from -6 to 6
- layer_gains: float32 [2, 2, 384], replicated, may hold values from 0.5 to 1.5
- layer_shifts: float32 [2, 2, 384], replicated, may hold values from -1.25 to 1.25
- w_qkv: bfloat16 [2, 384, 1152], replicated, may hold values from -0.3125 to 0.3125
- b_qv: float32 [2, 768], replicated, may hold values from -1.25 to 1.25
- w_out: bfloat16 [2, 384, 384], replicated, may hold values from -1.25 to 1.25
- b_out: float32 [2, 384], replicated, may hold values from -1.25 to 1.25
- w_fc1: bfloat16 [2, 384, 1536], replicated, may hold values from -0.3125 to 0.3125
- b_fc1: float32 [2, 1536], replicated, may hold values from -1.25 to 1.25
- w_fc2: bfloat16 [2, 1536, 384], replicated, may hold values from -0.15625 to 0.15625
- b_fc2: float32 [2, 384], replicated, may hold values from -1.25 to 1.25
- final_gain: float32 [384], replicated, may hold values from 0.5 to 1.5
- final_shift: float32 [384], replicated, may hold values from -1.25 to 1.25
- head_w1: bfloat16 [384, 2048], replicated, may hold values from -0.3125 to 0.3125
- head_b1: float32 [2048], replicated, may hold values from -1.25 to 1.25
- head_w2: bfloat16 [2048, 2048], replicated, may hold values from -0.125 to 0.125
- head_b2: float32 [2048], replicated, may hold values from -1.25 to 1.25
- head_w3: bfloat16 [2048, 256], replicated, may hold values from -0.125 to 0.125
- head_b3: float32 [256], replicated, may hold values from -1.25 to 1.25
- prototypes: bfloat16 [256, 8192], P(None, 'dp'), may hold values from -6 to 6
- crop_counts: int32 [256], replicated, may hold values from 2 to 10, as said below
- teacher_logits: float32 [256, 8192], P(None, 'dp'), may hold values from -0.625 to 0.625
- first_epoch: int32 [8192], P('dp'), may hold values 0 or 1
Outputs:
- tokens_grad: float32 [2560, 37, 384], P('dp')
- layer_gains_grad: float32 [2, 2, 384], replicated
- layer_shifts_grad: float32 [2, 2, 384], replicated
- w_qkv_grad: float32 [2, 384, 1152], replicated
- b_qv_grad: float32 [2, 768], replicated
- w_out_grad: float32 [2, 384, 384], replicated
- b_out_grad: float32 [2, 384], replicated
- w_fc1_grad: float32 [2, 384, 1536], replicated
- b_fc1_grad: float32 [2, 1536], replicated
- w_fc2_grad: float32 [2, 1536, 384], replicated
- b_fc2_grad: float32 [2, 384], replicated
- final_gain_grad: float32 [384], replicated
- final_shift_grad: float32 [384], replicated
- head_w1_grad: float32 [384, 2048], P(None, 'dp')
- head_b1_grad: float32 [2048], P('dp')
- head_w2_grad: float32 [2048, 2048], P('dp')
- head_b2_grad: float32 [2048], P('dp')
- head_w3_grad: float32 [2048, 256], P('dp')
- head_b3_grad: float32 [256], replicated
- prototypes_grad: float32 [256, 8192], P(None, 'dp')
The draws below stay inside these ranges and needn't reach their ends.
Inputs may be any that keep to these rules, and one draw needn't show every extreme that they name: `crop_counts`: every image has from 2 up to 10 local crops, and some image has exactly 10.
All inputs are finite; a program needn't handle non-finite values. No bound on the sum of `first_epoch` on one device may be relied on, other than what follows from the above.
Results may differ from the reference program's by a relative error of at most 0.022.
Values may be sent and summed in bfloat16 or wider, within the bound.
No kernel may reach another device: no remote copies, remote signals or barrier semaphores. Data moves between devices by JAX's collectives and lax.ppermute only.
A program may use at most 384 MiB of HBM per device.

```python
import jax
import jax.numpy as jnp
from jax import lax

D = 384
HEADS = 6
HD = 64
FF = 1536
HID = 2048
BOTTLE = 256
KDEV = 256
MOST_CROPS = 10
LEN = 37
SLOTS_DEV = 80
SLOTS = 2560
IMAGES = 256
K = 8192
N_DP = 32


def draw_crop_counts(key, part):
    key = jax.random.fold_in(key, 7)
    first_key, second_key = jax.random.split(key)
    counts = jax.random.randint(first_key, (IMAGES,), 2, MOST_CROPS + 1, dtype=jnp.int32)
    chosen = jax.random.randint(second_key, (), 0, IMAGES, dtype=jnp.int32)
    return jnp.where(jnp.arange(IMAGES, dtype=jnp.int32) == chosen, MOST_CROPS, counts).astype(jnp.int32)


def plant(result, own_key, least, top_value):
    longest = result.shape.index(max(result.shape))
    spots = []
    for shift in (0, 1):
        where = [jax.random.randint(jax.random.fold_in(own_key, axis), (), 0, length) for axis, length in enumerate(result.shape)]
        where[longest] = (where[longest] + shift) % result.shape[longest]
        spots.append(tuple(where))
    return result.at[spots[0]].set(least).at[spots[1]].set(top_value)


def steps_of(key, extent, cuts, least, top_value):
    level, own = 1.0, jax.random.fold_in(key, 6)
    for dim, parts in cuts:
        steps = jnp.exp(jax.random.uniform(jax.random.fold_in(own, dim), (parts,), jnp.float32, least / len(cuts), top_value / len(cuts)))
        level = level * jnp.repeat(steps, extent[dim] // parts).reshape([-1 if axis == dim else 1 for axis in range(len(extent))])
    return level


def bell_draw(rng, dims, scale, reach, cuts=(), kind=jnp.bfloat16):
    values = scale * jax.random.normal(rng, dims, jnp.float32)
    if cuts:
        values = values * steps_of(rng, dims, cuts, -0.22, 0.18)
    return jnp.clip(values, -reach, reach).astype(kind)


def setup_inputs(seed: int = 0) -> dict:
    splits = jax.random.split(jax.random.key(seed), 24)
    return {
        "tokens": bell_draw(splits[0], (SLOTS, LEN, D), 1.0, 6.0, ((0, 32),)),
        "layer_gains": jnp.clip(1.0 + 0.1 * jax.random.normal(splits[1], (2, 2, D), jnp.float32), 0.5, 1.5),
        "layer_shifts": bell_draw(splits[2], (2, 2, D), 0.2, 1.25, (), jnp.float32),
        "w_qkv": bell_draw(splits[3], (2, D, 3 * D), D ** -0.5, 0.3125),
        "b_qv": bell_draw(splits[4], (2, 2 * D), 0.2, 1.25, (), jnp.float32),
        "w_out": bell_draw(splits[5], (2, D, D), (D // 16) ** -0.5, 1.25),
        "b_out": bell_draw(splits[6], (2, D), 0.2, 1.25, (), jnp.float32),
        "w_fc1": bell_draw(splits[7], (2, D, FF), D ** -0.5, 0.3125),
        "b_fc1": bell_draw(splits[8], (2, FF), 0.2, 1.25, (), jnp.float32),
        "w_fc2": bell_draw(splits[9], (2, FF, D), FF ** -0.5, 0.15625),
        "b_fc2": bell_draw(splits[10], (2, D), 0.2, 1.25, (), jnp.float32),
        "final_gain": jnp.clip(1.0 + 0.1 * jax.random.normal(splits[11], (D,), jnp.float32), 0.5, 1.5),
        "final_shift": bell_draw(splits[12], (D,), 0.2, 1.25, (), jnp.float32),
        "head_w1": bell_draw(splits[13], (D, HID), D ** -0.5, 0.3125),
        "head_b1": bell_draw(splits[14], (HID,), 0.2, 1.25, (), jnp.float32),
        "head_w2": bell_draw(splits[15], (HID, HID), HID ** -0.5, 0.125),
        "head_b2": bell_draw(splits[16], (HID,), 0.2, 1.25, (), jnp.float32),
        "head_w3": bell_draw(splits[17], (HID, BOTTLE), HID ** -0.5, 0.125),
        "head_b3": bell_draw(splits[18], (BOTTLE,), 0.2, 1.25, (), jnp.float32),
        "prototypes": bell_draw(splits[19], (BOTTLE, K), 1.0, 6.0, ((1, 32),)),
        "crop_counts": draw_crop_counts(jax.random.fold_in(splits[23], 71), 0),
        "teacher_logits": bell_draw(splits[21], (IMAGES, K), 0.1, 0.625, ((1, 32),), jnp.float32),
        "first_epoch": plant((jax.random.randint(splits[22], (K,), 0, 2) < 1).astype(jnp.int32), jax.random.fold_in(splits[22], 1), 0, 1),
    }


HIGH = lax.Precision.HIGHEST
STUDENT_TEMP = 0.1
TEACHER_TEMP = 0.04
EPS = 1e-06

@jax.custom_vjp
def low(v):
    return lax.optimization_barrier(v.astype(jnp.bfloat16)).astype(jnp.float32)

@jax.custom_vjp
def low_back(v):
    return v

def low_keep(v):
    return (low(v), None)

def low_pass(kept, grad):
    return (grad,)

def back_keep(v):
    return (v, None)

def back_low(kept, grad):
    return (low(grad),)
low.defvjp(low_keep, low_pass)
low_back.defvjp(back_keep, back_low)

def layer_norm(values, gain, shift):
    mean = lax.optimization_barrier(jnp.mean(values, axis=-1, keepdims=True))
    centered = values - mean
    return centered * lax.rsqrt(lax.optimization_barrier(jnp.mean(centered * centered, axis=-1, keepdims=True)) + EPS) * gain + shift

def project(values, weight):
    return jnp.einsum('...d,de->...e', values, weight, precision=HIGH)

def block(inputs, gains, shifts, wqkv, bqv, wout, bout, wfc1, bfc1, wfc2, bfc2):
    count, length, width = inputs.shape
    normed = low(layer_norm(inputs, gains[0], shifts[0]))
    bias = jnp.concatenate([bqv[:width], jnp.zeros((width,), jnp.float32), bqv[width:]])
    qkv = low(low_back(project(normed, wqkv) + bias)).reshape(count, length, 3, HEADS, HD)
    scores = low_back(jnp.einsum('gqhe,gkhe->ghqk', qkv[:, :, 0], qkv[:, :, 1], precision=HIGH) * HD ** (-0.5))
    probs = low(jax.nn.softmax(scores, axis=-1))
    attended = jnp.einsum('ghqk,gkhe->gqhe', probs, qkv[:, :, 2], precision=HIGH).reshape(count, length, width)
    attended = low(low_back(attended))
    middle = inputs + low_back(project(attended, wout) + bout)
    hidden = low(layer_norm(middle, gains[1], shifts[1]))
    pre_act = low_back(project(hidden, wfc1) + bfc1)
    return middle + low_back(project(low(jax.nn.gelu(pre_act, approximate=False)), wfc2) + bfc2)

def reference(tokens, layer_gains, layer_shifts, w_qkv, b_qv, w_out, b_out, w_fc1, b_fc1, w_fc2, b_fc2, final_gain, final_shift, head_w1, head_b1, head_w2, head_b2, head_w3, head_b3, prototypes, crop_counts, teacher_logits, first_epoch):
    floats = tuple((item.astype(jnp.float32) for item in (tokens, layer_gains, layer_shifts, w_qkv, b_qv, w_out, b_out, w_fc1, b_fc1, w_fc2, b_fc2, final_gain, final_shift, head_w1, head_b1, head_w2, head_b2, head_w3, head_b3, prototypes)))
    images = crop_counts.shape[0]
    live = (jnp.arange(MOST_CROPS, dtype=jnp.int32)[None, :] < crop_counts[:, None]).astype(jnp.float32).reshape(-1)
    teach = teacher_logits / TEACHER_TEMP
    teach_top = lax.optimization_barrier(jnp.max(teach, axis=1, keepdims=True))
    teach_log = teach_top + jnp.log(lax.optimization_barrier(jnp.sum(jnp.exp(teach - teach_top), axis=1, keepdims=True)))
    target = jnp.exp(teach - teach_log)
    target_blocks = target.reshape(images, N_DP, KDEV).transpose(1, 0, 2)

    def loss(tok, gains, shifts, wqkv, bqv, wout, bout, wfc1, bfc1, wfc2, bfc2, fgain, fshift, hw1, hb1, hw2, hb2, hw3, hb3, proto):

        def group(values):
            for index in range(2):
                values = block(values, gains[index], shifts[index], wqkv[index], bqv[index], wout[index], bout[index], wfc1[index], bfc1[index], wfc2[index], bfc2[index])
            return values[:, 0]
        classes = lax.map(jax.checkpoint(group), tok.reshape(N_DP, SLOTS_DEV, LEN, D)).reshape(SLOTS, D)
        normed = low(layer_norm(classes, fgain, fshift))
        first = low(jax.nn.gelu(low_back(project(normed, hw1) + hb1), approximate=False))
        second = low(jax.nn.gelu(low_back(project(first, hw2) + hb2), approximate=False))
        embed = low_back(project(second, hw3) + hb3)
        feats = low(embed * lax.rsqrt(lax.optimization_barrier(jnp.sum(embed * embed, axis=-1, keepdims=True)) + EPS))
        proto_blocks = proto.reshape(BOTTLE, N_DP, KDEV).transpose(1, 0, 2)

        def column_block(carry, pieces):
            row_top, row_total, cross = carry
            piece, target_piece = pieces
            unit = low(piece * lax.rsqrt(lax.optimization_barrier(jnp.sum(piece * piece, axis=0)) + EPS))
            logits = low_back(project(feats, unit)) / STUDENT_TEMP
            new_top = jnp.maximum(row_top, lax.optimization_barrier(jnp.max(logits, axis=1)))
            row_total = row_total * jnp.exp(row_top - new_top) + lax.optimization_barrier(jnp.sum(jnp.exp(logits - new_top[:, None]), axis=1))
            target_rows = jnp.broadcast_to(target_piece[:, None], (images, MOST_CROPS, KDEV)).reshape(SLOTS, KDEV)
            cross = cross + lax.optimization_barrier(jnp.sum(target_rows * logits, axis=1))
            return ((new_top, row_total, cross), None)
        start = (jnp.full((SLOTS,), -1e+30, jnp.float32), jnp.zeros((SLOTS,), jnp.float32), jnp.zeros((SLOTS,), jnp.float32))
        (row_top, row_total, cross), unused = lax.scan(jax.checkpoint(column_block), start, (proto_blocks, target_blocks))
        return jnp.sum(live * (row_top + jnp.log(row_total) - cross)) / N_DP
    value, pullback = jax.vjp(loss, *floats)
    grads = pullback(jnp.ones_like(value))
    thawed = (1 - first_epoch).astype(jnp.float32)[None, :]
    return (grads[0], grads[1], grads[2], grads[3], grads[4], grads[5], grads[6], grads[7], grads[8], grads[9], grads[10], grads[11], grads[12], grads[13], grads[14], grads[15], grads[16], grads[17], grads[18], grads[19] * thawed)
```

```python
import jax
import jax.numpy as jnp
from jax import lax
from jax.experimental import pallas as pl
from jax.experimental.pallas import tpu as pltpu
from jax.sharding import PartitionSpec as P

HEADS = 6
HD = 64
MOST_CROPS = 10


STUDENT_TEMP = 0.1
TEACHER_TEMP = 0.04
EPS = 1e-06
SHIFT = 10.0


def product(left, right):
    return jnp.dot(left, right, preferred_element_type=jnp.float32)


def against(left, right):
    return lax.dot_general(
        left, right, (((1,), (1,)), ((), ())), preferred_element_type=jnp.float32
    )


def inner_rows(left, right):
    return lax.dot_general(
        left, right, (((0,), (0,)), ((), ())), preferred_element_type=jnp.float32
    )


def column_sum(values):
    return jnp.sum(values.astype(jnp.float32), axis=0)


def smooth(values):
    return jax.nn.gelu(values, approximate=False)


def smooth_back(values, grad):
    return jax.vjp(smooth, values)[1](grad)[0]


def norm_forward(values, gain, shift):
    centered = values - jnp.mean(values, axis=-1, keepdims=True)
    rstd = lax.rsqrt(jnp.mean(centered * centered, axis=-1, keepdims=True) + EPS)
    normed = centered * rstd
    return (normed * gain + shift, normed, rstd)


def norm_backward(grad, normed, rstd, gain):
    scaled = grad * gain
    inner = (
        scaled
        - jnp.mean(scaled, axis=-1, keepdims=True)
        - normed * jnp.mean(scaled * normed, axis=-1, keepdims=True)
    )
    return (rstd * inner, jnp.sum(grad * normed, axis=0), jnp.sum(grad, axis=0))


def mlp_back(grad_out, act_low, pre_act, norm_low, w_first, w_second):
    grad_low = grad_out.astype(jnp.bfloat16)
    grad_bias2 = column_sum(grad_low)
    grad_weight2 = inner_rows(act_low, grad_low)
    grad_pre = smooth_back(pre_act, against(grad_low, w_second)).astype(jnp.bfloat16)
    grad_bias1 = column_sum(grad_pre)
    grad_weight1 = inner_rows(norm_low, grad_pre)
    return (against(grad_pre, w_first), grad_weight1, grad_bias1, grad_weight2, grad_bias2)


def axis_bits(n):
    bits = n.bit_length() - 1
    assert n == 1 << bits
    return bits


def swap(values, bit, n):
    return lax.ppermute(values, "dp", [(i, i ^ (1 << bit)) for i in range(n)])


def gather_any(block, n):
    out = block[None]
    for bit in reversed(range(axis_bits(n))):
        out = jnp.concatenate([out, swap(out, bit, n)], axis=0)
    return out


def gather_ordered(block, n):
    me = lax.axis_index("dp")
    bits = axis_bits(n)
    out = block
    for bit in reversed(range(bits)):
        other = swap(out, bit, n)
        first = ((me >> bit) & 1) == 0
        out = jnp.stack([jnp.where(first, out, other), jnp.where(first, other, out)])
    order = tuple(reversed(range(bits))) + tuple(range(bits, bits + block.ndim))
    return out.transpose(order).reshape((n,) + block.shape)


def scatter_sum(parts, n, wire):
    me = lax.axis_index("dp")
    bits = axis_bits(n)
    out = parts.reshape((2,) * bits + parts.shape[1:])
    for bit in range(bits):
        axis = bits - 1 - bit
        mine = (me >> bit) & 1
        keep = lax.dynamic_index_in_dim(out, mine, axis, keepdims=False)
        send = lax.dynamic_index_in_dim(out, 1 - mine, axis, keepdims=False).astype(wire)
        out = keep + swap(send, bit, n).astype(keep.dtype)
    return out


def sum_all(values, n):
    me = lax.axis_index("dp")
    bits = axis_bits(n)
    out = values
    for bit in range(bits):
        half = out.shape[0] // 2
        mine = (me >> bit) & 1
        keep = lax.dynamic_slice_in_dim(out, mine * half, half, 0)
        send = lax.dynamic_slice_in_dim(out, (1 - mine) * half, half, 0)
        out = keep + swap(send, bit, n)
    for bit in reversed(range(bits)):
        other = swap(out, bit, n)
        first = ((me >> bit) & 1) == 0
        out = jnp.concatenate([jnp.where(first, out, other), jnp.where(first, other, out)], axis=0)
    return out


def sum_small(values, n):
    out = values
    for bit in range(axis_bits(n)):
        out = out + swap(out, bit, n)
    return out


GROUP = 8
PITCH = 40
PAIR = 2 * PITCH
NEVER = -1e30


def smooth_both(values):
    size = jnp.abs(values)
    bell = jnp.exp(values * values * -0.5)
    t = 1.0 / (1.0 + 0.23164189 * size)
    tail = t * (0.127414796 + t * (-0.142248368 + t * (0.7107068705 + t * (-0.7265760135 + t * 0.5307027145))))
    upper = tail * bell
    area = jnp.where(values >= 0, 1.0 - upper, upper)
    return values * area, area + values * (bell * 0.3989422804014327)


def standardize(values):
    centered = values - jnp.mean(values, axis=-1, keepdims=True)
    rstd = lax.rsqrt(jnp.mean(centered * centered, axis=-1, keepdims=True) + EPS)
    return centered * rstd, rstd


def standard_back(grad, normed, rstd, gain):
    scaled = grad * gain
    return rstd * (
        scaled
        - jnp.mean(scaled, axis=-1, keepdims=True)
        - normed * jnp.mean(scaled * normed, axis=-1, keepdims=True)
    )


def fold_rows(values):
    return jnp.sum(values.reshape(-1, 8, values.shape[1]), axis=0)


def both_heads(values):
    lane = lax.broadcasted_iota(jnp.int32, values.shape, 1)
    zero = jnp.zeros_like(values)
    return jnp.concatenate([jnp.where(lane < HD, values, zero), jnp.where(lane < HD, zero, values)])


def join_heads(values):
    rows = values.shape[0] // 2
    lane = lax.broadcasted_iota(jnp.int32, (rows, values.shape[1]), 1)
    return jnp.where(lane < HD, values[:rows], values[rows:])


def spread_heads(values):
    lane = lax.broadcasted_iota(jnp.int32, values.shape, 1) // HD
    return jnp.concatenate([jnp.where(lane == h, values, 0.0) for h in range(HEADS)])


def gather_heads(values):
    lane = lax.broadcasted_iota(jnp.int32, (GROUP, values.shape[1]), 1) // HD
    out = jnp.zeros((GROUP, values.shape[1]), values.dtype)
    for h in range(HEADS):
        out = jnp.where(lane == h, values[h * GROUP : (h + 1) * GROUP], out)
    return out


def soft_columns(scores):
    expo = jnp.exp(scores - jnp.max(scores, axis=0, keepdims=True))
    return expo * (1.0 / jnp.sum(expo, axis=0, keepdims=True))


def take_slots(all_ref, rows_ref, step, seq_len, slots):
    for s in range(GROUP):
        for c in range(all_ref.shape[0]):
            rows_ref[s * PITCH : s * PITCH + seq_len, c * 128 : (c + 1) * 128] = all_ref[
                c, pl.ds(step * GROUP + s, seq_len, stride=slots), :
            ]


def first_rows(ref):
    return jnp.concatenate([ref[s * PITCH : s * PITCH + 1, :] for s in range(GROUP)])


def add_first_rows(ref, values):
    for s in range(GROUP):
        ref[s * PITCH : s * PITCH + 1, :] += values[s : s + 1]


def widen_tokens(tok_ref, all_ref):
    seq_len, slots, width = tok_ref.shape

    @pl.loop(0, seq_len)
    def _(t):
        wide = tok_ref[t].astype(jnp.float32)
        for c in range(all_ref.shape[0]):
            all_ref[c, pl.ds(pl.multiple_of(t * slots, 8), slots), :] = wide[:, c * 128 : (c + 1) * 128]


def forward_kernel(
    tok_ref, pair_mask_ref, class_mask_ref, gains_ref, shifts_ref,
    w_qkv_ref, b_qkv_ref, w_out_ref, b_out_ref, w_fc1_ref, b_fc1_ref, w_fc2_ref, b_fc2_ref,
    w_up_ref, b_up_ref,
    qkv_ref, o_ref, mid_ref, act_ref, slope_ref, x1_ref, kv_ref, cq_ref, co_ref, ch_ref, cx_ref,
    all_ref, x_ref, low_ref, wide_ref,
):
    step = pl.program_id(0)
    seq_len, slots, width = tok_ref.shape
    rows = GROUP * PITCH
    hidden = w_fc1_ref.shape[1]

    @pl.when(step == 0)
    def _():
        widen_tokens(tok_ref, all_ref)
        x_ref[...] = jnp.zeros_like(x_ref)

    take_slots(all_ref, x_ref, step, seq_len, slots)
    chunk = PAIR
    for r in range(0, rows, chunk):
        normed, _ = standardize(x_ref[r : r + chunk, :])
        low_ref[r : r + chunk, :] = (normed * gains_ref[0:1, :] + shifts_ref[0:1, :]).astype(jnp.bfloat16)
    for j in range(3):
        cols = slice(j * width, (j + 1) * width)
        part = product(low_ref[...], w_qkv_ref[:, cols]) + b_qkv_ref[:, cols]
        if j == 0:
            part = part.astype(jnp.bfloat16) * jnp.bfloat16(HD ** -0.5)
        qkv_ref[:, cols] = part.astype(jnp.bfloat16)
    for r in range(0, rows, PAIR):
        for c in range(0, width, 2 * HD):
            keys = qkv_ref[r : r + PAIR, width + c : width + c + 2 * HD]
            values = qkv_ref[r : r + PAIR, 2 * width + c : 2 * width + c + 2 * HD]
            queries = both_heads(qkv_ref[r : r + PAIR, c : c + 2 * HD])
            probs = soft_columns(against(keys, queries) + pair_mask_ref[...]).astype(jnp.bfloat16)
            o_ref[r : r + PAIR, c : c + 2 * HD] = join_heads(inner_rows(probs, values)).astype(jnp.bfloat16)
    mixed = product(o_ref[...], w_out_ref[...])
    for r in range(0, rows, chunk):
        part = x_ref[r : r + chunk, :] + mixed[r : r + chunk] + b_out_ref[...]
        mid_ref[r : r + chunk, :] = part
        normed, _ = standardize(part)
        low_ref[r : r + chunk, :] = (normed * gains_ref[1:2, :] + shifts_ref[1:2, :]).astype(jnp.bfloat16)
    for c in range(0, hidden, 256):
        pre = product(low_ref[...], w_fc1_ref[:, c : c + 256])
        for r in range(0, rows, 32):
            act, slope = smooth_both(pre[r : r + 32] + b_fc1_ref[:, c : c + 256])
            act_ref[r : r + 32, c : c + 256] = act.astype(jnp.bfloat16)
            slope_ref[r : r + 32, c : c + 256] = slope.astype(jnp.bfloat16)
    mixed = product(act_ref[...], w_fc2_ref[...])
    for r in range(0, rows, chunk):
        part = mid_ref[r : r + chunk, :] + mixed[r : r + chunk] + b_fc2_ref[...]
        x1_ref[r : r + chunk, :] = part
        normed, _ = standardize(part)
        wide = normed * gains_ref[2:3, :] + shifts_ref[2:3, :]
        wide_ref[r : r + chunk, :] = wide
        low_ref[r : r + chunk, :] = wide.astype(jnp.bfloat16)
    for j in range(2):
        cols = slice(j * width, (j + 1) * width)
        ups = slice((j + 1) * width, (j + 2) * width)
        kv_ref[:, cols] = (product(low_ref[...], w_up_ref[:, ups]) + b_up_ref[:, ups]).astype(jnp.bfloat16)
    cx_ref[...] = first_rows(x1_ref)
    first = first_rows(wide_ref).astype(jnp.bfloat16)
    ch_ref[...] = first.astype(jnp.float32)
    query = (product(first, w_up_ref[:, :width]) + b_up_ref[:, :width]).astype(jnp.bfloat16).astype(jnp.float32) * HD ** -0.5
    cq_ref[...] = query
    spread = spread_heads(query).astype(jnp.bfloat16)
    probs = soft_columns(against(kv_ref[:, :width], spread) + class_mask_ref[...]).astype(jnp.bfloat16)
    co_ref[...] = gather_heads(inner_rows(probs, kv_ref[:, width:]))


def upper_back_kernel(
    class_mask_ref, gains_ref, shifts_ref, w_up_ref, x1_ref, kv_ref, cq_ref, cg_ref, cres_ref,
    dx_ref, dq_ref, dw_ref, vec_ref,
    acc_ref, wide_ref,
):
    step = pl.program_id(0)
    rows, width = x1_ref.shape

    @pl.when(step == 0)
    def _():
        acc_ref[...] = jnp.zeros_like(acc_ref)
        vec_ref[...] = jnp.zeros_like(vec_ref)

    keys, values = kv_ref[:, :width], kv_ref[:, width:]
    spread = spread_heads(cq_ref[...]).astype(jnp.bfloat16)
    grads = spread_heads(cg_ref[...]).astype(jnp.bfloat16)
    probs = soft_columns(against(keys, spread) + class_mask_ref[...])
    back = against(values, grads)
    inner = (probs * (back - jnp.sum(back * probs, axis=0, keepdims=True))).astype(jnp.bfloat16)
    grad_values = product(probs.astype(jnp.bfloat16), grads).astype(jnp.bfloat16)
    grad_keys = product(inner, spread).astype(jnp.bfloat16)
    grad_query = (gather_heads(inner_rows(inner, keys)) * HD ** -0.5).astype(jnp.bfloat16)
    dq_ref[...] = grad_query.astype(jnp.float32)
    vec_ref[:, :width] += fold_rows(grad_values.astype(jnp.float32))
    wide_ref[...] = against(grad_keys, w_up_ref[:, width : 2 * width]) + against(grad_values, w_up_ref[:, 2 * width :])
    add_first_rows(wide_ref, against(grad_query, w_up_ref[:, :width]))
    chunk = PAIR
    parts = []
    for r in range(0, rows, chunk):
        normed, rstd = standardize(x1_ref[r : r + chunk, :])
        parts.append((normed * gains_ref[2:3, :] + shifts_ref[2:3, :]).astype(jnp.bfloat16))
        grad = wide_ref[r : r + chunk, :]
        vec_ref[:, width : 2 * width] += fold_rows(grad * normed)
        vec_ref[:, 2 * width : 3 * width] += fold_rows(grad)
        dx_ref[r : r + chunk, :] = standard_back(grad, normed, rstd, gains_ref[2:3, :])
    turned = jnp.concatenate(parts).T
    acc_ref[:, :width] += product(turned, grad_keys)
    acc_ref[:, width:] += product(turned, grad_values)
    add_first_rows(dx_ref, cres_ref[...])

    @pl.when(step == pl.num_programs(0) - 1)
    def _():
        dw_ref[...] = acc_ref[...].astype(jnp.bfloat16)


def mlp_back_kernel(
    gains_ref, shifts_ref, w_fc1_ref, w_fc2_ref, dx_ref, mid_ref, act_ref, slope_ref,
    dmid_ref, dw1_ref, dw2_ref, vec_ref, vec1_ref,
    acc1_ref, acc2_ref, dz_ref,
):
    step = pl.program_id(0)
    rows, width = dx_ref.shape
    hidden = act_ref.shape[1]

    @pl.when(step == 0)
    def _():
        acc1_ref[...] = jnp.zeros_like(acc1_ref)
        acc2_ref[...] = jnp.zeros_like(acc2_ref)
        vec_ref[...] = jnp.zeros_like(vec_ref)
        vec1_ref[...] = jnp.zeros_like(vec1_ref)

    low = dx_ref[...].astype(jnp.bfloat16)
    vec_ref[:, :width] += fold_rows(low.astype(jnp.float32))
    low_turned = low.T
    chunk = PAIR
    parts = []
    for r in range(0, rows, chunk):
        normed, _ = standardize(mid_ref[r : r + chunk, :])
        parts.append((normed * gains_ref[1:2, :] + shifts_ref[1:2, :]).astype(jnp.bfloat16))
    norm_turned = jnp.concatenate(parts).T
    for c in range(0, hidden, 256):
        cols = slice(c, c + 256)
        back = against(low, w_fc2_ref[cols, :])
        for r in range(0, rows, chunk):
            part = (back[r : r + chunk] * slope_ref[r : r + chunk, cols].astype(jnp.float32)).astype(jnp.bfloat16)
            dz_ref[r : r + chunk, cols] = part
            vec1_ref[:, cols] += fold_rows(part.astype(jnp.float32))
        acc1_ref[:, cols] += product(norm_turned, dz_ref[:, cols])
        acc2_ref[:, cols] += product(low_turned, act_ref[:, cols])
    mixed = against(dz_ref[...], w_fc1_ref[...])
    for r in range(0, rows, chunk):
        normed, rstd = standardize(mid_ref[r : r + chunk, :])
        grad = mixed[r : r + chunk]
        vec_ref[:, width : 2 * width] += fold_rows(grad * normed)
        vec_ref[:, 2 * width : 3 * width] += fold_rows(grad)
        dmid_ref[r : r + chunk, :] = dx_ref[r : r + chunk, :] + standard_back(grad, normed, rstd, gains_ref[1:2, :])

    @pl.when(step == pl.num_programs(0) - 1)
    def _():
        dw1_ref[...] = acc1_ref[...].astype(jnp.bfloat16)
        dw2_ref[...] = acc2_ref[...].T.astype(jnp.bfloat16)


def attend_back_kernel(
    tok_ref, pair_mask_ref, gains_ref, shifts_ref, w_qkv_ref, w_out_ref, dmid_ref, qkv_ref, o_ref,
    dtok_ref, dwo_ref, dwqkv_ref, vec_ref,
    all_ref, out_ref, x_ref, acco_ref, accqkv_ref, do_ref, dqkv_ref,
):
    step = pl.program_id(0)
    seq_len, slots, width = tok_ref.shape
    rows = GROUP * PITCH

    @pl.when(step == 0)
    def _():
        widen_tokens(tok_ref, all_ref)
        x_ref[...] = jnp.zeros_like(x_ref)
        acco_ref[...] = jnp.zeros_like(acco_ref)
        accqkv_ref[...] = jnp.zeros_like(accqkv_ref)
        vec_ref[...] = jnp.zeros_like(vec_ref)

    take_slots(all_ref, x_ref, step, seq_len, slots)
    low = dmid_ref[...].astype(jnp.bfloat16)
    vec_ref[:, :width] += fold_rows(low.astype(jnp.float32))
    do_ref[...] = against(low, w_out_ref[...]).astype(jnp.bfloat16)
    acco_ref[...] += product(o_ref[...].T, low)
    for r in range(0, rows, PAIR):
        for c in range(0, width, 2 * HD):
            keys = qkv_ref[r : r + PAIR, width + c : width + c + 2 * HD]
            values = qkv_ref[r : r + PAIR, 2 * width + c : 2 * width + c + 2 * HD]
            queries = both_heads(qkv_ref[r : r + PAIR, c : c + 2 * HD])
            grads = both_heads(do_ref[r : r + PAIR, c : c + 2 * HD])
            probs = soft_columns(against(keys, queries) + pair_mask_ref[...])
            back = against(values, grads)
            inner = (probs * (back - jnp.sum(back * probs, axis=0, keepdims=True))).astype(jnp.bfloat16)
            dqkv_ref[r : r + PAIR, 2 * width + c : 2 * width + c + 2 * HD] = product(
                probs.astype(jnp.bfloat16), grads
            ).astype(jnp.bfloat16)
            dqkv_ref[r : r + PAIR, width + c : width + c + 2 * HD] = product(inner, queries).astype(jnp.bfloat16)
            dqkv_ref[r : r + PAIR, c : c + 2 * HD] = (
                join_heads(inner_rows(inner, keys)) * HD ** -0.5
            ).astype(jnp.bfloat16)
    chunk = PAIR
    parts = []
    for r in range(0, rows, chunk):
        normed, _ = standardize(x_ref[r : r + chunk, :])
        parts.append((normed * gains_ref[0:1, :] + shifts_ref[0:1, :]).astype(jnp.bfloat16))
    turned = jnp.concatenate(parts).T
    for j in range(3):
        cols = slice(j * width, (j + 1) * width)
        vec_ref[:, (j + 1) * width : (j + 2) * width] += fold_rows(dqkv_ref[:, cols].astype(jnp.float32))
        accqkv_ref[:, cols] += product(turned, dqkv_ref[:, cols])
    mixed = against(dqkv_ref[...], w_qkv_ref[...])
    for r in range(0, rows, chunk):
        normed, rstd = standardize(x_ref[r : r + chunk, :])
        grad = mixed[r : r + chunk]
        vec_ref[:, 4 * width : 5 * width] += fold_rows(grad * normed)
        vec_ref[:, 5 * width : 6 * width] += fold_rows(grad)
        part = dmid_ref[r : r + chunk, :] + standard_back(grad, normed, rstd, gains_ref[0:1, :])
        for s in range(chunk // PITCH):
            for t in range(all_ref.shape[0]):
                out_ref[t, pl.ds(step * GROUP + r // PITCH + s, seq_len, stride=slots), :] = part[
                    s * PITCH : s * PITCH + seq_len, t * 128 : (t + 1) * 128
                ]

    @pl.when(step == pl.num_programs(0) - 1)
    def _():
        for t in range(out_ref.shape[0]):
            dtok_ref[:, t * 128 : (t + 1) * 128] = out_ref[t]
        dwo_ref[...] = acco_ref[...].astype(jnp.bfloat16)
        dwqkv_ref[...] = accqkv_ref[...].astype(jnp.bfloat16)


def whole(array):
    return pl.BlockSpec(array.shape, lambda i: (0,) * len(array.shape))


def by_step(rows, width):
    return pl.BlockSpec((rows, width), lambda i: (i, 0))


def run_kernel(body, steps, whole_in, step_in, outs, scratch, flops):
    in_specs = [whole(a) for a in whole_in] + [by_step(rows, a.shape[1]) for a, rows in step_in]
    out_specs = [
        by_step(rows, shape[1]) if rows else pl.BlockSpec(shape, lambda i, k=len(shape): (0,) * k)
        for shape, dtype, rows in outs
    ]
    return pl.pallas_call(
        body,
        grid=(steps,),
        in_specs=in_specs,
        out_specs=out_specs,
        out_shape=[jax.ShapeDtypeStruct(shape, dtype) for shape, dtype, rows in outs],
        scratch_shapes=scratch,
        compiler_params=pltpu.CompilerParams(
            dimension_semantics=("arbitrary",), vmem_limit_bytes=56 * 1024 * 1024
        ),
        cost_estimate=pl.CostEstimate(flops=flops, bytes_accessed=40 * 1024 * 1024, transcendentals=0),
    )(*whole_in, *[a for a, rows in step_in])


def score_masks(seq_len):
    key = jnp.arange(PAIR)[:, None]
    query = (jnp.arange(2 * PAIR) % PAIR)[None, :]
    pair = (key // PITCH == query // PITCH) & (key % PITCH < seq_len)
    key = jnp.arange(GROUP * PITCH)[:, None]
    column = (jnp.arange(HEADS * GROUP) % GROUP)[None, :]
    single = (key // PITCH == column) & (key % PITCH < seq_len)
    return [jnp.where(m, 0.0, NEVER).astype(jnp.float32) for m in (pair, single)]


def per_device(
    tokens,
    layer_gains,
    layer_shifts,
    w_qkv,
    b_qv,
    w_out,
    b_out,
    w_fc1,
    b_fc1,
    w_fc2,
    b_fc2,
    final_gain,
    final_shift,
    head_w1,
    head_b1,
    head_w2,
    head_b2,
    head_w3,
    head_b3,
    prototypes,
    crop_counts,
    teacher_logits,
    first_epoch,
):
    slot_count, seq_len, width = tokens.shape
    row_count = slot_count * seq_len
    scaling = HD ** (-0.5)
    devices = lax.axis_size("dp")
    proto_wide = prototypes.astype(jnp.float32)
    col_inv = lax.rsqrt(jnp.sum(proto_wide * proto_wide, axis=0) + EPS)
    unit_low = (proto_wide * col_inv).astype(jnp.bfloat16)
    unit_all = gather_any(unit_low.T, devices).reshape(-1, unit_low.shape[0])
    teach_expo = jnp.exp(teacher_logits * (1.0 / TEACHER_TEMP))
    teach_part = jnp.concatenate(
        [
            against(teach_expo.astype(jnp.bfloat16), unit_low),
            jnp.broadcast_to(jnp.sum(teach_expo, axis=1, keepdims=True), (teach_expo.shape[0], 128)),
        ],
        axis=1,
    )
    teach_sum = scatter_sum(
        teach_part.reshape(devices, -1, teach_part.shape[1]), devices, jnp.float32
    )
    live = (
        (jnp.arange(MOST_CROPS, dtype=jnp.int32)[None, :] < crop_counts[:, None])
        .astype(jnp.float32)
        .reshape(-1)
    )
    zero_bias = jnp.zeros((width,), jnp.float32)
    pair_mask, class_mask = score_masks(seq_len)
    gains = jnp.pad(layer_gains.reshape(4, width), ((0, 4), (0, 0)))
    shifts = jnp.pad(layer_shifts.reshape(4, width), ((0, 4), (0, 0)))
    full_bias = [jnp.concatenate([b_qv[l, :width], zero_bias, b_qv[l, width:]])[None] for l in range(2)]
    turned_tokens = tokens.transpose(1, 0, 2)
    steps = slot_count // GROUP
    rows = GROUP * PITCH
    padded = slot_count * PITCH
    hidden = w_fc1.shape[2]
    low, wide = jnp.bfloat16, jnp.float32
    qkv_a, attn_a, middle_a, act_a, slope_a, lower_out, kv_c, query_c, attn_c, first_low, first_in = run_kernel(
        forward_kernel,
        steps,
        [turned_tokens, pair_mask, class_mask, gains, shifts, w_qkv[0], full_bias[0], w_out[0], b_out[:1], w_fc1[0], b_fc1[:1], w_fc2[0], b_fc2[:1], w_qkv[1], full_bias[1]],
        [],
        [
            ((padded, 3 * width), low, rows),
            ((padded, width), low, rows),
            ((padded, width), wide, rows),
            ((padded, hidden), low, rows),
            ((padded, hidden), low, rows),
            ((padded, width), wide, rows),
            ((padded, 2 * width), low, rows),
            ((slot_count, width), wide, GROUP),
            ((slot_count, width), wide, GROUP),
            ((slot_count, width), wide, GROUP),
            ((slot_count, width), wide, GROUP),
        ],
        [
            pltpu.VMEM((width // 128, row_count, 128), wide),
            pltpu.VMEM((rows, width), wide),
            pltpu.VMEM((rows, width), low),
            pltpu.VMEM((rows, width), wide),
        ],
        12 * 10**9,
    )
    first_low = first_low.astype(low)
    attn_c_low = attn_c.astype(low)
    middle_c = first_in + product(attn_c_low, w_out[1]) + b_out[1]
    ln_d, normed_d, rstd_d = norm_forward(middle_c, layer_gains[1, 1], layer_shifts[1, 1])
    ln_d_low = ln_d.astype(jnp.bfloat16)
    pre_c = product(ln_d_low, w_fc1[1]) + b_fc1[1]
    act_c_low = smooth(pre_c).astype(jnp.bfloat16)
    class_out = middle_c + product(act_c_low, w_fc2[1]) + b_fc2[1]
    ln_f, normed_f, rstd_f = norm_forward(class_out, final_gain, final_shift)
    ln_f_low = ln_f.astype(jnp.bfloat16)
    hidden_one = product(ln_f_low, head_w1) + head_b1
    smooth_one = smooth(hidden_one).astype(jnp.bfloat16)
    hidden_two = product(smooth_one, head_w2) + head_b2
    smooth_two = smooth(hidden_two).astype(jnp.bfloat16)
    embedding = product(smooth_two, head_w3) + head_b3
    inv_length = lax.rsqrt(jnp.sum(embedding * embedding, axis=1, keepdims=True) + EPS)
    features = (embedding * inv_length).astype(jnp.bfloat16)
    all_features = gather_ordered(features, devices).reshape(-1, features.shape[1])
    logits = against(features, unit_all) * (1.0 / STUDENT_TEMP)
    expo = jnp.exp(logits - SHIFT)
    row_total = jnp.sum(expo, axis=1)
    own_live = lax.dynamic_slice_in_dim(live, lax.axis_index("dp") * slot_count, slot_count, 0)
    student_feat = product(expo.astype(jnp.bfloat16), unit_all) / row_total[:, None]
    teach_feat = teach_sum[:, : features.shape[1]] / teach_sum[:, features.shape[1] :][:, :1]
    grad_feat = (
        own_live[:, None]
        * (student_feat - jnp.repeat(teach_feat, MOST_CROPS, axis=0))
        * (1.0 / (STUDENT_TEMP * devices))
    )
    totals = gather_ordered(
        jnp.concatenate([row_total, teach_sum[:, features.shape[1]]])[None], devices
    ).reshape(devices, -1)
    all_row_total = totals[:, :slot_count].reshape(-1)
    all_teach_total = totals[:, slot_count:].reshape(-1)
    all_logits = product(all_features, unit_low) * (1.0 / STUDENT_TEMP)
    student_probs = jnp.exp(all_logits - SHIFT) / all_row_total[:, None]
    target = teach_expo / all_teach_total[:, None]
    images, local_cols = target.shape
    target_rows = jnp.broadcast_to(target[:, None], (images, MOST_CROPS, local_cols)).reshape(
        images * MOST_CROPS, local_cols
    )
    grad_raw = (
        live[:, None] * (student_probs - target_rows) * (1.0 / (STUDENT_TEMP * devices))
    ).astype(jnp.bfloat16)
    grad_unit = inner_rows(all_features, grad_raw)
    grad_proto = col_inv * grad_unit - proto_wide * col_inv**3 * jnp.sum(
        proto_wide * grad_unit, axis=0
    )
    prototypes_grad = grad_proto * (1 - first_epoch).astype(jnp.float32)[None, :]
    grad_embed = inv_length * grad_feat - embedding * inv_length**3 * jnp.sum(
        embedding * grad_feat, axis=1, keepdims=True
    )
    grad_embed_low = grad_embed.astype(jnp.bfloat16)
    grad_hb3 = column_sum(grad_embed_low)
    grad_hw3 = inner_rows(smooth_two, grad_embed_low)
    grad_hid2 = smooth_back(hidden_two, against(grad_embed_low, head_w3)).astype(jnp.bfloat16)
    grad_hb2 = column_sum(grad_hid2)
    grad_hw2 = inner_rows(smooth_one, grad_hid2)
    grad_hid1 = smooth_back(hidden_one, against(grad_hid2, head_w2)).astype(jnp.bfloat16)
    grad_hb1 = column_sum(grad_hid1)
    grad_hw1_turned = inner_rows(grad_hid1, ln_f_low)
    grad_class, grad_fgain, grad_fshift = norm_backward(
        against(grad_hid1, head_w1), normed_f, rstd_f, final_gain
    )
    head_parts = jnp.concatenate(
        [
            grad_hw1_turned.astype(jnp.bfloat16),
            grad_hw2.astype(jnp.bfloat16),
            grad_hw3.astype(jnp.bfloat16),
            jnp.broadcast_to(grad_hb1.astype(jnp.bfloat16)[:, None], (grad_hb1.shape[0], 128)),
            jnp.broadcast_to(grad_hb2.astype(jnp.bfloat16)[:, None], (grad_hb2.shape[0], 128)),
        ],
        axis=1,
    )
    head_sum = scatter_sum(
        head_parts.reshape(devices, -1, head_parts.shape[1]), devices, jnp.bfloat16
    ).astype(jnp.float32)
    hid = grad_hw2.shape[1]
    head_w1_grad = head_sum[:, :width].T
    head_w2_grad = head_sum[:, width : width + hid]
    head_w3_grad = head_sum[:, width + hid : width + hid + features.shape[1]]
    head_b1_grad = head_sum[:, width + hid + features.shape[1]]
    head_b2_grad = head_sum[:, width + hid + features.shape[1] + 128]
    grad_norm_d, grad_wfc1_c, grad_bfc1_c, grad_wfc2_c, grad_bfc2_c = mlp_back(
        grad_class, act_c_low, pre_c, ln_d_low, w_fc1[1], w_fc2[1]
    )
    grad_mid_in, grad_gain_d, grad_shift_d = norm_backward(
        grad_norm_d, normed_d, rstd_d, layer_gains[1, 1]
    )
    grad_middle_c = grad_class + grad_mid_in
    grad_attn_low = grad_middle_c.astype(jnp.bfloat16)
    grad_bout_c = column_sum(grad_attn_low)
    grad_wout_c = inner_rows(attn_c_low, grad_attn_low)
    grad_attended = against(grad_attn_low, w_out[1]).astype(low).astype(wide)
    grad_lower_out, grad_q_c, grad_kv_c, vec_c = run_kernel(
        upper_back_kernel,
        steps,
        [class_mask, gains, shifts, w_qkv[1]],
        [(lower_out, rows), (kv_c, rows), (query_c, GROUP), (grad_attended, GROUP), (grad_middle_c, GROUP)],
        [
            ((padded, width), wide, rows),
            ((slot_count, width), wide, GROUP),
            ((width, 2 * width), low, 0),
            ((8, 3 * width), wide, 0),
        ],
        [pltpu.VMEM((width, 2 * width), wide), pltpu.VMEM((rows, width), wide)],
        6 * 10**9,
    )
    grad_q_low = grad_q_c.astype(low)
    vec_c = jnp.sum(vec_c, axis=0)
    upper_parts = (
        jnp.stack([vec_c[width : 2 * width], grad_gain_d]),
        jnp.stack([vec_c[2 * width :], grad_shift_d]),
        jnp.concatenate([inner_rows(first_low, grad_q_low).astype(low), grad_kv_c], axis=1),
        jnp.concatenate([column_sum(grad_q_low), vec_c[:width]]),
        grad_wout_c,
        grad_bout_c,
        grad_wfc1_c,
        grad_bfc1_c,
        grad_wfc2_c,
        grad_bfc2_c,
    )
    grad_middle_a, grad_wfc1_a, grad_wfc2_a, vec_b, vec_hidden = run_kernel(
        mlp_back_kernel,
        steps,
        [gains, shifts, w_fc1[0], w_fc2[0]],
        [(grad_lower_out, rows), (middle_a, rows), (act_a, rows), (slope_a, rows)],
        [
            ((padded, width), wide, rows),
            ((width, hidden), low, 0),
            ((hidden, width), low, 0),
            ((8, 3 * width), wide, 0),
            ((8, hidden), wide, 0),
        ],
        [pltpu.VMEM((width, hidden), wide), pltpu.VMEM((width, hidden), wide), pltpu.VMEM((rows, hidden), low)],
        15 * 10**9,
    )
    grad_tokens, grad_wout_a, grad_qkv_a, vec_a = run_kernel(
        attend_back_kernel,
        steps,
        [turned_tokens, pair_mask, gains, shifts, w_qkv[0], w_out[0]],
        [(grad_middle_a, rows), (qkv_a, rows), (attn_a, rows)],
        [
            ((row_count, width), wide, 0),
            ((width, width), low, 0),
            ((width, 3 * width), low, 0),
            ((8, 6 * width), wide, 0),
        ],
        [
            pltpu.VMEM((width // 128, row_count, 128), wide),
            pltpu.VMEM((width // 128, row_count, 128), wide),
            pltpu.VMEM((rows, width), wide),
            pltpu.VMEM((width, width), wide),
            pltpu.VMEM((width, 3 * width), wide),
            pltpu.VMEM((rows, width), low),
            pltpu.VMEM((rows, 3 * width), low),
        ],
        10 * 10**9,
    )
    tokens_grad = grad_tokens.reshape(seq_len, slot_count, width).transpose(1, 0, 2)
    vec_a, vec_b, vec_hidden = jnp.sum(vec_a, axis=0), jnp.sum(vec_b, axis=0), jnp.sum(vec_hidden, axis=0)
    lower_parts = (
        jnp.stack([vec_a[4 * width : 5 * width], vec_b[width : 2 * width]]),
        jnp.stack([vec_a[5 * width :], vec_b[2 * width :]]),
        grad_qkv_a,
        jnp.concatenate([vec_a[width : 2 * width], vec_a[3 * width : 4 * width]]),
        grad_wout_a,
        vec_a[:width],
        grad_wfc1_a,
        vec_hidden,
        grad_wfc2_a,
        vec_b[:width],
    )

    def bulk(parts):
        return sum_all(
            jnp.concatenate(
                [
                    parts[2].T.astype(jnp.bfloat16),
                    parts[4].astype(jnp.bfloat16),
                    parts[6].T.astype(jnp.bfloat16),
                    parts[8].astype(jnp.bfloat16),
                ]
            ),
            devices,
        ).astype(jnp.float32)

    def small(parts):
        return [parts[0], parts[1], parts[3].reshape(-1, width), parts[5][None], parts[7].reshape(-1, width), parts[9][None]]

    upper_bulk, lower_bulk = bulk(upper_parts), bulk(lower_parts)
    vectors = small(lower_parts) + small(upper_parts) + [grad_fgain[None], grad_fshift[None], jnp.pad(grad_hb3, (0, width - grad_hb3.shape[0]))[None]]
    summed = sum_small(jnp.concatenate(vectors), devices)
    cuts = [0]
    for item in vectors:
        cuts.append(cuts[-1] + item.shape[0])
    pieces = [summed[cuts[i] : cuts[i + 1]] for i in range(len(vectors))]
    both = lambda i: jnp.stack([pieces[i], pieces[i + 6]])
    marks = (0, 3 * width, 4 * width, 4 * width + hidden, 4 * width + 2 * hidden)
    bulk_of = lambda i: [part[marks[i] : marks[i + 1]] for part in (lower_bulk, upper_bulk)]
    return (
        tokens_grad,
        both(0),
        both(1),
        jnp.stack([part.T for part in bulk_of(0)]),
        both(2).reshape(2, -1),
        jnp.stack(bulk_of(1)),
        both(3).reshape(2, -1),
        jnp.stack([part.T for part in bulk_of(2)]),
        both(4).reshape(2, -1),
        jnp.stack(bulk_of(3)),
        both(5).reshape(2, -1),
        summed[cuts[12]],
        summed[cuts[13]],
        head_w1_grad,
        head_b1_grad,
        head_w2_grad,
        head_b2_grad,
        head_w3_grad,
        summed[cuts[14], : grad_hb3.shape[0]],
        prototypes_grad,
    )


def solution(mesh):
    return jax.shard_map(
        per_device,
        mesh=mesh,
        in_specs=(
            P("dp", None, None),
            P(),
            P(),
            P(),
            P(),
            P(),
            P(),
            P(),
            P(),
            P(),
            P(),
            P(),
            P(),
            P(),
            P(),
            P(),
            P(),
            P(),
            P(),
            P(None, "dp"),
            P(),
            P(None, "dp"),
            P("dp"),
        ),
        out_specs=(
            P("dp", None, None),
            P(),
            P(),
            P(),
            P(),
            P(),
            P(),
            P(),
            P(),
            P(),
            P(),
            P(),
            P(),
            P(None, "dp"),
            P("dp"),
            P("dp", None),
            P("dp"),
            P("dp", None),
            P(),
            P(None, "dp"),
        ),
        check_vma=False,
    )
```

```python
import functools

import jax
import jax.numpy as jnp
from jax import lax
from jax.experimental import pallas as pl
from jax.experimental.pallas import tpu as pltpu
from jax.sharding import PartitionSpec as P

HEADS = 6
HD = 64
MOST_CROPS = 10

STUDENT_TEMP = 0.1
TEACHER_TEMP = 0.04
EPS = 1e-06
SHIFT = 10.0


def product(left, right):
    return jnp.dot(left, right, preferred_element_type=jnp.float32)


def against(left, right):
    return lax.dot_general(
        left, right, (((1,), (1,)), ((), ())), preferred_element_type=jnp.float32
    )


def inner_rows(left, right):
    return lax.dot_general(
        left, right, (((0,), (0,)), ((), ())), preferred_element_type=jnp.float32
    )


def column_sum(values):
    return jnp.sum(values.astype(jnp.float32), axis=0)


def norm_forward(values, gain, shift):
    centered = values - jnp.mean(values, axis=-1, keepdims=True)
    rstd = lax.rsqrt(jnp.mean(centered * centered, axis=-1, keepdims=True) + EPS)
    normed = centered * rstd
    return (normed * gain + shift, normed, rstd)


def norm_backward(grad, normed, rstd, gain):
    scaled = grad * gain
    inner = (
        scaled
        - jnp.mean(scaled, axis=-1, keepdims=True)
        - normed * jnp.mean(scaled * normed, axis=-1, keepdims=True)
    )
    return (rstd * inner, jnp.sum(grad * normed, axis=0), jnp.sum(grad, axis=0))


GROUP = 8
BLOCKS = 32
PITCH = 40
PAIR = 2 * PITCH
NEVER = -1e30


def smooth_both(values):
    size = jnp.abs(values)
    bell = jnp.exp(values * values * -0.5)
    t = 1.0 / (1.0 + 0.23164189 * size)
    tail = t * (0.127414796 + t * (-0.142248368 + t * (0.7107068705 + t * (-0.7265760135 + t * 0.5307027145))))
    upper = tail * bell
    area = jnp.where(values >= 0, 1.0 - upper, upper)
    return values * area, area + values * (bell * 0.3989422804014327)


def standardize(values):
    centered = values - jnp.mean(values, axis=-1, keepdims=True)
    rstd = lax.rsqrt(jnp.mean(centered * centered, axis=-1, keepdims=True) + EPS)
    return centered * rstd, rstd


def standard_back(grad, normed, rstd, gain):
    scaled = grad * gain
    return rstd * (
        scaled
        - jnp.mean(scaled, axis=-1, keepdims=True)
        - normed * jnp.mean(scaled * normed, axis=-1, keepdims=True)
    )


def fold_rows(values):
    return jnp.sum(values.reshape(-1, 8, values.shape[1]), axis=0)


def both_heads(values):
    lane = lax.broadcasted_iota(jnp.int32, values.shape, 1)
    zero = jnp.zeros_like(values)
    return jnp.concatenate([jnp.where(lane < HD, values, zero), jnp.where(lane < HD, zero, values)])


def join_heads(values):
    rows = values.shape[0] // 2
    lane = lax.broadcasted_iota(jnp.int32, (rows, values.shape[1]), 1)
    return jnp.where(lane < HD, values[:rows], values[rows:])


def spread_heads(values):
    lane = lax.broadcasted_iota(jnp.int32, values.shape, 1) // HD
    return jnp.concatenate([jnp.where(lane == h, values, 0.0) for h in range(HEADS)])


def gather_heads(values):
    lane = lax.broadcasted_iota(jnp.int32, (GROUP, values.shape[1]), 1) // HD
    out = jnp.zeros((GROUP, values.shape[1]), values.dtype)
    for h in range(HEADS):
        out = jnp.where(lane == h, values[h * GROUP : (h + 1) * GROUP], out)
    return out


def soft_columns(scores):
    expo = jnp.exp(scores - jnp.max(scores, axis=0, keepdims=True))
    return expo * (1.0 / jnp.sum(expo, axis=0, keepdims=True))


def take_slots(all_ref, rows_ref, step, seq_len, slots):
    for s in range(GROUP):
        for c in range(all_ref.shape[0]):
            rows_ref[s * PITCH : s * PITCH + seq_len, c * 128 : (c + 1) * 128] = all_ref[
                c, pl.ds(step * GROUP + s, seq_len, stride=slots), :
            ]


def first_rows(ref):
    return jnp.concatenate([ref[s * PITCH : s * PITCH + 1, :] for s in range(GROUP)])


def add_first_rows(ref, values):
    for s in range(GROUP):
        ref[s * PITCH : s * PITCH + 1, :] += values[s : s + 1]


def widen_tokens(tok_ref, all_ref):
    seq_len, slots, width = tok_ref.shape

    @pl.loop(0, seq_len)
    def _(t):
        wide = tok_ref[t].astype(jnp.float32)
        for c in range(all_ref.shape[0]):
            all_ref[c, pl.ds(pl.multiple_of(t * slots, 8), slots), :] = wide[:, c * 128 : (c + 1) * 128]


def ordered_masks():
    return [(p >> 4) | (((p >> 2) & 3) << 1) | ((p & 3) << 3) for p in range(BLOCKS)]


def write_unit(me, keep_ref, send_ref, unit, read):
    for p, mask in enumerate(ordered_masks()):
        owner = me ^ mask
        ref = keep_ref if p < BLOCKS // 2 else send_ref
        ref[p % (BLOCKS // 2), unit] = read(owner)


def from_square(ref, first=0):
    width = ref.shape[0]

    def read(owner):
        rows = pl.multiple_of((owner // 4) * (width // 8), 16)
        cols = pl.multiple_of((owner % 4) * width, 128)
        return ref[pl.ds(rows, width // 8), pl.ds(cols, width)].astype(jnp.bfloat16)

    return read


def from_tall(ref):
    size = ref.shape[0] // BLOCKS

    def read(owner):
        return ref[pl.ds(pl.multiple_of(owner * size, 16), size), :].astype(jnp.bfloat16)

    return read


def attend_kernel(
    tok_ref, pair_mask_ref, gains_ref, shifts_ref, w_qkv_ref, b_qkv_ref, w_out_ref, b_out_ref,
    qkv_ref, o_ref, mid_ref,
    all_ref, x_ref, low_ref,
):
    step = pl.program_id(0)
    seq_len, slots, width = tok_ref.shape
    rows = GROUP * PITCH
    chunk = PAIR

    @pl.when(step == 0)
    def _():
        widen_tokens(tok_ref, all_ref)
        x_ref[...] = jnp.zeros_like(x_ref)

    take_slots(all_ref, x_ref, step, seq_len, slots)
    for r in range(0, rows, chunk):
        normed, _ = standardize(x_ref[r : r + chunk, :])
        low_ref[r : r + chunk, :] = (normed * gains_ref[0:1, :] + shifts_ref[0:1, :]).astype(jnp.bfloat16)
    for j in range(3):
        cols = slice(j * width, (j + 1) * width)
        part = product(low_ref[...], w_qkv_ref[:, cols]) + b_qkv_ref[:, cols]
        if j == 0:
            part = part.astype(jnp.bfloat16) * jnp.bfloat16(HD ** -0.5)
        qkv_ref[:, cols] = part.astype(jnp.bfloat16)
    for r in range(0, rows, PAIR):
        for c in range(0, width, 2 * HD):
            keys = qkv_ref[r : r + PAIR, width + c : width + c + 2 * HD]
            values = qkv_ref[r : r + PAIR, 2 * width + c : 2 * width + c + 2 * HD]
            queries = both_heads(qkv_ref[r : r + PAIR, c : c + 2 * HD])
            probs = soft_columns(against(keys, queries) + pair_mask_ref[...]).astype(jnp.bfloat16)
            o_ref[r : r + PAIR, c : c + 2 * HD] = join_heads(inner_rows(probs, values)).astype(jnp.bfloat16)
    mixed = product(o_ref[...], w_out_ref[...])
    for r in range(0, rows, chunk):
        part = x_ref[r : r + chunk, :] + mixed[r : r + chunk] + b_out_ref[...]
        mid_ref[r : r + chunk, :] = part


def mlp_kernel(
    class_mask_ref, gains_ref, shifts_ref, w_fc1_ref, b_fc1_ref, w_fc2_ref, b_fc2_ref, w_up_ref, b_up_ref, mid_ref,
    act_ref, slope_ref, x1_ref, kv_ref, cq_ref, co_ref, ch_ref, cx_ref,
    low_ref, wide_ref,
):
    rows, width = mid_ref.shape
    hidden = w_fc1_ref.shape[1]
    chunk = PAIR
    for r in range(0, rows, chunk):
        normed, _ = standardize(mid_ref[r : r + chunk, :])
        low_ref[r : r + chunk, :] = (normed * gains_ref[1:2, :] + shifts_ref[1:2, :]).astype(jnp.bfloat16)
    for c in range(0, hidden, 256):
        pre = product(low_ref[...], w_fc1_ref[:, c : c + 256])
        for r in range(0, rows, 32):
            act, slope = smooth_both(pre[r : r + 32] + b_fc1_ref[:, c : c + 256])
            act_ref[r : r + 32, c : c + 256] = act.astype(jnp.bfloat16)
            slope_ref[r : r + 32, c : c + 256] = slope.astype(jnp.bfloat16)
    mixed = product(act_ref[...], w_fc2_ref[...])
    for r in range(0, rows, chunk):
        part = mid_ref[r : r + chunk, :] + mixed[r : r + chunk] + b_fc2_ref[...]
        x1_ref[r : r + chunk, :] = part
        normed, _ = standardize(part)
        wide = normed * gains_ref[2:3, :] + shifts_ref[2:3, :]
        wide_ref[r : r + chunk, :] = wide
        low_ref[r : r + chunk, :] = wide.astype(jnp.bfloat16)
    for j in range(2):
        cols = slice(j * width, (j + 1) * width)
        ups = slice((j + 1) * width, (j + 2) * width)
        kv_ref[:, cols] = (product(low_ref[...], w_up_ref[:, ups]) + b_up_ref[:, ups]).astype(jnp.bfloat16)
    cx_ref[...] = first_rows(x1_ref)
    first = first_rows(wide_ref).astype(jnp.bfloat16)
    ch_ref[...] = first.astype(jnp.float32)
    query = (product(first, w_up_ref[:, :width]) + b_up_ref[:, :width]).astype(jnp.bfloat16).astype(jnp.float32) * HD ** -0.5
    cq_ref[...] = query
    spread = spread_heads(query).astype(jnp.bfloat16)
    probs = soft_columns(against(kv_ref[:, :width], spread) + class_mask_ref[...]).astype(jnp.bfloat16)
    co_ref[...] = gather_heads(inner_rows(probs, kv_ref[:, width:]))


def upper_back_kernel(
    class_mask_ref, gains_ref, shifts_ref, w_up_ref, ch_ref, co_ref, da_ref,
    x1_ref, kv_ref, cq_ref, cg_ref, cres_ref,
    dx_ref, unit_ref, vec_ref,
    acc_ref, wide_ref, dqs_ref,
):
    step = pl.program_id(0)
    rows, width = x1_ref.shape

    @pl.when(step == 0)
    def _():
        acc_ref[...] = jnp.zeros_like(acc_ref)
        vec_ref[...] = jnp.zeros_like(vec_ref)

    keys, values = kv_ref[:, :width], kv_ref[:, width:]
    spread = spread_heads(cq_ref[...]).astype(jnp.bfloat16)
    grads = spread_heads(cg_ref[...]).astype(jnp.bfloat16)
    probs = soft_columns(against(keys, spread) + class_mask_ref[...])
    back = against(values, grads)
    inner = (probs * (back - jnp.sum(back * probs, axis=0, keepdims=True))).astype(jnp.bfloat16)
    grad_values = product(probs.astype(jnp.bfloat16), grads).astype(jnp.bfloat16)
    grad_keys = product(inner, spread).astype(jnp.bfloat16)
    grad_query = (gather_heads(inner_rows(inner, keys)) * HD ** -0.5).astype(jnp.bfloat16)
    dqs_ref[pl.ds(pl.multiple_of(step * GROUP, GROUP), GROUP), :] = grad_query.astype(jnp.float32)
    vec_ref[:, 3 * width :] += fold_rows(grad_query.astype(jnp.float32))
    vec_ref[:, :width] += fold_rows(grad_values.astype(jnp.float32))
    wide_ref[...] = against(grad_keys, w_up_ref[:, width : 2 * width]) + against(grad_values, w_up_ref[:, 2 * width :])
    add_first_rows(wide_ref, against(grad_query, w_up_ref[:, :width]))
    chunk = PAIR
    parts = []
    for r in range(0, rows, chunk):
        normed, rstd = standardize(x1_ref[r : r + chunk, :])
        parts.append((normed * gains_ref[2:3, :] + shifts_ref[2:3, :]).astype(jnp.bfloat16))
        grad = wide_ref[r : r + chunk, :]
        vec_ref[:, width : 2 * width] += fold_rows(grad * normed)
        vec_ref[:, 2 * width : 3 * width] += fold_rows(grad)
        dx_ref[r : r + chunk, :] = standard_back(grad, normed, rstd, gains_ref[2:3, :])
    turned = jnp.concatenate(parts).T
    acc_ref[:, width : 2 * width] += product(turned, grad_keys)
    acc_ref[:, 2 * width : 3 * width] += product(turned, grad_values)
    add_first_rows(dx_ref, cres_ref[...])

    @pl.when(step == pl.num_programs(0) - 1)
    def _():
        acc_ref[:, :width] = inner_rows(
            ch_ref[...].astype(jnp.bfloat16), dqs_ref[...].astype(jnp.bfloat16)
        )
        acc_ref[:, 3 * width :] = inner_rows(co_ref[...].astype(jnp.bfloat16), da_ref[...].astype(jnp.bfloat16))
        unit_ref[...] = acc_ref[...].astype(jnp.bfloat16)


def mlp_back_kernel(
    me_ref, unit_ref, up1_ref, up2_ref, gains_ref, shifts_ref, w_fc1_ref, w_fc2_ref, dx_ref, mid_ref, act_ref, slope_ref,
    dmid_ref, keep_ref, send_ref, vec_ref, vec1_ref,
    acc1_ref, acc2_ref, dz_ref, big_ref,
):
    step = pl.program_id(0)
    rows, width = dx_ref.shape
    hidden = act_ref.shape[1]

    @pl.when(step == 0)
    def _():
        acc1_ref[...] = jnp.zeros_like(acc1_ref)
        acc2_ref[...] = jnp.zeros_like(acc2_ref)
        vec_ref[...] = jnp.zeros_like(vec_ref)
        vec1_ref[...] = jnp.zeros_like(vec1_ref)

    low = dx_ref[...].astype(jnp.bfloat16)
    vec_ref[:, :width] += fold_rows(low.astype(jnp.float32))
    low_turned = low.T
    chunk = PAIR
    parts = []
    for r in range(0, rows, chunk):
        normed, _ = standardize(mid_ref[r : r + chunk, :])
        parts.append((normed * gains_ref[1:2, :] + shifts_ref[1:2, :]).astype(jnp.bfloat16))
    norm_turned = jnp.concatenate(parts).T
    for c in range(0, hidden, 256):
        cols = slice(c, c + 256)
        back = against(low, w_fc2_ref[cols, :])
        for r in range(0, rows, chunk):
            part = (back[r : r + chunk] * slope_ref[r : r + chunk, cols].astype(jnp.float32)).astype(jnp.bfloat16)
            dz_ref[r : r + chunk, cols] = part
            vec1_ref[:, cols] += fold_rows(part.astype(jnp.float32))
        acc1_ref[:, cols] += product(norm_turned, dz_ref[:, cols])
        acc2_ref[:, cols] += product(low_turned, act_ref[:, cols])
    mixed = against(dz_ref[...], w_fc1_ref[...])
    for r in range(0, rows, chunk):
        normed, rstd = standardize(mid_ref[r : r + chunk, :])
        grad = mixed[r : r + chunk]
        vec_ref[:, width : 2 * width] += fold_rows(grad * normed)
        vec_ref[:, 2 * width : 3 * width] += fold_rows(grad)
        dmid_ref[r : r + chunk, :] = dx_ref[r : r + chunk, :] + standard_back(grad, normed, rstd, gains_ref[1:2, :])

    @pl.when(step == pl.num_programs(0) - 1)
    def _():
        me = me_ref[0]
        write_unit(me, keep_ref, send_ref, 0, from_square(unit_ref))
        write_unit(me, keep_ref, send_ref, 1, from_square(acc1_ref))
        big_ref[...] = acc2_ref[...].T
        write_unit(me, keep_ref, send_ref, 2, from_tall(big_ref))
        write_unit(me, keep_ref, send_ref, 3, from_square(up1_ref))
        write_unit(me, keep_ref, send_ref, 4, from_tall(up2_ref))


def attend_back_kernel(
    pair_mask_ref, w_out_ref, dmid_ref, qkv_ref, o_ref,
    dqkv_ref, dwo_ref, vec_ref,
    do_ref,
):
    step = pl.program_id(0)
    rows, width = dmid_ref.shape

    @pl.when(step == 0)
    def _():
        dwo_ref[...] = jnp.zeros_like(dwo_ref)
        vec_ref[...] = jnp.zeros_like(vec_ref)

    low = dmid_ref[...].astype(jnp.bfloat16)
    vec_ref[:, :width] += fold_rows(low.astype(jnp.float32))
    do_ref[...] = against(low, w_out_ref[...]).astype(jnp.bfloat16)
    dwo_ref[...] += product(o_ref[...].T, low)
    for r in range(0, rows, PAIR):
        for c in range(0, width, 2 * HD):
            keys = qkv_ref[r : r + PAIR, width + c : width + c + 2 * HD]
            values = qkv_ref[r : r + PAIR, 2 * width + c : 2 * width + c + 2 * HD]
            queries = both_heads(qkv_ref[r : r + PAIR, c : c + 2 * HD])
            grads = both_heads(do_ref[r : r + PAIR, c : c + 2 * HD])
            probs = soft_columns(against(keys, queries) + pair_mask_ref[...])
            back = against(values, grads)
            inner = (probs * (back - jnp.sum(back * probs, axis=0, keepdims=True))).astype(jnp.bfloat16)
            dqkv_ref[r : r + PAIR, 2 * width + c : 2 * width + c + 2 * HD] = product(
                probs.astype(jnp.bfloat16), grads
            ).astype(jnp.bfloat16)
            dqkv_ref[r : r + PAIR, width + c : width + c + 2 * HD] = product(inner, queries).astype(jnp.bfloat16)
            dqkv_ref[r : r + PAIR, c : c + 2 * HD] = (
                join_heads(inner_rows(inner, keys)) * HD ** -0.5
            ).astype(jnp.bfloat16)
    for j in range(3):
        cols = slice(j * width, (j + 1) * width)
        vec_ref[:, (j + 1) * width : (j + 2) * width] += fold_rows(dqkv_ref[:, cols].astype(jnp.float32))


def weight_back_kernel(
    me_ref, tok_ref, gains_ref, shifts_ref, dwo_ref, dqkv_ref,
    keep_ref, send_ref,
    all_ref, x_ref, acc_ref,
):
    step = pl.program_id(0)
    seq_len, slots, width = tok_ref.shape
    rows = GROUP * PITCH

    @pl.when(step == 0)
    def _():
        widen_tokens(tok_ref, all_ref)
        x_ref[...] = jnp.zeros_like(x_ref)
        acc_ref[:, : 3 * width] = jnp.zeros((width, 3 * width), jnp.float32)
        acc_ref[:, 3 * width :] = dwo_ref[...]

    take_slots(all_ref, x_ref, step, seq_len, slots)
    chunk = PAIR
    parts = []
    for r in range(0, rows, chunk):
        normed, _ = standardize(x_ref[r : r + chunk, :])
        parts.append((normed * gains_ref[0:1, :] + shifts_ref[0:1, :]).astype(jnp.bfloat16))
    turned = jnp.concatenate(parts).T
    for j in range(3):
        cols = slice(j * width, (j + 1) * width)
        acc_ref[:, cols] += product(turned, dqkv_ref[:, cols])

    @pl.when(step == pl.num_programs(0) - 1)
    def _():
        write_unit(me_ref[0], keep_ref, send_ref, 0, from_square(acc_ref))


def input_back_kernel(
    tok_ref, gains_ref, w_qkv_ref, dmid_ref, dqkv_ref,
    dtok_ref, vec_ref,
    all_ref, out_ref, x_ref,
):
    step = pl.program_id(0)
    seq_len, slots, width = tok_ref.shape
    rows = GROUP * PITCH

    @pl.when(step == 0)
    def _():
        widen_tokens(tok_ref, all_ref)
        x_ref[...] = jnp.zeros_like(x_ref)
        vec_ref[...] = jnp.zeros_like(vec_ref)

    take_slots(all_ref, x_ref, step, seq_len, slots)
    chunk = PAIR
    mixed = against(dqkv_ref[...], w_qkv_ref[...])
    for r in range(0, rows, chunk):
        normed, rstd = standardize(x_ref[r : r + chunk, :])
        grad = mixed[r : r + chunk]
        vec_ref[:, :width] += fold_rows(grad * normed)
        vec_ref[:, width:] += fold_rows(grad)
        part = dmid_ref[r : r + chunk, :] + standard_back(grad, normed, rstd, gains_ref[0:1, :])
        for s in range(chunk // PITCH):
            for t in range(all_ref.shape[0]):
                out_ref[t, pl.ds(step * GROUP + r // PITCH + s, seq_len, stride=slots), :] = part[
                    s * PITCH : s * PITCH + seq_len, t * 128 : (t + 1) * 128
                ]

    @pl.when(step == pl.num_programs(0) - 1)
    def _():
        for t in range(out_ref.shape[0]):
            dtok_ref[:, t * 128 : (t + 1) * 128] = out_ref[t]


def unpack_kernel(
    me_ref, mlp_ref, attend_ref,
    qkv_ref, out_ref, fc1_ref, fc2_ref,
):
    step = pl.program_id(0)
    width = mlp_ref.shape[3]
    size = mlp_ref.shape[2]
    for c in range(4):
        mask = (step * 4 + c) ^ me_ref[0]
        place = ((mask & 1) << 4) | (((mask >> 1) & 3) << 2) | ((mask >> 3) & 3)
        cols = slice(c * width, (c + 1) * width)
        lower, upper = attend_ref[place, 0].astype(jnp.float32), mlp_ref[place, 0].astype(jnp.float32)
        if c < 3:
            qkv_ref[0, :, cols] = lower
            qkv_ref[1, :, cols] = upper
        else:
            out_ref[0] = lower
            out_ref[1] = upper
        fc1_ref[0, :, cols] = mlp_ref[place, 1].astype(jnp.float32)
        fc2_ref[0, c * size : (c + 1) * size, :] = mlp_ref[place, 2].astype(jnp.float32)
        fc1_ref[1, :, cols] = mlp_ref[place, 3].astype(jnp.float32)
        fc2_ref[1, c * size : (c + 1) * size, :] = mlp_ref[place, 4].astype(jnp.float32)


def prepare_kernel(
    proto_ref, teacher_ref,
    unit_ref, turned_ref, inv_ref, teach_ref, expo_ref,
):
    proto = proto_ref[...].astype(jnp.float32)
    inv = lax.rsqrt(jnp.sum(proto * proto, axis=0, keepdims=True) + EPS)
    inv_ref[...] = inv
    unit = (proto * inv).astype(jnp.bfloat16)
    unit_ref[...] = unit
    turned_ref[...] = unit.T
    bottle = proto.shape[0]
    images = teacher_ref.shape[0]
    for r in range(0, images, 64):
        expo = jnp.exp(teacher_ref[r : r + 64, :] * (1.0 / TEACHER_TEMP))
        expo_ref[r : r + 64, :] = expo
        teach_ref[r : r + 64, :bottle] = against(expo.astype(jnp.bfloat16), unit)
        teach_ref[r : r + 64, bottle:] = jnp.broadcast_to(jnp.sum(expo, axis=1, keepdims=True), (64, 128))


def repeat_rows(values):
    count = values.shape[0]
    image = lax.broadcasted_iota(jnp.int32, (count * MOST_CROPS, values.shape[1]), 0) // MOST_CROPS
    out = jnp.zeros((count * MOST_CROPS, values.shape[1]), values.dtype)
    for i in range(count):
        out = jnp.where(image == i, values[i : i + 1], out)
    return out


def three_parts(values):
    high = values.astype(jnp.bfloat16).astype(jnp.float32)
    middle = (values - high).astype(jnp.bfloat16).astype(jnp.float32)
    return [high, middle, values - high - middle]


def head_kernel(
    scale, own_columns, live_ref, teach_ref, co_ref, cx_ref, gains_ref, shifts_ref, final_ref,
    w_out_ref, b_out_ref, w_fc1_ref, b_fc1_ref, w_fc2_ref, b_fc2_ref,
    w1_ref, b1_ref, w2_ref, b2_ref, w3_ref, b3_ref, unit_ref,
    cg_ref, cres_ref, da_ref, common_ref, feats_ref, share_ref, up1_ref, up2_ref, vec_ref,
    act_ref, slope_ref, slope1_ref, slope2_ref, one_ref, two_ref, back_ref,
):
    width = cx_ref.shape[1]
    hidden = w_fc1_ref.shape[1]
    hid, bottle = w3_ref.shape
    low = jnp.bfloat16
    middle = cx_ref[...] + product(co_ref[...].astype(low), w_out_ref[...]) + b_out_ref[...]
    normed_d, rstd_d = standardize(middle)
    low_d = (normed_d * gains_ref[3:4, :] + shifts_ref[3:4, :]).astype(low)
    for c in range(0, hidden, 256):
        cols = slice(c, c + 256)
        act, slope = smooth_both(product(low_d, w_fc1_ref[:, cols]) + b_fc1_ref[:, cols])
        act_ref[:, cols] = act.astype(low)
        slope_ref[:, cols] = slope
    def share(kind, c, values):
        for u in range(256 // (4 * own_columns)):
            for j in range(4):
                start = kind * (hid // 4) + c // 4 + u * own_columns
                share_ref[j, :, start : start + own_columns] = values[
                    :, (u * 4 + j) * own_columns : (u * 4 + j + 1) * own_columns
                ]

    out = middle + product(act_ref[...], w_fc2_ref[...]) + b_fc2_ref[...]
    normed_f, rstd_f = standardize(out)
    low_f = (normed_f * final_ref[0:1, :] + final_ref[1:2, :]).astype(low)
    common_ref[:, hid : hid + width] = low_f
    for c in range(0, hid, 256):
        cols = slice(c, c + 256)
        act, slope = smooth_both(product(low_f, w1_ref[:, cols]) + b1_ref[:, cols])
        one_ref[:, cols] = act.astype(low)
        share(0, c, act.astype(low))
        slope1_ref[:, cols] = slope
    first = one_ref[...]
    for c in range(0, hid, 256):
        cols = slice(c, c + 256)
        act, slope = smooth_both(product(first, w2_ref[:, cols]) + b2_ref[:, cols])
        two_ref[:, cols] = act.astype(low)
        share(1, c, act.astype(low))
        slope2_ref[:, cols] = slope
    embed = product(two_ref[...], w3_ref[...]) + b3_ref[...]
    inv = lax.rsqrt(jnp.sum(embed * embed, axis=1, keepdims=True) + EPS)
    feats = (embed * inv).astype(low)
    slots = feats.shape[0]
    total = jnp.zeros((slots, 1), jnp.float32)
    student = jnp.zeros((slots, bottle), jnp.float32)
    total_protos = unit_ref.shape[0]
    size = 512

    def some(i, carry):
        total, student = carry
        part = unit_ref[pl.ds(pl.multiple_of(i * size, size), size), :]
        expo = jnp.exp(against(feats, part) * (1.0 / STUDENT_TEMP) - SHIFT)
        return (
            total + jnp.sum(expo, axis=1, keepdims=True),
            student + product(expo.astype(low), part),
        )

    total, student = lax.fori_loop(0, total_protos // size, some, (total, student), unroll=4)
    teach_total = teach_ref[:, bottle : bottle + 128]
    teach = repeat_rows(teach_ref[:, :bottle] * (1.0 / teach_total[:, :1]))
    grad_feat = live_ref[...] * (student * (1.0 / total) - teach) * scale
    logs = [live_ref[...]] + three_parts(SHIFT + jnp.log(total)) + three_parts(repeat_rows(jnp.log(teach_total))[:, :1])
    lane = lax.broadcasted_iota(jnp.int32, (slots, 128), 1)
    extra = jnp.zeros((slots, 128), jnp.float32)
    for i, part in enumerate(logs):
        extra = jnp.where(lane == i, part, extra)
    feats_ref[:, :bottle] = feats
    feats_ref[:, bottle:] = extra.astype(low)
    grad_embed = inv * grad_feat - embed * (inv * inv * inv) * jnp.sum(embed * grad_feat, axis=1, keepdims=True)
    grad_embed = grad_embed.astype(low)
    common_ref[:, hid + width :] = grad_embed
    vec_ref[...] = jnp.zeros_like(vec_ref)
    vec_ref[:, 6 * width + hidden : 6 * width + hidden + bottle] = fold_rows(grad_embed.astype(jnp.float32))
    for c in range(0, hid, 256):
        cols = slice(c, c + 256)
        grad = (slope2_ref[:, cols] * against(grad_embed, w3_ref[cols, :])).astype(low)
        common_ref[:, cols] = grad
        vec_ref[:, 7 * width + hidden + hid + c : 7 * width + hidden + hid + c + 256] = fold_rows(grad.astype(jnp.float32))
    grad_two = common_ref[:, :hid]
    for c in range(0, hid, 256):
        cols = slice(c, c + 256)
        grad = (slope1_ref[:, cols] * against(grad_two, w2_ref[cols, :])).astype(low)
        back_ref[:, cols] = grad
        vec_ref[:, 7 * width + hidden + c : 7 * width + hidden + c + 256] = fold_rows(grad.astype(jnp.float32))
        share(2, c, grad)
    grad = against(back_ref[...], w1_ref[...])
    vec_ref[:, 4 * width : 5 * width] = fold_rows(grad * normed_f)
    vec_ref[:, 5 * width : 6 * width] = fold_rows(grad)
    grad_class = standard_back(grad, normed_f, rstd_f, final_ref[0:1, :])
    grad_low = grad_class.astype(low)
    vec_ref[:, 3 * width : 4 * width] = fold_rows(grad_low.astype(jnp.float32))
    up2_ref[...] = inner_rows(act_ref[...], grad_low).astype(low)
    for c in range(0, hidden, 256):
        cols = slice(c, c + 256)
        grad = (slope_ref[:, cols] * against(grad_low, w_fc2_ref[cols, :])).astype(low)
        act_ref[:, cols] = grad
        vec_ref[:, 6 * width + c : 6 * width + c + 256] = fold_rows(grad.astype(jnp.float32))
    grad_pre = act_ref[...]
    up1_ref[...] = inner_rows(low_d, grad_pre).astype(low)
    grad = against(grad_pre, w_fc1_ref[...])
    vec_ref[:, :width] = fold_rows(grad * normed_d)
    vec_ref[:, width : 2 * width] = fold_rows(grad)
    grad_middle = grad_class + standard_back(grad, normed_d, rstd_d, gains_ref[3:4, :])
    cres_ref[...] = grad_middle
    grad_low = grad_middle.astype(low)
    da_ref[...] = grad_low.astype(jnp.float32)
    vec_ref[:, 2 * width : 3 * width] = fold_rows(grad_low.astype(jnp.float32))
    cg_ref[...] = against(grad_low, w_out_ref[...]).astype(low).astype(jnp.float32)


def head_sum_kernel(
    width, common0_ref, common1_ref, common2_ref, common3_ref, share0_ref, share1_ref, share2_ref, share3_ref,
    parts_ref,
):
    quarter = share0_ref.shape[1] // 3
    full = quarter * 4
    share = jnp.concatenate([ref[...] for ref in (share0_ref, share1_ref, share2_ref, share3_ref)])
    common = jnp.concatenate([ref[...] for ref in (common0_ref, common1_ref, common2_ref, common3_ref)])
    low = jnp.bfloat16
    parts = [share[:, i * quarter : (i + 1) * quarter].T for i in range(3)]
    parts_ref[:, :width] = product(parts[2], common[:, full : full + width]).astype(low)
    for c in range(0, full, 512):
        parts_ref[:, width + c : width + c + 512] = product(parts[0], common[:, c : c + 512]).astype(low)
    parts_ref[:, width + full :] = product(parts[1], common[:, width + full :]).astype(low)


def proto_back_kernel(
    scale, owner_ref, unit_ref, proto_ref, inv_ref, thawed_ref, expo_ref, feats_ref,
    grad_ref,
    acc_ref, raw_ref,
):
    step = pl.program_id(0)
    bottle = unit_ref.shape[0]

    @pl.when(step == 0)
    def _():
        acc_ref[...] = jnp.zeros_like(acc_ref)

    rows = feats_ref.shape[0]
    slots = rows // 8
    images = slots // MOST_CROPS
    for l in range(8):
        here = slice(l * slots, (l + 1) * slots)
        extra = feats_ref[here, bottle:].astype(jnp.float32)
        lane = lax.broadcasted_iota(jnp.int32, extra.shape, 1)
        pick = lambda a, b: jnp.sum(jnp.where((lane >= a) & (lane < b), extra, 0.0), axis=1, keepdims=True)
        logits = product(feats_ref[here, :bottle], unit_ref[...]) * (1.0 / STUDENT_TEMP)
        target = repeat_rows(expo_ref[pl.ds(pl.multiple_of(owner_ref[step * 8 + l] * images, 8), images), :])
        raw = pick(0, 1) * (jnp.exp(logits - pick(1, 4)) - target * jnp.exp(-pick(4, 7))) * scale
        raw_ref[here, :] = raw.astype(jnp.bfloat16)
    acc_ref[...] += inner_rows(feats_ref[:, :bottle], raw_ref[...])

    @pl.when(step == pl.num_programs(0) - 1)
    def _():
        proto = proto_ref[...].astype(jnp.float32)
        inv = inv_ref[...]
        grad = acc_ref[...]
        inner = jnp.sum(proto * grad, axis=0, keepdims=True)
        grad_ref[...] = (inv * grad - proto * (inv * inv * inv * inner)) * thawed_ref[...]


def whole(array):
    return pl.BlockSpec(array.shape, lambda *i: (0,) * len(array.shape))


class Layer:
    def __init__(self, array, layer):
        self.array, self.layer = array, layer


def spec_of(item):
    if isinstance(item, Layer):
        shape = item.array.shape[1:]
        return pl.BlockSpec((None,) + shape, lambda *i: (item.layer,) + (0,) * len(shape))
    return whole(item)


def array_of(item):
    return item.array if isinstance(item, Layer) else item


def by_step(rows, width):
    return pl.BlockSpec((rows, width), lambda i: (i, 0))


def run_kernel(body, steps, scalars, whole_in, step_in, outs, scratch, micros):
    in_specs = (
        [pl.BlockSpec(memory_space=pltpu.SMEM) for a in scalars]
        + [spec_of(a) for a in whole_in]
        + [by_step(rows, a.shape[1]) for a, rows in step_in]
    )
    out_specs = [
        by_step(rows, shape[1]) if rows else pl.BlockSpec(shape, lambda i, k=len(shape): (0,) * k)
        for shape, dtype, rows in outs
    ]
    return pl.pallas_call(
        body,
        grid=(steps,),
        in_specs=in_specs,
        out_specs=out_specs,
        out_shape=[jax.ShapeDtypeStruct(shape, dtype) for shape, dtype, rows in outs],
        scratch_shapes=scratch,
        compiler_params=pltpu.CompilerParams(
            dimension_semantics=("arbitrary",), vmem_limit_bytes=56 * 1024 * 1024
        ),
        cost_estimate=pl.CostEstimate(flops=micros * 10**9, bytes_accessed=2**20, transcendentals=0),
    )(*scalars, *[array_of(a) for a in whole_in], *[a for a, rows in step_in])


def score_masks(seq_len):
    key = jnp.arange(PAIR)[:, None]
    query = (jnp.arange(2 * PAIR) % PAIR)[None, :]
    pair = (key // PITCH == query // PITCH) & (key % PITCH < seq_len)
    key = jnp.arange(GROUP * PITCH)[:, None]
    column = (jnp.arange(HEADS * GROUP) % GROUP)[None, :]
    single = (key // PITCH == column) & (key % PITCH < seq_len)
    return [jnp.where(m, 0.0, NEVER).astype(jnp.float32) for m in (pair, single)]


def axis_bits(n):
    bits = n.bit_length() - 1
    assert n == 1 << bits
    return bits


def swap(values, mask, n):
    return lax.ppermute(values, "dp", [(i, i ^ mask) for i in range(n)])


def group_masks(group):
    return [k << group[0] for k in range(1 << len(group))]


def own_digit(group):
    return (lax.axis_index("dp") >> group[0]) & ((1 << len(group)) - 1)


def upper_groups(n, first):
    bits = list(range(first, axis_bits(n)))
    return [bits[i : i + 2] for i in range(0, len(bits), 2)][::-1]


def gather_loose(block, group, n):
    return jnp.stack([swap(block, mask, n) if mask else block for mask in group_masks(group)])


def tree_sum(parts):
    while len(parts) > 1:
        parts = [parts[i] + parts[i + 1] for i in range(0, len(parts), 2)]
    return parts[0]


def scatter_send(parts, group):
    size = 1 << len(group)
    parts = parts.reshape((size, parts.shape[0] // size) + parts.shape[1:])
    digit = own_digit(group)
    return [lax.dynamic_index_in_dim(parts, digit ^ k, 0, keepdims=False) for k in range(size)]


def swap_parts(parts, group, n):
    return [swap(part, mask, n) if mask else part for part, mask in zip(parts, group_masks(group))]


def scatter_stage(parts, group, n):
    got = swap_parts(scatter_send(parts, group), group, n)
    return tree_sum([part.astype(jnp.float32) for part in got]).astype(parts.dtype)


def sum_stage(values, group, n):
    return tree_sum(swap_parts([values] * (1 << len(group)), group, n))


def fold_send(parts, group):
    size = 1 << len(group)
    parts = parts.reshape((size, parts.shape[0] // size) + parts.shape[1:])
    return [parts[k] for k in range(size)]


def fold_sum(parts):
    return tree_sum([part.astype(jnp.float32) for part in parts]).astype(parts[0].dtype)


def unfold_stage(parts, group, n):
    return jnp.concatenate([swap(parts, mask, n) if mask else parts for mask in group_masks(group)])


def extra_sum(values, n):
    for bit in range(5, axis_bits(n)):
        values = values + swap(values, 1 << bit, n)
    return values


def together(*values):
    return lax.optimization_barrier(values)


CORE, PLANE, LINE = [0], [1, 2], [3, 4]


def per_device(
    tokens,
    layer_gains,
    layer_shifts,
    w_qkv,
    b_qv,
    w_out,
    b_out,
    w_fc1,
    b_fc1,
    w_fc2,
    b_fc2,
    final_gain,
    final_shift,
    head_w1,
    head_b1,
    head_w2,
    head_b2,
    head_w3,
    head_b3,
    prototypes,
    crop_counts,
    teacher_logits,
    first_epoch,
):
    low, wide = jnp.bfloat16, jnp.float32
    slot_count, seq_len, width = tokens.shape
    n = lax.axis_size("dp")
    device = lax.axis_index("dp")
    me = (device & (BLOCKS - 1)).reshape(1)
    bottle = prototypes.shape[0]
    hidden = w_fc1.shape[2]
    hid = head_w2.shape[0]
    steps = slot_count // GROUP
    rows = GROUP * PITCH
    padded = slot_count * PITCH
    row_count = slot_count * seq_len
    groups = upper_groups(n, 3)

    scale = 1.0 / (STUDENT_TEMP * n)
    images, protos = teacher_logits.shape
    unit_low, unit_turned, col_inv, teach_sum, teach_expo = run_kernel(
        prepare_kernel,
        1,
        [],
        [prototypes, teacher_logits],
        [],
        [
            ((bottle, protos), low, 0),
            ((protos, bottle), low, 0),
            ((1, protos), wide, 0),
            ((images, bottle + 128), wide, 0),
            ((images, protos), wide, 0),
        ],
        [],
        4,
    )
    unit_all = lax.all_gather(unit_turned, "dp", axis=0, tiled=True)
    teach_sum = teach_sum.reshape(n, -1, bottle + 128)
    for group in groups[:-1]:
        teach_sum = scatter_stage(teach_sum, group, n)
    live = (jnp.arange(MOST_CROPS, dtype=jnp.int32)[None, :] < crop_counts[:, None]).astype(wide).reshape(n, slot_count)
    own_live = lax.dynamic_index_in_dim(live, device, 0, keepdims=False)[:, None]

    zero_bias = jnp.zeros((2, width), wide)
    pair_mask, class_mask = score_masks(seq_len)
    gains = layer_gains.reshape(4, width)
    shifts = layer_shifts.reshape(4, width)
    full_bias = jnp.concatenate([b_qv[:, :width], zero_bias, b_qv[:, width:]], axis=1)[:, None]
    b_out, b_fc1, b_fc2 = b_out[:, None], b_fc1[:, None], b_fc2[:, None]
    turned_tokens = tokens.transpose(1, 0, 2)
    all_rows = pltpu.VMEM((width // 128, row_count, 128), wide)
    teach_parts = scatter_send(teach_sum, groups[-1])
    turned_tokens, *teach_parts = together(turned_tokens, *teach_parts)
    teach_parts = swap_parts(teach_parts, groups[-1], n)
    qkv_a, attn_a, middle_a = run_kernel(
        attend_kernel,
        steps,
        [],
        [turned_tokens, pair_mask, gains, shifts, Layer(w_qkv, 0), Layer(full_bias, 0), Layer(w_out, 0), Layer(b_out, 0)],
        [],
        [((padded, 3 * width), low, rows), ((padded, width), low, rows), ((padded, width), wide, rows)],
        [all_rows, pltpu.VMEM((rows, width), wide), pltpu.VMEM((rows, width), low)],
        35,
    )
    middle_a, *teach_parts = together(middle_a, *teach_parts)
    teach_sum = tree_sum(teach_parts)
    teach_parts = scatter_send(teach_sum, PLANE)
    middle_a, *teach_parts = together(middle_a, *teach_parts)
    teach_parts = swap_parts(teach_parts, PLANE, n)
    act_a, slope_a, lower_out, kv_c, query_c, attn_c, first_low, first_in = run_kernel(
        mlp_kernel,
        steps,
        [],
        [class_mask, gains, shifts, Layer(w_fc1, 0), Layer(b_fc1, 0), Layer(w_fc2, 0), Layer(b_fc2, 0), Layer(w_qkv, 1), Layer(full_bias, 1)],
        [(middle_a, rows)],
        [
            ((padded, hidden), low, rows),
            ((padded, hidden), low, rows),
            ((padded, width), wide, rows),
            ((padded, 2 * width), low, rows),
            ((slot_count, width), wide, GROUP),
            ((slot_count, width), wide, GROUP),
            ((slot_count, width), wide, GROUP),
            ((slot_count, width), wide, GROUP),
        ],
        [pltpu.VMEM((rows, width), low), pltpu.VMEM((rows, width), wide)],
        40,
    )
    first_in, *teach_parts = together(first_in, *teach_parts)
    teach_sum = scatter_stage(tree_sum(teach_parts), CORE, n)[0]

    finals = jnp.stack([final_gain, final_shift])
    vec_width = -(-(7 * width + hidden + 2 * hid) // width) * width
    grad_attended, grad_middle_c, grad_attn, common, feats, shares, up1, up2, vec_h = run_kernel(
        functools.partial(head_kernel, scale, hid // n),
        1,
        [],
        [own_live, teach_sum, attn_c, first_in, gains, shifts, finals, Layer(w_out, 1), Layer(b_out, 1), Layer(w_fc1, 1), Layer(b_fc1, 1), Layer(w_fc2, 1), Layer(b_fc2, 1),
         head_w1, head_b1[None], head_w2, head_b2[None], head_w3, head_b3[None], unit_all],
        [],
        [
            ((slot_count, width), wide, 0),
            ((slot_count, width), wide, 0),
            ((slot_count, width), wide, 0),
            ((slot_count, hid + width + bottle), low, 0),
            ((slot_count, bottle + 128), low, 0),
            ((4, slot_count, hid // 4 * 3), low, 0),
            ((width, hidden), low, 0),
            ((hidden, width), low, 0),
            ((8, vec_width), wide, 0),
        ],
        [
            pltpu.VMEM((slot_count, hidden), low),
            pltpu.VMEM((slot_count, hidden), wide),
            pltpu.VMEM((slot_count, hid), wide),
            pltpu.VMEM((slot_count, hid), wide),
            pltpu.VMEM((slot_count, hid), low),
            pltpu.VMEM((slot_count, hid), low),
            pltpu.VMEM((slot_count, hid), low),
        ],
        25,
    )
    shares = shares.reshape((2, 2) + shares.shape[1:])
    core = own_digit([0])
    share_own = lax.dynamic_index_in_dim(shares, core, 1, keepdims=False)
    share_got = swap(lax.dynamic_index_in_dim(shares, 1 - core, 1, keepdims=False), 1, n)
    common_got = swap(common, 1, n)
    spot = own_digit([1])
    share0, share1 = (lax.dynamic_index_in_dim(v, spot, 0, keepdims=False) for v in (share_own, share_got))
    share2, share3 = (lax.dynamic_index_in_dim(v, 1 - spot, 0, keepdims=False) for v in (share_own, share_got))
    grad_attended, common, share2, share3 = together(grad_attended, common, share2, share3)
    common2, share2, share3 = (swap(v, 2, n) for v in (common, share2, share3))
    grad_lower_out, unit_u, vec_c = run_kernel(
        upper_back_kernel,
        steps,
        [],
        [class_mask, gains, shifts, Layer(w_qkv, 1), first_low, attn_c, grad_attn],
        [(lower_out, rows), (kv_c, rows), (query_c, GROUP), (grad_attended, GROUP), (grad_middle_c, GROUP)],
        [
            ((padded, width), wide, rows),
            ((width, 4 * width), low, 0),
            ((8, 4 * width), wide, 0),
        ],
        [pltpu.VMEM((width, 4 * width), wide), pltpu.VMEM((rows, width), wide), pltpu.VMEM((slot_count, width), wide)],
        20,
    )
    grad_lower_out, common2, share2, share3 = together(grad_lower_out, common2, share2, share3)
    common3 = swap(common2, 1, n)
    head_parts = run_kernel(
        functools.partial(head_sum_kernel, width),
        1,
        [],
        [common, common_got, common2, common3, share0, share1, share2, share3],
        [],
        [((hid // 4, width + hid + bottle), low, 0)],
        [],
        6,
    )[0].reshape(n // 8, 2, hid // n, -1)
    spot = own_digit([2])
    head_keep = lax.dynamic_index_in_dim(head_parts, spot, 1, keepdims=False)
    head_send = lax.dynamic_index_in_dim(head_parts, 1 - spot, 1, keepdims=False)
    for group in groups[:-1]:
        feats = gather_loose(feats, group, n)
    grad_lower_out, head_send, feats = together(grad_lower_out, head_send, feats)
    head_got = swap(head_send, 4, n)
    feats_parts = swap_parts([feats] * (1 << len(groups[-1])), groups[-1], n)
    grad_middle_a, keep_m, send_m, vec_b, vec_hidden = run_kernel(
        mlp_back_kernel,
        steps,
        [me],
        [unit_u, up1, up2, gains, shifts, Layer(w_fc1, 0), Layer(w_fc2, 0)],
        [(grad_lower_out, rows), (middle_a, rows), (act_a, rows), (slope_a, rows)],
        [
            ((padded, width), wide, rows),
            ((BLOCKS // 2, 5, width // 8, width), low, 0),
            ((BLOCKS // 2, 5, width // 8, width), low, 0),
            ((8, 3 * width), wide, 0),
            ((8, hidden), wide, 0),
        ],
        [
            pltpu.VMEM((width, hidden), wide),
            pltpu.VMEM((width, hidden), wide),
            pltpu.VMEM((rows, hidden), low),
            pltpu.VMEM((hidden, width), wide),
        ],
        40,
    )
    grad_middle_a, head_got, send_m, *feats_parts = together(grad_middle_a, head_got, send_m, *feats_parts)
    feats = jnp.stack(feats_parts)
    head_parts = head_keep + head_got
    for bit in range(axis_bits(n) - 1, 4, -1):
        head_parts = scatter_stage(head_parts, [bit], n)
    head_keep, head_send = scatter_send(head_parts, [4])
    parts_m = fold_send(keep_m + swap(send_m, 1, n), PLANE)
    grad_middle_a, head_send, feats, *parts_m = together(grad_middle_a, head_send, feats, *parts_m)
    feats_got = swap(feats, 2, n)
    head_got = swap(head_send, 16, n)
    parts_m = swap_parts(parts_m, PLANE, n)
    grad_qkv, grad_wo, vec_a = run_kernel(
        attend_back_kernel,
        steps,
        [],
        [pair_mask, Layer(w_out, 0)],
        [(grad_middle_a, rows), (qkv_a, rows), (attn_a, rows)],
        [((padded, 3 * width), low, rows), ((width, width), wide, 0), ((8, 4 * width), wide, 0)],
        [pltpu.VMEM((rows, width), low)],
        40,
    )
    grad_qkv, head_got, feats_got, *parts_m = together(grad_qkv, head_got, feats_got, *parts_m)
    feats = jnp.stack([feats, feats_got])
    head_keep, head_send = scatter_send(head_keep + head_got, [3])
    parts_m = fold_send(fold_sum(parts_m), LINE)
    grad_qkv, head_send, feats, *parts_m = together(grad_qkv, head_send, feats, *parts_m)
    feats_got = swap(feats, 4, n)
    parts_m = swap_parts(parts_m, LINE, n)
    keep_a, send_a = run_kernel(
        weight_back_kernel,
        steps,
        [me],
        [turned_tokens, gains, shifts, grad_wo],
        [(grad_qkv, rows)],
        [
            ((BLOCKS // 2, 1, width // 8, width), low, 0),
            ((BLOCKS // 2, 1, width // 8, width), low, 0),
        ],
        [all_rows, pltpu.VMEM((rows, width), wide), pltpu.VMEM((width, 4 * width), wide)],
        10,
    )
    keep_a, send_a, feats_got, *parts_m = together(keep_a, send_a, feats_got, *parts_m)
    feats = jnp.stack([feats, feats_got])
    feats = jnp.stack([feats, swap(feats, 1, n)]).reshape(n * slot_count, -1)
    sum_m = extra_sum(fold_sum(parts_m), n)
    keep_a, send_a = fold_send(keep_a + swap(send_a, 1, n), [2])
    grad_qkv, sum_m, head_send, send_a = together(grad_qkv, sum_m, head_send, send_a)
    parts_m = swap_parts([sum_m] * 4, LINE, n)
    got_a = swap(send_a, 4, n)
    head_got = swap(head_send, 8, n)
    grad_tokens, vec_in = run_kernel(
        input_back_kernel,
        steps,
        [],
        [turned_tokens, gains, Layer(w_qkv, 0)],
        [(grad_middle_a, rows), (grad_qkv, rows)],
        [((row_count, width), wide, 0), ((8, 2 * width), wide, 0)],
        [all_rows, all_rows, pltpu.VMEM((rows, width), wide)],
        20,
    )
    tokens_grad = grad_tokens.reshape(seq_len, slot_count, width).transpose(1, 0, 2)
    vec_in, got_a, head_got, *parts_m = together(vec_in, got_a, head_got, *parts_m)
    sum_m = jnp.concatenate(parts_m)
    keep_a, send_a = fold_send(keep_a + got_a, [1])
    eights = jnp.concatenate([vec_in, vec_b, vec_c, vec_h, vec_a, vec_hidden], axis=1)
    vectors = jnp.sum(eights, axis=0).reshape(-1, width)
    feats, send_a, vectors = together(feats, send_a, vectors)

    got_a = swap(send_a, 2, n)
    got_v = swap(vectors, 1, n)
    masks = [0]
    for group in [g for g in groups] + [[1], [2], [0]]:
        masks = [low_part | high for high in group_masks(group) for low_part in masks]
    prototypes_grad = run_kernel(
        functools.partial(proto_back_kernel, scale),
        n // 8,
        [device ^ jnp.array(masks, jnp.int32)],
        [unit_low, prototypes, col_inv, (1 - first_epoch).astype(wide)[None], teach_expo],
        [(feats, 8 * slot_count)],
        [(prototypes.shape, wide, 0)],
        [pltpu.VMEM(prototypes.shape, wide), pltpu.VMEM((8 * slot_count, protos), low)],
        6,
    )[0]
    prototypes_grad, got_a, got_v = together(prototypes_grad, got_a, got_v)
    sum_a, vectors = keep_a + got_a, vectors + got_v
    for bit in (1, 2):
        vectors = vectors + swap(vectors, 1 << bit, n)
    sum_a, vectors, sum_m = together(sum_a, vectors, sum_m)
    parts_m = swap_parts([sum_m] * 4, PLANE, n)
    for bit in (4, 3):
        keep_a, send_a = fold_send(sum_a, [bit])
        sum_a = keep_a + swap(send_a, 1 << bit, n)
    sum_a = extra_sum(sum_a, n)
    for bit in range(3, axis_bits(n)):
        vectors = vectors + swap(vectors, 1 << bit, n)
    for bit in (3, 4):
        sum_a = unfold_stage(sum_a, [bit], n)
    sum_a, vectors, *parts_m = together(sum_a, vectors, *parts_m)
    sum_m = unfold_stage(jnp.concatenate(parts_m), CORE, n)
    for bit in (1, 2, 0):
        sum_a = unfold_stage(sum_a, [bit], n)
    qkv_grad, out_grad, fc1_grad, fc2_grad = pl.pallas_call(
        unpack_kernel,
        grid=(8,),
        in_specs=[pl.BlockSpec(memory_space=pltpu.SMEM), whole(sum_m), whole(sum_a)],
        out_specs=[
            pl.BlockSpec((2, width // 8, 3 * width), lambda i: (0, i, 0)),
            pl.BlockSpec((2, width // 8, width), lambda i: (0, i, 0)),
            pl.BlockSpec((2, width // 8, hidden), lambda i: (0, i, 0)),
            pl.BlockSpec((2, hidden // 8, width), lambda i: (0, i, 0)),
        ],
        out_shape=[
            jax.ShapeDtypeStruct(s, wide)
            for s in ((2, width, 3 * width), (2, width, width), (2, width, hidden), (2, hidden, width))
        ],
        compiler_params=pltpu.CompilerParams(
            dimension_semantics=("arbitrary",), vmem_limit_bytes=56 * 1024 * 1024
        ),
    )(me, sum_m, sum_a)
    head_sum = (head_keep.astype(wide) + head_got.astype(wide)).reshape(hid // n, -1)

    row_in, row_b, row_c, row_h = 0, 2, 5, 9
    row_a = row_h + vec_width // width
    row_hidden = row_a + 4
    pick = lambda *where: jnp.stack([vectors[i] for i in where])
    ends = vectors[row_h + 7 + hidden // width : row_a].reshape(-1)
    own_part = lambda start: lax.dynamic_slice_in_dim(ends, start + device * (hid // n), hid // n)

    return (
        tokens_grad,
        pick(row_in, row_b + 1, row_c + 1, row_h).reshape(2, 2, width),
        pick(row_in + 1, row_b + 2, row_c + 2, row_h + 1).reshape(2, 2, width),
        qkv_grad,
        pick(row_a + 1, row_a + 3, row_c + 3, row_c).reshape(2, 2 * width),
        out_grad,
        pick(row_a, row_h + 2),
        fc1_grad,
        jnp.concatenate([vectors[row_hidden:], vectors[row_h + 6 : row_h + 6 + hidden // width]]).reshape(2, hidden),
        fc2_grad,
        pick(row_b, row_h + 3),
        vectors[row_h + 4],
        vectors[row_h + 5],
        head_sum[:, :width].T,
        own_part(0),
        head_sum[:, width : width + hid],
        own_part(hid),
        head_sum[:, width + hid : width + hid + bottle],
        vectors[row_h + 6 + hidden // width, :bottle],
        prototypes_grad,
    )


def solution(mesh):
    return jax.shard_map(
        per_device,
        mesh=mesh,
        in_specs=(
            P("dp", None, None),
            P(),
            P(),
            P(),
            P(),
            P(),
            P(),
            P(),
            P(),
            P(),
            P(),
            P(),
            P(),
            P(),
            P(),
            P(),
            P(),
            P(),
            P(),
            P(None, "dp"),
            P(),
            P(None, "dp"),
            P("dp"),
        ),
        out_specs=(
            P("dp", None, None),
            P(),
            P(),
            P(),
            P(),
            P(),
            P(),
            P(),
            P(),
            P(),
            P(),
            P(),
            P(),
            P(None, "dp"),
            P("dp"),
            P("dp", None),
            P("dp"),
            P("dp", None),
            P(),
            P(None, "dp"),
        ),
        check_vma=False,
    )
```

```python
import functools

import jax
import jax.numpy as jnp
from jax import lax
from jax.experimental import pallas as pl
from jax.experimental.pallas import tpu as pltpu
from jax.sharding import PartitionSpec as P

HEADS = 6
HD = 64
MOST_CROPS = 10

STUDENT_TEMP = 0.1
TEACHER_TEMP = 0.04
EPS = 1e-06
SHIFT = 10.0


def product(left, right):
    return jnp.dot(left, right, preferred_element_type=jnp.float32)


def against(left, right):
    return lax.dot_general(
        left, right, (((1,), (1,)), ((), ())), preferred_element_type=jnp.float32
    )


def inner_rows(left, right):
    return lax.dot_general(
        left, right, (((0,), (0,)), ((), ())), preferred_element_type=jnp.float32
    )


def column_sum(values):
    return jnp.sum(values.astype(jnp.float32), axis=0)


def norm_forward(values, gain, shift):
    centered = values - jnp.mean(values, axis=-1, keepdims=True)
    rstd = lax.rsqrt(jnp.mean(centered * centered, axis=-1, keepdims=True) + EPS)
    normed = centered * rstd
    return (normed * gain + shift, normed, rstd)


def norm_backward(grad, normed, rstd, gain):
    scaled = grad * gain
    inner = (
        scaled
        - jnp.mean(scaled, axis=-1, keepdims=True)
        - normed * jnp.mean(scaled * normed, axis=-1, keepdims=True)
    )
    return (rstd * inner, jnp.sum(grad * normed, axis=0), jnp.sum(grad, axis=0))


GROUP = 16
BLOCKS = 32
PITCH = 40
PAIR = 2 * PITCH
NEVER = -1e30


def smooth_both(values):
    size = jnp.abs(values)
    bell = jnp.exp(values * values * -0.5)
    t = 1.0 / (1.0 + 0.23164189 * size)
    tail = t * (0.127414796 + t * (-0.142248368 + t * (0.7107068705 + t * (-0.7265760135 + t * 0.5307027145))))
    upper = tail * bell
    area = jnp.where(values >= 0, 1.0 - upper, upper)
    return values * area, area + values * (bell * 0.3989422804014327)


def standardize(values):
    centered = values - jnp.mean(values, axis=-1, keepdims=True)
    rstd = lax.rsqrt(jnp.mean(centered * centered, axis=-1, keepdims=True) + EPS)
    return centered * rstd, rstd


def standard_back(grad, normed, rstd, gain):
    scaled = grad * gain
    return rstd * (
        scaled
        - jnp.mean(scaled, axis=-1, keepdims=True)
        - normed * jnp.mean(scaled * normed, axis=-1, keepdims=True)
    )


def fold_rows(values):
    return jnp.sum(values.reshape(-1, 8, values.shape[1]), axis=0)


def finish_rows(ref):
    ref[0:1, :] = jnp.sum(ref[...], axis=0, keepdims=True)


def both_heads(values):
    lane = lax.broadcasted_iota(jnp.int32, values.shape, 1)
    zero = jnp.zeros_like(values)
    return jnp.concatenate([jnp.where(lane < HD, values, zero), jnp.where(lane < HD, zero, values)])


def join_heads(values):
    rows = values.shape[0] // 2
    lane = lax.broadcasted_iota(jnp.int32, (rows, values.shape[1]), 1)
    return jnp.where(lane < HD, values[:rows], values[rows:])


def spread_heads(values):
    lane = lax.broadcasted_iota(jnp.int32, values.shape, 1) // HD
    return jnp.concatenate([jnp.where(lane == h, values, 0.0) for h in range(HEADS)])


def gather_heads(values):
    lane = lax.broadcasted_iota(jnp.int32, (GROUP, values.shape[1]), 1) // HD
    out = jnp.zeros((GROUP, values.shape[1]), values.dtype)
    for h in range(HEADS):
        out = jnp.where(lane == h, values[h * GROUP : (h + 1) * GROUP], out)
    return out


def soft_columns(scores):
    expo = jnp.exp(scores - jnp.max(scores, axis=0, keepdims=True))
    return expo * (1.0 / jnp.sum(expo, axis=0, keepdims=True))


def take_slots(order_ref, all_ref, rows_ref, step, seq_len, slots):
    for s in range(GROUP):
        for c in range(all_ref.shape[0]):
            rows_ref[s * PITCH : s * PITCH + seq_len, c * 128 : (c + 1) * 128] = all_ref[
                c, pl.ds(order_ref[step * GROUP + s], seq_len, stride=slots), :
            ]


def first_rows(ref):
    return jnp.concatenate([ref[s * PITCH : s * PITCH + 1, :] for s in range(GROUP)])


def add_first_rows(ref, values):
    for s in range(GROUP):
        ref[s * PITCH : s * PITCH + 1, :] += values[s : s + 1]


def widen_tokens(tok_ref, all_ref):
    seq_len, slots, width = tok_ref.shape

    @pl.loop(0, seq_len)
    def _(t):
        wide = tok_ref[t].astype(jnp.float32)
        for c in range(all_ref.shape[0]):
            all_ref[c, pl.ds(pl.multiple_of(t * slots, 8), slots), :] = wide[:, c * 128 : (c + 1) * 128]


def ordered_masks(line_first=False):
    if line_first:
        return [(p >> 4) | ((p & 3) << 1) | (((p >> 2) & 3) << 3) for p in range(BLOCKS)]
    return [(p >> 4) | (((p >> 2) & 3) << 1) | ((p & 3) << 3) for p in range(BLOCKS)]


def write_unit(me, keep_ref, send_ref, unit, read, line_first=False):
    for p, mask in enumerate(ordered_masks(line_first)):
        owner = me ^ mask
        ref = keep_ref if p < BLOCKS // 2 else send_ref
        ref[p % (BLOCKS // 2), unit] = read(owner)


def from_square(ref, first=0):
    width = ref.shape[0]

    def read(owner):
        rows = pl.multiple_of((owner // 4) * (width // 8), 16)
        cols = pl.multiple_of((owner % 4) * width, 128)
        return ref[pl.ds(rows, width // 8), pl.ds(cols, width)].astype(jnp.bfloat16)

    return read


def from_tall(ref):
    size = ref.shape[0] // BLOCKS

    def read(owner):
        return ref[pl.ds(pl.multiple_of(owner * size, 16), size), :].astype(jnp.bfloat16)

    return read


def attend_kernel(
    count_ref, order_ref, tok_ref, pair_mask_ref, gains_ref, shifts_ref, w_qkv_ref, b_qkv_ref, w_out_ref, b_out_ref,
    qkv_ref, o_ref, mid_ref,
    all_ref, x_ref, low_ref,
):
    step = pl.program_id(0)
    seq_len, slots, width = tok_ref.shape
    rows = GROUP * PITCH
    chunk = PAIR

    @pl.when(step == 0)
    def _():
        widen_tokens(tok_ref, all_ref)
        x_ref[...] = jnp.zeros_like(x_ref)

    take_slots(order_ref, all_ref, x_ref, step, seq_len, slots)
    for r in range(0, rows, chunk):
        normed, _ = standardize(x_ref[r : r + chunk, :])
        low_ref[r : r + chunk, :] = (normed * gains_ref[0:1, :] + shifts_ref[0:1, :]).astype(jnp.bfloat16)
    for j in range(3):
        cols = slice(j * width, (j + 1) * width)
        part = product(low_ref[...], w_qkv_ref[:, cols]) + b_qkv_ref[:, cols]
        if j == 0:
            part = part.astype(jnp.bfloat16) * jnp.bfloat16(HD ** -0.5)
        qkv_ref[:, cols] = part.astype(jnp.bfloat16)
    mask = jnp.concatenate([pair_mask_ref[...]] * 2)
    spots = [(r, c) for r in range(0, rows, PAIR) for c in range(0, width, 2 * HD)]
    for b in range(0, len(spots), 24):
        group = spots[b : b + 24]
        scores = [
            against(
                both_heads(qkv_ref[r : r + PAIR, c : c + 2 * HD]), qkv_ref[r : r + PAIR, width + c : width + c + 2 * HD]
            )
            + mask
            for r, c in group
        ]
        probs, scales = [], []
        for score in scores:
            expo = jnp.exp(score - jnp.max(score, axis=1, keepdims=True))
            probs.append(expo.astype(jnp.bfloat16))
            scales.append(1.0 / jnp.sum(expo, axis=1, keepdims=True))
        outs = [
            product(prob, qkv_ref[r : r + PAIR, 2 * width + c : 2 * width + c + 2 * HD]) * scale
            for prob, scale, (r, c) in zip(probs, scales, group)
        ]
        for out, (r, c) in zip(outs, group):
            o_ref[r : r + PAIR, c : c + 2 * HD] = join_heads(out).astype(jnp.bfloat16)
    mixed = product(o_ref[...], w_out_ref[...])
    for r in range(0, rows, chunk):
        part = x_ref[r : r + chunk, :] + mixed[r : r + chunk] + b_out_ref[...]
        mid_ref[r : r + chunk, :] = part


def mlp_kernel(
    count_ref, class_mask_ref, gains_ref, shifts_ref, w_fc1_ref, b_fc1_ref, w_fc2_ref, b_fc2_ref, w_up_ref, b_up_ref, mid_ref,
    act_ref, slope_ref, x1_ref, kv_ref, cq_ref, co_ref, ch_ref, cx_ref,
    low_ref, wide_ref,
):
    rows, width = mid_ref.shape
    hidden = w_fc1_ref.shape[1]
    chunk = PAIR
    step = pl.program_id(0)
    here = pl.ds(pl.multiple_of(step * GROUP, GROUP), GROUP)

    @pl.when(step == 0)
    def _():
        for ref in (cq_ref, co_ref, ch_ref, cx_ref):
            ref[...] = jnp.zeros_like(ref)

    for r in range(0, rows, chunk):
        normed, _ = standardize(mid_ref[r : r + chunk, :])
        low_ref[r : r + chunk, :] = (normed * gains_ref[1:2, :] + shifts_ref[1:2, :]).astype(jnp.bfloat16)
    for c in range(0, hidden, 256):
        pre = product(low_ref[...], w_fc1_ref[:, c : c + 256])
        for r in range(0, rows, 32):
            act, slope = smooth_both(pre[r : r + 32] + b_fc1_ref[:, c : c + 256])
            act_ref[r : r + 32, c : c + 256] = act.astype(jnp.bfloat16)
            slope_ref[r : r + 32, c : c + 256] = slope.astype(jnp.bfloat16)
    mixed = product(act_ref[...], w_fc2_ref[...])
    for r in range(0, rows, chunk):
        part = mid_ref[r : r + chunk, :] + mixed[r : r + chunk] + b_fc2_ref[...]
        x1_ref[r : r + chunk, :] = part
        normed, _ = standardize(part)
        wide = normed * gains_ref[2:3, :] + shifts_ref[2:3, :]
        wide_ref[r : r + chunk, :] = wide
        low_ref[r : r + chunk, :] = wide.astype(jnp.bfloat16)
    for j in range(2):
        cols = slice(j * width, (j + 1) * width)
        ups = slice((j + 1) * width, (j + 2) * width)
        kv_ref[:, cols] = (product(low_ref[...], w_up_ref[:, ups]) + b_up_ref[:, ups]).astype(jnp.bfloat16)
    cx_ref[here, :] = first_rows(x1_ref)
    first = first_rows(wide_ref).astype(jnp.bfloat16)
    ch_ref[here, :] = first.astype(jnp.float32)
    query = (product(first, w_up_ref[:, :width]) + b_up_ref[:, :width]).astype(jnp.bfloat16).astype(jnp.float32) * HD ** -0.5
    cq_ref[here, :] = query
    spread = spread_heads(query).astype(jnp.bfloat16)
    probs = soft_columns(against(kv_ref[:, :width], spread) + class_mask_ref[...]).astype(jnp.bfloat16)
    co_ref[here, :] = gather_heads(inner_rows(probs, kv_ref[:, width:]))


def upper_back_kernel(
    count_ref, class_mask_ref, gains_ref, shifts_ref, w_up_ref, ch_ref, co_ref, da_ref,
    x1_ref, kv_ref, cq_ref, cg_ref, cres_ref,
    dx_ref, unit_ref, vec_ref,
    acc_ref, wide_ref, dqs_ref,
):
    step = pl.program_id(0)
    rows, width = x1_ref.shape

    @pl.when(step == 0)
    def _():
        acc_ref[...] = jnp.zeros_like(acc_ref)
        vec_ref[...] = jnp.zeros_like(vec_ref)

    keys, values = kv_ref[:, :width], kv_ref[:, width:]
    spread = spread_heads(cq_ref[...]).astype(jnp.bfloat16)
    grads = spread_heads(cg_ref[...]).astype(jnp.bfloat16)
    probs = soft_columns(against(keys, spread) + class_mask_ref[...])
    back = against(values, grads)
    inner = (probs * (back - jnp.sum(back * probs, axis=0, keepdims=True))).astype(jnp.bfloat16)
    grad_values = product(probs.astype(jnp.bfloat16), grads).astype(jnp.bfloat16)
    grad_keys = product(inner, spread).astype(jnp.bfloat16)
    grad_query = (gather_heads(inner_rows(inner, keys)) * HD ** -0.5).astype(jnp.bfloat16)
    @pl.when(step == 0)
    def _():
        dqs_ref[...] = jnp.zeros_like(dqs_ref)

    dqs_ref[pl.ds(pl.multiple_of(step * GROUP, GROUP), GROUP), :] = grad_query.astype(jnp.float32)
    vec_ref[:, 3 * width :] += fold_rows(grad_query.astype(jnp.float32))
    vec_ref[:, :width] += fold_rows(grad_values.astype(jnp.float32))
    wide_ref[...] = against(grad_keys, w_up_ref[:, width : 2 * width]) + against(grad_values, w_up_ref[:, 2 * width :])
    add_first_rows(wide_ref, against(grad_query, w_up_ref[:, :width]))
    chunk = PAIR
    parts = []
    for r in range(0, rows, chunk):
        normed, rstd = standardize(x1_ref[r : r + chunk, :])
        parts.append((normed * gains_ref[2:3, :] + shifts_ref[2:3, :]).astype(jnp.bfloat16))
        grad = wide_ref[r : r + chunk, :]
        vec_ref[:, width : 2 * width] += fold_rows(grad * normed)
        vec_ref[:, 2 * width : 3 * width] += fold_rows(grad)
        dx_ref[r : r + chunk, :] = standard_back(grad, normed, rstd, gains_ref[2:3, :])
    turned = jnp.concatenate(parts).T
    acc_ref[:, width : 2 * width] += product(turned, grad_keys)
    acc_ref[:, 2 * width : 3 * width] += product(turned, grad_values)
    add_first_rows(dx_ref, cres_ref[...])

    @pl.when(step == count_ref[0] - 1)
    def _():
        acc_ref[:, :width] = inner_rows(
            ch_ref[...].astype(jnp.bfloat16), dqs_ref[...].astype(jnp.bfloat16)
        )
        acc_ref[:, 3 * width :] = inner_rows(co_ref[...].astype(jnp.bfloat16), da_ref[...].astype(jnp.bfloat16))
        unit_ref[...] = acc_ref[...].astype(jnp.bfloat16)
        finish_rows(vec_ref)


def mlp_back_kernel(
    count_ref, me_ref, unit_ref, gains_ref, shifts_ref, w_fc1_ref, w_fc2_ref, dx_ref, mid_ref, act_ref, slope_ref,
    dmid_ref, keep_ref, send_ref, vec_ref, vec1_ref,
    acc1_ref, acc2_ref, dz_ref, big_ref,
):
    step = pl.program_id(0)
    rows, width = dx_ref.shape
    hidden = act_ref.shape[1]

    @pl.when(step == 0)
    def _():
        acc1_ref[...] = jnp.zeros_like(acc1_ref)
        acc2_ref[...] = jnp.zeros_like(acc2_ref)
        vec_ref[...] = jnp.zeros_like(vec_ref)
        vec1_ref[...] = jnp.zeros_like(vec1_ref)

    low = dx_ref[...].astype(jnp.bfloat16)
    vec_ref[:, :width] += fold_rows(low.astype(jnp.float32))
    low_turned = low.T
    chunk = PAIR
    parts = []
    for r in range(0, rows, chunk):
        normed, _ = standardize(mid_ref[r : r + chunk, :])
        parts.append((normed * gains_ref[1:2, :] + shifts_ref[1:2, :]).astype(jnp.bfloat16))
    norm_turned = jnp.concatenate(parts).T
    for c in range(0, hidden, 768):
        cols = slice(c, c + 768)
        back = against(low, w_fc2_ref[cols, :])
        for r in range(0, rows, chunk):
            part = (back[r : r + chunk] * slope_ref[r : r + chunk, cols].astype(jnp.float32)).astype(jnp.bfloat16)
            dz_ref[r : r + chunk, cols] = part
            vec1_ref[:, cols] += fold_rows(part.astype(jnp.float32))
        acc1_ref[:, cols] += product(norm_turned, dz_ref[:, cols])
        acc2_ref[:, cols] += product(low_turned, act_ref[:, cols])
    mixed = against(dz_ref[...], w_fc1_ref[...])
    for r in range(0, rows, chunk):
        normed, rstd = standardize(mid_ref[r : r + chunk, :])
        grad = mixed[r : r + chunk]
        vec_ref[:, width : 2 * width] += fold_rows(grad * normed)
        vec_ref[:, 2 * width : 3 * width] += fold_rows(grad)
        dmid_ref[r : r + chunk, :] = dx_ref[r : r + chunk, :] + standard_back(grad, normed, rstd, gains_ref[1:2, :])

    @pl.when(step == count_ref[0] - 1)
    def _():
        finish_rows(vec_ref)
        finish_rows(vec1_ref)
        me = me_ref[0]
        write_unit(me, keep_ref, send_ref, 0, from_square(unit_ref))
        write_unit(me, keep_ref, send_ref, 1, from_square(acc1_ref))
        big_ref[...] = acc2_ref[...].T
        write_unit(me, keep_ref, send_ref, 2, from_tall(big_ref))


def attend_back_kernel(
    count_ref, pair_mask_ref, w_out_ref, dmid_ref, qkv_ref, o_ref,
    dqkv_ref, dwo_ref, vec_ref,
    do_ref,
):
    step = pl.program_id(0)
    rows, width = dmid_ref.shape

    @pl.when(step == 0)
    def _():
        dwo_ref[...] = jnp.zeros_like(dwo_ref)
        vec_ref[...] = jnp.zeros_like(vec_ref)

    low = dmid_ref[...].astype(jnp.bfloat16)
    vec_ref[:, :width] += fold_rows(low.astype(jnp.float32))
    do_ref[...] = against(low, w_out_ref[...]).astype(jnp.bfloat16)
    dwo_ref[...] += product(o_ref[...].T, low)
    spots = [(r, c) for r in range(0, rows, PAIR) for c in range(0, width, 2 * HD)]
    for b in range(0, len(spots), 6):
        group = spots[b : b + 6]
        queries = [both_heads(qkv_ref[r : r + PAIR, c : c + 2 * HD]) for r, c in group]
        keys = [qkv_ref[r : r + PAIR, width + c : width + c + 2 * HD] for r, c in group]
        values = [qkv_ref[r : r + PAIR, 2 * width + c : 2 * width + c + 2 * HD] for r, c in group]
        grads = [both_heads(do_ref[r : r + PAIR, c : c + 2 * HD]) for r, c in group]
        scores = [against(key, query) + pair_mask_ref[...] for key, query in zip(keys, queries)]
        backs = [against(value, grad) for value, grad in zip(values, grads)]
        probs = [soft_columns(score) for score in scores]
        inners = [
            (prob * (back - jnp.sum(back * prob, axis=0, keepdims=True))).astype(jnp.bfloat16)
            for prob, back in zip(probs, backs)
        ]
        grad_values = [product(prob.astype(jnp.bfloat16), grad) for prob, grad in zip(probs, grads)]
        grad_keys = [product(inner, query) for inner, query in zip(inners, queries)]
        grad_queries = [inner_rows(inner, key) for inner, key in zip(inners, keys)]
        for (r, c), grad in zip(group, grad_values):
            dqkv_ref[r : r + PAIR, 2 * width + c : 2 * width + c + 2 * HD] = grad.astype(jnp.bfloat16)
        for (r, c), grad in zip(group, grad_keys):
            dqkv_ref[r : r + PAIR, width + c : width + c + 2 * HD] = grad.astype(jnp.bfloat16)
        for (r, c), grad in zip(group, grad_queries):
            dqkv_ref[r : r + PAIR, c : c + 2 * HD] = (join_heads(grad) * HD ** -0.5).astype(jnp.bfloat16)
    for j in range(3):
        cols = slice(j * width, (j + 1) * width)
        vec_ref[:, (j + 1) * width : (j + 2) * width] += fold_rows(dqkv_ref[:, cols].astype(jnp.float32))

    @pl.when(step == count_ref[0] - 1)
    def _():
        finish_rows(vec_ref)


def weight_back_kernel(
    count_ref, me_ref, order_ref, tok_ref, gains_ref, shifts_ref, dwo_ref, dqkv_ref,
    keep_ref, send_ref,
    all_ref, x_ref, acc_ref,
):
    step = pl.program_id(0)
    seq_len, slots, width = tok_ref.shape
    rows = GROUP * PITCH

    @pl.when(step == 0)
    def _():
        widen_tokens(tok_ref, all_ref)
        x_ref[...] = jnp.zeros_like(x_ref)
        acc_ref[:, : 3 * width] = jnp.zeros((width, 3 * width), jnp.float32)
        acc_ref[:, 3 * width :] = dwo_ref[...]

    take_slots(order_ref, all_ref, x_ref, step, seq_len, slots)
    chunk = PAIR
    parts = []
    for r in range(0, rows, chunk):
        normed, _ = standardize(x_ref[r : r + chunk, :])
        parts.append((normed * gains_ref[0:1, :] + shifts_ref[0:1, :]).astype(jnp.bfloat16))
    turned = jnp.concatenate(parts).T
    for j in range(3):
        cols = slice(j * width, (j + 1) * width)
        acc_ref[:, cols] += product(turned, dqkv_ref[:, cols])

    @pl.when(step == count_ref[0] - 1)
    def _():
        write_unit(me_ref[0], keep_ref, send_ref, 0, from_square(acc_ref))


def input_back_kernel(
    count_ref, order_ref, tok_ref, gains_ref, w_qkv_ref, dmid_ref, dqkv_ref,
    dtok_ref, vec_ref,
    all_ref, out_ref, x_ref,
):
    step = pl.program_id(0)
    seq_len, slots, width = tok_ref.shape
    rows = GROUP * PITCH

    @pl.when(step == 0)
    def _():
        widen_tokens(tok_ref, all_ref)
        x_ref[...] = jnp.zeros_like(x_ref)
        out_ref[...] = jnp.zeros_like(out_ref)
        vec_ref[...] = jnp.zeros_like(vec_ref)

    take_slots(order_ref, all_ref, x_ref, step, seq_len, slots)
    chunk = PAIR
    mixed = against(dqkv_ref[...], w_qkv_ref[...])
    for r in range(0, rows, chunk):
        normed, rstd = standardize(x_ref[r : r + chunk, :])
        grad = mixed[r : r + chunk]
        vec_ref[:, :width] += fold_rows(grad * normed)
        vec_ref[:, width:] += fold_rows(grad)
        part = dmid_ref[r : r + chunk, :] + standard_back(grad, normed, rstd, gains_ref[0:1, :])
        for s in range(chunk // PITCH):
            for t in range(all_ref.shape[0]):
                out_ref[t, pl.ds(order_ref[step * GROUP + r // PITCH + s], seq_len, stride=slots), :] = part[
                    s * PITCH : s * PITCH + seq_len, t * 128 : (t + 1) * 128
                ]

    @pl.when(step == count_ref[0] - 1)
    def _():
        finish_rows(vec_ref)
        for t in range(out_ref.shape[0]):
            dtok_ref[:, t * 128 : (t + 1) * 128] = out_ref[t]


def place_of(mask):
    return ((mask & 1) << 4) | (((mask >> 1) & 3) << 2) | ((mask >> 3) & 3)


def read_place(own_ref, got_ref, place, unit):
    inner = place & (BLOCKS // 2 - 1)
    block = jnp.where(place < BLOCKS // 2, own_ref[inner, unit], got_ref[inner, unit])
    return block.astype(jnp.float32)


def unpack_kernel(
    me_ref, own_ref, got_ref,
    qkv_ref, out_ref, fc1_ref, fc2_ref,
):
    step = pl.program_id(0)
    width, size = own_ref.shape[3], own_ref.shape[2]
    for c in range(4):
        place = place_of((step * 4 + c) ^ me_ref[0])
        cols = slice(c * width, (c + 1) * width)
        upper = read_place(own_ref, got_ref, place, 0)
        if c < 3:
            qkv_ref[:, cols] = upper
        else:
            out_ref[...] = upper
        fc1_ref[0, :, cols] = read_place(own_ref, got_ref, place, 1)
        fc2_ref[0, c * size : (c + 1) * size, :] = read_place(own_ref, got_ref, place, 2)
        fc1_ref[1, :, cols] = read_place(own_ref, got_ref, place, 3)
        fc2_ref[1, c * size : (c + 1) * size, :] = read_place(own_ref, got_ref, place, 4)


def unpack_first_kernel(
    me_ref, own_ref, got_ref, qkv_in_ref, out_in_ref,
    qkv_ref, out_ref,
):
    step = pl.program_id(0)
    width = own_ref.shape[3]
    for c in range(4):
        block = read_place(own_ref, got_ref, place_of((step * 4 + c) ^ me_ref[0]), 0)
        if c < 3:
            qkv_ref[:, c * width : (c + 1) * width] = block
        else:
            out_ref[...] = block


def prepare_kernel(
    proto_ref, teacher_ref,
    unit_ref, turned_ref, inv_ref, teach_ref, expo_ref,
):
    proto = proto_ref[...].astype(jnp.float32)
    inv = lax.rsqrt(jnp.sum(proto * proto, axis=0, keepdims=True) + EPS)
    inv_ref[...] = inv
    unit = (proto * inv).astype(jnp.bfloat16)
    unit_ref[...] = unit
    turned_ref[...] = unit.T
    bottle = proto.shape[0]
    images = teacher_ref.shape[0]
    for r in range(0, images, 64):
        expo = jnp.exp(teacher_ref[r : r + 64, :] * (1.0 / TEACHER_TEMP))
        expo_ref[r : r + 64, :] = expo
        teach_ref[r : r + 64, :bottle] = against(expo.astype(jnp.bfloat16), unit)
        teach_ref[r : r + 64, bottle:] = jnp.broadcast_to(jnp.sum(expo, axis=1, keepdims=True), (64, 128))


def repeat_rows(values, image):
    out = jnp.zeros((image.shape[0], values.shape[1]), values.dtype)
    for i in range(values.shape[0]):
        out = jnp.where(image == i, values[i : i + 1], out)
    return out


def three_parts(values):
    high = values.astype(jnp.bfloat16).astype(jnp.float32)
    middle = (values - high).astype(jnp.bfloat16).astype(jnp.float32)
    return [high, middle, values - high - middle]


def head_kernel(
    scale, own_columns, me_ref, live_ref, image_ref, teach_ref, co_ref, cx_ref, gains_ref, shifts_ref, final_ref,
    w_out_ref, b_out_ref, far_fc1_ref, b_fc1_ref, far_fc2_ref, b_fc2_ref,
    far_w1_ref, b1_ref, far_w2_ref, b2_ref, far_w3_ref, b3_ref, far_unit_ref,
    cg_ref, cres_ref, da_ref, common_ref, feats_ref, share_ref, keep_ref, send_ref, vec_ref,
    act_ref, slope_ref, slope1_ref, slope2_ref, one_ref, two_ref, back_ref, up1_ref, up2_ref,
    w_fc1_ref, w_fc2_ref, w1_ref, w2_ref, w3_ref, unit_ref, done_ref,
):
    far = (far_fc1_ref.at[1], far_fc2_ref.at[1], far_w1_ref, far_w2_ref, far_w3_ref, far_unit_ref)
    near = (w_fc1_ref, w_fc2_ref, w1_ref, w2_ref, w3_ref, unit_ref)
    copies = [pltpu.make_async_copy(a, b, done_ref.at[i]) for i, (a, b) in enumerate(zip(far, near))]
    for copy in copies:
        copy.start()
    width = cx_ref.shape[1]
    hidden = w_fc1_ref.shape[1]
    hid, bottle = w3_ref.shape
    low = jnp.bfloat16
    middle = cx_ref[...] + product(co_ref[...].astype(low), w_out_ref[...]) + b_out_ref[...]
    normed_d, rstd_d = standardize(middle)
    low_d = (normed_d * gains_ref[3:4, :] + shifts_ref[3:4, :]).astype(low)
    copies[0].wait()
    for c in range(0, hidden, 256):
        cols = slice(c, c + 256)
        act, slope = smooth_both(product(low_d, w_fc1_ref[:, cols]) + b_fc1_ref[:, cols])
        act_ref[:, cols] = act.astype(low)
        slope_ref[:, cols] = slope
    def share(kind, c, values):
        for u in range(256 // (4 * own_columns)):
            for j in range(4):
                start = kind * (hid // 4) + c // 4 + u * own_columns
                share_ref[j, :, start : start + own_columns] = values[
                    :, (u * 4 + j) * own_columns : (u * 4 + j + 1) * own_columns
                ]

    copies[1].wait()
    out = middle + product(act_ref[...], w_fc2_ref[...]) + b_fc2_ref[...]
    normed_f, rstd_f = standardize(out)
    low_f = (normed_f * final_ref[0:1, :] + final_ref[1:2, :]).astype(low)
    common_ref[:, hid : hid + width] = low_f
    copies[2].wait()
    for c in range(0, hid, 256):
        cols = slice(c, c + 256)
        act, slope = smooth_both(product(low_f, w1_ref[:, cols]) + b1_ref[:, cols])
        one_ref[:, cols] = act.astype(low)
        share(0, c, act.astype(low))
        slope1_ref[:, cols] = slope
    first = one_ref[...]
    copies[3].wait()
    for c in range(0, hid, 256):
        cols = slice(c, c + 256)
        act, slope = smooth_both(product(first, w2_ref[:, cols]) + b2_ref[:, cols])
        two_ref[:, cols] = act.astype(low)
        share(1, c, act.astype(low))
        slope2_ref[:, cols] = slope
    copies[4].wait()
    embed = product(two_ref[...], w3_ref[...]) + b3_ref[...]
    inv = lax.rsqrt(jnp.sum(embed * embed, axis=1, keepdims=True) + EPS)
    feats = (embed * inv).astype(low)
    slots = feats.shape[0]
    total = jnp.zeros((slots, 1), jnp.float32)
    student = jnp.zeros((slots, bottle), jnp.float32)
    total_protos = unit_ref.shape[0]
    copies[5].wait()
    size = 512

    def some(i, carry):
        total, student = carry
        part = unit_ref[pl.ds(pl.multiple_of(i * size, size), size), :]
        expo = jnp.exp(against(feats, part) * (1.0 / STUDENT_TEMP) - SHIFT)
        return (
            total + jnp.sum(expo, axis=1, keepdims=True),
            student + product(expo.astype(low), part),
        )

    total, student = lax.fori_loop(0, total_protos // size, some, (total, student), unroll=4)
    teach_total = teach_ref[:, bottle : bottle + 128]
    teach = repeat_rows(teach_ref[:, :bottle] * (1.0 / teach_total[:, :1]), image_ref[...])
    grad_feat = live_ref[...] * (student * (1.0 / total) - teach) * scale
    logs = [live_ref[...]] + three_parts(SHIFT + jnp.log(total)) + three_parts(repeat_rows(jnp.log(teach_total), image_ref[...])[:, :1]) + [image_ref[...]]
    lane = lax.broadcasted_iota(jnp.int32, (slots, 128), 1)
    extra = jnp.zeros((slots, 128), jnp.float32)
    for i, part in enumerate(logs):
        extra = jnp.where(lane == i, part, extra)
    mark = hid + width + bottle
    feats_ref[:, :bottle] = feats
    feats_ref[:, bottle:] = extra.astype(low)
    grad_embed = inv * grad_feat - embed * (inv * inv * inv) * jnp.sum(embed * grad_feat, axis=1, keepdims=True)
    grad_embed = grad_embed.astype(low)
    common_ref[:, hid + width : mark] = grad_embed
    vec_ref[...] = jnp.zeros_like(vec_ref)
    vec_ref[:, 6 * width + hidden : 6 * width + hidden + bottle] = fold_rows(grad_embed.astype(jnp.float32))
    for c in range(0, hid, 256):
        cols = slice(c, c + 256)
        grad = (slope2_ref[:, cols] * against(grad_embed, w3_ref[cols, :])).astype(low)
        common_ref[:, cols] = grad
        vec_ref[:, 7 * width + hidden + hid + c : 7 * width + hidden + hid + c + 256] = fold_rows(grad.astype(jnp.float32))
    grad_two = common_ref[:, :hid]
    for c in range(0, hid, 256):
        cols = slice(c, c + 256)
        grad = (slope1_ref[:, cols] * against(grad_two, w2_ref[cols, :])).astype(low)
        back_ref[:, cols] = grad
        vec_ref[:, 7 * width + hidden + c : 7 * width + hidden + c + 256] = fold_rows(grad.astype(jnp.float32))
        share(2, c, grad)
    grad = against(back_ref[...], w1_ref[...])
    vec_ref[:, 4 * width : 5 * width] = fold_rows(grad * normed_f)
    vec_ref[:, 5 * width : 6 * width] = fold_rows(grad)
    grad_class = standard_back(grad, normed_f, rstd_f, final_ref[0:1, :])
    grad_low = grad_class.astype(low)
    vec_ref[:, 3 * width : 4 * width] = fold_rows(grad_low.astype(jnp.float32))
    up2_ref[...] = inner_rows(act_ref[...], grad_low).astype(low)
    for c in range(0, hidden, 256):
        cols = slice(c, c + 256)
        grad = (slope_ref[:, cols] * against(grad_low, w_fc2_ref[cols, :])).astype(low)
        act_ref[:, cols] = grad
        vec_ref[:, 6 * width + c : 6 * width + c + 256] = fold_rows(grad.astype(jnp.float32))
    grad_pre = act_ref[...]
    up1_ref[...] = inner_rows(low_d, grad_pre).astype(low)
    grad = against(grad_pre, w_fc1_ref[...])
    vec_ref[:, :width] = fold_rows(grad * normed_d)
    vec_ref[:, width : 2 * width] = fold_rows(grad)
    grad_middle = grad_class + standard_back(grad, normed_d, rstd_d, gains_ref[3:4, :])
    cres_ref[...] = grad_middle
    grad_low = grad_middle.astype(low)
    da_ref[...] = grad_low.astype(jnp.float32)
    vec_ref[:, 2 * width : 3 * width] = fold_rows(grad_low.astype(jnp.float32))
    cg_ref[...] = against(grad_low, w_out_ref[...]).astype(low).astype(jnp.float32)
    finish_rows(vec_ref)
    write_unit(me_ref[0], keep_ref, send_ref, 0, from_square(up1_ref), True)
    write_unit(me_ref[0], keep_ref, send_ref, 1, from_tall(up2_ref), True)


def head_sum_kernel(
    width, common0_ref, common1_ref, common2_ref, common3_ref, share0_ref, share1_ref, share2_ref, share3_ref,
    parts_ref,
):
    quarter = share0_ref.shape[1] // 3
    full = quarter * 4
    share = jnp.concatenate([ref[...] for ref in (share0_ref, share1_ref, share2_ref, share3_ref)])
    common = jnp.concatenate([ref[...] for ref in (common0_ref, common1_ref, common2_ref, common3_ref)])
    low = jnp.bfloat16
    parts = [share[:, i * quarter : (i + 1) * quarter].T for i in range(3)]
    parts_ref[:, :width] = product(parts[2], common[:, full : full + width]).astype(low)
    for c in range(0, full, 512):
        parts_ref[:, width + c : width + c + 512] = product(parts[0], common[:, c : c + 512]).astype(low)
    mark = parts_ref.shape[1]
    parts_ref[:, width + full :] = product(parts[1], common[:, width + full : mark]).astype(low)


def proto_back_kernel(
    scale, owner_ref, unit_ref, proto_ref, inv_ref, thawed_ref, expo_ref, feats_ref,
    grad_ref,
    acc_ref, raw_ref,
):
    step = pl.program_id(0)
    bottle = unit_ref.shape[0]

    @pl.when(step == 0)
    def _():
        acc_ref[...] = jnp.zeros_like(acc_ref)

    rows = feats_ref.shape[0]
    slots = rows // 8
    images = slots // MOST_CROPS
    for l in range(8):
        here = slice(l * slots, (l + 1) * slots)
        extra = feats_ref[here, bottle:].astype(jnp.float32)
        lane = lax.broadcasted_iota(jnp.int32, extra.shape, 1)
        pick = lambda a, b: jnp.sum(jnp.where((lane >= a) & (lane < b), extra, 0.0), axis=1, keepdims=True)
        logits = product(feats_ref[here, :bottle], unit_ref[...]) * (1.0 / STUDENT_TEMP)
        target = repeat_rows(expo_ref[pl.ds(pl.multiple_of(owner_ref[step * 8 + l] * images, 8), images), :], pick(7, 8))
        raw = pick(0, 1) * (jnp.exp(logits - pick(1, 4)) - target * jnp.exp(-pick(4, 7))) * scale
        raw_ref[here, :] = raw.astype(jnp.bfloat16)
    acc_ref[...] += inner_rows(feats_ref[:, :bottle], raw_ref[...])

    @pl.when(step == pl.num_programs(0) - 1)
    def _():
        proto = proto_ref[...].astype(jnp.float32)
        inv = inv_ref[...]
        grad = acc_ref[...]
        inner = jnp.sum(proto * grad, axis=0, keepdims=True)
        grad_ref[...] = (inv * grad - proto * (inv * inv * inv * inner)) * thawed_ref[...]


def whole(array):
    return pl.BlockSpec(array.shape, lambda *i: (0,) * len(array.shape))


class Layer:
    def __init__(self, array, layer):
        self.array, self.layer = array, layer


class Far:
    def __init__(self, array):
        self.array = array


def spec_of(item):
    if isinstance(item, Far):
        return pl.BlockSpec(memory_space=pl.ANY)
    if isinstance(item, Layer):
        shape = item.array.shape[1:]
        return pl.BlockSpec((None,) + shape, lambda *i: (item.layer,) + (0,) * len(shape))
    return whole(item)


def array_of(item):
    return item.array if isinstance(item, (Layer, Far)) else item


def run_kernel(body, steps, scalars, whole_in, step_in, outs, scratch, micros, count=None):
    if count is not None:
        scalars = [count.reshape(1)] + scalars
        inner = body

        def body(count_ref, *refs):
            @pl.when(pl.program_id(0) < count_ref[0])
            def _():
                inner(count_ref, *refs)

    def by_step(rows, width):
        if count is None:
            return pl.BlockSpec((rows, width), lambda i, *s: (i, 0))
        return pl.BlockSpec((rows, width), lambda i, c, *s: (jnp.minimum(i, c[0] - 1), 0))

    return pl.pallas_call(
        body,
        grid_spec=pltpu.PrefetchScalarGridSpec(
            num_scalar_prefetch=len(scalars),
            grid=(steps,),
            in_specs=[spec_of(a) for a in whole_in] + [by_step(rows, a.shape[1]) for a, rows in step_in],
            out_specs=[
                by_step(rows, shape[1]) if rows else pl.BlockSpec(shape, lambda *i, k=len(shape): (0,) * k)
                for shape, dtype, rows in outs
            ],
            scratch_shapes=scratch,
        ),
        out_shape=[jax.ShapeDtypeStruct(shape, dtype) for shape, dtype, rows in outs],
        compiler_params=pltpu.CompilerParams(
            dimension_semantics=("arbitrary",), vmem_limit_bytes=56 * 1024 * 1024
        ),
        cost_estimate=pl.CostEstimate(flops=micros * 10**9, bytes_accessed=2**20, transcendentals=0),
    )(*scalars, *[array_of(a) for a in whole_in], *[a for a, rows in step_in])


def score_masks(seq_len):
    key = jnp.arange(PAIR)[:, None]
    query = (jnp.arange(2 * PAIR) % PAIR)[None, :]
    pair = (key // PITCH == query // PITCH) & (key % PITCH < seq_len)
    key = jnp.arange(GROUP * PITCH)[:, None]
    column = (jnp.arange(HEADS * GROUP) % GROUP)[None, :]
    single = (key // PITCH == column) & (key % PITCH < seq_len)
    return [jnp.where(m, 0.0, NEVER).astype(jnp.float32) for m in (pair, single, pair[:, :PAIR].T)]


def axis_bits(n):
    bits = n.bit_length() - 1
    assert n == 1 << bits
    return bits


def swap(values, mask, n):
    return lax.ppermute(values, "dp", [(i, i ^ mask) for i in range(n)])


def group_masks(group):
    return [k << group[0] for k in range(1 << len(group))]


def own_digit(group):
    return (lax.axis_index("dp") >> group[0]) & ((1 << len(group)) - 1)


def upper_groups(n, first):
    bits = list(range(first, axis_bits(n)))
    return [bits[i : i + 2] for i in range(0, len(bits), 2)][::-1]


def gather_loose(block, group, n):
    return jnp.stack([swap(block, mask, n) if mask else block for mask in group_masks(group)])


def tree_sum(parts):
    while len(parts) > 1:
        parts = [parts[i] + parts[i + 1] for i in range(0, len(parts), 2)]
    return parts[0]


def scatter_send(parts, group):
    size = 1 << len(group)
    parts = parts.reshape((size, parts.shape[0] // size) + parts.shape[1:])
    digit = own_digit(group)
    return [lax.dynamic_index_in_dim(parts, digit ^ k, 0, keepdims=False) for k in range(size)]


def double(mine, got):
    return jnp.concatenate([mine, got])


def pick_send(parts, axis, group):
    digit = own_digit(group)
    return [lax.dynamic_index_in_dim(parts, digit ^ k, axis, keepdims=False) for k in range(2)]


def swap_parts(parts, group, n):
    return [swap(part, mask, n) if mask else part for part, mask in zip(parts, group_masks(group))]


def scatter_stage(parts, group, n):
    got = swap_parts(scatter_send(parts, group), group, n)
    return tree_sum([part.astype(jnp.float32) for part in got]).astype(parts.dtype)


def sum_stage(values, group, n):
    return tree_sum(swap_parts([values] * (1 << len(group)), group, n))


def fold_send(parts, group):
    size = 1 << len(group)
    parts = parts.reshape((size, parts.shape[0] // size) + parts.shape[1:])
    return [parts[k] for k in range(size)]


def fold_sum(parts):
    return tree_sum([part.astype(jnp.float32) for part in parts]).astype(parts[0].dtype)


def unfold_stage(parts, group, n):
    return jnp.concatenate([swap(parts, mask, n) if mask else parts for mask in group_masks(group)])


def extra_sum(values, n):
    for bit in range(5, axis_bits(n)):
        values = values + swap(values, 1 << bit, n)
    return values


def together(*values):
    return lax.optimization_barrier(values)


CORE, PLANE, LINE = [0], [1, 2], [3, 4]


def per_device(
    tokens,
    layer_gains,
    layer_shifts,
    w_qkv,
    b_qv,
    w_out,
    b_out,
    w_fc1,
    b_fc1,
    w_fc2,
    b_fc2,
    final_gain,
    final_shift,
    head_w1,
    head_b1,
    head_w2,
    head_b2,
    head_w3,
    head_b3,
    prototypes,
    crop_counts,
    teacher_logits,
    first_epoch,
):
    low, wide = jnp.bfloat16, jnp.float32
    slot_count, seq_len, width = tokens.shape
    n = lax.axis_size("dp")
    device = lax.axis_index("dp")
    me = (device & (BLOCKS - 1)).reshape(1)
    bottle = prototypes.shape[0]
    hidden = w_fc1.shape[2]
    hid = head_w2.shape[0]
    rows = GROUP * PITCH
    padded = slot_count * PITCH
    row_count = slot_count * seq_len
    groups = upper_groups(n, 3)

    scale = 1.0 / (STUDENT_TEMP * n)
    images, protos = teacher_logits.shape
    unit_low, unit_turned, col_inv, teach_sum, teach_expo = run_kernel(
        prepare_kernel,
        1,
        [],
        [prototypes, teacher_logits],
        [],
        [
            ((bottle, protos), low, 0),
            ((protos, bottle), low, 0),
            ((1, protos), wide, 0),
            ((images, bottle + 128), wide, 0),
            ((images, protos), wide, 0),
        ],
        [],
        4,
    )
    unit_all = lax.all_gather(unit_turned, "dp", axis=0, tiled=True)
    teach_sum = teach_sum.reshape(n, -1, bottle + 128)
    for group in groups[:-1]:
        teach_sum = scatter_stage(teach_sum, group, n)

    per = slot_count // MOST_CROPS
    own_counts = lax.dynamic_slice_in_dim(crop_counts, device * per, per)
    place = jnp.arange(slot_count, dtype=jnp.int32)[:, None]

    def ranked(counts, place):
        ends = jnp.sum(jnp.where(jnp.arange(per)[:, None] <= jnp.arange(per)[None, :], counts[:, None], 0), axis=0)
        past = ends[None, :] <= place
        return jnp.sum(past, axis=1).astype(jnp.int32), place[:, 0] - jnp.sum(jnp.where(past, counts, 0), axis=1)

    live_count = jnp.sum(own_counts)
    live_image, live_rank = ranked(own_counts, place)
    dead_image, dead_rank = ranked(MOST_CROPS - own_counts, place - live_count)
    dead_start = jnp.sum(jnp.where(dead_image[:, None] == jnp.arange(per), own_counts, 0), axis=1)
    is_live = place[:, 0] < live_count
    image = jnp.where(is_live, live_image, dead_image)
    order = image * MOST_CROPS + jnp.where(is_live, live_rank, dead_start + dead_rank)
    count = (live_count + GROUP - 1) // GROUP
    steps = slot_count // GROUP
    own_live = is_live.astype(wide)[:, None]
    image = image.astype(wide)[:, None]

    zero_bias = jnp.zeros((2, width), wide)
    pair_mask, class_mask, key_mask = score_masks(seq_len)
    gains = layer_gains.reshape(4, width)
    shifts = layer_shifts.reshape(4, width)
    full_bias = jnp.concatenate([b_qv[:, :width], zero_bias, b_qv[:, width:]], axis=1)[:, None]
    b_out, b_fc1, b_fc2 = b_out[:, None], b_fc1[:, None], b_fc2[:, None]
    turned_tokens = tokens.transpose(1, 0, 2)
    all_rows = pltpu.VMEM((width // 128, row_count, 128), wide)
    teach_parts = scatter_send(teach_sum, groups[-1])
    turned_tokens, *teach_parts = together(turned_tokens, *teach_parts)
    teach_parts = swap_parts(teach_parts, groups[-1], n)
    qkv_a, attn_a, middle_a = run_kernel(
        attend_kernel,
        steps,
        [order],
        [turned_tokens, key_mask, gains, shifts, Layer(w_qkv, 0), Layer(full_bias, 0), Layer(w_out, 0), Layer(b_out, 0)],
        [],
        [((padded, 3 * width), low, rows), ((padded, width), low, rows), ((padded, width), wide, rows)],
        [all_rows, pltpu.VMEM((rows, width), wide), pltpu.VMEM((rows, width), low)],
        35,
        count,
    )
    middle_a, *teach_parts = together(middle_a, *teach_parts)
    teach_sum = tree_sum(teach_parts)
    teach_parts = scatter_send(teach_sum, PLANE)
    middle_a, *teach_parts = together(middle_a, *teach_parts)
    teach_parts = swap_parts(teach_parts, PLANE, n)
    act_a, slope_a, lower_out, kv_c, query_c, attn_c, first_low, first_in = run_kernel(
        mlp_kernel,
        steps,
        [],
        [class_mask, gains, shifts, Layer(w_fc1, 0), Layer(b_fc1, 0), Layer(w_fc2, 0), Layer(b_fc2, 0), Layer(w_qkv, 1), Layer(full_bias, 1)],
        [(middle_a, rows)],
        [
            ((padded, hidden), low, rows),
            ((padded, hidden), low, rows),
            ((padded, width), wide, rows),
            ((padded, 2 * width), low, rows),
            ((slot_count, width), wide, 0),
            ((slot_count, width), wide, 0),
            ((slot_count, width), wide, 0),
            ((slot_count, width), wide, 0),
        ],
        [pltpu.VMEM((rows, width), low), pltpu.VMEM((rows, width), wide)],
        40,
        count,
    )
    first_in, *teach_parts = together(first_in, *teach_parts)
    teach_sum = scatter_stage(tree_sum(teach_parts), CORE, n)[0]

    finals = jnp.stack([final_gain, final_shift])
    vec_width = -(-(7 * width + hidden + 2 * hid) // width) * width
    grad_attended, grad_middle_c, grad_attn, common, feats, shares, keep_u, send_u, vec_h = run_kernel(
        functools.partial(head_kernel, scale, hid // n),
        1,
        [me],
        [own_live, image, teach_sum, attn_c, first_in, gains, shifts, finals, Layer(w_out, 1), Layer(b_out, 1), Far(w_fc1), Layer(b_fc1, 1), Far(w_fc2), Layer(b_fc2, 1),
         Far(head_w1), head_b1[None], Far(head_w2), head_b2[None], Far(head_w3), head_b3[None], Far(unit_all)],
        [],
        [
            ((slot_count, width), wide, 0),
            ((slot_count, width), wide, 0),
            ((slot_count, width), wide, 0),
            ((slot_count, hid + width + bottle), low, 0),
            ((slot_count, bottle + 128), low, 0),
            ((4, slot_count, hid // 4 * 3), low, 0),
            ((BLOCKS // 2, 2, width // 8, width), low, 0),
            ((BLOCKS // 2, 2, width // 8, width), low, 0),
            ((8, vec_width), wide, 0),
        ],
        [
            pltpu.VMEM((slot_count, hidden), low),
            pltpu.VMEM((slot_count, hidden), wide),
            pltpu.VMEM((slot_count, hid), wide),
            pltpu.VMEM((slot_count, hid), wide),
            pltpu.VMEM((slot_count, hid), low),
            pltpu.VMEM((slot_count, hid), low),
            pltpu.VMEM((slot_count, hid), low),
            pltpu.VMEM((width, hidden), low),
            pltpu.VMEM((hidden, width), low),
        ]
        + [pltpu.VMEM(v.shape, low) for v in (w_fc1[0], w_fc2[0], head_w1, head_w2, head_w3, unit_all)]
        + [pltpu.SemaphoreType.DMA((6,))],
        20,
    )
    shares = shares.reshape((2, 2) + shares.shape[1:])
    core = own_digit([0])
    share_own = lax.dynamic_index_in_dim(shares, core, 1, keepdims=False)
    share_got = swap(lax.dynamic_index_in_dim(shares, 1 - core, 1, keepdims=False), 1, n)
    common_got = swap(common, 1, n)
    spot = own_digit([1])
    share0, share1 = (lax.dynamic_index_in_dim(v, spot, 0, keepdims=False) for v in (share_own, share_got))
    share2, share3 = (lax.dynamic_index_in_dim(v, 1 - spot, 0, keepdims=False) for v in (share_own, share_got))
    bits = list(range(5, axis_bits(n))) + [4, 3, 1, 2, 0]
    masks = [0]
    for bit in bits:
        masks = masks + [mask | (1 << bit) for mask in masks]
    for bit in bits[:-5]:
        feats = double(feats, swap(feats, 1 << bit, n))
    grad_attended, common, share2, share3, send_u, feats = together(grad_attended, common, share2, share3, send_u, feats)
    got_u = swap(send_u, 1, n)
    feats_got = swap(feats, 16, n)
    common2, share2, share3 = (swap(v, 2, n) for v in (common, share2, share3))
    grad_lower_out, unit_u, vec_c = run_kernel(
        upper_back_kernel,
        steps,
        [],
        [class_mask, gains, shifts, Layer(w_qkv, 1), first_low, attn_c, grad_attn],
        [(lower_out, rows), (kv_c, rows), (query_c, GROUP), (grad_attended, GROUP), (grad_middle_c, GROUP)],
        [
            ((padded, width), wide, rows),
            ((width, 4 * width), low, 0),
            ((8, 4 * width), wide, 0),
        ],
        [pltpu.VMEM((width, 4 * width), wide), pltpu.VMEM((rows, width), wide), pltpu.VMEM((slot_count, width), wide)],
        20,
        count,
    )
    grad_lower_out, common2, share2, share3, got_u, feats_got = together(
        grad_lower_out, common2, share2, share3, got_u, feats_got
    )
    feats = double(feats, feats_got)
    common3 = swap(common2, 1, n)
    parts_u = fold_send(keep_u + got_u, LINE)
    head_parts = run_kernel(
        functools.partial(head_sum_kernel, width),
        1,
        [],
        [common, common_got, common2, common3, share0, share1, share2, share3],
        [],
        [((hid // 4, width + hid + bottle), low, 0)],
        [],
        6,
    )[0]
    head_keep, head_send = pick_send(head_parts.reshape(n // 8, 2, hid // n, -1), 1, [2])
    grad_lower_out, head_send, feats, *parts_u = together(grad_lower_out, head_send, feats, *parts_u)
    head_got, feats_got = swap(head_send, 4, n), swap(feats, 8, n)
    parts_u = swap_parts(parts_u, LINE, n)
    grad_middle_a, keep_m, send_m, vec_b, vec_hidden = run_kernel(
        mlp_back_kernel,
        steps,
        [me],
        [unit_u, gains, shifts, Layer(w_fc1, 0), Layer(w_fc2, 0)],
        [(grad_lower_out, rows), (middle_a, rows), (act_a, rows), (slope_a, rows)],
        [
            ((padded, width), wide, rows),
            ((BLOCKS // 2, 3, width // 8, width), low, 0),
            ((BLOCKS // 2, 3, width // 8, width), low, 0),
            ((8, 3 * width), wide, 0),
            ((8, hidden), wide, 0),
        ],
        [
            pltpu.VMEM((width, hidden), wide),
            pltpu.VMEM((width, hidden), wide),
            pltpu.VMEM((rows, hidden), low),
            pltpu.VMEM((hidden, width), wide),
        ],
        40,
        count,
    )
    grad_middle_a, head_got, feats_got, send_m, *parts_u = together(grad_middle_a, head_got, feats_got, send_m, *parts_u)
    feats = double(feats, feats_got)
    head_parts = head_keep + head_got
    for bit in range(axis_bits(n) - 1, 4, -1):
        head_parts = scatter_stage(head_parts, [bit], n)
    head_keep, head_send = pick_send(head_parts.reshape((2, 2) + head_parts.shape[1:]), 1, [3])
    parts_m = [
        jnp.concatenate([a.reshape((-1,) + a.shape[2:]), b[0]])
        for a, b in zip(fold_send(keep_m + swap(send_m, 1, n), PLANE), fold_send(fold_sum(parts_u), PLANE))
    ]
    grad_middle_a, head_send, *parts_m = together(grad_middle_a, head_send, *parts_m)
    head_got = swap(head_send, 8, n)
    parts_m = swap_parts(parts_m, PLANE, n)
    grad_qkv, grad_wo, vec_a = run_kernel(
        attend_back_kernel,
        steps,
        [],
        [pair_mask, Layer(w_out, 0)],
        [(grad_middle_a, rows), (qkv_a, rows), (attn_a, rows)],
        [((padded, 3 * width), low, rows), ((width, width), wide, 0), ((8, 4 * width), wide, 0)],
        [pltpu.VMEM((rows, width), low)],
        40,
        count,
    )
    grad_qkv, head_got, *parts_m = together(grad_qkv, head_got, *parts_m)
    head_keep, head_send = pick_send(head_keep + head_got, 0, [4])
    sum_m = fold_sum(parts_m)
    sum_u = sum_m[None, 12:]
    parts_m = fold_send(sum_m[:12].reshape((4, 3) + sum_m.shape[1:]), LINE)
    grad_qkv, head_send, feats, *parts_m = together(grad_qkv, head_send, feats, *parts_m)
    feats_got = swap(feats, 2, n)
    parts_m = swap_parts(parts_m, LINE, n)
    keep_a, send_a = run_kernel(
        weight_back_kernel,
        steps,
        [me, order],
        [turned_tokens, gains, shifts, grad_wo],
        [(grad_qkv, rows)],
        [
            ((BLOCKS // 2, 1, width // 8, width), low, 0),
            ((BLOCKS // 2, 1, width // 8, width), low, 0),
        ],
        [all_rows, pltpu.VMEM((rows, width), wide), pltpu.VMEM((width, 4 * width), wide)],
        10,
        count,
    )
    keep_a, send_a, feats_got, *parts_m = together(keep_a, send_a, feats_got, *parts_m)
    feats = double(feats, feats_got)
    sum_m = extra_sum(jnp.concatenate([fold_sum(parts_m), sum_u], axis=1), n)
    keep_a, send_a = fold_send(keep_a + swap(send_a, 1, n), [2])
    grad_qkv, sum_m, send_a, feats = together(grad_qkv, sum_m, send_a, feats)
    feats_got = swap(feats, 4, n)
    parts_m = swap_parts([sum_m] * 4, LINE, n)
    got_a = swap(send_a, 4, n)
    grad_tokens, vec_in = run_kernel(
        input_back_kernel,
        steps,
        [order],
        [turned_tokens, gains, Layer(w_qkv, 0)],
        [(grad_middle_a, rows), (grad_qkv, rows)],
        [((row_count, width), wide, 0), ((8, 2 * width), wide, 0)],
        [all_rows, all_rows, pltpu.VMEM((rows, width), wide)],
        20,
        count,
    )
    tokens_grad = grad_tokens.reshape(seq_len, slot_count, width).transpose(1, 0, 2)
    vec_in, got_a, feats_got, *parts_m = together(vec_in, got_a, feats_got, *parts_m)
    feats = double(feats, feats_got)
    feats = double(feats, swap(feats, 1, n))

    keep_a, send_a = fold_send(keep_a + got_a, [1])
    vectors = jnp.concatenate(
        [v[:1] for v in (vec_in, vec_b, vec_c, vec_h, vec_a, vec_hidden)], axis=1
    )
    vectors = vectors + swap(vectors, 1, n)
    sum_a = keep_a + swap(send_a, 2, n)
    sum_m = jnp.concatenate(parts_m)
    half = sum_m.shape[0] // 2
    feats, vectors, sum_a, sum_m = together(feats, vectors, sum_a, sum_m)
    one, two = sum_m[:half], sum_m[half:]
    one, two = [one, swap(one, 2, n)], [two, swap(two, 4, n)]
    prototypes_grad = run_kernel(
        functools.partial(proto_back_kernel, scale),
        n // 8,
        [device ^ jnp.array(masks, jnp.int32)],
        [unit_low, prototypes, col_inv, (1 - first_epoch).astype(wide)[None], teach_expo],
        [(feats, 8 * slot_count)],
        [(prototypes.shape, wide, 0)],
        [pltpu.VMEM(prototypes.shape, wide), pltpu.VMEM((8 * slot_count, protos), low)],
        6,
    )[0]
    prototypes_grad, *parts_m = together(prototypes_grad, *one, *two)
    one, two = jnp.stack(parts_m[:2]), jnp.stack(parts_m[2:])
    one, two = [one, swap(one, 4, n)], [two, swap(two, 2, n)]
    for bit in (4, 3):
        keep_a, send_a = fold_send(sum_a, [bit])
        sum_a = keep_a + swap(send_a, 1 << bit, n)
    sum_a = extra_sum(sum_a, n)
    for bit in range(3, axis_bits(n)):
        vectors = vectors + swap(vectors, 1 << bit, n)
    for bit in (3, 4):
        sum_a = unfold_stage(sum_a, [bit], n)
    head_send, sum_a, vectors, *parts_m = together(head_send, sum_a, vectors, *one, *two)
    head_got = swap(head_send, 16, n)
    one = jnp.stack(parts_m[:2]).reshape((4,) + parts_m[0].shape[1:])
    two = jnp.stack(parts_m[2:], axis=1).reshape((4,) + parts_m[0].shape[1:])
    sum_m = jnp.concatenate([one, two], axis=1).reshape((BLOCKS // 2,) + one.shape[2:])
    got_m = swap(sum_m, 1, n)
    for bit in (1, 2):
        sum_a = unfold_stage(sum_a, [bit], n)
        vectors = vectors + swap(vectors, 1 << bit, n)
    vectors = vectors.reshape(-1, width)
    got_a = swap(sum_a, 1, n)
    specs = [
        pl.BlockSpec((None, width // 8, 3 * width), lambda i: (1, i, 0)),
        pl.BlockSpec((None, width // 8, width), lambda i: (1, i, 0)),
    ]
    shapes = [jax.ShapeDtypeStruct(s, wide) for s in ((2, width, 3 * width), (2, width, width))]
    params = pltpu.CompilerParams(dimension_semantics=("arbitrary",), vmem_limit_bytes=56 * 1024 * 1024)
    qkv_grad, out_grad, fc1_grad, fc2_grad = pl.pallas_call(
        unpack_kernel,
        grid=(8,),
        in_specs=[pl.BlockSpec(memory_space=pltpu.SMEM), whole(sum_m), whole(got_m)],
        out_specs=specs
        + [
            pl.BlockSpec((2, width // 8, hidden), lambda i: (0, i, 0)),
            pl.BlockSpec((2, hidden // 8, width), lambda i: (0, i, 0)),
        ],
        out_shape=shapes + [jax.ShapeDtypeStruct(s, wide) for s in ((2, width, hidden), (2, hidden, width))],
        compiler_params=params,
        cost_estimate=pl.CostEstimate(flops=8 * 10**9, bytes_accessed=2**20, transcendentals=0),
    )(me, sum_m, got_m)
    specs = [pl.BlockSpec(spec.block_shape, lambda i: (0, i, 0)) for spec in specs]
    qkv_grad, out_grad = pl.pallas_call(
        unpack_first_kernel,
        grid=(8,),
        in_specs=[pl.BlockSpec(memory_space=pltpu.SMEM), whole(sum_a), whole(got_a)] + [pl.BlockSpec(memory_space=pl.ANY)] * 2,
        out_specs=specs,
        out_shape=shapes,
        input_output_aliases={3: 0, 4: 1},
        compiler_params=params,
    )(me, sum_a, got_a, qkv_grad, out_grad)
    head_sum = (head_keep.astype(wide) + head_got.astype(wide)).reshape(hid // n, -1)

    row_in, row_b, row_c, row_h = 0, 2, 5, 9
    row_a = row_h + vec_width // width
    row_hidden = row_a + 4
    pick = lambda *where: jnp.stack([vectors[i] for i in where])
    ends = vectors[row_h + 7 + hidden // width : row_a].reshape(-1)
    own_part = lambda start: lax.dynamic_slice_in_dim(ends, start + device * (hid // n), hid // n)

    return (
        tokens_grad,
        pick(row_in, row_b + 1, row_c + 1, row_h).reshape(2, 2, width),
        pick(row_in + 1, row_b + 2, row_c + 2, row_h + 1).reshape(2, 2, width),
        qkv_grad,
        pick(row_a + 1, row_a + 3, row_c + 3, row_c).reshape(2, 2 * width),
        out_grad,
        pick(row_a, row_h + 2),
        fc1_grad,
        jnp.concatenate([vectors[row_hidden:], vectors[row_h + 6 : row_h + 6 + hidden // width]]).reshape(2, hidden),
        fc2_grad,
        pick(row_b, row_h + 3),
        vectors[row_h + 4],
        vectors[row_h + 5],
        head_sum[:, :width].T,
        own_part(0),
        head_sum[:, width : width + hid],
        own_part(hid),
        head_sum[:, width + hid : width + hid + bottle],
        vectors[row_h + 6 + hidden // width, :bottle],
        prototypes_grad,
    )


def solution(mesh):
    return jax.shard_map(
        per_device,
        mesh=mesh,
        in_specs=(
            P("dp", None, None),
            P(),
            P(),
            P(),
            P(),
            P(),
            P(),
            P(),
            P(),
            P(),
            P(),
            P(),
            P(),
            P(),
            P(),
            P(),
            P(),
            P(),
            P(),
            P(None, "dp"),
            P(),
            P(None, "dp"),
            P("dp"),
        ),
        out_specs=(
            P("dp", None, None),
            P(),
            P(),
            P(),
            P(),
            P(),
            P(),
            P(),
            P(),
            P(),
            P(),
            P(),
            P(),
            P(None, "dp"),
            P("dp"),
            P("dp", None),
            P("dp"),
            P("dp", None),
            P(),
            P(None, "dp"),
        ),
        check_vma=False,
    )
```

```python
import functools

import jax
import jax.numpy as jnp
from jax import lax
from jax.experimental import pallas as pl
from jax.experimental.pallas import tpu as pltpu
from jax.sharding import PartitionSpec as P

HEADS = 6
HD = 64
MOST_CROPS = 10

STUDENT_TEMP = 0.1
TEACHER_TEMP = 0.04
EPS = 1e-06
SHIFT = 10.0


def product(left, right):
    return jnp.dot(left, right, preferred_element_type=jnp.float32)


def against(left, right):
    return lax.dot_general(
        left, right, (((1,), (1,)), ((), ())), preferred_element_type=jnp.float32
    )


def inner_rows(left, right):
    return lax.dot_general(
        left, right, (((0,), (0,)), ((), ())), preferred_element_type=jnp.float32
    )


def column_sum(values):
    return jnp.sum(values.astype(jnp.float32), axis=0)


def norm_forward(values, gain, shift):
    centered = values - jnp.mean(values, axis=-1, keepdims=True)
    rstd = lax.rsqrt(jnp.mean(centered * centered, axis=-1, keepdims=True) + EPS)
    normed = centered * rstd
    return (normed * gain + shift, normed, rstd)


def norm_backward(grad, normed, rstd, gain):
    scaled = grad * gain
    inner = (
        scaled
        - jnp.mean(scaled, axis=-1, keepdims=True)
        - normed * jnp.mean(scaled * normed, axis=-1, keepdims=True)
    )
    return (rstd * inner, jnp.sum(grad * normed, axis=0), jnp.sum(grad, axis=0))


GROUP = 16
BLOCKS = 32
PITCH = 40
PAIR = 2 * PITCH
NEVER = -1e30
SEQ_LEN = 37


def smooth_both(values):
    size = jnp.abs(values)
    bell = jnp.exp(values * values * -0.5)
    t = 1.0 / (1.0 + 0.23164189 * size)
    tail = t * (0.127414796 + t * (-0.142248368 + t * (0.7107068705 + t * (-0.7265760135 + t * 0.5307027145))))
    upper = tail * bell
    area = jnp.where(values >= 0, 1.0 - upper, upper)
    return values * area, area + values * (bell * 0.3989422804014327)


def norm_row(ref, index):
    return ref[index // 2, index % 2 : index % 2 + 1, :]


def qkv_bias(ref, layer, part, width):
    if part == 1:
        return 0.0
    return ref[layer : layer + 1, part // 2 * width : (part // 2 + 1) * width]


def standardize(values):
    centered = values - jnp.mean(values, axis=-1, keepdims=True)
    rstd = lax.rsqrt(jnp.mean(centered * centered, axis=-1, keepdims=True) + EPS)
    return centered * rstd, rstd


def standard_back(grad, normed, rstd, gain):
    scaled = grad * gain
    return rstd * (
        scaled
        - jnp.mean(scaled, axis=-1, keepdims=True)
        - normed * jnp.mean(scaled * normed, axis=-1, keepdims=True)
    )


def fold_rows(values):
    return jnp.sum(values.reshape(-1, 8, values.shape[1]), axis=0)


def finish_rows(ref):
    ref[0:1, :] = jnp.sum(ref[...], axis=0, keepdims=True)


def both_heads(values):
    lane = lax.broadcasted_iota(jnp.int32, values.shape, 1)
    zero = jnp.zeros_like(values)
    return jnp.concatenate([jnp.where(lane < HD, values, zero), jnp.where(lane < HD, zero, values)])


def join_heads(values):
    rows = values.shape[0] // 2
    lane = lax.broadcasted_iota(jnp.int32, (rows, values.shape[1]), 1)
    return jnp.where(lane < HD, values[:rows], values[rows:])


def spread_heads(values):
    lane = lax.broadcasted_iota(jnp.int32, values.shape, 1) // HD
    return jnp.concatenate([jnp.where(lane == h, values, 0.0) for h in range(HEADS)])


def gather_heads(values):
    lane = lax.broadcasted_iota(jnp.int32, (GROUP, values.shape[1]), 1) // HD
    out = jnp.zeros((GROUP, values.shape[1]), values.dtype)
    for h in range(HEADS):
        out = jnp.where(lane == h, values[h * GROUP : (h + 1) * GROUP], out)
    return out


def slot_and_valid(shape, dim, seq_len):
    index = lax.broadcasted_iota(jnp.int32, shape, dim)
    slot = index // PITCH
    return slot, index - slot * PITCH < seq_len


def pair_mask(rows_are_keys, seq_len, copies=1):
    shape = (PAIR, PAIR)
    key, valid = slot_and_valid(shape, 0 if rows_are_keys else 1, seq_len)
    query, _ = slot_and_valid(shape, 1 if rows_are_keys else 0, seq_len)
    mask = jnp.where((key == query) & valid, 0.0, NEVER)
    return jnp.concatenate([mask] * copies, axis=1 if rows_are_keys else 0)


def class_mask(seq_len):
    shape = (GROUP * PITCH, GROUP)
    key, valid = slot_and_valid(shape, 0, seq_len)
    mask = jnp.where((key == lax.broadcasted_iota(jnp.int32, shape, 1)) & valid, 0.0, NEVER)
    return jnp.concatenate([mask] * HEADS, axis=1)


def soft_columns(scores):
    expo = jnp.exp(scores - jnp.max(scores, axis=0, keepdims=True))
    return expo * (1.0 / jnp.sum(expo, axis=0, keepdims=True))


def take_slots(order_ref, all_ref, rows_ref, step, seq_len, slots):
    for s in range(GROUP):
        for c in range(all_ref.shape[0]):
            rows_ref[s * PITCH : s * PITCH + seq_len, c * 128 : (c + 1) * 128] = all_ref[
                c, pl.ds(order_ref[step * GROUP + s], seq_len, stride=slots), :
            ]


def first_rows(ref):
    return jnp.concatenate([ref[s * PITCH : s * PITCH + 1, :] for s in range(GROUP)])


def add_first_rows(ref, values):
    for s in range(GROUP):
        ref[s * PITCH : s * PITCH + 1, :] += values[s : s + 1]


def widen_tokens(tok_ref, all_ref):
    seq_len, slots, width = tok_ref.shape

    @pl.loop(0, seq_len)
    def _(t):
        wide = tok_ref[t].astype(jnp.float32)
        for c in range(all_ref.shape[0]):
            all_ref[c, pl.ds(pl.multiple_of(t * slots, 8), slots), :] = wide[:, c * 128 : (c + 1) * 128]


def ordered_masks(line_first=False):
    if line_first:
        return [(p >> 4) | ((p & 3) << 1) | (((p >> 2) & 3) << 3) for p in range(BLOCKS)]
    return [(p >> 4) | (((p >> 2) & 3) << 1) | ((p & 3) << 3) for p in range(BLOCKS)]


def write_unit(me, keep_ref, send_ref, unit, read, line_first=False):
    for p, mask in enumerate(ordered_masks(line_first)):
        owner = me ^ mask
        ref = keep_ref if p < BLOCKS // 2 else send_ref
        ref[p % (BLOCKS // 2), unit] = read(owner)


def from_square(ref, first=0):
    width = ref.shape[0]

    def read(owner):
        rows = pl.multiple_of((owner // 4) * (width // 8), 16)
        cols = pl.multiple_of((owner % 4) * width, 128)
        return ref[pl.ds(rows, width // 8), pl.ds(cols, width)].astype(jnp.bfloat16)

    return read


def from_tall(ref):
    size = ref.shape[0] // BLOCKS

    def read(owner):
        return ref[pl.ds(pl.multiple_of(owner * size, 16), size), :].astype(jnp.bfloat16)

    return read


def attend_kernel(
    count_ref, order_ref, tok_ref, gains_ref, shifts_ref, w_qkv_ref, b_qkv_ref, w_out_ref, b_out_ref,
    qkv_ref, o_ref, mid_ref,
    all_ref, x_ref, low_ref,
):
    step = pl.program_id(0)
    seq_len, slots, width = tok_ref.shape
    rows = GROUP * PITCH
    chunk = PAIR

    @pl.when(step == 0)
    def _():
        widen_tokens(tok_ref, all_ref)
        x_ref[...] = jnp.zeros_like(x_ref)

    take_slots(order_ref, all_ref, x_ref, step, seq_len, slots)
    for r in range(0, rows, chunk):
        normed, _ = standardize(x_ref[r : r + chunk, :])
        low_ref[r : r + chunk, :] = (normed * norm_row(gains_ref, 0) + norm_row(shifts_ref, 0)).astype(jnp.bfloat16)
    whole = product(low_ref[...], w_qkv_ref[:, : 2 * width])
    part = (whole[:, :width] + qkv_bias(b_qkv_ref, 0, 0, width)).astype(jnp.bfloat16)
    qkv_ref[:, :width] = part * jnp.bfloat16(HD ** -0.5)
    qkv_ref[:, width : 2 * width] = whole[:, width:].astype(jnp.bfloat16)
    part = product(low_ref[...], w_qkv_ref[:, 2 * width :]) + qkv_bias(b_qkv_ref, 0, 2, width)
    qkv_ref[:, 2 * width :] = part.astype(jnp.bfloat16)
    mask = pair_mask(False, seq_len, 2)
    spots = [(r, c) for r in range(0, rows, PAIR) for c in range(0, width, 2 * HD)]
    for b in range(0, len(spots), 24):
        group = spots[b : b + 24]
        scores = [
            against(
                both_heads(qkv_ref[r : r + PAIR, c : c + 2 * HD]), qkv_ref[r : r + PAIR, width + c : width + c + 2 * HD]
            )
            + mask
            for r, c in group
        ]
        probs, scales = [], []
        for score in scores:
            expo = jnp.exp(score - jnp.max(score, axis=1, keepdims=True))
            probs.append(expo.astype(jnp.bfloat16))
            scales.append(1.0 / jnp.sum(expo, axis=1, keepdims=True))
        outs = [
            product(prob, qkv_ref[r : r + PAIR, 2 * width + c : 2 * width + c + 2 * HD]) * scale
            for prob, scale, (r, c) in zip(probs, scales, group)
        ]
        for out, (r, c) in zip(outs, group):
            o_ref[r : r + PAIR, c : c + 2 * HD] = join_heads(out).astype(jnp.bfloat16)
    mixed = product(o_ref[...], w_out_ref[...])
    for r in range(0, rows, chunk):
        part = x_ref[r : r + chunk, :] + mixed[r : r + chunk] + b_out_ref[0:1, :]
        mid_ref[r : r + chunk, :] = part


def mlp_kernel(
    count_ref, gains_ref, shifts_ref, w_fc1_ref, b_fc1_ref, w_fc2_ref, b_fc2_ref, w_up_ref, b_up_ref, mid_ref,
    act_ref, slope_ref, x1_ref, kv_ref, cq_ref, co_ref, ch_ref, cx_ref,
    low_ref, wide_ref, mask_ref,
):
    rows, width = mid_ref.shape
    hidden = w_fc1_ref.shape[1]
    chunk = PAIR
    step = pl.program_id(0)
    here = pl.ds(pl.multiple_of(step * GROUP, GROUP), GROUP)

    @pl.when(step == 0)
    def _():
        mask_ref[...] = class_mask(SEQ_LEN)
        for ref in (cq_ref, co_ref, ch_ref, cx_ref):
            ref[...] = jnp.zeros_like(ref)

    for r in range(0, rows, chunk):
        normed, _ = standardize(mid_ref[r : r + chunk, :])
        low_ref[r : r + chunk, :] = (normed * norm_row(gains_ref, 1) + norm_row(shifts_ref, 1)).astype(jnp.bfloat16)
    for c in range(0, hidden, 256):
        pre = product(low_ref[...], w_fc1_ref[:, c : c + 256])
        for r in range(0, rows, 32):
            act, slope = smooth_both(pre[r : r + 32] + b_fc1_ref[0:1, c : c + 256])
            act_ref[r : r + 32, c : c + 256] = act.astype(jnp.bfloat16)
            slope_ref[r : r + 32, c : c + 256] = slope.astype(jnp.bfloat16)
    mixed = product(act_ref[...], w_fc2_ref[...])
    for r in range(0, rows, chunk):
        part = mid_ref[r : r + chunk, :] + mixed[r : r + chunk] + b_fc2_ref[0:1, :]
        x1_ref[r : r + chunk, :] = part
        normed, _ = standardize(part)
        wide = normed * norm_row(gains_ref, 2) + norm_row(shifts_ref, 2)
        wide_ref[r : r + chunk, :] = wide
        low_ref[r : r + chunk, :] = wide.astype(jnp.bfloat16)
    whole = product(low_ref[...], w_up_ref[:, width:])
    kv_ref[:, :width] = whole[:, :width].astype(jnp.bfloat16)
    kv_ref[:, width:] = (whole[:, width:] + qkv_bias(b_up_ref, 1, 2, width)).astype(jnp.bfloat16)
    cx_ref[here, :] = first_rows(x1_ref)
    first = first_rows(wide_ref).astype(jnp.bfloat16)
    ch_ref[here, :] = first.astype(jnp.float32)
    query = (product(first, w_up_ref[:, :width]) + qkv_bias(b_up_ref, 1, 0, width)).astype(jnp.bfloat16).astype(jnp.float32) * HD ** -0.5
    cq_ref[here, :] = query
    spread = spread_heads(query).astype(jnp.bfloat16)
    probs = soft_columns(against(kv_ref[:, :width], spread) + mask_ref[...]).astype(jnp.bfloat16)
    co_ref[here, :] = gather_heads(inner_rows(probs, kv_ref[:, width:]))


def upper_back_kernel(
    count_ref, gains_ref, shifts_ref, w_up_ref, ch_ref, co_ref, da_ref,
    x1_ref, kv_ref, cq_ref, cg_ref, cres_ref,
    dx_ref, unit_ref, vec_ref,
    acc_ref, wide_ref, dqs_ref, mask_ref, dkv_ref,
):
    step = pl.program_id(0)
    rows, width = x1_ref.shape

    @pl.when(step == 0)
    def _():
        acc_ref[...] = jnp.zeros_like(acc_ref)
        mask_ref[...] = class_mask(SEQ_LEN)
        vec_ref[...] = jnp.zeros_like(vec_ref)

    keys, values = kv_ref[:, :width], kv_ref[:, width:]
    spread = spread_heads(cq_ref[...]).astype(jnp.bfloat16)
    grads = spread_heads(cg_ref[...]).astype(jnp.bfloat16)
    probs = soft_columns(against(keys, spread) + mask_ref[...])
    back = against(values, grads)
    inner = (probs * (back - jnp.sum(back * probs, axis=0, keepdims=True))).astype(jnp.bfloat16)
    dkv_ref[:, :width] = product(inner, spread).astype(jnp.bfloat16)
    dkv_ref[:, width:] = product(probs.astype(jnp.bfloat16), grads).astype(jnp.bfloat16)
    grad_query = (gather_heads(inner_rows(inner, keys)) * HD ** -0.5).astype(jnp.bfloat16)
    @pl.when(step == 0)
    def _():
        dqs_ref[...] = jnp.zeros_like(dqs_ref)

    dqs_ref[pl.ds(pl.multiple_of(step * GROUP, GROUP), GROUP), :] = grad_query.astype(jnp.float32)
    vec_ref[:, 3 * width :] += fold_rows(grad_query.astype(jnp.float32))
    vec_ref[:, :width] += fold_rows(dkv_ref[:, width:].astype(jnp.float32))
    wide_ref[...] = against(dkv_ref[...], w_up_ref[:, width:])
    add_first_rows(wide_ref, against(grad_query, w_up_ref[:, :width]))
    chunk = PAIR
    parts = []
    for r in range(0, rows, chunk):
        normed, rstd = standardize(x1_ref[r : r + chunk, :])
        parts.append((normed * norm_row(gains_ref, 2) + norm_row(shifts_ref, 2)).astype(jnp.bfloat16))
        grad = wide_ref[r : r + chunk, :]
        vec_ref[:, width : 2 * width] += fold_rows(grad * normed)
        vec_ref[:, 2 * width : 3 * width] += fold_rows(grad)
        dx_ref[r : r + chunk, :] = standard_back(grad, normed, rstd, norm_row(gains_ref, 2))
    turned = jnp.concatenate(parts).T
    acc_ref[:, width : 3 * width] += product(turned, dkv_ref[...])
    add_first_rows(dx_ref, cres_ref[...])

    @pl.when(step == count_ref[0] - 1)
    def _():
        acc_ref[:, :width] = inner_rows(
            ch_ref[...].astype(jnp.bfloat16), dqs_ref[...].astype(jnp.bfloat16)
        )
        acc_ref[:, 3 * width :] = inner_rows(co_ref[...].astype(jnp.bfloat16), da_ref[...].astype(jnp.bfloat16))
        unit_ref[...] = acc_ref[...].astype(jnp.bfloat16)
        finish_rows(vec_ref)


def mlp_back_kernel(
    count_ref, me_ref, unit_ref, gains_ref, shifts_ref, w_fc1_ref, w_fc2_ref, dx_ref, mid_ref, act_ref, slope_ref,
    dmid_ref, keep_ref, send_ref, vec_ref, vec1_ref,
    acc1_ref, acc2_ref, dz_ref, big_ref, normed_ref, rstd_ref,
):
    step = pl.program_id(0)
    rows, width = dx_ref.shape
    hidden = act_ref.shape[1]

    @pl.when(step == 0)
    def _():
        acc1_ref[...] = jnp.zeros_like(acc1_ref)
        acc2_ref[...] = jnp.zeros_like(acc2_ref)
        vec_ref[...] = jnp.zeros_like(vec_ref)
        vec1_ref[...] = jnp.zeros_like(vec1_ref)

    low = dx_ref[...].astype(jnp.bfloat16)
    vec_ref[:, :width] += fold_rows(low.astype(jnp.float32))
    low_turned = low.T
    chunk = PAIR
    parts = []
    for r in range(0, rows, chunk):
        normed, rstd = standardize(mid_ref[r : r + chunk, :])
        normed_ref[r : r + chunk, :] = normed
        rstd_ref[r : r + chunk, :] = rstd
        parts.append((normed * norm_row(gains_ref, 1) + norm_row(shifts_ref, 1)).astype(jnp.bfloat16))
    norm_turned = jnp.concatenate(parts).T
    for c in range(0, hidden, 768):
        cols = slice(c, c + 768)
        back = against(low, w_fc2_ref[cols, :])
        for r in range(0, rows, chunk):
            part = (back[r : r + chunk] * slope_ref[r : r + chunk, cols].astype(jnp.float32)).astype(jnp.bfloat16)
            dz_ref[r : r + chunk, cols] = part
            vec1_ref[:, cols] += fold_rows(part.astype(jnp.float32))
        acc1_ref[:, cols] += product(norm_turned, dz_ref[:, cols])
        acc2_ref[:, cols] += product(low_turned, act_ref[:, cols])
    mixed = against(dz_ref[...], w_fc1_ref[...])
    for r in range(0, rows, chunk):
        normed, rstd = normed_ref[r : r + chunk, :], rstd_ref[r : r + chunk, :]
        grad = mixed[r : r + chunk]
        vec_ref[:, width : 2 * width] += fold_rows(grad * normed)
        vec_ref[:, 2 * width : 3 * width] += fold_rows(grad)
        dmid_ref[r : r + chunk, :] = dx_ref[r : r + chunk, :] + standard_back(grad, normed, rstd, norm_row(gains_ref, 1))

    @pl.when(step == count_ref[0] - 1)
    def _():
        finish_rows(vec_ref)
        finish_rows(vec1_ref)
        me = me_ref[0]
        write_unit(me, keep_ref, send_ref, 0, from_square(unit_ref))
        write_unit(me, keep_ref, send_ref, 1, from_square(acc1_ref))
        big_ref[...] = acc2_ref[...].T
        write_unit(me, keep_ref, send_ref, 2, from_tall(big_ref))


def attend_back_kernel(
    count_ref, w_out_ref, dmid_ref, qkv_ref, o_ref,
    dqkv_ref, dwo_ref, vec_ref,
    do_ref,
):
    step = pl.program_id(0)
    rows, width = dmid_ref.shape

    @pl.when(step == 0)
    def _():
        dwo_ref[...] = jnp.zeros_like(dwo_ref)
        vec_ref[...] = jnp.zeros_like(vec_ref)

    low = dmid_ref[...].astype(jnp.bfloat16)
    vec_ref[:, :width] += fold_rows(low.astype(jnp.float32))
    do_ref[...] = against(low, w_out_ref[...]).astype(jnp.bfloat16)
    dwo_ref[...] += product(o_ref[...].T, low)
    mask = pair_mask(True, SEQ_LEN, 2)
    spots = [(r, c) for r in range(0, rows, PAIR) for c in range(0, width, 2 * HD)]
    for b in range(0, len(spots), 6):
        group = spots[b : b + 6]
        queries = [both_heads(qkv_ref[r : r + PAIR, c : c + 2 * HD]) for r, c in group]
        keys = [qkv_ref[r : r + PAIR, width + c : width + c + 2 * HD] for r, c in group]
        values = [qkv_ref[r : r + PAIR, 2 * width + c : 2 * width + c + 2 * HD] for r, c in group]
        grads = [both_heads(do_ref[r : r + PAIR, c : c + 2 * HD]) for r, c in group]
        scores = [against(key, query) + mask for key, query in zip(keys, queries)]
        backs = [against(value, grad) for value, grad in zip(values, grads)]
        probs = [soft_columns(score) for score in scores]
        inners = [
            (prob * (back - jnp.sum(back * prob, axis=0, keepdims=True))).astype(jnp.bfloat16)
            for prob, back in zip(probs, backs)
        ]
        grad_values = [product(prob.astype(jnp.bfloat16), grad) for prob, grad in zip(probs, grads)]
        grad_keys = [product(inner, query) for inner, query in zip(inners, queries)]
        grad_queries = [inner_rows(inner, key) for inner, key in zip(inners, keys)]
        for (r, c), grad in zip(group, grad_values):
            dqkv_ref[r : r + PAIR, 2 * width + c : 2 * width + c + 2 * HD] = grad.astype(jnp.bfloat16)
        for (r, c), grad in zip(group, grad_keys):
            dqkv_ref[r : r + PAIR, width + c : width + c + 2 * HD] = grad.astype(jnp.bfloat16)
        for (r, c), grad in zip(group, grad_queries):
            dqkv_ref[r : r + PAIR, c : c + 2 * HD] = (join_heads(grad) * HD ** -0.5).astype(jnp.bfloat16)
    for j in range(3):
        cols = slice(j * width, (j + 1) * width)
        vec_ref[:, (j + 1) * width : (j + 2) * width] += fold_rows(dqkv_ref[:, cols].astype(jnp.float32))

    @pl.when(step == count_ref[0] - 1)
    def _():
        finish_rows(vec_ref)


def weight_back_kernel(
    count_ref, me_ref, order_ref, tok_ref, gains_ref, shifts_ref, dwo_ref, dqkv_ref,
    keep_ref, send_ref,
    all_ref, x_ref, acc_ref,
):
    step = pl.program_id(0)
    seq_len, slots, width = tok_ref.shape
    rows = GROUP * PITCH

    @pl.when(step == 0)
    def _():
        widen_tokens(tok_ref, all_ref)
        x_ref[...] = jnp.zeros_like(x_ref)
        acc_ref[:, : 3 * width] = jnp.zeros((width, 3 * width), jnp.float32)
        acc_ref[:, 3 * width :] = dwo_ref[...]

    take_slots(order_ref, all_ref, x_ref, step, seq_len, slots)
    chunk = PAIR
    parts = []
    for r in range(0, rows, chunk):
        normed, _ = standardize(x_ref[r : r + chunk, :])
        parts.append((normed * norm_row(gains_ref, 0) + norm_row(shifts_ref, 0)).astype(jnp.bfloat16))
    turned = jnp.concatenate(parts).T
    acc_ref[:, : 3 * width] += product(turned, dqkv_ref[...])

    @pl.when(step == count_ref[0] - 1)
    def _():
        write_unit(me_ref[0], keep_ref, send_ref, 0, from_square(acc_ref))


def input_back_kernel(
    count_ref, order_ref, tok_ref, gains_ref, w_qkv_ref, vec1_ref, vec2_ref, vec3_ref, vec4_ref, vec5_ref, dmid_ref, dqkv_ref,
    dtok_ref, all_vec_ref,
    all_ref, out_ref, x_ref, vec_ref,
):
    step = pl.program_id(0)
    seq_len, slots, width = tok_ref.shape
    rows = GROUP * PITCH

    @pl.when(step == 0)
    def _():
        widen_tokens(tok_ref, all_ref)
        x_ref[...] = jnp.zeros_like(x_ref)
        out_ref[...] = jnp.zeros_like(out_ref)
        vec_ref[...] = jnp.zeros_like(vec_ref)

    take_slots(order_ref, all_ref, x_ref, step, seq_len, slots)
    chunk = PAIR
    mixed = against(dqkv_ref[...], w_qkv_ref[...])
    for r in range(0, rows, chunk):
        normed, rstd = standardize(x_ref[r : r + chunk, :])
        grad = mixed[r : r + chunk]
        vec_ref[:, :width] += fold_rows(grad * normed)
        vec_ref[:, width:] += fold_rows(grad)
        part = dmid_ref[r : r + chunk, :] + standard_back(grad, normed, rstd, norm_row(gains_ref, 0))
        for s in range(chunk // PITCH):
            for t in range(all_ref.shape[0]):
                out_ref[t, pl.ds(order_ref[step * GROUP + r // PITCH + s], seq_len, stride=slots), :] = part[
                    s * PITCH : s * PITCH + seq_len, t * 128 : (t + 1) * 128
                ]

    @pl.when(step == count_ref[0] - 1)
    def _():
        finish_rows(vec_ref)
        start = 0
        for ref in (vec_ref, vec1_ref, vec2_ref, vec3_ref, vec4_ref, vec5_ref):
            size = ref.shape[1]
            all_vec_ref[:, start : start + size] = ref[0:1, :]
            start += size
        for t in range(out_ref.shape[0]):
            dtok_ref[:, t * 128 : (t + 1) * 128] = out_ref[t]


def place_of(mask):
    return ((mask & 1) << 4) | (((mask >> 1) & 3) << 2) | ((mask >> 3) & 3)


def read_place(own_ref, got_ref, place, unit):
    inner = place & (BLOCKS // 2 - 1)
    block = jnp.where(place < BLOCKS // 2, own_ref[inner, unit], got_ref[inner, unit])
    return block.astype(jnp.float32)


def unpack_kernel(
    me_ref, own_ref, got_ref,
    qkv_ref, out_ref, fc1_ref, fc2_ref,
):
    step = pl.program_id(0)
    width, size = own_ref.shape[3], own_ref.shape[2]
    count = out_ref.shape[0] // size
    for r, c in [(r, c) for r in range(count) for c in range(4)]:
        place = place_of(((step * count + r) * 4 + c) ^ me_ref[0])
        cols, rows = slice(c * width, (c + 1) * width), slice(r * size, (r + 1) * size)
        tall = slice((r * 4 + c) * size, (r * 4 + c + 1) * size)
        upper = read_place(own_ref, got_ref, place, 0)
        if c < 3:
            qkv_ref[rows, cols] = upper
        else:
            out_ref[rows, :] = upper
        fc1_ref[0, rows, cols] = read_place(own_ref, got_ref, place, 1)
        fc2_ref[0, tall, :] = read_place(own_ref, got_ref, place, 2)
        fc1_ref[1, rows, cols] = read_place(own_ref, got_ref, place, 3)
        fc2_ref[1, tall, :] = read_place(own_ref, got_ref, place, 4)


def unpack_first_kernel(
    me_ref, own_ref, got_ref, vec_ref, qkv_in_ref, out_in_ref,
    qkv_ref, out_ref, gains_ref, shifts_ref, bqv_ref, bout_ref, bfc1_ref, bfc2_ref, final1_ref, final2_ref, bottle_ref,
):
    step = pl.program_id(0)
    width = own_ref.shape[3]
    size = own_ref.shape[2]
    count = out_ref.shape[0] // size
    for r, c in [(r, c) for r in range(count) for c in range(4)]:
        block = read_place(own_ref, got_ref, place_of(((step * count + r) * 4 + c) ^ me_ref[0]), 0)
        rows = slice(r * size, (r + 1) * size)
        if c < 3:
            qkv_ref[rows, c * width : (c + 1) * width] = block
        else:
            out_ref[rows, :] = block

    @pl.when(step == 0)
    def _():
        hidden = bfc1_ref.shape[1]
        row_b, row_c, row_h = 2, 5, 9
        row_hidden = vec_ref.shape[1] // width - hidden // width
        row_a = row_hidden - 4

        def put(ref, place, row, count=1):
            ref[place] = vec_ref[:, row * width : (row + count) * width]

        for i, row in enumerate((0, row_b + 1, row_c + 1, row_h)):
            put(gains_ref, (i // 2, slice(i % 2, i % 2 + 1)), row)
            put(shifts_ref, (i // 2, slice(i % 2, i % 2 + 1)), row + 1)
        put(bqv_ref, (slice(0, 1), slice(0, width)), row_a + 1)
        put(bqv_ref, (slice(0, 1), slice(width, 2 * width)), row_a + 3)
        put(bqv_ref, (slice(1, 2), slice(0, width)), row_c + 3)
        put(bqv_ref, (slice(1, 2), slice(width, 2 * width)), row_c)
        put(bout_ref, slice(0, 1), row_a)
        put(bout_ref, slice(1, 2), row_h + 2)
        put(bfc1_ref, slice(0, 1), row_hidden, hidden // width)
        put(bfc1_ref, slice(1, 2), row_h + 6, hidden // width)
        put(bfc2_ref, slice(0, 1), row_b)
        put(bfc2_ref, slice(1, 2), row_h + 3)
        put(final1_ref, slice(0, 1), row_h + 4)
        put(final2_ref, slice(0, 1), row_h + 5)
        start = (row_h + 6) * width + hidden
        bottle_ref[...] = vec_ref[:, start : start + bottle_ref.shape[1]]


def prepare_kernel(
    device_ref, counts_ref, proto_ref, teacher_ref,
    info_ref, live_ref, image_ref, unit_ref, turned_ref, inv_ref, teach_ref, expo_ref,
):
    slots = live_ref.shape[0]
    images_here = slots // MOST_CROPS
    counts = [counts_ref[device_ref[0] * images_here + i] for i in range(images_here)]
    total = functools.reduce(lambda a, b: a + b, counts)
    place = lax.broadcasted_iota(jnp.int32, (slots, 1), 0)
    live_ref[...] = (place < total).astype(jnp.float32)
    image = jnp.zeros((slots, 1), jnp.float32)
    live_before, dead_before = 0, total
    for i, amount in enumerate(counts):
        dead = MOST_CROPS - amount
        for k in range(MOST_CROPS):
            at = jnp.where(k < amount, live_before + k, dead_before + k - amount)
            info_ref[at + 2] = i * MOST_CROPS + k
        live_spot = (place >= live_before) & (place < live_before + amount)
        dead_spot = (place >= dead_before) & (place < dead_before + dead)
        image = jnp.where(live_spot | dead_spot, float(i), image)
        live_before = live_before + amount
        dead_before = dead_before + dead
    image_ref[...] = image
    info_ref[0] = (total + GROUP - 1) // GROUP
    info_ref[1] = device_ref[0] & (BLOCKS - 1)
    proto = proto_ref[...].astype(jnp.float32)
    inv = lax.rsqrt(jnp.sum(proto * proto, axis=0, keepdims=True) + EPS)
    inv_ref[...] = inv
    unit = (proto * inv).astype(jnp.bfloat16)
    unit_ref[...] = unit
    turned_ref[...] = unit.T
    bottle = proto.shape[0]
    images = teacher_ref.shape[0]
    for r in range(0, images, 64):
        expo = jnp.exp(teacher_ref[r : r + 64, :] * (1.0 / TEACHER_TEMP))
        expo_ref[r : r + 64, :] = expo
        teach_ref[r : r + 64, :bottle] = against(expo.astype(jnp.bfloat16), unit)
        teach_ref[r : r + 64, bottle:] = jnp.broadcast_to(jnp.sum(expo, axis=1, keepdims=True), (64, 128))


def repeat_rows(values, image):
    out = jnp.zeros((image.shape[0], values.shape[1]), values.dtype)
    for i in range(values.shape[0]):
        out = jnp.where(image == i, values[i : i + 1], out)
    return out


def three_parts(values):
    high = values.astype(jnp.bfloat16).astype(jnp.float32)
    middle = (values - high).astype(jnp.bfloat16).astype(jnp.float32)
    return [high, middle, values - high - middle]


def head_kernel(
    scale, own_columns, me_ref, live_ref, image_ref, teach_ref, co_ref, cx_ref, gains_ref, shifts_ref, final_ref,
    w_out_ref, b_out_ref, far_fc1_ref, b_fc1_ref, far_fc2_ref, b_fc2_ref,
    far_w1_ref, b1_ref, far_w2_ref, b2_ref, far_w3_ref, b3_ref, far_unit_ref,
    cg_ref, cres_ref, da_ref, common_ref, feats_ref, share0_ref, share1_ref, share2_ref, share3_ref, keep_ref, send_ref, vec_ref,
    act_ref, slope_ref, slope1_ref, slope2_ref, one_ref, two_ref, back_ref, up1_ref, up2_ref,
    w_fc1_ref, w_fc2_ref, w1_ref, w2_ref, w3_ref, unit_ref, done_ref,
):
    far = (far_fc1_ref.at[1], far_fc2_ref.at[1], far_w1_ref, far_w2_ref, far_w3_ref, far_unit_ref)
    near = (w_fc1_ref, w_fc2_ref, w1_ref, w2_ref, w3_ref, unit_ref)
    copies = [pltpu.make_async_copy(a, b, done_ref.at[i]) for i, (a, b) in enumerate(zip(far, near))]
    for copy in copies:
        copy.start()
    width = cx_ref.shape[1]
    hidden = w_fc1_ref.shape[1]
    hid, bottle = w3_ref.shape
    low = jnp.bfloat16
    middle = cx_ref[...] + product(co_ref[...].astype(low), w_out_ref[...]) + b_out_ref[1:2, :]
    normed_d, rstd_d = standardize(middle)
    low_d = (normed_d * norm_row(gains_ref, 3) + norm_row(shifts_ref, 3)).astype(low)
    copies[0].wait()
    for c in range(0, hidden, 256):
        cols = slice(c, c + 256)
        act, slope = smooth_both(product(low_d, w_fc1_ref[:, cols]) + b_fc1_ref[1:2, cols])
        act_ref[:, cols] = act.astype(low)
        slope_ref[:, cols] = slope
    def share(kind, c, values):
        for u in range(256 // (4 * own_columns)):
            start = kind * (hid // 4) + c // 4 + u * own_columns
            here = slice(start, start + own_columns)
            parts = [values[:, (u * 4 + j) * own_columns : (u * 4 + j + 1) * own_columns] for j in range(4)]
            for bit in (0, 1):
                flip = (me_ref[0] >> bit) & 1 == 1
                parts = [jnp.where(flip, parts[j ^ (1 << bit)], parts[j]) for j in range(4)]
            for ref, part in zip((share0_ref, share1_ref, share2_ref, share3_ref), parts):
                ref[:, here] = part

    copies[1].wait()
    out = middle + product(act_ref[...], w_fc2_ref[...]) + b_fc2_ref[1:2, :]
    normed_f, rstd_f = standardize(out)
    low_f = (normed_f * final_ref[0:1, :] + final_ref[1:2, :]).astype(low)
    common_ref[:, hid : hid + width] = low_f
    copies[2].wait()
    for c in range(0, hid, 256):
        cols = slice(c, c + 256)
        act, slope = smooth_both(product(low_f, w1_ref[:, cols]) + b1_ref[:, cols])
        one_ref[:, cols] = act.astype(low)
        share(0, c, act.astype(low))
        slope1_ref[:, cols] = slope
    first = one_ref[...]
    copies[3].wait()
    for c in range(0, hid, 256):
        cols = slice(c, c + 256)
        act, slope = smooth_both(product(first, w2_ref[:, cols]) + b2_ref[:, cols])
        two_ref[:, cols] = act.astype(low)
        share(1, c, act.astype(low))
        slope2_ref[:, cols] = slope
    copies[4].wait()
    embed = product(two_ref[...], w3_ref[...]) + b3_ref[...]
    inv = lax.rsqrt(jnp.sum(embed * embed, axis=1, keepdims=True) + EPS)
    feats = (embed * inv).astype(low)
    slots = feats.shape[0]
    total = jnp.zeros((slots, 1), jnp.float32)
    student = jnp.zeros((slots, bottle), jnp.float32)
    total_protos = unit_ref.shape[0]
    copies[5].wait()
    size = 512

    def some(i, carry):
        total, student = carry
        part = unit_ref[pl.ds(pl.multiple_of(i * size, size), size), :]
        expo = jnp.exp(against(feats, part) * (1.0 / STUDENT_TEMP) - SHIFT)
        return (
            total + jnp.sum(expo, axis=1, keepdims=True),
            student + product(expo.astype(low), part),
        )

    total, student = lax.fori_loop(0, total_protos // size, some, (total, student), unroll=4)
    teach_total = teach_ref[:, bottle : bottle + 128]
    teach = repeat_rows(teach_ref[:, :bottle] * (1.0 / teach_total[:, :1]), image_ref[...])
    grad_feat = live_ref[...] * (student * (1.0 / total) - teach) * scale
    logs = [live_ref[...]] + three_parts(SHIFT + jnp.log(total)) + three_parts(repeat_rows(jnp.log(teach_total), image_ref[...])[:, :1]) + [image_ref[...]]
    lane = lax.broadcasted_iota(jnp.int32, (slots, 128), 1)
    extra = jnp.zeros((slots, 128), jnp.float32)
    for i, part in enumerate(logs):
        extra = jnp.where(lane == i, part, extra)
    mark = hid + width + bottle
    feats_ref[:, :bottle] = feats
    feats_ref[:, bottle:] = extra.astype(low)
    grad_embed = inv * grad_feat - embed * (inv * inv * inv) * jnp.sum(embed * grad_feat, axis=1, keepdims=True)
    grad_embed = grad_embed.astype(low)
    common_ref[:, hid + width : mark] = grad_embed
    vec_ref[...] = jnp.zeros_like(vec_ref)
    vec_ref[:, 6 * width + hidden : 6 * width + hidden + bottle] = fold_rows(grad_embed.astype(jnp.float32))
    for c in range(0, hid, 256):
        cols = slice(c, c + 256)
        grad = (slope2_ref[:, cols] * against(grad_embed, w3_ref[cols, :])).astype(low)
        common_ref[:, cols] = grad
        vec_ref[:, 7 * width + hidden + hid + c : 7 * width + hidden + hid + c + 256] = fold_rows(grad.astype(jnp.float32))
    grad_two = common_ref[:, :hid]
    for c in range(0, hid, 256):
        cols = slice(c, c + 256)
        grad = (slope1_ref[:, cols] * against(grad_two, w2_ref[cols, :])).astype(low)
        back_ref[:, cols] = grad
        vec_ref[:, 7 * width + hidden + c : 7 * width + hidden + c + 256] = fold_rows(grad.astype(jnp.float32))
        share(2, c, grad)
    grad = against(back_ref[...], w1_ref[...])
    vec_ref[:, 4 * width : 5 * width] = fold_rows(grad * normed_f)
    vec_ref[:, 5 * width : 6 * width] = fold_rows(grad)
    grad_class = standard_back(grad, normed_f, rstd_f, final_ref[0:1, :])
    grad_low = grad_class.astype(low)
    vec_ref[:, 3 * width : 4 * width] = fold_rows(grad_low.astype(jnp.float32))
    up2_ref[...] = inner_rows(act_ref[...], grad_low).astype(low)
    for c in range(0, hidden, 256):
        cols = slice(c, c + 256)
        grad = (slope_ref[:, cols] * against(grad_low, w_fc2_ref[cols, :])).astype(low)
        act_ref[:, cols] = grad
        vec_ref[:, 6 * width + c : 6 * width + c + 256] = fold_rows(grad.astype(jnp.float32))
    grad_pre = act_ref[...]
    up1_ref[...] = inner_rows(low_d, grad_pre).astype(low)
    grad = against(grad_pre, w_fc1_ref[...])
    vec_ref[:, :width] = fold_rows(grad * normed_d)
    vec_ref[:, width : 2 * width] = fold_rows(grad)
    grad_middle = grad_class + standard_back(grad, normed_d, rstd_d, norm_row(gains_ref, 3))
    cres_ref[...] = grad_middle
    grad_low = grad_middle.astype(low)
    da_ref[...] = grad_low.astype(jnp.float32)
    vec_ref[:, 2 * width : 3 * width] = fold_rows(grad_low.astype(jnp.float32))
    cg_ref[...] = against(grad_low, w_out_ref[...]).astype(low).astype(jnp.float32)
    finish_rows(vec_ref)
    write_unit(me_ref[0], keep_ref, send_ref, 0, from_square(up1_ref), True)
    write_unit(me_ref[0], keep_ref, send_ref, 1, from_tall(up2_ref), True)


def head_sum_kernel(
    width, info_ref, common0_ref, common1_ref, common2_ref, common3_ref, share0_ref, share1_ref, share2_ref, share3_ref,
    kept_ref, sent_ref,
    parts_ref,
):
    quarter = share0_ref.shape[1] // 3
    full = quarter * 4
    share = jnp.concatenate([ref[...] for ref in (share0_ref, share1_ref, share2_ref, share3_ref)])
    common = jnp.concatenate([ref[...] for ref in (common0_ref, common1_ref, common2_ref, common3_ref)])
    low = jnp.bfloat16
    parts = [share[:, i * quarter : (i + 1) * quarter].T for i in range(3)]
    parts_ref[:, :width] = product(parts[2], common[:, full : full + width])
    for c in range(0, full, 512):
        parts_ref[:, width + c : width + c + 512] = product(parts[0], common[:, c : c + 512])
    mark = parts_ref.shape[1]
    parts_ref[:, width + full :] = product(parts[1], common[:, width + full : mark])
    size = kept_ref.shape[1]
    spot = (info_ref[1] >> 2) & 1
    for z in range(kept_ref.shape[0]):
        for ref, digit in ((kept_ref, spot), (sent_ref, 1 - spot)):
            ref[z] = parts_ref[pl.ds(pl.multiple_of((2 * z + digit) * size, 8), size), :].astype(jnp.bfloat16)


def proto_back_kernel(
    scale, owner_ref, unit_ref, proto_ref, inv_ref, thawed_ref, expo_ref, feats_ref,
    grad_ref,
    acc_ref, raw_ref,
):
    step = pl.program_id(0)
    bottle = unit_ref.shape[0]

    @pl.when(step == 0)
    def _():
        acc_ref[...] = jnp.zeros_like(acc_ref)

    rows = feats_ref.shape[0]
    slots = rows // 8
    images = slots // MOST_CROPS
    for l in range(8):
        here = slice(l * slots, (l + 1) * slots)
        extra = feats_ref[here, bottle:].astype(jnp.float32)
        lane = lax.broadcasted_iota(jnp.int32, extra.shape, 1)
        pick = lambda a, b: jnp.sum(jnp.where((lane >= a) & (lane < b), extra, 0.0), axis=1, keepdims=True)
        logits = product(feats_ref[here, :bottle], unit_ref[...]) * (1.0 / STUDENT_TEMP)
        target = repeat_rows(expo_ref[pl.ds(pl.multiple_of(owner_ref[step * 8 + l] * images, 8), images), :], pick(7, 8))
        raw = pick(0, 1) * (jnp.exp(logits - pick(1, 4)) - target * jnp.exp(-pick(4, 7))) * scale
        raw_ref[here, :] = raw.astype(jnp.bfloat16)
    acc_ref[...] += inner_rows(feats_ref[:, :bottle], raw_ref[...])

    @pl.when(step == pl.num_programs(0) - 1)
    def _():
        proto = proto_ref[...].astype(jnp.float32)
        inv = inv_ref[...]
        grad = acc_ref[...]
        inner = jnp.sum(proto * grad, axis=0, keepdims=True)
        grad_ref[...] = (inv * grad - proto * (inv * inv * inv * inner)) * thawed_ref[...]


def whole(array):
    return pl.BlockSpec(array.shape, lambda *i: (0,) * len(array.shape))


class Layer:
    def __init__(self, array, layer):
        self.array, self.layer = array, layer


class Far:
    def __init__(self, array):
        self.array = array


def spec_of(item):
    if isinstance(item, Far):
        return pl.BlockSpec(memory_space=pl.ANY)
    if isinstance(item, Layer):
        shape = item.array.shape[1:]
        return pl.BlockSpec((None,) + shape, lambda *i: (item.layer,) + (0,) * len(shape))
    return whole(item)


def array_of(item):
    return item.array if isinstance(item, (Layer, Far)) else item


class Shifted:
    def __init__(self, ref, first):
        self.ref, self.first = ref, first

    def __getitem__(self, index):
        return self.ref[self.first + index]


def run_kernel(body, steps, scalars, whole_in, step_in, outs, scratch, micros, info=None):
    count = info
    if info is not None:
        inner, firsts = body, scalars
        scalars = [info]

        def body(info_ref, *refs):
            @pl.when(pl.program_id(0) < info_ref[0])
            def _():
                inner(info_ref, *[Shifted(info_ref, first) for first in firsts], *refs)

    def by_step(rows, width):
        if count is None:
            return pl.BlockSpec((rows, width), lambda i, *s: (i, 0))
        return pl.BlockSpec((rows, width), lambda i, c, *s: (jnp.minimum(i, c[0] - 1), 0))

    return pl.pallas_call(
        body,
        grid_spec=pltpu.PrefetchScalarGridSpec(
            num_scalar_prefetch=len(scalars),
            grid=(steps,),
            in_specs=[spec_of(a) for a in whole_in] + [by_step(rows, a.shape[1]) for a, rows in step_in],
            out_specs=[
                by_step(rows, shape[1])
                if rows
                else pl.BlockSpec(memory_space=pltpu.SMEM)
                if rows is None
                else pl.BlockSpec(shape, lambda *i, k=len(shape): (0,) * k)
                for shape, dtype, rows in outs
            ],
            scratch_shapes=scratch,
        ),
        out_shape=[jax.ShapeDtypeStruct(shape, dtype) for shape, dtype, rows in outs],
        compiler_params=pltpu.CompilerParams(
            dimension_semantics=("arbitrary",), vmem_limit_bytes=56 * 1024 * 1024
        ),
        cost_estimate=pl.CostEstimate(flops=micros * 10**9, bytes_accessed=2**20, transcendentals=0),
    )(*scalars, *[array_of(a) for a in whole_in], *[a for a, rows in step_in])


def axis_bits(n):
    bits = n.bit_length() - 1
    assert n == 1 << bits
    return bits


def swap(values, mask, n):
    return lax.ppermute(values, "dp", [(i, i ^ mask) for i in range(n)])


def group_masks(group):
    return [k << group[0] for k in range(1 << len(group))]


def own_digit(group):
    return (lax.axis_index("dp") >> group[0]) & ((1 << len(group)) - 1)


def upper_groups(n, first):
    bits = list(range(first, axis_bits(n)))
    return [bits[i : i + 2] for i in range(0, len(bits), 2)][::-1]


def gather_loose(block, group, n):
    return jnp.stack([swap(block, mask, n) if mask else block for mask in group_masks(group)])


def tree_sum(parts):
    while len(parts) > 1:
        parts = [parts[i] + parts[i + 1] for i in range(0, len(parts), 2)]
    return parts[0]


def scatter_send(parts, group):
    size = 1 << len(group)
    parts = parts.reshape((size, parts.shape[0] // size) + parts.shape[1:])
    digit = own_digit(group)
    return [lax.dynamic_index_in_dim(parts, digit ^ k, 0, keepdims=False) for k in range(size)]


def double(mine, got):
    return jnp.concatenate([mine, got])


def pick_send(parts, axis, group):
    digit = own_digit(group)
    return [lax.dynamic_index_in_dim(parts, digit ^ k, axis, keepdims=False) for k in range(2)]


def swap_parts(parts, group, n):
    return [swap(part, mask, n) if mask else part for part, mask in zip(parts, group_masks(group))]


def scatter_stage(parts, group, n):
    got = swap_parts(scatter_send(parts, group), group, n)
    return tree_sum([part.astype(jnp.float32) for part in got]).astype(parts.dtype)


def sum_stage(values, group, n):
    return tree_sum(swap_parts([values] * (1 << len(group)), group, n))


def fold_send(parts, group):
    size = 1 << len(group)
    parts = parts.reshape((size, parts.shape[0] // size) + parts.shape[1:])
    return [parts[k] for k in range(size)]


def fold_sum(parts):
    return tree_sum([part.astype(jnp.float32) for part in parts]).astype(parts[0].dtype)


def unfold_stage(parts, group, n):
    return jnp.concatenate([swap(parts, mask, n) if mask else parts for mask in group_masks(group)])


def extra_sum(values, n):
    for bit in range(5, axis_bits(n)):
        values = values + swap(values, 1 << bit, n)
    return values


def together(*values):
    return lax.optimization_barrier(values)


CORE, PLANE, LINE = [0], [1, 2], [3, 4]
UNPACK = 4


def per_device(
    tokens,
    layer_gains,
    layer_shifts,
    w_qkv,
    b_qv,
    w_out,
    b_out,
    w_fc1,
    b_fc1,
    w_fc2,
    b_fc2,
    final_gain,
    final_shift,
    head_w1,
    head_b1,
    head_w2,
    head_b2,
    head_w3,
    head_b3,
    prototypes,
    crop_counts,
    teacher_logits,
    first_epoch,
):
    low, wide = jnp.bfloat16, jnp.float32
    slot_count, seq_len, width = tokens.shape
    n = lax.axis_size("dp")
    device = lax.axis_index("dp")
    me = (device & (BLOCKS - 1)).reshape(1)
    bottle = prototypes.shape[0]
    hidden = w_fc1.shape[2]
    hid = head_w2.shape[0]
    rows = GROUP * PITCH
    steps = slot_count // GROUP
    padded = slot_count * PITCH
    row_count = slot_count * seq_len
    groups = upper_groups(n, 3)

    scale = 1.0 / (STUDENT_TEMP * n)
    images, protos = teacher_logits.shape
    info, own_live, image, unit_low, unit_turned, col_inv, teach_sum, teach_expo = run_kernel(
        prepare_kernel,
        1,
        [device.reshape(1), crop_counts],
        [prototypes, teacher_logits],
        [],
        [
            ((slot_count + 2,), jnp.int32, None),
            ((slot_count, 1), wide, 0),
            ((slot_count, 1), wide, 0),
            ((bottle, protos), low, 0),
            ((protos, bottle), low, 0),
            ((1, protos), wide, 0),
            ((images, bottle + 128), wide, 0),
            ((images, protos), wide, 0),
        ],
        [],
        4,
    )
    unit_all = lax.all_gather(unit_turned, "dp", axis=0, tiled=True)
    teach_sum = teach_sum.reshape(n, -1, bottle + 128)
    for group in groups[:-1]:
        teach_sum = scatter_stage(teach_sum, group, n)

    gains, shifts = layer_gains, layer_shifts
    turned_tokens = tokens.transpose(1, 0, 2)
    all_rows = pltpu.VMEM((width // 128, row_count, 128), wide)
    teach_parts = scatter_send(teach_sum, groups[-1])
    turned_tokens, *teach_parts = together(turned_tokens, *teach_parts)
    teach_parts = swap_parts(teach_parts, groups[-1], n)
    qkv_a, attn_a, middle_a = run_kernel(
        attend_kernel,
        steps,
        [2],
        [turned_tokens, gains, shifts, Layer(w_qkv, 0), b_qv, Layer(w_out, 0), b_out],
        [],
        [((padded, 3 * width), low, rows), ((padded, width), low, rows), ((padded, width), wide, rows)],
        [all_rows, pltpu.VMEM((rows, width), wide), pltpu.VMEM((rows, width), low)],
        35,
        info,
    )
    middle_a, *teach_parts = together(middle_a, *teach_parts)
    teach_sum = tree_sum(teach_parts)
    teach_parts = scatter_send(teach_sum, PLANE)
    middle_a, *teach_parts = together(middle_a, *teach_parts)
    teach_parts = swap_parts(teach_parts, PLANE, n)
    act_a, slope_a, lower_out, kv_c, query_c, attn_c, first_low, first_in = run_kernel(
        mlp_kernel,
        steps,
        [],
        [gains, shifts, Layer(w_fc1, 0), b_fc1, Layer(w_fc2, 0), b_fc2, Layer(w_qkv, 1), b_qv],
        [(middle_a, rows)],
        [
            ((padded, hidden), low, rows),
            ((padded, hidden), low, rows),
            ((padded, width), wide, rows),
            ((padded, 2 * width), low, rows),
            ((slot_count, width), wide, 0),
            ((slot_count, width), wide, 0),
            ((slot_count, width), wide, 0),
            ((slot_count, width), wide, 0),
        ],
        [pltpu.VMEM((rows, width), low), pltpu.VMEM((rows, width), wide), pltpu.VMEM((rows, HEADS * GROUP), wide)],
        40,
        info,
    )
    first_in, *teach_parts = together(first_in, *teach_parts)
    teach_sum = scatter_stage(tree_sum(teach_parts), CORE, n)[0]

    finals = jnp.stack([final_gain, final_shift])
    vec_width = -(-(7 * width + hidden + 2 * hid) // width) * width
    grad_attended, grad_middle_c, grad_attn, common, feats, *shares, keep_u, send_u, vec_h = run_kernel(
        functools.partial(head_kernel, scale, hid // n),
        1,
        [me],
        [own_live, image, teach_sum, attn_c, first_in, gains, shifts, finals, Layer(w_out, 1), b_out, Far(w_fc1), b_fc1, Far(w_fc2), b_fc2,
         Far(head_w1), head_b1[None], Far(head_w2), head_b2[None], Far(head_w3), head_b3[None], Far(unit_all)],
        [],
        [
            ((slot_count, width), wide, 0),
            ((slot_count, width), wide, 0),
            ((slot_count, width), wide, 0),
            ((slot_count, hid + width + bottle), low, 0),
            ((slot_count, bottle + 128), low, 0),
            *[((slot_count, hid // 4 * 3), low, 0)] * 4,
            ((BLOCKS // 2, 2, width // 8, width), low, 0),
            ((BLOCKS // 2, 2, width // 8, width), low, 0),
            ((8, vec_width), wide, 0),
        ],
        [
            pltpu.VMEM((slot_count, hidden), low),
            pltpu.VMEM((slot_count, hidden), wide),
            pltpu.VMEM((slot_count, hid), wide),
            pltpu.VMEM((slot_count, hid), wide),
            pltpu.VMEM((slot_count, hid), low),
            pltpu.VMEM((slot_count, hid), low),
            pltpu.VMEM((slot_count, hid), low),
            pltpu.VMEM((width, hidden), low),
            pltpu.VMEM((hidden, width), low),
        ]
        + [pltpu.VMEM(v.shape, low) for v in (w_fc1[0], w_fc2[0], head_w1, head_w2, head_w3, unit_all)]
        + [pltpu.SemaphoreType.DMA((6,))],
        20,
    )
    common_got = swap(common, 1, n)
    share0, share2 = shares[0], shares[2]
    share1, share3 = swap(shares[1], 1, n), swap(shares[3], 1, n)
    bits = list(range(5, axis_bits(n))) + [4, 3, 1, 2, 0]
    masks = [0]
    for bit in bits:
        masks = masks + [mask | (1 << bit) for mask in masks]
    for bit in bits[:-5]:
        feats = double(feats, swap(feats, 1 << bit, n))
    grad_attended, common, share2, share3, send_u, feats = together(grad_attended, common, share2, share3, send_u, feats)
    got_u = swap(send_u, 1, n)
    feats_got = swap(feats, 16, n)
    common2, share2, share3 = (swap(v, 2, n) for v in (common, share2, share3))
    grad_lower_out, unit_u, vec_c = run_kernel(
        upper_back_kernel,
        steps,
        [],
        [gains, shifts, Layer(w_qkv, 1), first_low, attn_c, grad_attn],
        [(lower_out, rows), (kv_c, rows), (query_c, GROUP), (grad_attended, GROUP), (grad_middle_c, GROUP)],
        [
            ((padded, width), wide, rows),
            ((width, 4 * width), low, 0),
            ((8, 4 * width), wide, 0),
        ],
        [
            pltpu.VMEM((width, 4 * width), wide),
            pltpu.VMEM((rows, width), wide),
            pltpu.VMEM((slot_count, width), wide),
            pltpu.VMEM((rows, HEADS * GROUP), wide),
            pltpu.VMEM((rows, 2 * width), low),
        ],
        20,
        info,
    )
    grad_lower_out, common2, share2, share3, got_u, feats_got = together(
        grad_lower_out, common2, share2, share3, got_u, feats_got
    )
    feats = double(feats, feats_got)
    common3 = swap(common2, 1, n)
    parts_u = fold_send(keep_u + got_u, LINE)
    head_keep, head_send = run_kernel(
        functools.partial(head_sum_kernel, width),
        1,
        [info],
        [common, common_got, common2, common3, share0, share1, share2, share3],
        [],
        [((n // 8, hid // n, width + hid + bottle), low, 0)] * 2,
        [pltpu.VMEM((hid // 4, width + hid + bottle), wide)],
        6,
    )
    grad_lower_out, head_send, feats, *parts_u = together(grad_lower_out, head_send, feats, *parts_u)
    head_got, feats_got = swap(head_send, 4, n), swap(feats, 8, n)
    parts_u = swap_parts(parts_u, LINE, n)
    grad_middle_a, keep_m, send_m, vec_b, vec_hidden = run_kernel(
        mlp_back_kernel,
        steps,
        [1],
        [unit_u, gains, shifts, Layer(w_fc1, 0), Layer(w_fc2, 0)],
        [(grad_lower_out, rows), (middle_a, rows), (act_a, rows), (slope_a, rows)],
        [
            ((padded, width), wide, rows),
            ((BLOCKS // 2, 3, width // 8, width), low, 0),
            ((BLOCKS // 2, 3, width // 8, width), low, 0),
            ((8, 3 * width), wide, 0),
            ((8, hidden), wide, 0),
        ],
        [
            pltpu.VMEM((width, hidden), wide),
            pltpu.VMEM((width, hidden), wide),
            pltpu.VMEM((rows, hidden), low),
            pltpu.VMEM((hidden, width), wide),
            pltpu.VMEM((rows, width), wide),
            pltpu.VMEM((rows, 1), wide),
        ],
        40,
        info,
    )
    grad_middle_a, head_got, feats_got, send_m, *parts_u = together(grad_middle_a, head_got, feats_got, send_m, *parts_u)
    feats = double(feats, feats_got)
    head_parts = head_keep + head_got
    for bit in range(axis_bits(n) - 1, 4, -1):
        head_parts = scatter_stage(head_parts, [bit], n)
    head_keep, head_send = pick_send(head_parts.reshape((2, 2) + head_parts.shape[1:]), 1, [3])
    parts_m = [
        jnp.concatenate([a.reshape((-1,) + a.shape[2:]), b[0]])
        for a, b in zip(fold_send(keep_m + swap(send_m, 1, n), PLANE), fold_send(fold_sum(parts_u), PLANE))
    ]
    grad_middle_a, head_send, *parts_m = together(grad_middle_a, head_send, *parts_m)
    head_got = swap(head_send, 8, n)
    parts_m = swap_parts(parts_m, PLANE, n)
    grad_qkv, grad_wo, vec_a = run_kernel(
        attend_back_kernel,
        steps,
        [],
        [Layer(w_out, 0)],
        [(grad_middle_a, rows), (qkv_a, rows), (attn_a, rows)],
        [((padded, 3 * width), low, rows), ((width, width), wide, 0), ((8, 4 * width), wide, 0)],
        [pltpu.VMEM((rows, width), low)],
        40,
        info,
    )
    grad_qkv, head_got, *parts_m = together(grad_qkv, head_got, *parts_m)
    head_keep, head_send = pick_send(head_keep + head_got, 0, [4])
    sum_m = fold_sum(parts_m)
    sum_u = sum_m[None, 12:]
    parts_m = fold_send(sum_m[:12].reshape((4, 3) + sum_m.shape[1:]), LINE)
    grad_qkv, head_send, feats, *parts_m = together(grad_qkv, head_send, feats, *parts_m)
    feats_got = swap(feats, 2, n)
    parts_m = swap_parts(parts_m, LINE, n)
    keep_a, send_a = run_kernel(
        weight_back_kernel,
        steps,
        [1, 2],
        [turned_tokens, gains, shifts, grad_wo],
        [(grad_qkv, rows)],
        [
            ((BLOCKS // 2, 1, width // 8, width), low, 0),
            ((BLOCKS // 2, 1, width // 8, width), low, 0),
        ],
        [all_rows, pltpu.VMEM((rows, width), wide), pltpu.VMEM((width, 4 * width), wide)],
        10,
        info,
    )
    keep_a, send_a, feats_got, *parts_m = together(keep_a, send_a, feats_got, *parts_m)
    feats = double(feats, feats_got)
    sum_m = extra_sum(jnp.concatenate([fold_sum(parts_m), sum_u], axis=1), n)
    keep_a, send_a = fold_send(keep_a + swap(send_a, 1, n), [2])
    grad_qkv, sum_m, send_a, feats = together(grad_qkv, sum_m, send_a, feats)
    feats_got = swap(feats, 4, n)
    parts_m = swap_parts([sum_m] * 4, LINE, n)
    got_a = swap(send_a, 4, n)
    grad_tokens, vectors = run_kernel(
        input_back_kernel,
        steps,
        [2],
        [turned_tokens, gains, Layer(w_qkv, 0), vec_b, vec_c, vec_h, vec_a, vec_hidden],
        [(grad_middle_a, rows), (grad_qkv, rows)],
        [((row_count, width), wide, 0), ((1, 13 * width + hidden + vec_width), wide, 0)],
        [all_rows, all_rows, pltpu.VMEM((rows, width), wide), pltpu.VMEM((8, 2 * width), wide)],
        20,
        info,
    )
    tokens_grad = grad_tokens.reshape(seq_len, slot_count, width).transpose(1, 0, 2)
    vectors, got_a, feats_got, *parts_m = together(vectors, got_a, feats_got, *parts_m)
    feats = double(feats, feats_got)
    feats = double(feats, swap(feats, 1, n))

    keep_a, send_a = fold_send(keep_a + got_a, [1])
    send_a, vectors = together(send_a, vectors)
    got_a, got_v = swap(send_a, 2, n), swap(vectors, 1, n)
    vectors = vectors + got_v
    sum_m = jnp.concatenate(parts_m)
    half = sum_m.shape[0] // 2
    feats, vectors, sum_m = together(feats, vectors, sum_m)
    one, two = sum_m[:half], sum_m[half:]
    one, two = [one, swap(one, 2, n)], [two, swap(two, 4, n)]
    prototypes_grad = run_kernel(
        functools.partial(proto_back_kernel, scale),
        n // 8,
        [device ^ jnp.array(masks, jnp.int32)],
        [unit_low, prototypes, col_inv, (1 - first_epoch).astype(wide)[None], teach_expo],
        [(feats, 8 * slot_count)],
        [(prototypes.shape, wide, 0)],
        [pltpu.VMEM(prototypes.shape, wide), pltpu.VMEM((8 * slot_count, protos), low)],
        6,
    )[0]
    prototypes_grad, got_a, *parts_m = together(prototypes_grad, got_a, *one, *two)
    one, two = jnp.stack(parts_m[:2]), jnp.stack(parts_m[2:])
    sum_a = keep_a + got_a
    sum_a, vectors, one, two = together(sum_a, vectors, one, two)
    one, two = [one, swap(one, 4, n)], [two, swap(two, 2, n)]
    for bit in (4, 3):
        keep_a, send_a = fold_send(sum_a, [bit])
        got_a, got_v = swap(send_a, 1 << bit, n), swap(vectors, 1 << bit, n)
        sum_a, vectors = keep_a + got_a, vectors + got_v
    sum_a = extra_sum(sum_a, n)
    vectors = extra_sum(vectors, n)
    for bit in (3, 4):
        sum_a = unfold_stage(sum_a, [bit], n)
    sum_a, vectors, head_send, *parts_m = together(sum_a, vectors, head_send, *one, *two)
    head_got = swap(head_send, 16, n)
    one = jnp.stack(parts_m[:2]).reshape((4,) + parts_m[0].shape[1:])
    two = jnp.stack(parts_m[2:], axis=1).reshape((4,) + parts_m[0].shape[1:])
    sum_m = jnp.concatenate([one, two], axis=1).reshape((BLOCKS // 2,) + one.shape[2:])
    got_m, got_a, got_v = swap(sum_m, 1, n), swap(sum_a, 2, n), swap(vectors, 2, n)
    got_m, got_a, got_v = together(got_m, got_a, got_v)
    sum_a, vectors = double(sum_a, got_a), vectors + got_v
    got_a, got_v = swap(sum_a, 4, n), swap(vectors, 4, n)
    specs = [
        pl.BlockSpec((None, width // UNPACK, 3 * width), lambda i: (1, i, 0)),
        pl.BlockSpec((None, width // UNPACK, width), lambda i: (1, i, 0)),
    ]
    shapes = [jax.ShapeDtypeStruct(s, wide) for s in ((2, width, 3 * width), (2, width, width))]
    params = pltpu.CompilerParams(dimension_semantics=("arbitrary",), vmem_limit_bytes=56 * 1024 * 1024)
    qkv_grad, out_grad, fc1_grad, fc2_grad = pl.pallas_call(
        unpack_kernel,
        grid=(UNPACK,),
        in_specs=[pl.BlockSpec(memory_space=pltpu.SMEM), whole(sum_m), whole(got_m)],
        out_specs=specs
        + [
            pl.BlockSpec((2, width // UNPACK, hidden), lambda i: (0, i, 0)),
            pl.BlockSpec((2, hidden // UNPACK, width), lambda i: (0, i, 0)),
        ],
        out_shape=shapes + [jax.ShapeDtypeStruct(s, wide) for s in ((2, width, hidden), (2, hidden, width))],
        compiler_params=params,
        cost_estimate=pl.CostEstimate(flops=8 * 10**9, bytes_accessed=2**20, transcendentals=0),
    )(me, sum_m, got_m)
    qkv_grad, out_grad, got_a, got_v, head_got = together(qkv_grad, out_grad, got_a, got_v, head_got)
    head_sum = (head_keep.astype(wide) + head_got.astype(wide)).reshape(hid // n, -1)
    w1_grad, w2_grad, w3_grad = head_sum[:, :width].T, head_sum[:, width : width + hid], head_sum[:, width + hid :]
    sum_a, vectors = double(sum_a, got_a), vectors + got_v
    got_a = swap(sum_a, 1, n)
    specs = [pl.BlockSpec(spec.block_shape, lambda i: (0, i, 0)) for spec in specs]
    small = [(2, 2, width), (2, 2, width), (2, 2 * width), (2, width), (2, hidden), (2, width), (1, width), (1, width), (1, bottle)]
    qkv_grad, out_grad, gains_grad, shifts_grad, bqv_grad, bout_grad, bfc1_grad, bfc2_grad, *finals = pl.pallas_call(
        unpack_first_kernel,
        grid=(UNPACK,),
        in_specs=[pl.BlockSpec(memory_space=pltpu.SMEM), whole(sum_a), whole(got_a), whole(vectors)]
        + [pl.BlockSpec(memory_space=pl.ANY)] * 2,
        out_specs=specs + [pl.BlockSpec(shape, lambda i, k=len(shape): (0,) * k) for shape in small],
        out_shape=shapes + [jax.ShapeDtypeStruct(shape, wide) for shape in small],
        input_output_aliases={4: 0, 5: 1},
        compiler_params=params,
    )(me, sum_a, got_a, vectors, qkv_grad, out_grad)
    row_h = 9
    ends = vectors[0, (row_h + 7) * width + hidden : (row_h + 7) * width + hidden + 2 * hid]
    own_part = lambda start: lax.dynamic_slice_in_dim(ends, start + device * (hid // n), hid // n)

    return (
        tokens_grad,
        gains_grad,
        shifts_grad,
        qkv_grad,
        bqv_grad,
        out_grad,
        bout_grad,
        fc1_grad,
        bfc1_grad,
        fc2_grad,
        bfc2_grad,
        finals[0].reshape(-1),
        finals[1].reshape(-1),
        w1_grad,
        own_part(0),
        w2_grad,
        own_part(hid),
        w3_grad,
        finals[2].reshape(-1),
        prototypes_grad,
    )


def solution(mesh):
    return jax.shard_map(
        per_device,
        mesh=mesh,
        in_specs=(
            P("dp", None, None),
            P(),
            P(),
            P(),
            P(),
            P(),
            P(),
            P(),
            P(),
            P(),
            P(),
            P(),
            P(),
            P(),
            P(),
            P(),
            P(),
            P(),
            P(),
            P(None, "dp"),
            P(),
            P(None, "dp"),
            P("dp"),
        ),
        out_specs=(
            P("dp", None, None),
            P(),
            P(),
            P(),
            P(),
            P(),
            P(),
            P(),
            P(),
            P(),
            P(),
            P(),
            P(),
            P(None, "dp"),
            P("dp"),
            P("dp", None),
            P("dp"),
            P("dp", None),
            P(),
            P(None, "dp"),
        ),
        check_vma=False,
    )
```

```python
import functools

import jax
import jax.numpy as jnp
from jax import lax
from jax.experimental import pallas as pl
from jax.experimental.pallas import tpu as pltpu
from jax.sharding import PartitionSpec as P

HEADS = 6
HD = 64
MOST_CROPS = 10

STUDENT_TEMP = 0.1
TEACHER_TEMP = 0.04
EPS = 1e-06
SHIFT = 10.0


def product(left, right):
    return jnp.dot(left, right, preferred_element_type=jnp.float32)


def against(left, right):
    return lax.dot_general(
        left, right, (((1,), (1,)), ((), ())), preferred_element_type=jnp.float32
    )


def inner_rows(left, right):
    return lax.dot_general(
        left, right, (((0,), (0,)), ((), ())), preferred_element_type=jnp.float32
    )


def column_sum(values):
    return jnp.sum(values.astype(jnp.float32), axis=0)


def norm_forward(values, gain, shift):
    centered = values - jnp.mean(values, axis=-1, keepdims=True)
    rstd = lax.rsqrt(jnp.mean(centered * centered, axis=-1, keepdims=True) + EPS)
    normed = centered * rstd
    return (normed * gain + shift, normed, rstd)


def norm_backward(grad, normed, rstd, gain):
    scaled = grad * gain
    inner = (
        scaled
        - jnp.mean(scaled, axis=-1, keepdims=True)
        - normed * jnp.mean(scaled * normed, axis=-1, keepdims=True)
    )
    return (rstd * inner, jnp.sum(grad * normed, axis=0), jnp.sum(grad, axis=0))


GROUP = 16
BLOCKS = 32
PITCH = 40
PAIR = 2 * PITCH
NEVER = -1e30
SEQ_LEN = 37


def smooth_both(values):
    size = jnp.abs(values)
    bell = jnp.exp(values * values * -0.5)
    t = 1.0 / (1.0 + 0.23164189 * size)
    tail = t * (0.127414796 + t * (-0.142248368 + t * (0.7107068705 + t * (-0.7265760135 + t * 0.5307027145))))
    upper = tail * bell
    area = jnp.where(values >= 0, 1.0 - upper, upper)
    return values * area, area + values * (bell * 0.3989422804014327)


def norm_row(ref, index):
    return ref[index // 2, index % 2 : index % 2 + 1, :]


def qkv_bias(ref, layer, part, width):
    if part == 1:
        return 0.0
    return ref[layer : layer + 1, part // 2 * width : (part // 2 + 1) * width]


def standardize(values):
    centered = values - jnp.mean(values, axis=-1, keepdims=True)
    rstd = lax.rsqrt(jnp.mean(centered * centered, axis=-1, keepdims=True) + EPS)
    return centered * rstd, rstd


def standard_back(grad, normed, rstd, gain):
    scaled = grad * gain
    return rstd * (
        scaled
        - jnp.mean(scaled, axis=-1, keepdims=True)
        - normed * jnp.mean(scaled * normed, axis=-1, keepdims=True)
    )


def fold_rows(values):
    return jnp.sum(values.reshape(-1, 8, values.shape[1]), axis=0)


def finish_rows(ref):
    ref[0:1, :] = jnp.sum(ref[...], axis=0, keepdims=True)


def both_heads(values):
    lane = lax.broadcasted_iota(jnp.int32, values.shape, 1)
    zero = jnp.zeros_like(values)
    return jnp.concatenate([jnp.where(lane < HD, values, zero), jnp.where(lane < HD, zero, values)])


def join_heads(values):
    rows = values.shape[0] // 2
    lane = lax.broadcasted_iota(jnp.int32, (rows, values.shape[1]), 1)
    return jnp.where(lane < HD, values[:rows], values[rows:])


def spread_heads(values):
    lane = lax.broadcasted_iota(jnp.int32, values.shape, 1) // HD
    return jnp.concatenate([jnp.where(lane == h, values, 0.0) for h in range(HEADS)])


def gather_heads(values):
    lane = lax.broadcasted_iota(jnp.int32, (GROUP, values.shape[1]), 1) // HD
    out = jnp.zeros((GROUP, values.shape[1]), values.dtype)
    for h in range(HEADS):
        out = jnp.where(lane == h, values[h * GROUP : (h + 1) * GROUP], out)
    return out


def slot_and_valid(shape, dim, seq_len):
    index = lax.broadcasted_iota(jnp.int32, shape, dim)
    slot = index // PITCH
    return slot, index - slot * PITCH < seq_len


def pair_mask(rows_are_keys, seq_len, copies=1):
    shape = (PAIR, PAIR)
    key, valid = slot_and_valid(shape, 0 if rows_are_keys else 1, seq_len)
    query, _ = slot_and_valid(shape, 1 if rows_are_keys else 0, seq_len)
    mask = jnp.where((key == query) & valid, 0.0, NEVER)
    return jnp.concatenate([mask] * copies, axis=1 if rows_are_keys else 0)


def class_mask(seq_len):
    shape = (GROUP * PITCH, GROUP)
    key, valid = slot_and_valid(shape, 0, seq_len)
    mask = jnp.where((key == lax.broadcasted_iota(jnp.int32, shape, 1)) & valid, 0.0, NEVER)
    return jnp.concatenate([mask] * HEADS, axis=1)


def soft_columns(scores):
    expo = jnp.exp(scores - jnp.max(scores, axis=0, keepdims=True))
    return expo * (1.0 / jnp.sum(expo, axis=0, keepdims=True))


def take_slots(order_ref, all_ref, rows_ref, step, seq_len, slots):
    for s in range(GROUP):
        for c in range(all_ref.shape[0]):
            rows_ref[s * PITCH : s * PITCH + seq_len, c * 128 : (c + 1) * 128] = all_ref[
                c, pl.ds(order_ref[step * GROUP + s], seq_len, stride=slots), :
            ]


def first_rows(ref):
    return jnp.concatenate([ref[s * PITCH : s * PITCH + 1, :] for s in range(GROUP)])


def add_first_rows(ref, values):
    for s in range(GROUP):
        ref[s * PITCH : s * PITCH + 1, :] += values[s : s + 1]


def widen_tokens(tok_ref, all_ref):
    seq_len, slots, width = tok_ref.shape

    @pl.loop(0, seq_len)
    def _(t):
        wide = tok_ref[t].astype(jnp.float32)
        for c in range(all_ref.shape[0]):
            all_ref[c, pl.ds(pl.multiple_of(t * slots, 8), slots), :] = wide[:, c * 128 : (c + 1) * 128]


def ordered_masks(line_first=False):
    if line_first:
        return [(p >> 4) | ((p & 3) << 1) | (((p >> 2) & 3) << 3) for p in range(BLOCKS)]
    return [(p >> 4) | (((p >> 2) & 3) << 1) | ((p & 3) << 3) for p in range(BLOCKS)]


def write_unit(me, keep_ref, send_ref, unit, read, line_first=False):
    for p, mask in enumerate(ordered_masks(line_first)):
        owner = me ^ mask
        ref = keep_ref if p < BLOCKS // 2 else send_ref
        ref[p % (BLOCKS // 2), unit] = read(owner)


def from_square(ref, first=0):
    width = ref.shape[0]

    def read(owner):
        rows = pl.multiple_of((owner // 4) * (width // 8), 16)
        cols = pl.multiple_of((owner % 4) * width, 128)
        return ref[pl.ds(rows, width // 8), pl.ds(cols, width)].astype(jnp.bfloat16)

    return read


def from_tall(ref):
    size = ref.shape[0] // BLOCKS

    def read(owner):
        return ref[pl.ds(pl.multiple_of(owner * size, 16), size), :].astype(jnp.bfloat16)

    return read


def attend_kernel(
    count_ref, order_ref, tok_ref, gains_ref, shifts_ref, w_qkv_ref, b_qkv_ref, w_out_ref, b_out_ref,
    qkv_ref, o_ref, mid_ref,
    all_ref, x_ref, low_ref,
):
    step = pl.program_id(0)
    seq_len, slots, width = tok_ref.shape
    rows = GROUP * PITCH
    chunk = PAIR

    @pl.when(step == 0)
    def _():
        widen_tokens(tok_ref, all_ref)
        x_ref[...] = jnp.zeros_like(x_ref)

    take_slots(order_ref, all_ref, x_ref, step, seq_len, slots)
    for r in range(0, rows, chunk):
        normed, _ = standardize(x_ref[r : r + chunk, :])
        low_ref[r : r + chunk, :] = (normed * norm_row(gains_ref, 0) + norm_row(shifts_ref, 0)).astype(jnp.bfloat16)
    whole = product(low_ref[...], w_qkv_ref[:, : 2 * width])
    part = (whole[:, :width] + qkv_bias(b_qkv_ref, 0, 0, width)).astype(jnp.bfloat16)
    qkv_ref[:, :width] = part * jnp.bfloat16(HD ** -0.5)
    qkv_ref[:, width : 2 * width] = whole[:, width:].astype(jnp.bfloat16)
    part = product(low_ref[...], w_qkv_ref[:, 2 * width :]) + qkv_bias(b_qkv_ref, 0, 2, width)
    qkv_ref[:, 2 * width :] = part.astype(jnp.bfloat16)
    mask = pair_mask(False, seq_len, 2)
    spots = [(r, c) for r in range(0, rows, PAIR) for c in range(0, width, 2 * HD)]
    for b in range(0, len(spots), 24):
        group = spots[b : b + 24]
        scores = [
            against(
                both_heads(qkv_ref[r : r + PAIR, c : c + 2 * HD]), qkv_ref[r : r + PAIR, width + c : width + c + 2 * HD]
            )
            + mask
            for r, c in group
        ]
        probs, scales = [], []
        for score in scores:
            expo = jnp.exp(score - jnp.max(score, axis=1, keepdims=True))
            probs.append(expo.astype(jnp.bfloat16))
            scales.append(1.0 / jnp.sum(expo, axis=1, keepdims=True))
        outs = [
            product(prob, qkv_ref[r : r + PAIR, 2 * width + c : 2 * width + c + 2 * HD]) * scale
            for prob, scale, (r, c) in zip(probs, scales, group)
        ]
        for out, (r, c) in zip(outs, group):
            o_ref[r : r + PAIR, c : c + 2 * HD] = join_heads(out).astype(jnp.bfloat16)
    mixed = product(o_ref[...], w_out_ref[...])
    for r in range(0, rows, chunk):
        part = x_ref[r : r + chunk, :] + mixed[r : r + chunk] + b_out_ref[0:1, :]
        mid_ref[r : r + chunk, :] = part


def mlp_kernel(
    count_ref, gains_ref, shifts_ref, w_fc1_ref, b_fc1_ref, w_fc2_ref, b_fc2_ref, w_up_ref, b_up_ref, mid_ref,
    act_ref, slope_ref, x1_ref, kv_ref, cq_ref, co_ref, ch_ref, cx_ref,
    low_ref, wide_ref, mask_ref,
):
    rows, width = mid_ref.shape
    hidden = w_fc1_ref.shape[1]
    chunk = PAIR
    step = pl.program_id(0)
    here = pl.ds(pl.multiple_of(step * GROUP, GROUP), GROUP)

    @pl.when(step == 0)
    def _():
        mask_ref[...] = class_mask(SEQ_LEN)
        for ref in (cq_ref, co_ref, ch_ref, cx_ref):
            ref[...] = jnp.zeros_like(ref)

    for r in range(0, rows, chunk):
        normed, _ = standardize(mid_ref[r : r + chunk, :])
        low_ref[r : r + chunk, :] = (normed * norm_row(gains_ref, 1) + norm_row(shifts_ref, 1)).astype(jnp.bfloat16)
    for c in range(0, hidden, 256):
        pre = product(low_ref[...], w_fc1_ref[:, c : c + 256])
        for r in range(0, rows, 32):
            act, slope = smooth_both(pre[r : r + 32] + b_fc1_ref[0:1, c : c + 256])
            act_ref[r : r + 32, c : c + 256] = act.astype(jnp.bfloat16)
            slope_ref[r : r + 32, c : c + 256] = slope.astype(jnp.bfloat16)
    mixed = product(act_ref[...], w_fc2_ref[...])
    for r in range(0, rows, chunk):
        part = mid_ref[r : r + chunk, :] + mixed[r : r + chunk] + b_fc2_ref[0:1, :]
        x1_ref[r : r + chunk, :] = part
        normed, _ = standardize(part)
        wide = normed * norm_row(gains_ref, 2) + norm_row(shifts_ref, 2)
        wide_ref[r : r + chunk, :] = wide
        low_ref[r : r + chunk, :] = wide.astype(jnp.bfloat16)
    whole = product(low_ref[...], w_up_ref[:, width:])
    kv_ref[:, :width] = whole[:, :width].astype(jnp.bfloat16)
    kv_ref[:, width:] = (whole[:, width:] + qkv_bias(b_up_ref, 1, 2, width)).astype(jnp.bfloat16)
    cx_ref[here, :] = first_rows(x1_ref)
    first = first_rows(wide_ref).astype(jnp.bfloat16)
    ch_ref[here, :] = first.astype(jnp.float32)
    query = (product(first, w_up_ref[:, :width]) + qkv_bias(b_up_ref, 1, 0, width)).astype(jnp.bfloat16).astype(jnp.float32) * HD ** -0.5
    cq_ref[here, :] = query
    spread = spread_heads(query).astype(jnp.bfloat16)
    probs = soft_columns(against(kv_ref[:, :width], spread) + mask_ref[...]).astype(jnp.bfloat16)
    co_ref[here, :] = gather_heads(inner_rows(probs, kv_ref[:, width:]))


def upper_back_kernel(
    count_ref, gains_ref, shifts_ref, w_up_ref, ch_ref, co_ref, da_ref,
    x1_ref, kv_ref, cq_ref, cg_ref, cres_ref,
    dx_ref, unit_ref, vec_ref,
    acc_ref, wide_ref, dqs_ref, mask_ref, dkv_ref,
):
    step = pl.program_id(0)
    rows, width = x1_ref.shape

    @pl.when(step == 0)
    def _():
        acc_ref[...] = jnp.zeros_like(acc_ref)
        mask_ref[...] = class_mask(SEQ_LEN)
        vec_ref[...] = jnp.zeros_like(vec_ref)

    keys, values = kv_ref[:, :width], kv_ref[:, width:]
    spread = spread_heads(cq_ref[...]).astype(jnp.bfloat16)
    grads = spread_heads(cg_ref[...]).astype(jnp.bfloat16)
    probs = soft_columns(against(keys, spread) + mask_ref[...])
    back = against(values, grads)
    inner = (probs * (back - jnp.sum(back * probs, axis=0, keepdims=True))).astype(jnp.bfloat16)
    dkv_ref[:, :width] = product(inner, spread).astype(jnp.bfloat16)
    dkv_ref[:, width:] = product(probs.astype(jnp.bfloat16), grads).astype(jnp.bfloat16)
    grad_query = (gather_heads(inner_rows(inner, keys)) * HD ** -0.5).astype(jnp.bfloat16)
    @pl.when(step == 0)
    def _():
        dqs_ref[...] = jnp.zeros_like(dqs_ref)

    dqs_ref[pl.ds(pl.multiple_of(step * GROUP, GROUP), GROUP), :] = grad_query.astype(jnp.float32)
    vec_ref[:, 3 * width :] += fold_rows(grad_query.astype(jnp.float32))
    vec_ref[:, :width] += fold_rows(dkv_ref[:, width:].astype(jnp.float32))
    wide_ref[...] = against(dkv_ref[...], w_up_ref[:, width:])
    add_first_rows(wide_ref, against(grad_query, w_up_ref[:, :width]))
    chunk = PAIR
    parts = []
    for r in range(0, rows, chunk):
        normed, rstd = standardize(x1_ref[r : r + chunk, :])
        parts.append((normed * norm_row(gains_ref, 2) + norm_row(shifts_ref, 2)).astype(jnp.bfloat16))
        grad = wide_ref[r : r + chunk, :]
        vec_ref[:, width : 2 * width] += fold_rows(grad * normed)
        vec_ref[:, 2 * width : 3 * width] += fold_rows(grad)
        dx_ref[r : r + chunk, :] = standard_back(grad, normed, rstd, norm_row(gains_ref, 2))
    turned = jnp.concatenate(parts).T
    acc_ref[:, width : 3 * width] += product(turned, dkv_ref[...])
    add_first_rows(dx_ref, cres_ref[...])

    @pl.when(step == count_ref[0] - 1)
    def _():
        acc_ref[:, :width] = inner_rows(
            ch_ref[...].astype(jnp.bfloat16), dqs_ref[...].astype(jnp.bfloat16)
        )
        acc_ref[:, 3 * width :] = inner_rows(co_ref[...].astype(jnp.bfloat16), da_ref[...].astype(jnp.bfloat16))
        unit_ref[...] = acc_ref[...].astype(jnp.bfloat16)
        finish_rows(vec_ref)


def mlp_back_kernel(
    count_ref, me_ref, unit_ref, gains_ref, shifts_ref, w_fc1_ref, w_fc2_ref, dx_ref, mid_ref, act_ref, slope_ref,
    dmid_ref, keep_ref, send_ref, vec_ref, vec1_ref,
    acc1_ref, acc2_ref, dz_ref, big_ref, normed_ref, rstd_ref,
):
    step = pl.program_id(0)
    rows, width = dx_ref.shape
    hidden = act_ref.shape[1]

    @pl.when(step == 0)
    def _():
        acc1_ref[...] = jnp.zeros_like(acc1_ref)
        acc2_ref[...] = jnp.zeros_like(acc2_ref)
        vec_ref[...] = jnp.zeros_like(vec_ref)
        vec1_ref[...] = jnp.zeros_like(vec1_ref)

    low = dx_ref[...].astype(jnp.bfloat16)
    vec_ref[:, :width] += fold_rows(low.astype(jnp.float32))
    low_turned = low.T
    chunk = PAIR
    parts = []
    for r in range(0, rows, chunk):
        normed, rstd = standardize(mid_ref[r : r + chunk, :])
        normed_ref[r : r + chunk, :] = normed
        rstd_ref[r : r + chunk, :] = rstd
        parts.append((normed * norm_row(gains_ref, 1) + norm_row(shifts_ref, 1)).astype(jnp.bfloat16))
    norm_turned = jnp.concatenate(parts).T
    for c in range(0, hidden, 768):
        cols = slice(c, c + 768)
        back = against(low, w_fc2_ref[cols, :])
        for r in range(0, rows, chunk):
            part = (back[r : r + chunk] * slope_ref[r : r + chunk, cols].astype(jnp.float32)).astype(jnp.bfloat16)
            dz_ref[r : r + chunk, cols] = part
            vec1_ref[:, cols] += fold_rows(part.astype(jnp.float32))
        acc1_ref[:, cols] += product(norm_turned, dz_ref[:, cols])
        acc2_ref[:, cols] += product(low_turned, act_ref[:, cols])
    mixed = against(dz_ref[...], w_fc1_ref[...])
    for r in range(0, rows, chunk):
        normed, rstd = normed_ref[r : r + chunk, :], rstd_ref[r : r + chunk, :]
        grad = mixed[r : r + chunk]
        vec_ref[:, width : 2 * width] += fold_rows(grad * normed)
        vec_ref[:, 2 * width : 3 * width] += fold_rows(grad)
        dmid_ref[r : r + chunk, :] = dx_ref[r : r + chunk, :] + standard_back(grad, normed, rstd, norm_row(gains_ref, 1))

    @pl.when(step == count_ref[0] - 1)
    def _():
        finish_rows(vec_ref)
        finish_rows(vec1_ref)
        me = me_ref[0]
        write_unit(me, keep_ref, send_ref, 0, from_square(unit_ref))
        write_unit(me, keep_ref, send_ref, 1, from_square(acc1_ref))
        big_ref[...] = acc2_ref[...].T
        write_unit(me, keep_ref, send_ref, 2, from_tall(big_ref))


def attend_back_kernel(
    count_ref, w_out_ref, dmid_ref, qkv_ref, o_ref,
    dqkv_ref, dwo_ref, vec_ref,
    do_ref,
):
    step = pl.program_id(0)
    rows, width = dmid_ref.shape

    @pl.when(step == 0)
    def _():
        dwo_ref[...] = jnp.zeros_like(dwo_ref)
        vec_ref[...] = jnp.zeros_like(vec_ref)

    low = dmid_ref[...].astype(jnp.bfloat16)
    vec_ref[:, :width] += fold_rows(low.astype(jnp.float32))
    do_ref[...] = against(low, w_out_ref[...]).astype(jnp.bfloat16)
    dwo_ref[...] += product(o_ref[...].T, low)
    mask = pair_mask(True, SEQ_LEN, 2)
    spots = [(r, c) for r in range(0, rows, PAIR) for c in range(0, width, 2 * HD)]
    for b in range(0, len(spots), 6):
        group = spots[b : b + 6]
        queries = [both_heads(qkv_ref[r : r + PAIR, c : c + 2 * HD]) for r, c in group]
        keys = [qkv_ref[r : r + PAIR, width + c : width + c + 2 * HD] for r, c in group]
        values = [qkv_ref[r : r + PAIR, 2 * width + c : 2 * width + c + 2 * HD] for r, c in group]
        grads = [both_heads(do_ref[r : r + PAIR, c : c + 2 * HD]) for r, c in group]
        scores = [against(key, query) + mask for key, query in zip(keys, queries)]
        backs = [against(value, grad) for value, grad in zip(values, grads)]
        probs = [soft_columns(score) for score in scores]
        inners = [
            (prob * (back - jnp.sum(back * prob, axis=0, keepdims=True))).astype(jnp.bfloat16)
            for prob, back in zip(probs, backs)
        ]
        grad_values = [product(prob.astype(jnp.bfloat16), grad) for prob, grad in zip(probs, grads)]
        grad_keys = [product(inner, query) for inner, query in zip(inners, queries)]
        grad_queries = [inner_rows(inner, key) for inner, key in zip(inners, keys)]
        for (r, c), grad in zip(group, grad_values):
            dqkv_ref[r : r + PAIR, 2 * width + c : 2 * width + c + 2 * HD] = grad.astype(jnp.bfloat16)
        for (r, c), grad in zip(group, grad_keys):
            dqkv_ref[r : r + PAIR, width + c : width + c + 2 * HD] = grad.astype(jnp.bfloat16)
        for (r, c), grad in zip(group, grad_queries):
            dqkv_ref[r : r + PAIR, c : c + 2 * HD] = (join_heads(grad) * HD ** -0.5).astype(jnp.bfloat16)
    for j in range(3):
        cols = slice(j * width, (j + 1) * width)
        vec_ref[:, (j + 1) * width : (j + 2) * width] += fold_rows(dqkv_ref[:, cols].astype(jnp.float32))

    @pl.when(step == count_ref[0] - 1)
    def _():
        finish_rows(vec_ref)


def weight_back_kernel(
    count_ref, me_ref, order_ref, tok_ref, gains_ref, shifts_ref, dwo_ref, dqkv_ref,
    keep_ref, send_ref,
    all_ref, x_ref, acc_ref,
):
    step = pl.program_id(0)
    seq_len, slots, width = tok_ref.shape
    rows = GROUP * PITCH

    @pl.when(step == 0)
    def _():
        widen_tokens(tok_ref, all_ref)
        x_ref[...] = jnp.zeros_like(x_ref)
        acc_ref[:, : 3 * width] = jnp.zeros((width, 3 * width), jnp.float32)
        acc_ref[:, 3 * width :] = dwo_ref[...]

    take_slots(order_ref, all_ref, x_ref, step, seq_len, slots)
    chunk = PAIR
    parts = []
    for r in range(0, rows, chunk):
        normed, _ = standardize(x_ref[r : r + chunk, :])
        parts.append((normed * norm_row(gains_ref, 0) + norm_row(shifts_ref, 0)).astype(jnp.bfloat16))
    turned = jnp.concatenate(parts).T
    acc_ref[:, : 3 * width] += product(turned, dqkv_ref[...])

    @pl.when(step == count_ref[0] - 1)
    def _():
        write_unit(me_ref[0], keep_ref, send_ref, 0, from_square(acc_ref))


def input_back_kernel(
    count_ref, order_ref, tok_ref, gains_ref, w_qkv_ref, vec1_ref, vec2_ref, vec3_ref, vec4_ref, vec5_ref, dmid_ref, dqkv_ref,
    dtok_ref, all_vec_ref,
    all_ref, out_ref, x_ref, vec_ref,
):
    step = pl.program_id(0)
    seq_len, slots, width = tok_ref.shape
    rows = GROUP * PITCH

    @pl.when(step == 0)
    def _():
        widen_tokens(tok_ref, all_ref)
        x_ref[...] = jnp.zeros_like(x_ref)
        out_ref[...] = jnp.zeros_like(out_ref)
        vec_ref[...] = jnp.zeros_like(vec_ref)

    take_slots(order_ref, all_ref, x_ref, step, seq_len, slots)
    chunk = PAIR
    mixed = against(dqkv_ref[...], w_qkv_ref[...])
    for r in range(0, rows, chunk):
        normed, rstd = standardize(x_ref[r : r + chunk, :])
        grad = mixed[r : r + chunk]
        vec_ref[:, :width] += fold_rows(grad * normed)
        vec_ref[:, width:] += fold_rows(grad)
        part = dmid_ref[r : r + chunk, :] + standard_back(grad, normed, rstd, norm_row(gains_ref, 0))
        for s in range(chunk // PITCH):
            for t in range(all_ref.shape[0]):
                out_ref[t, pl.ds(order_ref[step * GROUP + r // PITCH + s], seq_len, stride=slots), :] = part[
                    s * PITCH : s * PITCH + seq_len, t * 128 : (t + 1) * 128
                ]

    @pl.when(step == count_ref[0] - 1)
    def _():
        finish_rows(vec_ref)
        start = 0
        for ref in (vec_ref, vec1_ref, vec2_ref, vec3_ref, vec4_ref, vec5_ref):
            size = ref.shape[1]
            all_vec_ref[:, start : start + size] = ref[0:1, :]
            start += size
        for t in range(out_ref.shape[0]):
            dtok_ref[:, t * 128 : (t + 1) * 128] = out_ref[t]


def place_of(mask):
    return ((mask & 1) << 4) | (((mask >> 1) & 3) << 2) | ((mask >> 3) & 3)


def read_place(own_ref, got_ref, place, unit):
    inner = place & (BLOCKS // 2 - 1)
    block = jnp.where(place < BLOCKS // 2, own_ref[inner, unit], got_ref[inner, unit])
    return block.astype(jnp.float32)


def unpack_kernel(
    me_ref, own_ref, got_ref,
    qkv_ref, out_ref, fc1_ref, fc2_ref,
):
    step = pl.program_id(0)
    width, size = own_ref.shape[3], own_ref.shape[2]
    count = out_ref.shape[0] // size
    for r, c in [(r, c) for r in range(count) for c in range(4)]:
        place = place_of(((step * count + r) * 4 + c) ^ me_ref[0])
        cols, rows = slice(c * width, (c + 1) * width), slice(r * size, (r + 1) * size)
        tall = slice((r * 4 + c) * size, (r * 4 + c + 1) * size)
        upper = read_place(own_ref, got_ref, place, 0)
        if c < 3:
            qkv_ref[rows, cols] = upper
        else:
            out_ref[rows, :] = upper
        fc1_ref[0, rows, cols] = read_place(own_ref, got_ref, place, 1)
        fc2_ref[0, tall, :] = read_place(own_ref, got_ref, place, 2)
        fc1_ref[1, rows, cols] = read_place(own_ref, got_ref, place, 3)
        fc2_ref[1, tall, :] = read_place(own_ref, got_ref, place, 4)


def unpack_first_kernel(
    me_ref, own_ref, got_ref, vec_ref, qkv_in_ref, out_in_ref,
    qkv_ref, out_ref, gains_ref, shifts_ref, bqv_ref, bout_ref, bfc1_ref, bfc2_ref, final1_ref, final2_ref, bottle_ref,
):
    step = pl.program_id(0)
    width = own_ref.shape[3]
    size = own_ref.shape[2]
    count = out_ref.shape[0] // size
    for r, c in [(r, c) for r in range(count) for c in range(4)]:
        block = read_place(own_ref, got_ref, place_of(((step * count + r) * 4 + c) ^ me_ref[0]), 0)
        rows = slice(r * size, (r + 1) * size)
        if c < 3:
            qkv_ref[rows, c * width : (c + 1) * width] = block
        else:
            out_ref[rows, :] = block

    @pl.when(step == 0)
    def _():
        hidden = bfc1_ref.shape[1]
        row_b, row_c, row_h = 2, 5, 9
        row_hidden = vec_ref.shape[1] // width - hidden // width
        row_a = row_hidden - 4

        def put(ref, place, row, count=1):
            ref[place] = vec_ref[:, row * width : (row + count) * width]

        for i, row in enumerate((0, row_b + 1, row_c + 1, row_h)):
            put(gains_ref, (i // 2, slice(i % 2, i % 2 + 1)), row)
            put(shifts_ref, (i // 2, slice(i % 2, i % 2 + 1)), row + 1)
        put(bqv_ref, (slice(0, 1), slice(0, width)), row_a + 1)
        put(bqv_ref, (slice(0, 1), slice(width, 2 * width)), row_a + 3)
        put(bqv_ref, (slice(1, 2), slice(0, width)), row_c + 3)
        put(bqv_ref, (slice(1, 2), slice(width, 2 * width)), row_c)
        put(bout_ref, slice(0, 1), row_a)
        put(bout_ref, slice(1, 2), row_h + 2)
        put(bfc1_ref, slice(0, 1), row_hidden, hidden // width)
        put(bfc1_ref, slice(1, 2), row_h + 6, hidden // width)
        put(bfc2_ref, slice(0, 1), row_b)
        put(bfc2_ref, slice(1, 2), row_h + 3)
        put(final1_ref, slice(0, 1), row_h + 4)
        put(final2_ref, slice(0, 1), row_h + 5)
        start = (row_h + 6) * width + hidden
        bottle_ref[...] = vec_ref[:, start : start + bottle_ref.shape[1]]


def prepare_kernel(
    device_ref, counts_ref, proto_ref, teacher_ref,
    info_ref, live_ref, image_ref, unit_ref, turned_ref, inv_ref, teach_ref, expo_ref,
):
    slots = live_ref.shape[0]
    images_here = slots // MOST_CROPS
    counts = [counts_ref[device_ref[0] * images_here + i] for i in range(images_here)]
    total = functools.reduce(lambda a, b: a + b, counts)
    place = lax.broadcasted_iota(jnp.int32, (slots, 1), 0)
    live_ref[...] = (place < total).astype(jnp.float32)
    image = jnp.zeros((slots, 1), jnp.float32)
    live_before, dead_before = 0, total
    for i, amount in enumerate(counts):
        dead = MOST_CROPS - amount
        for k in range(MOST_CROPS):
            at = jnp.where(k < amount, live_before + k, dead_before + k - amount)
            info_ref[at + 2] = i * MOST_CROPS + k
        live_spot = (place >= live_before) & (place < live_before + amount)
        dead_spot = (place >= dead_before) & (place < dead_before + dead)
        image = jnp.where(live_spot | dead_spot, float(i), image)
        live_before = live_before + amount
        dead_before = dead_before + dead
    image_ref[...] = image
    info_ref[0] = (total + GROUP - 1) // GROUP
    info_ref[1] = device_ref[0] & (BLOCKS - 1)
    proto = proto_ref[...].astype(jnp.float32)
    inv = lax.rsqrt(jnp.sum(proto * proto, axis=0, keepdims=True) + EPS)
    inv_ref[...] = inv
    unit = (proto * inv).astype(jnp.bfloat16)
    unit_ref[...] = unit
    turned_ref[...] = unit.T
    bottle = proto.shape[0]
    images = teacher_ref.shape[0]
    for r in range(0, images, 64):
        expo = jnp.exp(teacher_ref[r : r + 64, :] * (1.0 / TEACHER_TEMP))
        expo_ref[r : r + 64, :] = expo
        teach_ref[r : r + 64, :bottle] = against(expo.astype(jnp.bfloat16), unit)
        teach_ref[r : r + 64, bottle:] = jnp.broadcast_to(jnp.sum(expo, axis=1, keepdims=True), (64, 128))


def repeat_rows(values, image):
    out = jnp.zeros((image.shape[0], values.shape[1]), values.dtype)
    for i in range(values.shape[0]):
        out = jnp.where(image == i, values[i : i + 1], out)
    return out


def three_parts(values):
    high = values.astype(jnp.bfloat16).astype(jnp.float32)
    middle = (values - high).astype(jnp.bfloat16).astype(jnp.float32)
    return [high, middle, values - high - middle]


def head_kernel(
    scale, own_columns, me_ref, live_ref, image_ref, teach_ref, co_ref, cx_ref, gains_ref, shifts_ref, final_ref,
    w_out_ref, b_out_ref, far_fc1_ref, b_fc1_ref, far_fc2_ref, b_fc2_ref,
    far_w1_ref, b1_ref, far_w2_ref, b2_ref, far_w3_ref, b3_ref, far_unit_ref,
    cg_ref, cres_ref, da_ref, common_ref, feats_ref, share0_ref, share1_ref, share2_ref, share3_ref, keep_ref, send_ref, vec_ref,
    act_ref, slope_ref, slope1_ref, slope2_ref, one_ref, two_ref, back_ref, up1_ref, up2_ref,
    w_fc1_ref, w_fc2_ref, w1_ref, w2_ref, w3_ref, unit_ref, done_ref,
):
    far = (far_fc1_ref.at[1], far_fc2_ref.at[1], far_w1_ref, far_w2_ref, far_w3_ref, far_unit_ref)
    near = (w_fc1_ref, w_fc2_ref, w1_ref, w2_ref, w3_ref, unit_ref)
    copies = [pltpu.make_async_copy(a, b, done_ref.at[i]) for i, (a, b) in enumerate(zip(far, near))]
    for copy in copies:
        copy.start()
    width = cx_ref.shape[1]
    hidden = w_fc1_ref.shape[1]
    hid, bottle = w3_ref.shape
    low = jnp.bfloat16
    middle = cx_ref[...] + product(co_ref[...].astype(low), w_out_ref[...]) + b_out_ref[1:2, :]
    normed_d, rstd_d = standardize(middle)
    low_d = (normed_d * norm_row(gains_ref, 3) + norm_row(shifts_ref, 3)).astype(low)
    copies[0].wait()
    for c in range(0, hidden, 256):
        cols = slice(c, c + 256)
        act, slope = smooth_both(product(low_d, w_fc1_ref[:, cols]) + b_fc1_ref[1:2, cols])
        act_ref[:, cols] = act.astype(low)
        slope_ref[:, cols] = slope
    def share(kind, c, values):
        for u in range(256 // (4 * own_columns)):
            start = kind * (hid // 4) + c // 4 + u * own_columns
            here = slice(start, start + own_columns)
            parts = [values[:, (u * 4 + j) * own_columns : (u * 4 + j + 1) * own_columns] for j in range(4)]
            for bit in (0, 1):
                flip = (me_ref[0] >> bit) & 1 == 1
                parts = [jnp.where(flip, parts[j ^ (1 << bit)], parts[j]) for j in range(4)]
            for ref, part in zip((share0_ref, share1_ref, share2_ref, share3_ref), parts):
                ref[:, here] = part

    copies[1].wait()
    out = middle + product(act_ref[...], w_fc2_ref[...]) + b_fc2_ref[1:2, :]
    normed_f, rstd_f = standardize(out)
    low_f = (normed_f * final_ref[0:1, :] + final_ref[1:2, :]).astype(low)
    common_ref[:, hid : hid + width] = low_f
    copies[2].wait()
    for c in range(0, hid, 256):
        cols = slice(c, c + 256)
        act, slope = smooth_both(product(low_f, w1_ref[:, cols]) + b1_ref[:, cols])
        one_ref[:, cols] = act.astype(low)
        share(0, c, act.astype(low))
        slope1_ref[:, cols] = slope
    first = one_ref[...]
    copies[3].wait()
    for c in range(0, hid, 256):
        cols = slice(c, c + 256)
        act, slope = smooth_both(product(first, w2_ref[:, cols]) + b2_ref[:, cols])
        two_ref[:, cols] = act.astype(low)
        share(1, c, act.astype(low))
        slope2_ref[:, cols] = slope
    copies[4].wait()
    embed = product(two_ref[...], w3_ref[...]) + b3_ref[...]
    inv = lax.rsqrt(jnp.sum(embed * embed, axis=1, keepdims=True) + EPS)
    feats = (embed * inv).astype(low)
    slots = feats.shape[0]
    total = jnp.zeros((slots, 1), jnp.float32)
    student = jnp.zeros((slots, bottle), jnp.float32)
    total_protos = unit_ref.shape[0]
    copies[5].wait()
    size = 512

    def some(i, carry):
        total, student = carry
        part = unit_ref[pl.ds(pl.multiple_of(i * size, size), size), :]
        expo = jnp.exp(against(feats, part) * (1.0 / STUDENT_TEMP) - SHIFT)
        return (
            total + jnp.sum(expo, axis=1, keepdims=True),
            student + product(expo.astype(low), part),
        )

    total, student = lax.fori_loop(0, total_protos // size, some, (total, student), unroll=4)
    teach_total = teach_ref[:, bottle : bottle + 128]
    teach = repeat_rows(teach_ref[:, :bottle] * (1.0 / teach_total[:, :1]), image_ref[...])
    grad_feat = live_ref[...] * (student * (1.0 / total) - teach) * scale
    logs = [live_ref[...]] + three_parts(SHIFT + jnp.log(total)) + three_parts(repeat_rows(jnp.log(teach_total), image_ref[...])[:, :1]) + [image_ref[...]]
    lane = lax.broadcasted_iota(jnp.int32, (slots, 128), 1)
    extra = jnp.zeros((slots, 128), jnp.float32)
    for i, part in enumerate(logs):
        extra = jnp.where(lane == i, part, extra)
    mark = hid + width + bottle
    feats_ref[:, :bottle] = feats
    feats_ref[:, bottle:] = extra.astype(low)
    grad_embed = inv * grad_feat - embed * (inv * inv * inv) * jnp.sum(embed * grad_feat, axis=1, keepdims=True)
    grad_embed = grad_embed.astype(low)
    common_ref[:, hid + width : mark] = grad_embed
    vec_ref[...] = jnp.zeros_like(vec_ref)
    vec_ref[:, 6 * width + hidden : 6 * width + hidden + bottle] = fold_rows(grad_embed.astype(jnp.float32))
    for c in range(0, hid, 256):
        cols = slice(c, c + 256)
        grad = (slope2_ref[:, cols] * against(grad_embed, w3_ref[cols, :])).astype(low)
        common_ref[:, cols] = grad
        vec_ref[:, 7 * width + hidden + hid + c : 7 * width + hidden + hid + c + 256] = fold_rows(grad.astype(jnp.float32))
    grad_two = common_ref[:, :hid]
    for c in range(0, hid, 256):
        cols = slice(c, c + 256)
        grad = (slope1_ref[:, cols] * against(grad_two, w2_ref[cols, :])).astype(low)
        back_ref[:, cols] = grad
        vec_ref[:, 7 * width + hidden + c : 7 * width + hidden + c + 256] = fold_rows(grad.astype(jnp.float32))
        share(2, c, grad)
    grad = against(back_ref[...], w1_ref[...])
    vec_ref[:, 4 * width : 5 * width] = fold_rows(grad * normed_f)
    vec_ref[:, 5 * width : 6 * width] = fold_rows(grad)
    grad_class = standard_back(grad, normed_f, rstd_f, final_ref[0:1, :])
    grad_low = grad_class.astype(low)
    vec_ref[:, 3 * width : 4 * width] = fold_rows(grad_low.astype(jnp.float32))
    up2_ref[...] = inner_rows(act_ref[...], grad_low).astype(low)
    for c in range(0, hidden, 256):
        cols = slice(c, c + 256)
        grad = (slope_ref[:, cols] * against(grad_low, w_fc2_ref[cols, :])).astype(low)
        act_ref[:, cols] = grad
        vec_ref[:, 6 * width + c : 6 * width + c + 256] = fold_rows(grad.astype(jnp.float32))
    grad_pre = act_ref[...]
    up1_ref[...] = inner_rows(low_d, grad_pre).astype(low)
    grad = against(grad_pre, w_fc1_ref[...])
    vec_ref[:, :width] = fold_rows(grad * normed_d)
    vec_ref[:, width : 2 * width] = fold_rows(grad)
    grad_middle = grad_class + standard_back(grad, normed_d, rstd_d, norm_row(gains_ref, 3))
    cres_ref[...] = grad_middle
    grad_low = grad_middle.astype(low)
    da_ref[...] = grad_low.astype(jnp.float32)
    vec_ref[:, 2 * width : 3 * width] = fold_rows(grad_low.astype(jnp.float32))
    cg_ref[...] = against(grad_low, w_out_ref[...]).astype(low).astype(jnp.float32)
    finish_rows(vec_ref)
    write_unit(me_ref[0], keep_ref, send_ref, 0, from_square(up1_ref), True)
    write_unit(me_ref[0], keep_ref, send_ref, 1, from_tall(up2_ref), True)


def head_sum_kernel(
    width, info_ref, common0_ref, common1_ref, common2_ref, common3_ref, share0_ref, share1_ref, share2_ref, share3_ref,
    kept_ref, sent_ref,
    parts_ref,
):
    quarter = share0_ref.shape[1] // 3
    full = quarter * 4
    share = jnp.concatenate([ref[...] for ref in (share0_ref, share1_ref, share2_ref, share3_ref)])
    common = jnp.concatenate([ref[...] for ref in (common0_ref, common1_ref, common2_ref, common3_ref)])
    low = jnp.bfloat16
    parts = [share[:, i * quarter : (i + 1) * quarter].T for i in range(3)]
    parts_ref[:, :width] = product(parts[2], common[:, full : full + width])
    for c in range(0, full, 512):
        parts_ref[:, width + c : width + c + 512] = product(parts[0], common[:, c : c + 512])
    mark = parts_ref.shape[1]
    parts_ref[:, width + full :] = product(parts[1], common[:, width + full : mark])
    size = kept_ref.shape[1]
    spot = (info_ref[1] >> 2) & 1
    for z in range(kept_ref.shape[0]):
        for ref, digit in ((kept_ref, spot), (sent_ref, 1 - spot)):
            ref[z] = parts_ref[pl.ds(pl.multiple_of((2 * z + digit) * size, 8), size), :].astype(jnp.bfloat16)


def proto_back_kernel(
    scale, owner_ref, unit_ref, proto_ref, inv_ref, thawed_ref, expo_ref, feats_ref,
    grad_ref,
    acc_ref, raw_ref,
):
    step = pl.program_id(0)
    bottle = unit_ref.shape[0]

    @pl.when(step == 0)
    def _():
        acc_ref[...] = jnp.zeros_like(acc_ref)

    rows = feats_ref.shape[0]
    slots = rows // 8
    images = slots // MOST_CROPS
    for l in range(8):
        here = slice(l * slots, (l + 1) * slots)
        extra = feats_ref[here, bottle:].astype(jnp.float32)
        lane = lax.broadcasted_iota(jnp.int32, extra.shape, 1)
        pick = lambda a, b: jnp.sum(jnp.where((lane >= a) & (lane < b), extra, 0.0), axis=1, keepdims=True)
        logits = product(feats_ref[here, :bottle], unit_ref[...]) * (1.0 / STUDENT_TEMP)
        target = repeat_rows(expo_ref[pl.ds(pl.multiple_of(owner_ref[step * 8 + l] * images, 8), images), :], pick(7, 8))
        raw = pick(0, 1) * (jnp.exp(logits - pick(1, 4)) - target * jnp.exp(-pick(4, 7))) * scale
        raw_ref[here, :] = raw.astype(jnp.bfloat16)
    acc_ref[...] += inner_rows(feats_ref[:, :bottle], raw_ref[...])

    @pl.when(step == pl.num_programs(0) - 1)
    def _():
        proto = proto_ref[...].astype(jnp.float32)
        inv = inv_ref[...]
        grad = acc_ref[...]
        inner = jnp.sum(proto * grad, axis=0, keepdims=True)
        grad_ref[...] = (inv * grad - proto * (inv * inv * inv * inner)) * thawed_ref[...]


def whole(array):
    return pl.BlockSpec(array.shape, lambda *i: (0,) * len(array.shape))


class Layer:
    def __init__(self, array, layer):
        self.array, self.layer = array, layer


class Far:
    def __init__(self, array):
        self.array = array


def spec_of(item):
    if isinstance(item, Far):
        return pl.BlockSpec(memory_space=pl.ANY)
    if isinstance(item, Layer):
        shape = item.array.shape[1:]
        return pl.BlockSpec((None,) + shape, lambda *i: (item.layer,) + (0,) * len(shape))
    return whole(item)


def array_of(item):
    return item.array if isinstance(item, (Layer, Far)) else item


class Shifted:
    def __init__(self, ref, first):
        self.ref, self.first = ref, first

    def __getitem__(self, index):
        return self.ref[self.first + index]


def run_kernel(body, steps, scalars, whole_in, step_in, outs, scratch, micros, info=None, limit=32):
    count = info
    if info is not None:
        inner, firsts = body, scalars
        scalars = [info]

        def body(info_ref, *refs):
            @pl.when(pl.program_id(0) < info_ref[0])
            def _():
                inner(info_ref, *[Shifted(info_ref, first) for first in firsts], *refs)

    def by_step(rows, width):
        if count is None:
            return pl.BlockSpec((rows, width), lambda i, *s: (i, 0))
        return pl.BlockSpec((rows, width), lambda i, c, *s: (jnp.minimum(i, c[0] - 1), 0))

    return pl.pallas_call(
        body,
        grid_spec=pltpu.PrefetchScalarGridSpec(
            num_scalar_prefetch=len(scalars),
            grid=(steps,),
            in_specs=[spec_of(a) for a in whole_in] + [by_step(rows, a.shape[1]) for a, rows in step_in],
            out_specs=[
                by_step(rows, shape[1])
                if rows
                else pl.BlockSpec(memory_space=pltpu.SMEM)
                if rows is None
                else pl.BlockSpec(shape, lambda *i, k=len(shape): (0,) * k)
                for shape, dtype, rows in outs
            ],
            scratch_shapes=scratch,
        ),
        out_shape=[jax.ShapeDtypeStruct(shape, dtype) for shape, dtype, rows in outs],
        compiler_params=pltpu.CompilerParams(
            dimension_semantics=("arbitrary",), vmem_limit_bytes=limit * 1024 * 1024
        ),
        cost_estimate=pl.CostEstimate(flops=micros * 10**9, bytes_accessed=2**20, transcendentals=0),
    )(*scalars, *[array_of(a) for a in whole_in], *[a for a, rows in step_in])


def axis_bits(n):
    bits = n.bit_length() - 1
    assert n == 1 << bits
    return bits


def swap(values, mask, n):
    return lax.ppermute(values, "dp", [(i, i ^ mask) for i in range(n)])


def group_masks(group):
    return [k << group[0] for k in range(1 << len(group))]


def own_digit(group):
    return (lax.axis_index("dp") >> group[0]) & ((1 << len(group)) - 1)


def upper_groups(n, first):
    bits = list(range(first, axis_bits(n)))
    return [bits[i : i + 2] for i in range(0, len(bits), 2)][::-1]


def gather_loose(block, group, n):
    return jnp.stack([swap(block, mask, n) if mask else block for mask in group_masks(group)])


def tree_sum(parts):
    while len(parts) > 1:
        parts = [parts[i] + parts[i + 1] for i in range(0, len(parts), 2)]
    return parts[0]


def scatter_send(parts, group):
    size = 1 << len(group)
    parts = parts.reshape((size, parts.shape[0] // size) + parts.shape[1:])
    digit = own_digit(group)
    return [lax.dynamic_index_in_dim(parts, digit ^ k, 0, keepdims=False) for k in range(size)]


def double(mine, got):
    return jnp.concatenate([mine, got])


def pick_send(parts, axis, group):
    digit = own_digit(group)
    return [lax.dynamic_index_in_dim(parts, digit ^ k, axis, keepdims=False) for k in range(2)]


def swap_parts(parts, group, n):
    return [swap(part, mask, n) if mask else part for part, mask in zip(parts, group_masks(group))]


def scatter_stage(parts, group, n):
    got = swap_parts(scatter_send(parts, group), group, n)
    return tree_sum([part.astype(jnp.float32) for part in got]).astype(parts.dtype)


def sum_stage(values, group, n):
    return tree_sum(swap_parts([values] * (1 << len(group)), group, n))


def fold_send(parts, group):
    size = 1 << len(group)
    parts = parts.reshape((size, parts.shape[0] // size) + parts.shape[1:])
    return [parts[k] for k in range(size)]


def fold_sum(parts):
    return tree_sum([part.astype(jnp.float32) for part in parts]).astype(parts[0].dtype)


def unfold_stage(parts, group, n):
    return jnp.concatenate([swap(parts, mask, n) if mask else parts for mask in group_masks(group)])


def extra_sum(values, n):
    for bit in range(5, axis_bits(n)):
        values = values + swap(values, 1 << bit, n)
    return values


def together(*values):
    return lax.optimization_barrier(values)


CORE, PLANE, LINE = [0], [1, 2], [3, 4]
UNPACK = 4


def per_device(
    tokens,
    layer_gains,
    layer_shifts,
    w_qkv,
    b_qv,
    w_out,
    b_out,
    w_fc1,
    b_fc1,
    w_fc2,
    b_fc2,
    final_gain,
    final_shift,
    head_w1,
    head_b1,
    head_w2,
    head_b2,
    head_w3,
    head_b3,
    prototypes,
    crop_counts,
    teacher_logits,
    first_epoch,
):
    low, wide = jnp.bfloat16, jnp.float32
    slot_count, seq_len, width = tokens.shape
    n = lax.axis_size("dp")
    device = lax.axis_index("dp")
    me = (device & (BLOCKS - 1)).reshape(1)
    bottle = prototypes.shape[0]
    hidden = w_fc1.shape[2]
    hid = head_w2.shape[0]
    rows = GROUP * PITCH
    steps = slot_count // GROUP
    padded = slot_count * PITCH
    row_count = slot_count * seq_len
    groups = upper_groups(n, 3)

    scale = 1.0 / (STUDENT_TEMP * n)
    images, protos = teacher_logits.shape
    info, own_live, image, unit_low, unit_turned, col_inv, teach_sum, teach_expo = run_kernel(
        prepare_kernel,
        1,
        [device.reshape(1), crop_counts],
        [prototypes, teacher_logits],
        [],
        [
            ((slot_count + 2,), jnp.int32, None),
            ((slot_count, 1), wide, 0),
            ((slot_count, 1), wide, 0),
            ((bottle, protos), low, 0),
            ((protos, bottle), low, 0),
            ((1, protos), wide, 0),
            ((images, bottle + 128), wide, 0),
            ((images, protos), wide, 0),
        ],
        [],
        4,
        limit=56,
    )
    unit_all = lax.all_gather(unit_turned, "dp", axis=0, tiled=True)
    teach_sum = teach_sum.reshape(n, -1, bottle + 128)
    for group in groups[:-1]:
        teach_sum = scatter_stage(teach_sum, group, n)

    gains, shifts = layer_gains, layer_shifts
    turned_tokens = tokens.transpose(1, 0, 2)
    all_rows = pltpu.VMEM((width // 128, row_count, 128), wide)
    teach_parts = scatter_send(teach_sum, groups[-1])
    turned_tokens, *teach_parts = together(turned_tokens, *teach_parts)
    teach_parts = swap_parts(teach_parts, groups[-1], n)
    qkv_a, attn_a, middle_a = run_kernel(
        attend_kernel,
        steps,
        [2],
        [turned_tokens, gains, shifts, Layer(w_qkv, 0), b_qv, Layer(w_out, 0), b_out],
        [],
        [((padded, 3 * width), low, rows), ((padded, width), low, rows), ((padded, width), wide, rows)],
        [all_rows, pltpu.VMEM((rows, width), wide), pltpu.VMEM((rows, width), low)],
        35,
        info,
        limit=56,
    )
    middle_a, *teach_parts = together(middle_a, *teach_parts)
    teach_sum = tree_sum(teach_parts)
    teach_parts = scatter_send(teach_sum, PLANE)
    middle_a, *teach_parts = together(middle_a, *teach_parts)
    teach_parts = swap_parts(teach_parts, PLANE, n)
    act_a, slope_a, lower_out, kv_c, query_c, attn_c, first_low, first_in = run_kernel(
        mlp_kernel,
        steps,
        [],
        [gains, shifts, Layer(w_fc1, 0), b_fc1, Layer(w_fc2, 0), b_fc2, Layer(w_qkv, 1), b_qv],
        [(middle_a, rows)],
        [
            ((padded, hidden), low, rows),
            ((padded, hidden), low, rows),
            ((padded, width), wide, rows),
            ((padded, 2 * width), low, rows),
            ((slot_count, width), wide, 0),
            ((slot_count, width), wide, 0),
            ((slot_count, width), wide, 0),
            ((slot_count, width), wide, 0),
        ],
        [pltpu.VMEM((rows, width), low), pltpu.VMEM((rows, width), wide), pltpu.VMEM((rows, HEADS * GROUP), wide)],
        40,
        info,
        limit=56,
    )
    first_in, *teach_parts = together(first_in, *teach_parts)
    teach_sum = scatter_stage(tree_sum(teach_parts), CORE, n)[0]

    finals = jnp.stack([final_gain, final_shift])
    vec_width = -(-(7 * width + hidden + 2 * hid) // width) * width
    grad_attended, grad_middle_c, grad_attn, common, feats, *shares, keep_u, send_u, vec_h = run_kernel(
        functools.partial(head_kernel, scale, hid // n),
        1,
        [me],
        [own_live, image, teach_sum, attn_c, first_in, gains, shifts, finals, Layer(w_out, 1), b_out, Far(w_fc1), b_fc1, Far(w_fc2), b_fc2,
         Far(head_w1), head_b1[None], Far(head_w2), head_b2[None], Far(head_w3), head_b3[None], Far(unit_all)],
        [],
        [
            ((slot_count, width), wide, 0),
            ((slot_count, width), wide, 0),
            ((slot_count, width), wide, 0),
            ((slot_count, hid + width + bottle), low, 0),
            ((slot_count, bottle + 128), low, 0),
            *[((slot_count, hid // 4 * 3), low, 0)] * 4,
            ((BLOCKS // 2, 2, width // 8, width), low, 0),
            ((BLOCKS // 2, 2, width // 8, width), low, 0),
            ((8, vec_width), wide, 0),
        ],
        [
            pltpu.VMEM((slot_count, hidden), low),
            pltpu.VMEM((slot_count, hidden), wide),
            pltpu.VMEM((slot_count, hid), wide),
            pltpu.VMEM((slot_count, hid), wide),
            pltpu.VMEM((slot_count, hid), low),
            pltpu.VMEM((slot_count, hid), low),
            pltpu.VMEM((slot_count, hid), low),
            pltpu.VMEM((width, hidden), low),
            pltpu.VMEM((hidden, width), low),
        ]
        + [pltpu.VMEM(v.shape, low) for v in (w_fc1[0], w_fc2[0], head_w1, head_w2, head_w3, unit_all)]
        + [pltpu.SemaphoreType.DMA((6,))],
        20,
        limit=min(56, 40 + unit_all.size // 2**19),
    )
    common_got = swap(common, 1, n)
    share0, share2 = shares[0], shares[2]
    share1, share3 = swap(shares[1], 1, n), swap(shares[3], 1, n)
    bits = list(range(5, axis_bits(n))) + [4, 3, 1, 2, 0]
    masks = [0]
    for bit in bits:
        masks = masks + [mask | (1 << bit) for mask in masks]
    for bit in bits[:-5]:
        feats = double(feats, swap(feats, 1 << bit, n))
    grad_attended, common, share2, share3, send_u, feats = together(grad_attended, common, share2, share3, send_u, feats)
    got_u = swap(send_u, 1, n)
    feats_got = swap(feats, 16, n)
    common2, share2, share3 = (swap(v, 2, n) for v in (common, share2, share3))
    grad_lower_out, unit_u, vec_c = run_kernel(
        upper_back_kernel,
        steps,
        [],
        [gains, shifts, Layer(w_qkv, 1), first_low, attn_c, grad_attn],
        [(lower_out, rows), (kv_c, rows), (query_c, GROUP), (grad_attended, GROUP), (grad_middle_c, GROUP)],
        [
            ((padded, width), wide, rows),
            ((width, 4 * width), low, 0),
            ((8, 4 * width), wide, 0),
        ],
        [
            pltpu.VMEM((width, 4 * width), wide),
            pltpu.VMEM((rows, width), wide),
            pltpu.VMEM((slot_count, width), wide),
            pltpu.VMEM((rows, HEADS * GROUP), wide),
            pltpu.VMEM((rows, 2 * width), low),
        ],
        20,
        info,
    )
    grad_lower_out, common2, share2, share3, got_u, feats_got = together(
        grad_lower_out, common2, share2, share3, got_u, feats_got
    )
    feats = double(feats, feats_got)
    common3 = swap(common2, 1, n)
    parts_u = fold_send(keep_u + got_u, LINE)
    head_keep, head_send = run_kernel(
        functools.partial(head_sum_kernel, width),
        1,
        [info],
        [common, common_got, common2, common3, share0, share1, share2, share3],
        [],
        [((n // 8, hid // n, width + hid + bottle), low, 0)] * 2,
        [pltpu.VMEM((hid // 4, width + hid + bottle), wide)],
        6,
    )
    grad_lower_out, head_send, feats, *parts_u = together(grad_lower_out, head_send, feats, *parts_u)
    head_got, feats_got = swap(head_send, 4, n), swap(feats, 8, n)
    parts_u = swap_parts(parts_u, LINE, n)
    grad_middle_a, keep_m, send_m, vec_b, vec_hidden = run_kernel(
        mlp_back_kernel,
        steps,
        [1],
        [unit_u, gains, shifts, Layer(w_fc1, 0), Layer(w_fc2, 0)],
        [(grad_lower_out, rows), (middle_a, rows), (act_a, rows), (slope_a, rows)],
        [
            ((padded, width), wide, rows),
            ((BLOCKS // 2, 3, width // 8, width), low, 0),
            ((BLOCKS // 2, 3, width // 8, width), low, 0),
            ((8, 3 * width), wide, 0),
            ((8, hidden), wide, 0),
        ],
        [
            pltpu.VMEM((width, hidden), wide),
            pltpu.VMEM((width, hidden), wide),
            pltpu.VMEM((rows, hidden), low),
            pltpu.VMEM((hidden, width), wide),
            pltpu.VMEM((rows, width), wide),
            pltpu.VMEM((rows, 1), wide),
        ],
        40,
        info,
        limit=44,
    )
    grad_middle_a, head_got, feats_got, send_m, *parts_u = together(grad_middle_a, head_got, feats_got, send_m, *parts_u)
    feats = double(feats, feats_got)
    head_parts = head_keep + head_got
    for bit in range(axis_bits(n) - 1, 4, -1):
        head_parts = scatter_stage(head_parts, [bit], n)
    head_keep, head_send = pick_send(head_parts.reshape((2, 2) + head_parts.shape[1:]), 1, [3])
    parts_m = [
        jnp.concatenate([a.reshape((-1,) + a.shape[2:]), b[0]])
        for a, b in zip(fold_send(keep_m + swap(send_m, 1, n), PLANE), fold_send(fold_sum(parts_u), PLANE))
    ]
    grad_middle_a, head_send, *parts_m = together(grad_middle_a, head_send, *parts_m)
    head_got = swap(head_send, 8, n)
    parts_m = swap_parts(parts_m, PLANE, n)
    grad_qkv, grad_wo, vec_a = run_kernel(
        attend_back_kernel,
        steps,
        [],
        [Layer(w_out, 0)],
        [(grad_middle_a, rows), (qkv_a, rows), (attn_a, rows)],
        [((padded, 3 * width), low, rows), ((width, width), wide, 0), ((8, 4 * width), wide, 0)],
        [pltpu.VMEM((rows, width), low)],
        40,
        info,
    )
    grad_qkv, head_got, *parts_m = together(grad_qkv, head_got, *parts_m)
    head_keep, head_send = pick_send(head_keep + head_got, 0, [4])
    sum_m = fold_sum(parts_m)
    sum_u = sum_m[None, 12:]
    parts_m = fold_send(sum_m[:12].reshape((4, 3) + sum_m.shape[1:]), LINE)
    grad_qkv, head_send, feats, *parts_m = together(grad_qkv, head_send, feats, *parts_m)
    feats_got = swap(feats, 2, n)
    parts_m = swap_parts(parts_m, LINE, n)
    keep_a, send_a = run_kernel(
        weight_back_kernel,
        steps,
        [1, 2],
        [turned_tokens, gains, shifts, grad_wo],
        [(grad_qkv, rows)],
        [
            ((BLOCKS // 2, 1, width // 8, width), low, 0),
            ((BLOCKS // 2, 1, width // 8, width), low, 0),
        ],
        [all_rows, pltpu.VMEM((rows, width), wide), pltpu.VMEM((width, 4 * width), wide)],
        10,
        info,
    )
    keep_a, send_a, feats_got, *parts_m = together(keep_a, send_a, feats_got, *parts_m)
    feats = double(feats, feats_got)
    sum_m = extra_sum(jnp.concatenate([fold_sum(parts_m), sum_u], axis=1), n)
    keep_a, send_a = fold_send(keep_a + swap(send_a, 1, n), [2])
    grad_qkv, sum_m, send_a, feats = together(grad_qkv, sum_m, send_a, feats)
    feats_got = swap(feats, 4, n)
    parts_m = swap_parts([sum_m] * 4, LINE, n)
    got_a = swap(send_a, 4, n)
    grad_tokens, vectors = run_kernel(
        input_back_kernel,
        steps,
        [2],
        [turned_tokens, gains, Layer(w_qkv, 0), vec_b, vec_c, vec_h, vec_a, vec_hidden],
        [(grad_middle_a, rows), (grad_qkv, rows)],
        [((row_count, width), wide, 0), ((1, 13 * width + hidden + vec_width), wide, 0)],
        [all_rows, all_rows, pltpu.VMEM((rows, width), wide), pltpu.VMEM((8, 2 * width), wide)],
        20,
        info,
    )
    tokens_grad = grad_tokens.reshape(seq_len, slot_count, width).transpose(1, 0, 2)
    vectors, got_a, feats_got, *parts_m = together(vectors, got_a, feats_got, *parts_m)
    feats = double(feats, feats_got)
    feats = double(feats, swap(feats, 1, n))

    keep_a, send_a = fold_send(keep_a + got_a, [1])
    send_a, vectors = together(send_a, vectors)
    got_a, got_v = swap(send_a, 2, n), swap(vectors, 1, n)
    vectors = vectors + got_v
    sum_m = jnp.concatenate(parts_m)
    half = sum_m.shape[0] // 2
    feats, vectors, sum_m = together(feats, vectors, sum_m)
    one, two = sum_m[:half], sum_m[half:]
    one, two = [one, swap(one, 2, n)], [two, swap(two, 4, n)]
    prototypes_grad = run_kernel(
        functools.partial(proto_back_kernel, scale),
        n // 8,
        [device ^ jnp.array(masks, jnp.int32)],
        [unit_low, prototypes, col_inv, (1 - first_epoch).astype(wide)[None], teach_expo],
        [(feats, 8 * slot_count)],
        [(prototypes.shape, wide, 0)],
        [pltpu.VMEM(prototypes.shape, wide), pltpu.VMEM((8 * slot_count, protos), low)],
        6,
    )[0]
    prototypes_grad, got_a, *parts_m = together(prototypes_grad, got_a, *one, *two)
    one, two = jnp.stack(parts_m[:2]), jnp.stack(parts_m[2:])
    sum_a = keep_a + got_a
    sum_a, vectors, one, two = together(sum_a, vectors, one, two)
    one, two = [one, swap(one, 4, n)], [two, swap(two, 2, n)]
    for bit in (4, 3):
        keep_a, send_a = fold_send(sum_a, [bit])
        got_a, got_v = swap(send_a, 1 << bit, n), swap(vectors, 1 << bit, n)
        sum_a, vectors = keep_a + got_a, vectors + got_v
    sum_a = extra_sum(sum_a, n)
    vectors = extra_sum(vectors, n)
    for bit in (3, 4):
        sum_a = unfold_stage(sum_a, [bit], n)
    sum_a, vectors, head_send, *parts_m = together(sum_a, vectors, head_send, *one, *two)
    head_got = swap(head_send, 16, n)
    one = jnp.stack(parts_m[:2]).reshape((4,) + parts_m[0].shape[1:])
    two = jnp.stack(parts_m[2:], axis=1).reshape((4,) + parts_m[0].shape[1:])
    sum_m = jnp.concatenate([one, two], axis=1).reshape((BLOCKS // 2,) + one.shape[2:])
    got_m, got_a, got_v = swap(sum_m, 1, n), swap(sum_a, 2, n), swap(vectors, 2, n)
    got_m, got_a, got_v = together(got_m, got_a, got_v)
    sum_a, vectors = double(sum_a, got_a), vectors + got_v
    got_a, got_v = swap(sum_a, 4, n), swap(vectors, 4, n)
    specs = [
        pl.BlockSpec((None, width // UNPACK, 3 * width), lambda i: (1, i, 0)),
        pl.BlockSpec((None, width // UNPACK, width), lambda i: (1, i, 0)),
    ]
    shapes = [jax.ShapeDtypeStruct(s, wide) for s in ((2, width, 3 * width), (2, width, width))]
    params = pltpu.CompilerParams(dimension_semantics=("arbitrary",), vmem_limit_bytes=32 * 1024 * 1024)
    qkv_grad, out_grad, fc1_grad, fc2_grad = pl.pallas_call(
        unpack_kernel,
        grid=(UNPACK,),
        in_specs=[pl.BlockSpec(memory_space=pltpu.SMEM), whole(sum_m), whole(got_m)],
        out_specs=specs
        + [
            pl.BlockSpec((2, width // UNPACK, hidden), lambda i: (0, i, 0)),
            pl.BlockSpec((2, hidden // UNPACK, width), lambda i: (0, i, 0)),
        ],
        out_shape=shapes + [jax.ShapeDtypeStruct(s, wide) for s in ((2, width, hidden), (2, hidden, width))],
        compiler_params=params,
        cost_estimate=pl.CostEstimate(flops=8 * 10**9, bytes_accessed=2**20, transcendentals=0),
    )(me, sum_m, got_m)
    qkv_grad, out_grad, got_a, got_v, head_got = together(qkv_grad, out_grad, got_a, got_v, head_got)
    head_sum = (head_keep.astype(wide) + head_got.astype(wide)).reshape(hid // n, -1)
    w1_grad, w2_grad, w3_grad = head_sum[:, :width].T, head_sum[:, width : width + hid], head_sum[:, width + hid :]
    sum_a, vectors = double(sum_a, got_a), vectors + got_v
    got_a = swap(sum_a, 1, n)
    specs = [pl.BlockSpec(spec.block_shape, lambda i: (0, i, 0)) for spec in specs]
    small = [(2, 2, width), (2, 2, width), (2, 2 * width), (2, width), (2, hidden), (2, width), (1, width), (1, width), (1, bottle)]
    qkv_grad, out_grad, gains_grad, shifts_grad, bqv_grad, bout_grad, bfc1_grad, bfc2_grad, *finals = pl.pallas_call(
        unpack_first_kernel,
        grid=(UNPACK,),
        in_specs=[pl.BlockSpec(memory_space=pltpu.SMEM), whole(sum_a), whole(got_a), whole(vectors)]
        + [pl.BlockSpec(memory_space=pl.ANY)] * 2,
        out_specs=specs + [pl.BlockSpec(shape, lambda i, k=len(shape): (0,) * k) for shape in small],
        out_shape=shapes + [jax.ShapeDtypeStruct(shape, wide) for shape in small],
        input_output_aliases={4: 0, 5: 1},
        compiler_params=params,
    )(me, sum_a, got_a, vectors, qkv_grad, out_grad)
    row_h = 9
    ends = vectors[0, (row_h + 7) * width + hidden : (row_h + 7) * width + hidden + 2 * hid]
    own_part = lambda start: lax.dynamic_slice_in_dim(ends, start + device * (hid // n), hid // n)

    return (
        tokens_grad,
        gains_grad,
        shifts_grad,
        qkv_grad,
        bqv_grad,
        out_grad,
        bout_grad,
        fc1_grad,
        bfc1_grad,
        fc2_grad,
        bfc2_grad,
        finals[0].reshape(-1),
        finals[1].reshape(-1),
        w1_grad,
        own_part(0),
        w2_grad,
        own_part(hid),
        w3_grad,
        finals[2].reshape(-1),
        prototypes_grad,
    )


def solution(mesh):
    return jax.shard_map(
        per_device,
        mesh=mesh,
        in_specs=(
            P("dp", None, None),
            P(),
            P(),
            P(),
            P(),
            P(),
            P(),
            P(),
            P(),
            P(),
            P(),
            P(),
            P(),
            P(),
            P(),
            P(),
            P(),
            P(),
            P(),
            P(None, "dp"),
            P(),
            P(None, "dp"),
            P("dp"),
        ),
        out_specs=(
            P("dp", None, None),
            P(),
            P(),
            P(),
            P(),
            P(),
            P(),
            P(),
            P(),
            P(),
            P(),
            P(),
            P(),
            P(None, "dp"),
            P("dp"),
            P("dp", None),
            P("dp"),
            P("dp", None),
            P(),
            P(None, "dp"),
        ),
        check_vma=False,
    )
```

```python
import functools

import jax
import jax.numpy as jnp
from jax import lax
from jax.experimental import pallas as pl
from jax.experimental.pallas import tpu as pltpu
from jax.sharding import PartitionSpec as P

HEADS = 6
HD = 64
MOST_CROPS = 10

STUDENT_TEMP = 0.1
TEACHER_TEMP = 0.04
EPS = 1e-06
SHIFT = 10.0


def product(left, right):
    return jnp.dot(left, right, preferred_element_type=jnp.float32)


def against(left, right):
    return lax.dot_general(
        left, right, (((1,), (1,)), ((), ())), preferred_element_type=jnp.float32
    )


def inner_rows(left, right):
    return lax.dot_general(
        left, right, (((0,), (0,)), ((), ())), preferred_element_type=jnp.float32
    )


def column_sum(values):
    return jnp.sum(values.astype(jnp.float32), axis=0)


def norm_forward(values, gain, shift):
    centered = values - jnp.mean(values, axis=-1, keepdims=True)
    rstd = lax.rsqrt(jnp.mean(centered * centered, axis=-1, keepdims=True) + EPS)
    normed = centered * rstd
    return (normed * gain + shift, normed, rstd)


def norm_backward(grad, normed, rstd, gain):
    scaled = grad * gain
    inner = (
        scaled
        - jnp.mean(scaled, axis=-1, keepdims=True)
        - normed * jnp.mean(scaled * normed, axis=-1, keepdims=True)
    )
    return (rstd * inner, jnp.sum(grad * normed, axis=0), jnp.sum(grad, axis=0))


GROUP = 16
BLOCKS = 32
PITCH = 40
PAIR = 2 * PITCH
NEVER = -1e30
SEQ_LEN = 37


def smooth_both(values):
    size = jnp.abs(values)
    bell = jnp.exp(values * values * -0.5)
    t = 1.0 / (1.0 + 0.23164189 * size)
    tail = t * (0.127414796 + t * (-0.142248368 + t * (0.7107068705 + t * (-0.7265760135 + t * 0.5307027145))))
    upper = tail * bell
    area = jnp.where(values >= 0, 1.0 - upper, upper)
    return values * area, area + values * (bell * 0.3989422804014327)


def norm_row(ref, index):
    return ref[index // 2, index % 2 : index % 2 + 1, :]


def qkv_bias(ref, layer, part, width):
    if part == 1:
        return 0.0
    return ref[layer : layer + 1, part // 2 * width : (part // 2 + 1) * width]


def standardize(values):
    centered = values - jnp.mean(values, axis=-1, keepdims=True)
    rstd = lax.rsqrt(jnp.mean(centered * centered, axis=-1, keepdims=True) + EPS)
    return centered * rstd, rstd


def standard_back(grad, normed, rstd, gain):
    scaled = grad * gain
    return rstd * (
        scaled
        - jnp.mean(scaled, axis=-1, keepdims=True)
        - normed * jnp.mean(scaled * normed, axis=-1, keepdims=True)
    )


def fold_rows(values):
    return jnp.sum(values.reshape(-1, 8, values.shape[1]), axis=0)


def finish_rows(ref):
    ref[0:1, :] = jnp.sum(ref[...], axis=0, keepdims=True)


def both_heads(values):
    lane = lax.broadcasted_iota(jnp.int32, values.shape, 1)
    zero = jnp.zeros_like(values)
    return jnp.concatenate([jnp.where(lane < HD, values, zero), jnp.where(lane < HD, zero, values)])


def join_heads(values):
    rows = values.shape[0] // 2
    lane = lax.broadcasted_iota(jnp.int32, (rows, values.shape[1]), 1)
    return jnp.where(lane < HD, values[:rows], values[rows:])


def spread_heads(values):
    lane = lax.broadcasted_iota(jnp.int32, values.shape, 1) // HD
    return jnp.concatenate([jnp.where(lane == h, values, 0.0) for h in range(HEADS)])


def gather_heads(values):
    lane = lax.broadcasted_iota(jnp.int32, (GROUP, values.shape[1]), 1) // HD
    out = jnp.zeros((GROUP, values.shape[1]), values.dtype)
    for h in range(HEADS):
        out = jnp.where(lane == h, values[h * GROUP : (h + 1) * GROUP], out)
    return out


def slot_and_valid(shape, dim, seq_len):
    index = lax.broadcasted_iota(jnp.int32, shape, dim)
    slot = index // PITCH
    return slot, index - slot * PITCH < seq_len


def pair_mask(rows_are_keys, seq_len, copies=1):
    shape = (PAIR, PAIR)
    key, valid = slot_and_valid(shape, 0 if rows_are_keys else 1, seq_len)
    query, _ = slot_and_valid(shape, 1 if rows_are_keys else 0, seq_len)
    mask = jnp.where((key == query) & valid, 0.0, NEVER)
    return jnp.concatenate([mask] * copies, axis=1 if rows_are_keys else 0)


def class_mask(seq_len):
    shape = (GROUP * PITCH, GROUP)
    key, valid = slot_and_valid(shape, 0, seq_len)
    mask = jnp.where((key == lax.broadcasted_iota(jnp.int32, shape, 1)) & valid, 0.0, NEVER)
    return jnp.concatenate([mask] * HEADS, axis=1)


def soft_columns(scores):
    expo = jnp.exp(scores - jnp.max(scores, axis=0, keepdims=True))
    return expo * (1.0 / jnp.sum(expo, axis=0, keepdims=True))


def take_slots(order_ref, all_ref, rows_ref, step, seq_len, slots):
    for s in range(GROUP):
        for c in range(all_ref.shape[0]):
            rows_ref[s * PITCH : s * PITCH + seq_len, c * 128 : (c + 1) * 128] = all_ref[
                c, pl.ds(order_ref[step * GROUP + s], seq_len, stride=slots), :
            ]


def first_rows(ref):
    return jnp.concatenate([ref[s * PITCH : s * PITCH + 1, :] for s in range(GROUP)])


def add_first_rows(ref, values):
    for s in range(GROUP):
        ref[s * PITCH : s * PITCH + 1, :] += values[s : s + 1]


def widen_tokens(tok_ref, all_ref):
    seq_len, slots, width = tok_ref.shape

    @pl.loop(0, seq_len)
    def _(t):
        wide = tok_ref[t].astype(jnp.float32)
        for c in range(all_ref.shape[0]):
            all_ref[c, pl.ds(pl.multiple_of(t * slots, 8), slots), :] = wide[:, c * 128 : (c + 1) * 128]


def ordered_masks(line_first=False):
    if line_first:
        return [(p >> 4) | ((p & 3) << 1) | (((p >> 2) & 3) << 3) for p in range(BLOCKS)]
    return [(p >> 4) | (((p >> 2) & 3) << 1) | ((p & 3) << 3) for p in range(BLOCKS)]


def write_unit(me, keep_ref, send_ref, unit, read, line_first=False):
    for p, mask in enumerate(ordered_masks(line_first)):
        owner = me ^ mask
        ref = keep_ref if p < BLOCKS // 2 else send_ref
        ref[p % (BLOCKS // 2), unit] = read(owner)


def from_square(ref, first=0):
    width = ref.shape[0]

    def read(owner):
        rows = pl.multiple_of((owner // 4) * (width // 8), 16)
        cols = pl.multiple_of((owner % 4) * width, 128)
        return ref[pl.ds(rows, width // 8), pl.ds(cols, width)].astype(jnp.bfloat16)

    return read


def from_tall(ref):
    size = ref.shape[0] // BLOCKS

    def read(owner):
        return ref[pl.ds(pl.multiple_of(owner * size, 16), size), :].astype(jnp.bfloat16)

    return read


def attend_kernel(
    count_ref, order_ref, tok_ref, gains_ref, shifts_ref, w_qkv_ref, b_qkv_ref, w_out_ref, b_out_ref,
    qkv_ref, o_ref, mid_ref,
    all_ref, x_ref, low_ref,
):
    step = pl.program_id(0)
    seq_len, slots, width = tok_ref.shape
    rows = GROUP * PITCH
    chunk = PAIR

    @pl.when(step == 0)
    def _():
        widen_tokens(tok_ref, all_ref)
        x_ref[...] = jnp.zeros_like(x_ref)

    take_slots(order_ref, all_ref, x_ref, step, seq_len, slots)
    for r in range(0, rows, chunk):
        normed, _ = standardize(x_ref[r : r + chunk, :])
        low_ref[r : r + chunk, :] = (normed * norm_row(gains_ref, 0) + norm_row(shifts_ref, 0)).astype(jnp.bfloat16)
    whole = product(low_ref[...], w_qkv_ref[:, : 2 * width])
    part = (whole[:, :width] + qkv_bias(b_qkv_ref, 0, 0, width)).astype(jnp.bfloat16)
    qkv_ref[:, :width] = part * jnp.bfloat16(HD ** -0.5)
    qkv_ref[:, width : 2 * width] = whole[:, width:].astype(jnp.bfloat16)
    part = product(low_ref[...], w_qkv_ref[:, 2 * width :]) + qkv_bias(b_qkv_ref, 0, 2, width)
    qkv_ref[:, 2 * width :] = part.astype(jnp.bfloat16)
    mask = pair_mask(False, seq_len, 2)
    spots = [(r, c) for r in range(0, rows, PAIR) for c in range(0, width, 2 * HD)]
    for b in range(0, len(spots), 24):
        group = spots[b : b + 24]
        scores = [
            against(
                both_heads(qkv_ref[r : r + PAIR, c : c + 2 * HD]), qkv_ref[r : r + PAIR, width + c : width + c + 2 * HD]
            )
            + mask
            for r, c in group
        ]
        probs, scales = [], []
        for score in scores:
            expo = jnp.exp(score - jnp.max(score, axis=1, keepdims=True))
            probs.append(expo.astype(jnp.bfloat16))
            scales.append(1.0 / jnp.sum(expo, axis=1, keepdims=True))
        outs = [
            product(prob, qkv_ref[r : r + PAIR, 2 * width + c : 2 * width + c + 2 * HD]) * scale
            for prob, scale, (r, c) in zip(probs, scales, group)
        ]
        for out, (r, c) in zip(outs, group):
            o_ref[r : r + PAIR, c : c + 2 * HD] = join_heads(out).astype(jnp.bfloat16)
    mixed = product(o_ref[...], w_out_ref[...])
    for r in range(0, rows, chunk):
        part = x_ref[r : r + chunk, :] + mixed[r : r + chunk] + b_out_ref[0:1, :]
        mid_ref[r : r + chunk, :] = part


def mlp_kernel(
    count_ref, gains_ref, shifts_ref, w_fc1_ref, b_fc1_ref, w_fc2_ref, b_fc2_ref, w_up_ref, b_up_ref, mid_ref,
    act_ref, slope_ref, x1_ref, kv_ref, cq_ref, co_ref, ch_ref, cx_ref,
    low_ref, wide_ref, mask_ref,
):
    rows, width = mid_ref.shape
    hidden = w_fc1_ref.shape[1]
    chunk = PAIR
    step = pl.program_id(0)
    here = pl.ds(pl.multiple_of(step * GROUP, GROUP), GROUP)

    @pl.when(step == 0)
    def _():
        mask_ref[...] = class_mask(SEQ_LEN)
        for ref in (cq_ref, co_ref, ch_ref, cx_ref):
            ref[...] = jnp.zeros_like(ref)

    for r in range(0, rows, chunk):
        normed, _ = standardize(mid_ref[r : r + chunk, :])
        low_ref[r : r + chunk, :] = (normed * norm_row(gains_ref, 1) + norm_row(shifts_ref, 1)).astype(jnp.bfloat16)
    for c in range(0, hidden, 256):
        pre = product(low_ref[...], w_fc1_ref[:, c : c + 256])
        for r in range(0, rows, 32):
            act, slope = smooth_both(pre[r : r + 32] + b_fc1_ref[0:1, c : c + 256])
            act_ref[r : r + 32, c : c + 256] = act.astype(jnp.bfloat16)
            slope_ref[r : r + 32, c : c + 256] = slope.astype(jnp.bfloat16)
    mixed = product(act_ref[...], w_fc2_ref[...])
    for r in range(0, rows, chunk):
        part = mid_ref[r : r + chunk, :] + mixed[r : r + chunk] + b_fc2_ref[0:1, :]
        x1_ref[r : r + chunk, :] = part
        normed, _ = standardize(part)
        wide = normed * norm_row(gains_ref, 2) + norm_row(shifts_ref, 2)
        wide_ref[r : r + chunk, :] = wide
        low_ref[r : r + chunk, :] = wide.astype(jnp.bfloat16)
    whole = product(low_ref[...], w_up_ref[:, width:])
    kv_ref[:, :width] = whole[:, :width].astype(jnp.bfloat16)
    kv_ref[:, width:] = (whole[:, width:] + qkv_bias(b_up_ref, 1, 2, width)).astype(jnp.bfloat16)
    cx_ref[here, :] = first_rows(x1_ref)
    first = first_rows(wide_ref).astype(jnp.bfloat16)
    ch_ref[here, :] = first.astype(jnp.float32)
    query = (product(first, w_up_ref[:, :width]) + qkv_bias(b_up_ref, 1, 0, width)).astype(jnp.bfloat16).astype(jnp.float32) * HD ** -0.5
    cq_ref[here, :] = query
    spread = spread_heads(query).astype(jnp.bfloat16)
    probs = soft_columns(against(kv_ref[:, :width], spread) + mask_ref[...]).astype(jnp.bfloat16)
    co_ref[here, :] = gather_heads(inner_rows(probs, kv_ref[:, width:]))


def upper_back_kernel(
    count_ref, gains_ref, shifts_ref, w_up_ref, ch_ref, co_ref, da_ref,
    x1_ref, kv_ref, cq_ref, cg_ref, cres_ref,
    dx_ref, unit_ref, vec_ref,
    acc_ref, wide_ref, dqs_ref, mask_ref, dkv_ref,
):
    step = pl.program_id(0)
    rows, width = x1_ref.shape

    @pl.when(step == 0)
    def _():
        acc_ref[...] = jnp.zeros_like(acc_ref)
        mask_ref[...] = class_mask(SEQ_LEN)
        vec_ref[...] = jnp.zeros_like(vec_ref)

    keys, values = kv_ref[:, :width], kv_ref[:, width:]
    spread = spread_heads(cq_ref[...]).astype(jnp.bfloat16)
    grads = spread_heads(cg_ref[...]).astype(jnp.bfloat16)
    probs = soft_columns(against(keys, spread) + mask_ref[...])
    back = against(values, grads)
    inner = (probs * (back - jnp.sum(back * probs, axis=0, keepdims=True))).astype(jnp.bfloat16)
    dkv_ref[:, :width] = product(inner, spread).astype(jnp.bfloat16)
    dkv_ref[:, width:] = product(probs.astype(jnp.bfloat16), grads).astype(jnp.bfloat16)
    grad_query = (gather_heads(inner_rows(inner, keys)) * HD ** -0.5).astype(jnp.bfloat16)
    @pl.when(step == 0)
    def _():
        dqs_ref[...] = jnp.zeros_like(dqs_ref)

    dqs_ref[pl.ds(pl.multiple_of(step * GROUP, GROUP), GROUP), :] = grad_query.astype(jnp.float32)
    vec_ref[:, 3 * width :] += fold_rows(grad_query.astype(jnp.float32))
    vec_ref[:, :width] += fold_rows(dkv_ref[:, width:].astype(jnp.float32))
    wide_ref[...] = against(dkv_ref[...], w_up_ref[:, width:])
    add_first_rows(wide_ref, against(grad_query, w_up_ref[:, :width]))
    chunk = PAIR
    parts = []
    for r in range(0, rows, chunk):
        normed, rstd = standardize(x1_ref[r : r + chunk, :])
        parts.append((normed * norm_row(gains_ref, 2) + norm_row(shifts_ref, 2)).astype(jnp.bfloat16))
        grad = wide_ref[r : r + chunk, :]
        vec_ref[:, width : 2 * width] += fold_rows(grad * normed)
        vec_ref[:, 2 * width : 3 * width] += fold_rows(grad)
        dx_ref[r : r + chunk, :] = standard_back(grad, normed, rstd, norm_row(gains_ref, 2))
    turned = jnp.concatenate(parts).T
    acc_ref[:, width : 3 * width] += product(turned, dkv_ref[...])
    add_first_rows(dx_ref, cres_ref[...])

    @pl.when(step == count_ref[0] - 1)
    def _():
        acc_ref[:, :width] = inner_rows(
            ch_ref[...].astype(jnp.bfloat16), dqs_ref[...].astype(jnp.bfloat16)
        )
        acc_ref[:, 3 * width :] = inner_rows(co_ref[...].astype(jnp.bfloat16), da_ref[...].astype(jnp.bfloat16))
        unit_ref[...] = acc_ref[...].astype(jnp.bfloat16)
        finish_rows(vec_ref)


def mlp_back_kernel(
    count_ref, me_ref, unit_ref, gains_ref, shifts_ref, w_fc1_ref, w_fc2_ref, dx_ref, mid_ref, act_ref, slope_ref,
    dmid_ref, keep_ref, send_ref, vec_ref, vec1_ref,
    acc1_ref, acc2_ref, dz_ref, big_ref, normed_ref, rstd_ref,
):
    step = pl.program_id(0)
    rows, width = dx_ref.shape
    hidden = act_ref.shape[1]

    @pl.when(step == 0)
    def _():
        acc1_ref[...] = jnp.zeros_like(acc1_ref)
        acc2_ref[...] = jnp.zeros_like(acc2_ref)
        vec_ref[...] = jnp.zeros_like(vec_ref)
        vec1_ref[...] = jnp.zeros_like(vec1_ref)

    low = dx_ref[...].astype(jnp.bfloat16)
    vec_ref[:, :width] += fold_rows(low.astype(jnp.float32))
    low_turned = low.T
    chunk = PAIR
    parts = []
    for r in range(0, rows, chunk):
        normed, rstd = standardize(mid_ref[r : r + chunk, :])
        normed_ref[r : r + chunk, :] = normed
        rstd_ref[r : r + chunk, :] = rstd
        parts.append((normed * norm_row(gains_ref, 1) + norm_row(shifts_ref, 1)).astype(jnp.bfloat16))
    norm_turned = jnp.concatenate(parts).T
    for c in range(0, hidden, 768):
        cols = slice(c, c + 768)
        back = against(low, w_fc2_ref[cols, :])
        for r in range(0, rows, chunk):
            part = (back[r : r + chunk] * slope_ref[r : r + chunk, cols].astype(jnp.float32)).astype(jnp.bfloat16)
            dz_ref[r : r + chunk, cols] = part
            vec1_ref[:, cols] += fold_rows(part.astype(jnp.float32))
        acc1_ref[:, cols] += product(norm_turned, dz_ref[:, cols])
        acc2_ref[:, cols] += product(low_turned, act_ref[:, cols])
    mixed = against(dz_ref[...], w_fc1_ref[...])
    for r in range(0, rows, chunk):
        normed, rstd = normed_ref[r : r + chunk, :], rstd_ref[r : r + chunk, :]
        grad = mixed[r : r + chunk]
        vec_ref[:, width : 2 * width] += fold_rows(grad * normed)
        vec_ref[:, 2 * width : 3 * width] += fold_rows(grad)
        dmid_ref[r : r + chunk, :] = dx_ref[r : r + chunk, :] + standard_back(grad, normed, rstd, norm_row(gains_ref, 1))

    @pl.when(step == count_ref[0] - 1)
    def _():
        finish_rows(vec_ref)
        finish_rows(vec1_ref)
        me = me_ref[0]
        write_unit(me, keep_ref, send_ref, 0, from_square(unit_ref))
        write_unit(me, keep_ref, send_ref, 1, from_square(acc1_ref))
        big_ref[...] = acc2_ref[...].T
        write_unit(me, keep_ref, send_ref, 2, from_tall(big_ref))


def attend_back_kernel(
    count_ref, w_out_ref, dmid_ref, qkv_ref, o_ref,
    dqkv_ref, dwo_ref, vec_ref,
    do_ref,
):
    step = pl.program_id(0)
    rows, width = dmid_ref.shape

    @pl.when(step == 0)
    def _():
        dwo_ref[...] = jnp.zeros_like(dwo_ref)
        vec_ref[...] = jnp.zeros_like(vec_ref)

    low = dmid_ref[...].astype(jnp.bfloat16)
    vec_ref[:, :width] += fold_rows(low.astype(jnp.float32))
    do_ref[...] = against(low, w_out_ref[...]).astype(jnp.bfloat16)
    dwo_ref[...] += product(o_ref[...].T, low)
    mask = pair_mask(True, SEQ_LEN, 2)
    spots = [(r, c) for r in range(0, rows, PAIR) for c in range(0, width, 2 * HD)]
    for b in range(0, len(spots), 6):
        group = spots[b : b + 6]
        queries = [both_heads(qkv_ref[r : r + PAIR, c : c + 2 * HD]) for r, c in group]
        keys = [qkv_ref[r : r + PAIR, width + c : width + c + 2 * HD] for r, c in group]
        values = [qkv_ref[r : r + PAIR, 2 * width + c : 2 * width + c + 2 * HD] for r, c in group]
        grads = [both_heads(do_ref[r : r + PAIR, c : c + 2 * HD]) for r, c in group]
        scores = [against(key, query) + mask for key, query in zip(keys, queries)]
        backs = [against(value, grad) for value, grad in zip(values, grads)]
        probs = [soft_columns(score) for score in scores]
        inners = [
            (prob * (back - jnp.sum(back * prob, axis=0, keepdims=True))).astype(jnp.bfloat16)
            for prob, back in zip(probs, backs)
        ]
        grad_values = [product(prob.astype(jnp.bfloat16), grad) for prob, grad in zip(probs, grads)]
        grad_keys = [product(inner, query) for inner, query in zip(inners, queries)]
        grad_queries = [inner_rows(inner, key) for inner, key in zip(inners, keys)]
        for (r, c), grad in zip(group, grad_values):
            dqkv_ref[r : r + PAIR, 2 * width + c : 2 * width + c + 2 * HD] = grad.astype(jnp.bfloat16)
        for (r, c), grad in zip(group, grad_keys):
            dqkv_ref[r : r + PAIR, width + c : width + c + 2 * HD] = grad.astype(jnp.bfloat16)
        for (r, c), grad in zip(group, grad_queries):
            dqkv_ref[r : r + PAIR, c : c + 2 * HD] = (join_heads(grad) * HD ** -0.5).astype(jnp.bfloat16)
    for j in range(3):
        cols = slice(j * width, (j + 1) * width)
        vec_ref[:, (j + 1) * width : (j + 2) * width] += fold_rows(dqkv_ref[:, cols].astype(jnp.float32))

    @pl.when(step == count_ref[0] - 1)
    def _():
        finish_rows(vec_ref)


def weight_back_kernel(
    count_ref, me_ref, order_ref, tok_ref, gains_ref, shifts_ref, dwo_ref, dqkv_ref,
    keep_ref, send_ref,
    all_ref, x_ref, acc_ref,
):
    step = pl.program_id(0)
    seq_len, slots, width = tok_ref.shape
    rows = GROUP * PITCH

    @pl.when(step == 0)
    def _():
        widen_tokens(tok_ref, all_ref)
        x_ref[...] = jnp.zeros_like(x_ref)
        acc_ref[:, : 3 * width] = jnp.zeros((width, 3 * width), jnp.float32)
        acc_ref[:, 3 * width :] = dwo_ref[...]

    take_slots(order_ref, all_ref, x_ref, step, seq_len, slots)
    chunk = PAIR
    parts = []
    for r in range(0, rows, chunk):
        normed, _ = standardize(x_ref[r : r + chunk, :])
        parts.append((normed * norm_row(gains_ref, 0) + norm_row(shifts_ref, 0)).astype(jnp.bfloat16))
    turned = jnp.concatenate(parts).T
    acc_ref[:, : 3 * width] += product(turned, dqkv_ref[...])

    @pl.when(step == count_ref[0] - 1)
    def _():
        write_unit(me_ref[0], keep_ref, send_ref, 0, from_square(acc_ref))


def input_back_kernel(
    count_ref, order_ref, tok_ref, gains_ref, w_qkv_ref, vec1_ref, vec2_ref, vec3_ref, vec4_ref, vec5_ref, dmid_ref, dqkv_ref,
    dtok_ref, all_vec_ref,
    all_ref, out_ref, x_ref, vec_ref,
):
    step = pl.program_id(0)
    seq_len, slots, width = tok_ref.shape
    rows = GROUP * PITCH

    @pl.when(step == 0)
    def _():
        widen_tokens(tok_ref, all_ref)
        x_ref[...] = jnp.zeros_like(x_ref)
        out_ref[...] = jnp.zeros_like(out_ref)
        vec_ref[...] = jnp.zeros_like(vec_ref)

    take_slots(order_ref, all_ref, x_ref, step, seq_len, slots)
    chunk = PAIR
    mixed = against(dqkv_ref[...], w_qkv_ref[...])
    for r in range(0, rows, chunk):
        normed, rstd = standardize(x_ref[r : r + chunk, :])
        grad = mixed[r : r + chunk]
        vec_ref[:, :width] += fold_rows(grad * normed)
        vec_ref[:, width:] += fold_rows(grad)
        part = dmid_ref[r : r + chunk, :] + standard_back(grad, normed, rstd, norm_row(gains_ref, 0))
        for s in range(chunk // PITCH):
            for t in range(all_ref.shape[0]):
                out_ref[t, pl.ds(order_ref[step * GROUP + r // PITCH + s], seq_len, stride=slots), :] = part[
                    s * PITCH : s * PITCH + seq_len, t * 128 : (t + 1) * 128
                ]

    @pl.when(step == count_ref[0] - 1)
    def _():
        finish_rows(vec_ref)
        start = 0
        for ref in (vec_ref, vec1_ref, vec2_ref, vec3_ref, vec4_ref, vec5_ref):
            size = ref.shape[1]
            all_vec_ref[:, start : start + size] = ref[0:1, :]
            start += size
        for t in range(out_ref.shape[0]):
            dtok_ref[:, t * 128 : (t + 1) * 128] = out_ref[t]


def place_of(mask):
    return ((mask & 1) << 4) | (((mask >> 1) & 3) << 2) | ((mask >> 3) & 3)


def read_place(own_ref, got_ref, place, unit):
    inner = place & (BLOCKS // 2 - 1)
    block = jnp.where(place < BLOCKS // 2, own_ref[inner, unit], got_ref[inner, unit])
    return block.astype(jnp.float32)


def unpack_kernel(
    me_ref, own_ref, got_ref,
    qkv_ref, out_ref, fc1_ref, fc2_ref,
):
    step = pl.program_id(0)
    width, size = own_ref.shape[3], own_ref.shape[2]
    count = out_ref.shape[0] // size
    for r, c in [(r, c) for r in range(count) for c in range(4)]:
        place = place_of(((step * count + r) * 4 + c) ^ me_ref[0])
        cols, rows = slice(c * width, (c + 1) * width), slice(r * size, (r + 1) * size)
        tall = slice((r * 4 + c) * size, (r * 4 + c + 1) * size)
        upper = read_place(own_ref, got_ref, place, 0)
        if c < 3:
            qkv_ref[rows, cols] = upper
        else:
            out_ref[rows, :] = upper
        fc1_ref[0, rows, cols] = read_place(own_ref, got_ref, place, 1)
        fc2_ref[0, tall, :] = read_place(own_ref, got_ref, place, 2)
        fc1_ref[1, rows, cols] = read_place(own_ref, got_ref, place, 3)
        fc2_ref[1, tall, :] = read_place(own_ref, got_ref, place, 4)


def unpack_first_kernel(
    me_ref, own_ref, got_ref, vec_ref, qkv_in_ref, out_in_ref,
    qkv_ref, out_ref, gains_ref, shifts_ref, bqv_ref, bout_ref, bfc1_ref, bfc2_ref,
):
    step = pl.program_id(0)
    width = own_ref.shape[3]
    size = own_ref.shape[2]
    count = out_ref.shape[0] // size
    for r, c in [(r, c) for r in range(count) for c in range(4)]:
        block = read_place(own_ref, got_ref, place_of(((step * count + r) * 4 + c) ^ me_ref[0]), 0)
        rows = slice(r * size, (r + 1) * size)
        if c < 3:
            qkv_ref[rows, c * width : (c + 1) * width] = block
        else:
            out_ref[rows, :] = block

    @pl.when(step == 0)
    def _():
        hidden = bfc1_ref.shape[1]
        row_b, row_c, row_h = 2, 5, 9
        row_hidden = vec_ref.shape[1] // width - hidden // width
        row_a = row_hidden - 4

        def put(ref, place, row, count=1):
            ref[place] = vec_ref[:, row * width : (row + count) * width]

        for i, row in enumerate((0, row_b + 1, row_c + 1, row_h)):
            put(gains_ref, (i // 2, slice(i % 2, i % 2 + 1)), row)
            put(shifts_ref, (i // 2, slice(i % 2, i % 2 + 1)), row + 1)
        put(bqv_ref, (slice(0, 1), slice(0, width)), row_a + 1)
        put(bqv_ref, (slice(0, 1), slice(width, 2 * width)), row_a + 3)
        put(bqv_ref, (slice(1, 2), slice(0, width)), row_c + 3)
        put(bqv_ref, (slice(1, 2), slice(width, 2 * width)), row_c)
        put(bout_ref, slice(0, 1), row_a)
        put(bout_ref, slice(1, 2), row_h + 2)
        put(bfc1_ref, slice(0, 1), row_hidden, hidden // width)
        put(bfc1_ref, slice(1, 2), row_h + 6, hidden // width)
        put(bfc2_ref, slice(0, 1), row_b)
        put(bfc2_ref, slice(1, 2), row_h + 3)


def prepare_kernel(
    device_ref, counts_ref, proto_ref, teacher_ref,
    info_ref, live_ref, image_ref, unit_ref, turned_ref, inv_ref, teach_ref, expo_ref,
):
    slots = live_ref.shape[0]
    images_here = slots // MOST_CROPS
    counts = [counts_ref[device_ref[0] * images_here + i] for i in range(images_here)]
    total = functools.reduce(lambda a, b: a + b, counts)
    place = lax.broadcasted_iota(jnp.int32, (slots, 1), 0)
    live_ref[...] = (place < total).astype(jnp.float32)
    image = jnp.zeros((slots, 1), jnp.float32)
    live_before, dead_before = 0, total
    for i, amount in enumerate(counts):
        dead = MOST_CROPS - amount
        for k in range(MOST_CROPS):
            at = jnp.where(k < amount, live_before + k, dead_before + k - amount)
            info_ref[at + 2] = i * MOST_CROPS + k
        live_spot = (place >= live_before) & (place < live_before + amount)
        dead_spot = (place >= dead_before) & (place < dead_before + dead)
        image = jnp.where(live_spot | dead_spot, float(i), image)
        live_before = live_before + amount
        dead_before = dead_before + dead
    image_ref[...] = image
    info_ref[0] = (total + GROUP - 1) // GROUP
    info_ref[1] = device_ref[0] & (BLOCKS - 1)
    proto = proto_ref[...].astype(jnp.float32)
    inv = lax.rsqrt(jnp.sum(proto * proto, axis=0, keepdims=True) + EPS)
    inv_ref[...] = inv
    unit = (proto * inv).astype(jnp.bfloat16)
    unit_ref[...] = unit
    turned_ref[...] = unit.T
    bottle = proto.shape[0]
    images = teacher_ref.shape[0]
    for r in range(0, images, 64):
        expo = jnp.exp(teacher_ref[r : r + 64, :] * (1.0 / TEACHER_TEMP))
        expo_ref[r : r + 64, :] = expo
        teach_ref[r : r + 64, :bottle] = against(expo.astype(jnp.bfloat16), unit)
        teach_ref[r : r + 64, bottle:] = jnp.broadcast_to(jnp.sum(expo, axis=1, keepdims=True), (64, 128))


def repeat_rows(values, image):
    out = jnp.zeros((image.shape[0], values.shape[1]), values.dtype)
    for i in range(values.shape[0]):
        out = jnp.where(image == i, values[i : i + 1], out)
    return out


def three_parts(values):
    high = values.astype(jnp.bfloat16).astype(jnp.float32)
    middle = (values - high).astype(jnp.bfloat16).astype(jnp.float32)
    return [high, middle, values - high - middle]


def head_kernel(
    scale, own_columns, me_ref, live_ref, image_ref, teach_ref, co_ref, cx_ref, gains_ref, shifts_ref, final_ref,
    w_out_ref, b_out_ref, far_fc1_ref, b_fc1_ref, far_fc2_ref, b_fc2_ref,
    far_w1_ref, b1_ref, far_w2_ref, b2_ref, far_w3_ref, b3_ref, far_unit_ref,
    cg_ref, cres_ref, da_ref, common_ref, feats_ref, share0_ref, share1_ref, share2_ref, share3_ref, keep_ref, send_ref, vec_ref,
    act_ref, slope_ref, slope1_ref, slope2_ref, one_ref, two_ref, back_ref, up1_ref, up2_ref,
    w_fc1_ref, w_fc2_ref, w1_ref, w2_ref, w3_ref, unit_ref, done_ref,
):
    far = (far_fc1_ref.at[1], far_fc2_ref.at[1], far_w1_ref, far_w2_ref, far_w3_ref, far_unit_ref)
    near = (w_fc1_ref, w_fc2_ref, w1_ref, w2_ref, w3_ref, unit_ref)
    copies = [pltpu.make_async_copy(a, b, done_ref.at[i]) for i, (a, b) in enumerate(zip(far, near))]
    for copy in copies:
        copy.start()
    width = cx_ref.shape[1]
    hidden = w_fc1_ref.shape[1]
    hid, bottle = w3_ref.shape
    low = jnp.bfloat16
    middle = cx_ref[...] + product(co_ref[...].astype(low), w_out_ref[...]) + b_out_ref[1:2, :]
    normed_d, rstd_d = standardize(middle)
    low_d = (normed_d * norm_row(gains_ref, 3) + norm_row(shifts_ref, 3)).astype(low)
    copies[0].wait()
    for c in range(0, hidden, 256):
        cols = slice(c, c + 256)
        act, slope = smooth_both(product(low_d, w_fc1_ref[:, cols]) + b_fc1_ref[1:2, cols])
        act_ref[:, cols] = act.astype(low)
        slope_ref[:, cols] = slope
    def share(kind, c, values):
        for u in range(256 // (4 * own_columns)):
            start = kind * (hid // 4) + c // 4 + u * own_columns
            here = slice(start, start + own_columns)
            parts = [values[:, (u * 4 + j) * own_columns : (u * 4 + j + 1) * own_columns] for j in range(4)]
            for bit in (0, 1):
                flip = (me_ref[0] >> bit) & 1 == 1
                parts = [jnp.where(flip, parts[j ^ (1 << bit)], parts[j]) for j in range(4)]
            for ref, part in zip((share0_ref, share1_ref, share2_ref, share3_ref), parts):
                ref[:, here] = part

    copies[1].wait()
    out = middle + product(act_ref[...], w_fc2_ref[...]) + b_fc2_ref[1:2, :]
    normed_f, rstd_f = standardize(out)
    low_f = (normed_f * final_ref[0:1, :] + final_ref[1:2, :]).astype(low)
    common_ref[:, hid : hid + width] = low_f
    copies[2].wait()
    for c in range(0, hid, 256):
        cols = slice(c, c + 256)
        act, slope = smooth_both(product(low_f, w1_ref[:, cols]) + b1_ref[:, cols])
        one_ref[:, cols] = act.astype(low)
        share(0, c, act.astype(low))
        slope1_ref[:, cols] = slope
    first = one_ref[...]
    copies[3].wait()
    for c in range(0, hid, 256):
        cols = slice(c, c + 256)
        act, slope = smooth_both(product(first, w2_ref[:, cols]) + b2_ref[:, cols])
        two_ref[:, cols] = act.astype(low)
        share(1, c, act.astype(low))
        slope2_ref[:, cols] = slope
    copies[4].wait()
    embed = product(two_ref[...], w3_ref[...]) + b3_ref[...]
    inv = lax.rsqrt(jnp.sum(embed * embed, axis=1, keepdims=True) + EPS)
    feats = (embed * inv).astype(low)
    slots = feats.shape[0]
    total = jnp.zeros((slots, 1), jnp.float32)
    student = jnp.zeros((slots, bottle), jnp.float32)
    total_protos = unit_ref.shape[0]
    copies[5].wait()
    size = 512

    def some(i, carry):
        total, student = carry
        part = unit_ref[pl.ds(pl.multiple_of(i * size, size), size), :]
        expo = jnp.exp(against(feats, part) * (1.0 / STUDENT_TEMP) - SHIFT)
        return (
            total + jnp.sum(expo, axis=1, keepdims=True),
            student + product(expo.astype(low), part),
        )

    total, student = lax.fori_loop(0, total_protos // size, some, (total, student), unroll=4)
    teach_total = teach_ref[:, bottle : bottle + 128]
    teach = repeat_rows(teach_ref[:, :bottle] * (1.0 / teach_total[:, :1]), image_ref[...])
    grad_feat = live_ref[...] * (student * (1.0 / total) - teach) * scale
    logs = [live_ref[...]] + three_parts(SHIFT + jnp.log(total)) + three_parts(repeat_rows(jnp.log(teach_total), image_ref[...])[:, :1]) + [image_ref[...]]
    lane = lax.broadcasted_iota(jnp.int32, (slots, 128), 1)
    extra = jnp.zeros((slots, 128), jnp.float32)
    for i, part in enumerate(logs):
        extra = jnp.where(lane == i, part, extra)
    mark = hid + width + bottle
    feats_ref[:, :bottle] = feats
    feats_ref[:, bottle:] = extra.astype(low)
    grad_embed = inv * grad_feat - embed * (inv * inv * inv) * jnp.sum(embed * grad_feat, axis=1, keepdims=True)
    grad_embed = grad_embed.astype(low)
    common_ref[:, hid + width : mark] = grad_embed
    vec_ref[...] = jnp.zeros_like(vec_ref)
    vec_ref[:, 6 * width + hidden : 6 * width + hidden + bottle] = fold_rows(grad_embed.astype(jnp.float32))
    for c in range(0, hid, 256):
        cols = slice(c, c + 256)
        grad = (slope2_ref[:, cols] * against(grad_embed, w3_ref[cols, :])).astype(low)
        common_ref[:, cols] = grad
        vec_ref[:, 7 * width + hidden + hid + c : 7 * width + hidden + hid + c + 256] = fold_rows(grad.astype(jnp.float32))
    grad_two = common_ref[:, :hid]
    for c in range(0, hid, 256):
        cols = slice(c, c + 256)
        grad = (slope1_ref[:, cols] * against(grad_two, w2_ref[cols, :])).astype(low)
        back_ref[:, cols] = grad
        vec_ref[:, 7 * width + hidden + c : 7 * width + hidden + c + 256] = fold_rows(grad.astype(jnp.float32))
        share(2, c, grad)
    grad = against(back_ref[...], w1_ref[...])
    vec_ref[:, 4 * width : 5 * width] = fold_rows(grad * normed_f)
    vec_ref[:, 5 * width : 6 * width] = fold_rows(grad)
    grad_class = standard_back(grad, normed_f, rstd_f, final_ref[0:1, :])
    grad_low = grad_class.astype(low)
    vec_ref[:, 3 * width : 4 * width] = fold_rows(grad_low.astype(jnp.float32))
    up2_ref[...] = inner_rows(act_ref[...], grad_low).astype(low)
    for c in range(0, hidden, 256):
        cols = slice(c, c + 256)
        grad = (slope_ref[:, cols] * against(grad_low, w_fc2_ref[cols, :])).astype(low)
        act_ref[:, cols] = grad
        vec_ref[:, 6 * width + c : 6 * width + c + 256] = fold_rows(grad.astype(jnp.float32))
    grad_pre = act_ref[...]
    up1_ref[...] = inner_rows(low_d, grad_pre).astype(low)
    grad = against(grad_pre, w_fc1_ref[...])
    vec_ref[:, :width] = fold_rows(grad * normed_d)
    vec_ref[:, width : 2 * width] = fold_rows(grad)
    grad_middle = grad_class + standard_back(grad, normed_d, rstd_d, norm_row(gains_ref, 3))
    cres_ref[...] = grad_middle
    grad_low = grad_middle.astype(low)
    da_ref[...] = grad_low.astype(jnp.float32)
    vec_ref[:, 2 * width : 3 * width] = fold_rows(grad_low.astype(jnp.float32))
    cg_ref[...] = against(grad_low, w_out_ref[...]).astype(low).astype(jnp.float32)
    finish_rows(vec_ref)
    write_unit(me_ref[0], keep_ref, send_ref, 0, from_square(up1_ref), True)
    write_unit(me_ref[0], keep_ref, send_ref, 1, from_tall(up2_ref), True)


def head_sum_kernel(
    width, info_ref, common0_ref, common1_ref, common2_ref, common3_ref, share0_ref, share1_ref, share2_ref, share3_ref,
    kept_ref, sent_ref,
    parts_ref,
):
    quarter = share0_ref.shape[1] // 3
    full = quarter * 4
    share = jnp.concatenate([ref[...] for ref in (share0_ref, share1_ref, share2_ref, share3_ref)])
    common = jnp.concatenate([ref[...] for ref in (common0_ref, common1_ref, common2_ref, common3_ref)])
    low = jnp.bfloat16
    parts = [share[:, i * quarter : (i + 1) * quarter].T for i in range(3)]
    parts_ref[:, :width] = product(parts[2], common[:, full : full + width])
    for c in range(0, full, 512):
        parts_ref[:, width + c : width + c + 512] = product(parts[0], common[:, c : c + 512])
    mark = parts_ref.shape[1]
    parts_ref[:, width + full :] = product(parts[1], common[:, width + full : mark])
    size = kept_ref.shape[1]
    spot = (info_ref[1] >> 2) & 1
    for z in range(kept_ref.shape[0]):
        for ref, digit in ((kept_ref, spot), (sent_ref, 1 - spot)):
            ref[z] = parts_ref[pl.ds(pl.multiple_of((2 * z + digit) * size, 8), size), :].astype(jnp.bfloat16)


def proto_back_kernel(
    scale, owner_ref, unit_ref, proto_ref, inv_ref, thawed_ref, expo_ref, feats_ref,
    grad_ref,
    acc_ref, raw_ref,
):
    step = pl.program_id(0)
    bottle = unit_ref.shape[0]

    @pl.when(step == 0)
    def _():
        acc_ref[...] = jnp.zeros_like(acc_ref)

    rows = feats_ref.shape[0]
    slots = rows // 8
    images = slots // MOST_CROPS
    for l in range(8):
        here = slice(l * slots, (l + 1) * slots)
        extra = feats_ref[here, bottle:].astype(jnp.float32)
        lane = lax.broadcasted_iota(jnp.int32, extra.shape, 1)
        pick = lambda a, b: jnp.sum(jnp.where((lane >= a) & (lane < b), extra, 0.0), axis=1, keepdims=True)
        logits = product(feats_ref[here, :bottle], unit_ref[...]) * (1.0 / STUDENT_TEMP)
        target = repeat_rows(expo_ref[pl.ds(pl.multiple_of(owner_ref[step * 8 + l] * images, 8), images), :], pick(7, 8))
        raw = pick(0, 1) * (jnp.exp(logits - pick(1, 4)) - target * jnp.exp(-pick(4, 7))) * scale
        raw_ref[here, :] = raw.astype(jnp.bfloat16)
    acc_ref[...] += inner_rows(feats_ref[:, :bottle], raw_ref[...])

    @pl.when(step == pl.num_programs(0) - 1)
    def _():
        proto = proto_ref[...].astype(jnp.float32)
        inv = inv_ref[...]
        grad = acc_ref[...]
        inner = jnp.sum(proto * grad, axis=0, keepdims=True)
        grad_ref[...] = (inv * grad - proto * (inv * inv * inv * inner)) * thawed_ref[...]


def whole(array):
    return pl.BlockSpec(array.shape, lambda *i: (0,) * len(array.shape))


class Layer:
    def __init__(self, array, layer):
        self.array, self.layer = array, layer


class Far:
    def __init__(self, array):
        self.array = array


def spec_of(item):
    if isinstance(item, Far):
        return pl.BlockSpec(memory_space=pl.ANY)
    if isinstance(item, Layer):
        shape = item.array.shape[1:]
        return pl.BlockSpec((None,) + shape, lambda *i: (item.layer,) + (0,) * len(shape))
    return whole(item)


def array_of(item):
    return item.array if isinstance(item, (Layer, Far)) else item


class Shifted:
    def __init__(self, ref, first):
        self.ref, self.first = ref, first

    def __getitem__(self, index):
        return self.ref[self.first + index]


def run_kernel(body, steps, scalars, whole_in, step_in, outs, scratch, micros, info=None, limit=32):
    count = info
    if info is not None:
        inner, firsts = body, scalars
        scalars = [info]

        def body(info_ref, *refs):
            @pl.when(pl.program_id(0) < info_ref[0])
            def _():
                inner(info_ref, *[Shifted(info_ref, first) for first in firsts], *refs)

    def by_step(rows, width):
        if count is None:
            return pl.BlockSpec((rows, width), lambda i, *s: (i, 0))
        return pl.BlockSpec((rows, width), lambda i, c, *s: (jnp.minimum(i, c[0] - 1), 0))

    return pl.pallas_call(
        body,
        grid_spec=pltpu.PrefetchScalarGridSpec(
            num_scalar_prefetch=len(scalars),
            grid=(steps,),
            in_specs=[spec_of(a) for a in whole_in] + [by_step(rows, a.shape[1]) for a, rows in step_in],
            out_specs=[
                by_step(rows, shape[1])
                if rows
                else pl.BlockSpec(memory_space=pltpu.SMEM)
                if rows is None
                else pl.BlockSpec(shape, lambda *i, k=len(shape): (0,) * k)
                for shape, dtype, rows in outs
            ],
            scratch_shapes=scratch,
        ),
        out_shape=[jax.ShapeDtypeStruct(shape, dtype) for shape, dtype, rows in outs],
        compiler_params=pltpu.CompilerParams(
            dimension_semantics=("arbitrary",), vmem_limit_bytes=limit * 1024 * 1024
        ),
        cost_estimate=pl.CostEstimate(flops=micros * 10**9, bytes_accessed=2**20, transcendentals=0),
    )(*scalars, *[array_of(a) for a in whole_in], *[a for a, rows in step_in])


def axis_bits(n):
    bits = n.bit_length() - 1
    assert n == 1 << bits
    return bits


def swap(values, mask, n):
    return lax.ppermute(values, "dp", [(i, i ^ mask) for i in range(n)])


def group_masks(group):
    return [k << group[0] for k in range(1 << len(group))]


def own_digit(group):
    return (lax.axis_index("dp") >> group[0]) & ((1 << len(group)) - 1)


def upper_groups(n, first):
    bits = list(range(first, axis_bits(n)))
    return [bits[i : i + 2] for i in range(0, len(bits), 2)][::-1]


def gather_loose(block, group, n):
    return jnp.stack([swap(block, mask, n) if mask else block for mask in group_masks(group)])


def tree_sum(parts):
    while len(parts) > 1:
        parts = [parts[i] + parts[i + 1] for i in range(0, len(parts), 2)]
    return parts[0]


def scatter_send(parts, group):
    size = 1 << len(group)
    parts = parts.reshape((size, parts.shape[0] // size) + parts.shape[1:])
    digit = own_digit(group)
    return [lax.dynamic_index_in_dim(parts, digit ^ k, 0, keepdims=False) for k in range(size)]


def double(mine, got):
    return jnp.concatenate([mine, got])


def pick_send(parts, axis, group):
    digit = own_digit(group)
    return [lax.dynamic_index_in_dim(parts, digit ^ k, axis, keepdims=False) for k in range(2)]


def swap_parts(parts, group, n):
    return [swap(part, mask, n) if mask else part for part, mask in zip(parts, group_masks(group))]


def scatter_stage(parts, group, n):
    got = swap_parts(scatter_send(parts, group), group, n)
    return tree_sum([part.astype(jnp.float32) for part in got]).astype(parts.dtype)


def sum_stage(values, group, n):
    return tree_sum(swap_parts([values] * (1 << len(group)), group, n))


def fold_send(parts, group):
    size = 1 << len(group)
    parts = parts.reshape((size, parts.shape[0] // size) + parts.shape[1:])
    return [parts[k] for k in range(size)]


def fold_sum(parts):
    return tree_sum([part.astype(jnp.float32) for part in parts]).astype(parts[0].dtype)


def unfold_stage(parts, group, n):
    return jnp.concatenate([swap(parts, mask, n) if mask else parts for mask in group_masks(group)])


def extra_sum(values, n):
    for bit in range(5, axis_bits(n)):
        values = values + swap(values, 1 << bit, n)
    return values


def together(*values):
    return lax.optimization_barrier(values)


CORE, PLANE, LINE = [0], [1, 2], [3, 4]
UNPACK = 4


def per_device(
    tokens,
    layer_gains,
    layer_shifts,
    w_qkv,
    b_qv,
    w_out,
    b_out,
    w_fc1,
    b_fc1,
    w_fc2,
    b_fc2,
    final_gain,
    final_shift,
    head_w1,
    head_b1,
    head_w2,
    head_b2,
    head_w3,
    head_b3,
    prototypes,
    crop_counts,
    teacher_logits,
    first_epoch,
):
    low, wide = jnp.bfloat16, jnp.float32
    slot_count, seq_len, width = tokens.shape
    n = lax.axis_size("dp")
    device = lax.axis_index("dp")
    me = (device & (BLOCKS - 1)).reshape(1)
    bottle = prototypes.shape[0]
    hidden = w_fc1.shape[2]
    hid = head_w2.shape[0]
    rows = GROUP * PITCH
    steps = slot_count // GROUP
    padded = slot_count * PITCH
    row_count = slot_count * seq_len
    groups = upper_groups(n, 3)

    scale = 1.0 / (STUDENT_TEMP * n)
    images, protos = teacher_logits.shape
    info, own_live, image, unit_low, unit_turned, col_inv, teach_sum, teach_expo = run_kernel(
        prepare_kernel,
        1,
        [device.reshape(1), crop_counts],
        [prototypes, teacher_logits],
        [],
        [
            ((slot_count + 2,), jnp.int32, None),
            ((slot_count, 1), wide, 0),
            ((slot_count, 1), wide, 0),
            ((bottle, protos), low, 0),
            ((protos, bottle), low, 0),
            ((1, protos), wide, 0),
            ((images, bottle + 128), wide, 0),
            ((images, protos), wide, 0),
        ],
        [],
        4,
        limit=56,
    )
    unit_all = lax.all_gather(unit_turned, "dp", axis=0, tiled=True)
    teach_sum = teach_sum.reshape(n, -1, bottle + 128)
    for group in groups[:-1]:
        teach_sum = scatter_stage(teach_sum, group, n)

    gains, shifts = layer_gains, layer_shifts
    turned_tokens = tokens.transpose(1, 0, 2)
    all_rows = pltpu.VMEM((width // 128, row_count, 128), wide)
    teach_parts = scatter_send(teach_sum, groups[-1])
    turned_tokens, *teach_parts = together(turned_tokens, *teach_parts)
    teach_parts = swap_parts(teach_parts, groups[-1], n)
    qkv_a, attn_a, middle_a = run_kernel(
        attend_kernel,
        steps,
        [2],
        [turned_tokens, gains, shifts, Layer(w_qkv, 0), b_qv, Layer(w_out, 0), b_out],
        [],
        [((padded, 3 * width), low, rows), ((padded, width), low, rows), ((padded, width), wide, rows)],
        [all_rows, pltpu.VMEM((rows, width), wide), pltpu.VMEM((rows, width), low)],
        35,
        info,
        limit=56,
    )
    middle_a, *teach_parts = together(middle_a, *teach_parts)
    teach_sum = tree_sum(teach_parts)
    teach_parts = scatter_send(teach_sum, PLANE)
    middle_a, *teach_parts = together(middle_a, *teach_parts)
    teach_parts = swap_parts(teach_parts, PLANE, n)
    act_a, slope_a, lower_out, kv_c, query_c, attn_c, first_low, first_in = run_kernel(
        mlp_kernel,
        steps,
        [],
        [gains, shifts, Layer(w_fc1, 0), b_fc1, Layer(w_fc2, 0), b_fc2, Layer(w_qkv, 1), b_qv],
        [(middle_a, rows)],
        [
            ((padded, hidden), low, rows),
            ((padded, hidden), low, rows),
            ((padded, width), wide, rows),
            ((padded, 2 * width), low, rows),
            ((slot_count, width), wide, 0),
            ((slot_count, width), wide, 0),
            ((slot_count, width), wide, 0),
            ((slot_count, width), wide, 0),
        ],
        [pltpu.VMEM((rows, width), low), pltpu.VMEM((rows, width), wide), pltpu.VMEM((rows, HEADS * GROUP), wide)],
        40,
        info,
        limit=56,
    )
    first_in, *teach_parts = together(first_in, *teach_parts)
    teach_sum = scatter_stage(tree_sum(teach_parts), CORE, n)[0]

    finals = jnp.stack([final_gain, final_shift])
    vec_width = -(-(7 * width + hidden + 2 * hid) // width) * width
    grad_attended, grad_middle_c, grad_attn, common, feats, *shares, keep_u, send_u, vec_h = run_kernel(
        functools.partial(head_kernel, scale, hid // n),
        1,
        [me],
        [own_live, image, teach_sum, attn_c, first_in, gains, shifts, finals, Layer(w_out, 1), b_out, Far(w_fc1), b_fc1, Far(w_fc2), b_fc2,
         Far(head_w1), head_b1[None], Far(head_w2), head_b2[None], Far(head_w3), head_b3[None], Far(unit_all)],
        [],
        [
            ((slot_count, width), wide, 0),
            ((slot_count, width), wide, 0),
            ((slot_count, width), wide, 0),
            ((slot_count, hid + width + bottle), low, 0),
            ((slot_count, bottle + 128), low, 0),
            *[((slot_count, hid // 4 * 3), low, 0)] * 4,
            ((BLOCKS // 2, 2, width // 8, width), low, 0),
            ((BLOCKS // 2, 2, width // 8, width), low, 0),
            ((8, vec_width), wide, 0),
        ],
        [
            pltpu.VMEM((slot_count, hidden), low),
            pltpu.VMEM((slot_count, hidden), wide),
            pltpu.VMEM((slot_count, hid), wide),
            pltpu.VMEM((slot_count, hid), wide),
            pltpu.VMEM((slot_count, hid), low),
            pltpu.VMEM((slot_count, hid), low),
            pltpu.VMEM((slot_count, hid), low),
            pltpu.VMEM((width, hidden), low),
            pltpu.VMEM((hidden, width), low),
        ]
        + [pltpu.VMEM(v.shape, low) for v in (w_fc1[0], w_fc2[0], head_w1, head_w2, head_w3, unit_all)]
        + [pltpu.SemaphoreType.DMA((6,))],
        20,
        limit=min(56, 40 + unit_all.size // 2**19),
    )
    common_got = swap(common, 1, n)
    share0, share2 = shares[0], shares[2]
    share1, share3 = swap(shares[1], 1, n), swap(shares[3], 1, n)
    bits = list(range(5, axis_bits(n))) + [4, 3, 1, 2, 0]
    masks = [0]
    for bit in bits:
        masks = masks + [mask | (1 << bit) for mask in masks]
    for bit in bits[:-5]:
        feats = double(feats, swap(feats, 1 << bit, n))
    grad_attended, common, share2, share3, send_u, feats = together(grad_attended, common, share2, share3, send_u, feats)
    got_u = swap(send_u, 1, n)
    feats_got = swap(feats, 16, n)
    common2, share2, share3 = (swap(v, 2, n) for v in (common, share2, share3))
    grad_lower_out, unit_u, vec_c = run_kernel(
        upper_back_kernel,
        steps,
        [],
        [gains, shifts, Layer(w_qkv, 1), first_low, attn_c, grad_attn],
        [(lower_out, rows), (kv_c, rows), (query_c, GROUP), (grad_attended, GROUP), (grad_middle_c, GROUP)],
        [
            ((padded, width), wide, rows),
            ((width, 4 * width), low, 0),
            ((8, 4 * width), wide, 0),
        ],
        [
            pltpu.VMEM((width, 4 * width), wide),
            pltpu.VMEM((rows, width), wide),
            pltpu.VMEM((slot_count, width), wide),
            pltpu.VMEM((rows, HEADS * GROUP), wide),
            pltpu.VMEM((rows, 2 * width), low),
        ],
        20,
        info,
    )
    grad_lower_out, common2, share2, share3, got_u, feats_got = together(
        grad_lower_out, common2, share2, share3, got_u, feats_got
    )
    feats = double(feats, feats_got)
    common3 = swap(common2, 1, n)
    parts_u = fold_send(keep_u + got_u, LINE)
    head_keep, head_send = run_kernel(
        functools.partial(head_sum_kernel, width),
        1,
        [info],
        [common, common_got, common2, common3, share0, share1, share2, share3],
        [],
        [((n // 8, hid // n, width + hid + bottle), low, 0)] * 2,
        [pltpu.VMEM((hid // 4, width + hid + bottle), wide)],
        6,
    )
    grad_lower_out, head_send, feats, *parts_u = together(grad_lower_out, head_send, feats, *parts_u)
    head_got, feats_got = swap(head_send, 4, n), swap(feats, 8, n)
    parts_u = swap_parts(parts_u, LINE, n)
    grad_middle_a, keep_m, send_m, vec_b, vec_hidden = run_kernel(
        mlp_back_kernel,
        steps,
        [1],
        [unit_u, gains, shifts, Layer(w_fc1, 0), Layer(w_fc2, 0)],
        [(grad_lower_out, rows), (middle_a, rows), (act_a, rows), (slope_a, rows)],
        [
            ((padded, width), wide, rows),
            ((BLOCKS // 2, 3, width // 8, width), low, 0),
            ((BLOCKS // 2, 3, width // 8, width), low, 0),
            ((8, 3 * width), wide, 0),
            ((8, hidden), wide, 0),
        ],
        [
            pltpu.VMEM((width, hidden), wide),
            pltpu.VMEM((width, hidden), wide),
            pltpu.VMEM((rows, hidden), low),
            pltpu.VMEM((hidden, width), wide),
            pltpu.VMEM((rows, width), wide),
            pltpu.VMEM((rows, 1), wide),
        ],
        40,
        info,
        limit=44,
    )
    grad_middle_a, head_got, feats_got, send_m, *parts_u = together(grad_middle_a, head_got, feats_got, send_m, *parts_u)
    feats = double(feats, feats_got)
    head_parts = head_keep + head_got
    for bit in range(axis_bits(n) - 1, 4, -1):
        head_parts = scatter_stage(head_parts, [bit], n)
    head_keep, head_send = pick_send(head_parts.reshape((2, 2) + head_parts.shape[1:]), 1, [3])
    parts_m = [
        jnp.concatenate([a.reshape((-1,) + a.shape[2:]), b[0]])
        for a, b in zip(fold_send(keep_m + swap(send_m, 1, n), PLANE), fold_send(fold_sum(parts_u), PLANE))
    ]
    grad_middle_a, head_send, *parts_m = together(grad_middle_a, head_send, *parts_m)
    head_got = swap(head_send, 8, n)
    parts_m = swap_parts(parts_m, PLANE, n)
    grad_qkv, grad_wo, vec_a = run_kernel(
        attend_back_kernel,
        steps,
        [],
        [Layer(w_out, 0)],
        [(grad_middle_a, rows), (qkv_a, rows), (attn_a, rows)],
        [((padded, 3 * width), low, rows), ((width, width), wide, 0), ((8, 4 * width), wide, 0)],
        [pltpu.VMEM((rows, width), low)],
        40,
        info,
    )
    grad_qkv, head_got, *parts_m = together(grad_qkv, head_got, *parts_m)
    head_keep, head_send = pick_send(head_keep + head_got, 0, [4])
    sum_m = fold_sum(parts_m)
    sum_u = sum_m[None, 12:]
    parts_m = fold_send(sum_m[:12].reshape((4, 3) + sum_m.shape[1:]), LINE)
    grad_qkv, head_send, feats, *parts_m = together(grad_qkv, head_send, feats, *parts_m)
    feats_got = swap(feats, 2, n)
    parts_m = swap_parts(parts_m, LINE, n)
    keep_a, send_a = run_kernel(
        weight_back_kernel,
        steps,
        [1, 2],
        [turned_tokens, gains, shifts, grad_wo],
        [(grad_qkv, rows)],
        [
            ((BLOCKS // 2, 1, width // 8, width), low, 0),
            ((BLOCKS // 2, 1, width // 8, width), low, 0),
        ],
        [all_rows, pltpu.VMEM((rows, width), wide), pltpu.VMEM((width, 4 * width), wide)],
        10,
        info,
    )
    keep_a, send_a, feats_got, *parts_m = together(keep_a, send_a, feats_got, *parts_m)
    feats = double(feats, feats_got)
    sum_m = extra_sum(jnp.concatenate([fold_sum(parts_m), sum_u], axis=1), n)
    keep_a, send_a = fold_send(keep_a + swap(send_a, 1, n), [2])
    grad_qkv, sum_m, send_a, feats = together(grad_qkv, sum_m, send_a, feats)
    feats_got = swap(feats, 4, n)
    parts_m = swap_parts([sum_m] * 4, LINE, n)
    got_a = swap(send_a, 4, n)
    grad_tokens, vectors = run_kernel(
        input_back_kernel,
        steps,
        [2],
        [turned_tokens, gains, Layer(w_qkv, 0), vec_b, vec_c, vec_h, vec_a, vec_hidden],
        [(grad_middle_a, rows), (grad_qkv, rows)],
        [((row_count, width), wide, 0), ((1, 13 * width + hidden + vec_width), wide, 0)],
        [all_rows, all_rows, pltpu.VMEM((rows, width), wide), pltpu.VMEM((8, 2 * width), wide)],
        20,
        info,
    )
    tokens_grad = grad_tokens.reshape(seq_len, slot_count, width).transpose(1, 0, 2)
    vectors, got_a, feats_got, *parts_m = together(vectors, got_a, feats_got, *parts_m)
    feats = double(feats, feats_got)
    feats = double(feats, swap(feats, 1, n))

    keep_a, send_a = fold_send(keep_a + got_a, [1])
    send_a, vectors = together(send_a, vectors)
    got_a, got_v = swap(send_a, 2, n), swap(vectors, 1, n)
    vectors = vectors + got_v
    sum_m = jnp.concatenate(parts_m)
    half = sum_m.shape[0] // 2
    feats, vectors, sum_m = together(feats, vectors, sum_m)
    one, two = sum_m[:half], sum_m[half:]
    one, two = [one, swap(one, 2, n)], [two, swap(two, 4, n)]
    prototypes_grad = run_kernel(
        functools.partial(proto_back_kernel, scale),
        n // 8,
        [device ^ jnp.array(masks, jnp.int32)],
        [unit_low, prototypes, col_inv, (1 - first_epoch).astype(wide)[None], teach_expo],
        [(feats, 8 * slot_count)],
        [(prototypes.shape, wide, 0)],
        [pltpu.VMEM(prototypes.shape, wide), pltpu.VMEM((8 * slot_count, protos), low)],
        6,
    )[0]
    prototypes_grad, got_a, *parts_m = together(prototypes_grad, got_a, *one, *two)
    one, two = jnp.stack(parts_m[:2]), jnp.stack(parts_m[2:])
    sum_a = keep_a + got_a
    sum_a, vectors, one, two = together(sum_a, vectors, one, two)
    one, two = [one, swap(one, 4, n)], [two, swap(two, 2, n)]
    for bit in (4, 3):
        keep_a, send_a = fold_send(sum_a, [bit])
        got_a, got_v = swap(send_a, 1 << bit, n), swap(vectors, 1 << bit, n)
        sum_a, vectors = keep_a + got_a, vectors + got_v
    sum_a = extra_sum(sum_a, n)
    vectors = extra_sum(vectors, n)
    for bit in (3, 4):
        sum_a = unfold_stage(sum_a, [bit], n)
    sum_a, vectors, head_send, *parts_m = together(sum_a, vectors, head_send, *one, *two)
    head_got = swap(head_send, 16, n)
    one = jnp.stack(parts_m[:2]).reshape((4,) + parts_m[0].shape[1:])
    two = jnp.stack(parts_m[2:], axis=1).reshape((4,) + parts_m[0].shape[1:])
    sum_m = jnp.concatenate([one, two], axis=1).reshape((BLOCKS // 2,) + one.shape[2:])
    got_m, got_a, got_v = swap(sum_m, 1, n), swap(sum_a, 2, n), swap(vectors, 2, n)
    got_m, got_a, got_v = together(got_m, got_a, got_v)
    sum_a, vectors = double(sum_a, got_a), vectors + got_v
    got_a, got_v = swap(sum_a, 4, n), swap(vectors, 4, n)
    specs = [
        pl.BlockSpec((None, width // UNPACK, 3 * width), lambda i: (1, i, 0)),
        pl.BlockSpec((None, width // UNPACK, width), lambda i: (1, i, 0)),
    ]
    shapes = [jax.ShapeDtypeStruct(s, wide) for s in ((2, width, 3 * width), (2, width, width))]
    params = pltpu.CompilerParams(dimension_semantics=("arbitrary",), vmem_limit_bytes=32 * 1024 * 1024)
    qkv_grad, out_grad, fc1_grad, fc2_grad = pl.pallas_call(
        unpack_kernel,
        grid=(UNPACK,),
        in_specs=[pl.BlockSpec(memory_space=pltpu.SMEM), whole(sum_m), whole(got_m)],
        out_specs=specs
        + [
            pl.BlockSpec((2, width // UNPACK, hidden), lambda i: (0, i, 0)),
            pl.BlockSpec((2, hidden // UNPACK, width), lambda i: (0, i, 0)),
        ],
        out_shape=shapes + [jax.ShapeDtypeStruct(s, wide) for s in ((2, width, hidden), (2, hidden, width))],
        compiler_params=params,
        cost_estimate=pl.CostEstimate(flops=8 * 10**9, bytes_accessed=2**20, transcendentals=0),
    )(me, sum_m, got_m)
    qkv_grad, out_grad, got_a, got_v, head_got = together(qkv_grad, out_grad, got_a, got_v, head_got)
    head_sum = (head_keep.astype(wide) + head_got.astype(wide)).reshape(hid // n, -1)
    w1_grad, w2_grad, w3_grad = head_sum[:, :width].T, head_sum[:, width : width + hid], head_sum[:, width + hid :]
    sum_a, vectors = double(sum_a, got_a), vectors + got_v
    got_a = swap(sum_a, 1, n)
    specs = [pl.BlockSpec(spec.block_shape, lambda i: (0, i, 0)) for spec in specs]
    small = [(2, 2, width), (2, 2, width), (2, 2 * width), (2, width), (2, hidden), (2, width)]
    qkv_grad, out_grad, gains_grad, shifts_grad, bqv_grad, bout_grad, bfc1_grad, bfc2_grad = pl.pallas_call(
        unpack_first_kernel,
        grid=(UNPACK,),
        in_specs=[pl.BlockSpec(memory_space=pltpu.SMEM), whole(sum_a), whole(got_a), whole(vectors)]
        + [pl.BlockSpec(memory_space=pl.ANY)] * 2,
        out_specs=specs + [pl.BlockSpec(shape, lambda i, k=len(shape): (0,) * k) for shape in small],
        out_shape=shapes + [jax.ShapeDtypeStruct(shape, wide) for shape in small],
        input_output_aliases={4: 0, 5: 1},
        compiler_params=params,
    )(me, sum_a, got_a, vectors, qkv_grad, out_grad)
    row_h = 9
    ends = vectors[0, (row_h + 7) * width + hidden : (row_h + 7) * width + hidden + 2 * hid]
    row_part = lambda row, size: vectors[0, row * width : row * width + size]
    own_part = lambda start: lax.dynamic_slice_in_dim(ends, start + device * (hid // n), hid // n)

    return (
        tokens_grad,
        gains_grad,
        shifts_grad,
        qkv_grad,
        bqv_grad,
        out_grad,
        bout_grad,
        fc1_grad,
        bfc1_grad,
        fc2_grad,
        bfc2_grad,
        row_part(row_h + 4, width),
        row_part(row_h + 5, width),
        w1_grad,
        own_part(0),
        w2_grad,
        own_part(hid),
        w3_grad,
        row_part(row_h + 6 + hidden // width, bottle),
        prototypes_grad,
    )


def solution(mesh):
    return jax.shard_map(
        per_device,
        mesh=mesh,
        in_specs=(
            P("dp", None, None),
            P(),
            P(),
            P(),
            P(),
            P(),
            P(),
            P(),
            P(),
            P(),
            P(),
            P(),
            P(),
            P(),
            P(),
            P(),
            P(),
            P(),
            P(),
            P(None, "dp"),
            P(),
            P(None, "dp"),
            P("dp"),
        ),
        out_specs=(
            P("dp", None, None),
            P(),
            P(),
            P(),
            P(),
            P(),
            P(),
            P(),
            P(),
            P(),
            P(),
            P(),
            P(),
            P(None, "dp"),
            P("dp"),
            P("dp", None),
            P("dp"),
            P("dp", None),
            P(),
            P(None, "dp"),
        ),
        check_vma=False,
    )
```

```python
import functools

import jax
import jax.numpy as jnp
from jax import lax
from jax.experimental import pallas as pl
from jax.experimental.pallas import tpu as pltpu
from jax.sharding import PartitionSpec as P

HEADS = 6
HD = 64
MOST_CROPS = 10

STUDENT_TEMP = 0.1
TEACHER_TEMP = 0.04
EPS = 1e-06
SHIFT = 10.0


def product(left, right):
    return jnp.dot(left, right, preferred_element_type=jnp.float32)


def against(left, right):
    return lax.dot_general(
        left, right, (((1,), (1,)), ((), ())), preferred_element_type=jnp.float32
    )


def inner_rows(left, right):
    return lax.dot_general(
        left, right, (((0,), (0,)), ((), ())), preferred_element_type=jnp.float32
    )


def column_sum(values):
    return jnp.sum(values.astype(jnp.float32), axis=0)


def norm_forward(values, gain, shift):
    centered = values - jnp.mean(values, axis=-1, keepdims=True)
    rstd = lax.rsqrt(jnp.mean(centered * centered, axis=-1, keepdims=True) + EPS)
    normed = centered * rstd
    return (normed * gain + shift, normed, rstd)


def norm_backward(grad, normed, rstd, gain):
    scaled = grad * gain
    inner = (
        scaled
        - jnp.mean(scaled, axis=-1, keepdims=True)
        - normed * jnp.mean(scaled * normed, axis=-1, keepdims=True)
    )
    return (rstd * inner, jnp.sum(grad * normed, axis=0), jnp.sum(grad, axis=0))


GROUP = 16
BLOCKS = 32
PITCH = 40
PAIR = 2 * PITCH
NEVER = -1e30
SEQ_LEN = 37


def smooth_both(values):
    size = jnp.abs(values)
    bell = jnp.exp(values * values * -0.5)
    t = 1.0 / (1.0 + 0.23164189 * size)
    tail = t * (0.127414796 + t * (-0.142248368 + t * (0.7107068705 + t * (-0.7265760135 + t * 0.5307027145))))
    upper = tail * bell
    area = jnp.where(values >= 0, 1.0 - upper, upper)
    return values * area, area + values * (bell * 0.3989422804014327)


def norm_row(ref, index):
    return ref[index // 2, index % 2 : index % 2 + 1, :]


def qkv_bias(ref, layer, part, width):
    if part == 1:
        return 0.0
    return ref[layer : layer + 1, part // 2 * width : (part // 2 + 1) * width]


def standardize(values):
    centered = values - jnp.mean(values, axis=-1, keepdims=True)
    rstd = lax.rsqrt(jnp.mean(centered * centered, axis=-1, keepdims=True) + EPS)
    return centered * rstd, rstd


def standard_back(grad, normed, rstd, gain):
    scaled = grad * gain
    return rstd * (
        scaled
        - jnp.mean(scaled, axis=-1, keepdims=True)
        - normed * jnp.mean(scaled * normed, axis=-1, keepdims=True)
    )


def fold_rows(values):
    return jnp.sum(values.reshape(-1, 8, values.shape[1]), axis=0)


def finish_rows(ref):
    ref[0:1, :] = jnp.sum(ref[...], axis=0, keepdims=True)


def both_heads(values):
    lane = lax.broadcasted_iota(jnp.int32, values.shape, 1)
    zero = jnp.zeros_like(values)
    return jnp.concatenate([jnp.where(lane < HD, values, zero), jnp.where(lane < HD, zero, values)])


def join_heads(values):
    rows = values.shape[0] // 2
    lane = lax.broadcasted_iota(jnp.int32, (rows, values.shape[1]), 1)
    return jnp.where(lane < HD, values[:rows], values[rows:])


def spread_heads(values):
    lane = lax.broadcasted_iota(jnp.int32, values.shape, 1) // HD
    return jnp.concatenate([jnp.where(lane == h, values, 0.0) for h in range(HEADS)])


def gather_heads(values):
    lane = lax.broadcasted_iota(jnp.int32, (GROUP, values.shape[1]), 1) // HD
    out = jnp.zeros((GROUP, values.shape[1]), values.dtype)
    for h in range(HEADS):
        out = jnp.where(lane == h, values[h * GROUP : (h + 1) * GROUP], out)
    return out


def slot_and_valid(shape, dim, seq_len):
    index = lax.broadcasted_iota(jnp.int32, shape, dim)
    slot = index // PITCH
    return slot, index - slot * PITCH < seq_len


def pair_mask(rows_are_keys, seq_len, copies=1):
    shape = (PAIR, PAIR)
    key, valid = slot_and_valid(shape, 0 if rows_are_keys else 1, seq_len)
    query, _ = slot_and_valid(shape, 1 if rows_are_keys else 0, seq_len)
    mask = jnp.where((key == query) & valid, 0.0, NEVER)
    return jnp.concatenate([mask] * copies, axis=1 if rows_are_keys else 0)


def class_mask(seq_len):
    shape = (GROUP * PITCH, GROUP)
    key, valid = slot_and_valid(shape, 0, seq_len)
    mask = jnp.where((key == lax.broadcasted_iota(jnp.int32, shape, 1)) & valid, 0.0, NEVER)
    return jnp.concatenate([mask] * HEADS, axis=1)


def soft_columns(scores):
    expo = jnp.exp(scores - jnp.max(scores, axis=0, keepdims=True))
    return expo * (1.0 / jnp.sum(expo, axis=0, keepdims=True))


def take_slots(order_ref, all_ref, rows_ref, step, seq_len, slots):
    for s in range(GROUP):
        for c in range(all_ref.shape[0]):
            rows_ref[s * PITCH : s * PITCH + seq_len, c * 128 : (c + 1) * 128] = all_ref[
                c, pl.ds(order_ref[step * GROUP + s], seq_len, stride=slots), :
            ]


def first_rows(ref):
    return jnp.concatenate([ref[s * PITCH : s * PITCH + 1, :] for s in range(GROUP)])


def add_first_rows(ref, values):
    for s in range(GROUP):
        ref[s * PITCH : s * PITCH + 1, :] += values[s : s + 1]


def widen_tokens(tok_ref, all_ref):
    seq_len, slots, width = tok_ref.shape

    @pl.loop(0, seq_len)
    def _(t):
        wide = tok_ref[t].astype(jnp.float32)
        for c in range(all_ref.shape[0]):
            all_ref[c, pl.ds(pl.multiple_of(t * slots, 8), slots), :] = wide[:, c * 128 : (c + 1) * 128]


def ordered_masks(line_first=False):
    if line_first:
        return [(p >> 4) | ((p & 3) << 1) | (((p >> 2) & 3) << 3) for p in range(BLOCKS)]
    return [(p >> 4) | (((p >> 2) & 3) << 1) | ((p & 3) << 3) for p in range(BLOCKS)]


def write_unit(me, keep_ref, send_ref, unit, read, line_first=False):
    for p, mask in enumerate(ordered_masks(line_first)):
        owner = me ^ mask
        ref = keep_ref if p < BLOCKS // 2 else send_ref
        ref[p % (BLOCKS // 2), unit] = read(owner)


def from_square(ref, first=0):
    width = ref.shape[0]

    def read(owner):
        rows = pl.multiple_of((owner // 4) * (width // 8), 16)
        cols = pl.multiple_of((owner % 4) * width, 128)
        return ref[pl.ds(rows, width // 8), pl.ds(cols, width)].astype(jnp.bfloat16)

    return read


def from_tall(ref):
    size = ref.shape[0] // BLOCKS

    def read(owner):
        return ref[pl.ds(pl.multiple_of(owner * size, 16), size), :].astype(jnp.bfloat16)

    return read


def attend_kernel(
    count_ref, order_ref, tok_ref, gains_ref, shifts_ref, w_qkv_ref, b_qkv_ref, w_out_ref, b_out_ref,
    qkv_ref, o_ref, mid_ref,
    all_ref, x_ref, low_ref,
):
    step = pl.program_id(0)
    seq_len, slots, width = tok_ref.shape
    rows = GROUP * PITCH
    chunk = PAIR

    @pl.when(step == 0)
    def _():
        widen_tokens(tok_ref, all_ref)
        x_ref[...] = jnp.zeros_like(x_ref)

    take_slots(order_ref, all_ref, x_ref, step, seq_len, slots)
    for r in range(0, rows, chunk):
        normed, _ = standardize(x_ref[r : r + chunk, :])
        low_ref[r : r + chunk, :] = (normed * norm_row(gains_ref, 0) + norm_row(shifts_ref, 0)).astype(jnp.bfloat16)
    whole = product(low_ref[...], w_qkv_ref[:, : 2 * width])
    part = (whole[:, :width] + qkv_bias(b_qkv_ref, 0, 0, width)).astype(jnp.bfloat16)
    qkv_ref[:, :width] = part * jnp.bfloat16(HD ** -0.5)
    qkv_ref[:, width : 2 * width] = whole[:, width:].astype(jnp.bfloat16)
    part = product(low_ref[...], w_qkv_ref[:, 2 * width :]) + qkv_bias(b_qkv_ref, 0, 2, width)
    qkv_ref[:, 2 * width :] = part.astype(jnp.bfloat16)
    mask = pair_mask(False, seq_len, 2)
    spots = [(r, c) for r in range(0, rows, PAIR) for c in range(0, width, 2 * HD)]
    for b in range(0, len(spots), 24):
        group = spots[b : b + 24]
        scores = [
            against(
                both_heads(qkv_ref[r : r + PAIR, c : c + 2 * HD]), qkv_ref[r : r + PAIR, width + c : width + c + 2 * HD]
            )
            + mask
            for r, c in group
        ]
        probs, scales = [], []
        for score in scores:
            expo = jnp.exp(score - jnp.max(score, axis=1, keepdims=True))
            probs.append(expo.astype(jnp.bfloat16))
            scales.append(1.0 / jnp.sum(expo, axis=1, keepdims=True))
        outs = [
            product(prob, qkv_ref[r : r + PAIR, 2 * width + c : 2 * width + c + 2 * HD]) * scale
            for prob, scale, (r, c) in zip(probs, scales, group)
        ]
        for out, (r, c) in zip(outs, group):
            o_ref[r : r + PAIR, c : c + 2 * HD] = join_heads(out).astype(jnp.bfloat16)
    mixed = product(o_ref[...], w_out_ref[...])
    for r in range(0, rows, chunk):
        part = x_ref[r : r + chunk, :] + mixed[r : r + chunk] + b_out_ref[0:1, :]
        mid_ref[r : r + chunk, :] = part


def mlp_kernel(
    count_ref, gains_ref, shifts_ref, w_fc1_ref, b_fc1_ref, w_fc2_ref, b_fc2_ref, w_up_ref, b_up_ref, mid_ref,
    act_ref, slope_ref, x1_ref, kv_ref, cq_ref, co_ref, ch_ref, cx_ref,
    low_ref, wide_ref, mask_ref,
):
    rows, width = mid_ref.shape
    hidden = w_fc1_ref.shape[1]
    chunk = PAIR
    step = pl.program_id(0)
    here = pl.ds(pl.multiple_of(step * GROUP, GROUP), GROUP)

    @pl.when(step == 0)
    def _():
        mask_ref[...] = class_mask(SEQ_LEN)
        for ref in (cq_ref, co_ref, ch_ref, cx_ref):
            ref[...] = jnp.zeros_like(ref)

    for r in range(0, rows, chunk):
        normed, _ = standardize(mid_ref[r : r + chunk, :])
        low_ref[r : r + chunk, :] = (normed * norm_row(gains_ref, 1) + norm_row(shifts_ref, 1)).astype(jnp.bfloat16)
    for c in range(0, hidden, 256):
        pre = product(low_ref[...], w_fc1_ref[:, c : c + 256])
        for r in range(0, rows, 32):
            act, slope = smooth_both(pre[r : r + 32] + b_fc1_ref[0:1, c : c + 256])
            act_ref[r : r + 32, c : c + 256] = act.astype(jnp.bfloat16)
            slope_ref[r : r + 32, c : c + 256] = slope.astype(jnp.bfloat16)
    mixed = product(act_ref[...], w_fc2_ref[...])
    for r in range(0, rows, chunk):
        part = mid_ref[r : r + chunk, :] + mixed[r : r + chunk] + b_fc2_ref[0:1, :]
        x1_ref[r : r + chunk, :] = part
        normed, _ = standardize(part)
        wide = normed * norm_row(gains_ref, 2) + norm_row(shifts_ref, 2)
        wide_ref[r : r + chunk, :] = wide
        low_ref[r : r + chunk, :] = wide.astype(jnp.bfloat16)
    whole = product(low_ref[...], w_up_ref[:, width:])
    kv_ref[:, :width] = whole[:, :width].astype(jnp.bfloat16)
    kv_ref[:, width:] = (whole[:, width:] + qkv_bias(b_up_ref, 1, 2, width)).astype(jnp.bfloat16)
    cx_ref[here, :] = first_rows(x1_ref)
    first = first_rows(wide_ref).astype(jnp.bfloat16)
    ch_ref[here, :] = first.astype(jnp.float32)
    query = (product(first, w_up_ref[:, :width]) + qkv_bias(b_up_ref, 1, 0, width)).astype(jnp.bfloat16).astype(jnp.float32) * HD ** -0.5
    cq_ref[here, :] = query
    spread = spread_heads(query).astype(jnp.bfloat16)
    probs = soft_columns(against(kv_ref[:, :width], spread) + mask_ref[...]).astype(jnp.bfloat16)
    co_ref[here, :] = gather_heads(inner_rows(probs, kv_ref[:, width:]))


def upper_back_kernel(
    count_ref, gains_ref, shifts_ref, w_up_ref, ch_ref, co_ref, da_ref,
    x1_ref, kv_ref, cq_ref, cg_ref, cres_ref,
    dx_ref, unit_ref, vec_ref,
    acc_ref, wide_ref, dqs_ref, mask_ref, dkv_ref,
):
    step = pl.program_id(0)
    rows, width = x1_ref.shape

    @pl.when(step == 0)
    def _():
        acc_ref[...] = jnp.zeros_like(acc_ref)
        mask_ref[...] = class_mask(SEQ_LEN)
        vec_ref[...] = jnp.zeros_like(vec_ref)

    keys, values = kv_ref[:, :width], kv_ref[:, width:]
    spread = spread_heads(cq_ref[...]).astype(jnp.bfloat16)
    grads = spread_heads(cg_ref[...]).astype(jnp.bfloat16)
    probs = soft_columns(against(keys, spread) + mask_ref[...])
    back = against(values, grads)
    inner = (probs * (back - jnp.sum(back * probs, axis=0, keepdims=True))).astype(jnp.bfloat16)
    dkv_ref[:, :width] = product(inner, spread).astype(jnp.bfloat16)
    dkv_ref[:, width:] = product(probs.astype(jnp.bfloat16), grads).astype(jnp.bfloat16)
    grad_query = (gather_heads(inner_rows(inner, keys)) * HD ** -0.5).astype(jnp.bfloat16)
    @pl.when(step == 0)
    def _():
        dqs_ref[...] = jnp.zeros_like(dqs_ref)

    dqs_ref[pl.ds(pl.multiple_of(step * GROUP, GROUP), GROUP), :] = grad_query.astype(jnp.float32)
    vec_ref[:, 3 * width :] += fold_rows(grad_query.astype(jnp.float32))
    vec_ref[:, :width] += fold_rows(dkv_ref[:, width:].astype(jnp.float32))
    wide_ref[...] = against(dkv_ref[...], w_up_ref[:, width:])
    add_first_rows(wide_ref, against(grad_query, w_up_ref[:, :width]))
    chunk = PAIR
    parts = []
    for r in range(0, rows, chunk):
        normed, rstd = standardize(x1_ref[r : r + chunk, :])
        parts.append((normed * norm_row(gains_ref, 2) + norm_row(shifts_ref, 2)).astype(jnp.bfloat16))
        grad = wide_ref[r : r + chunk, :]
        vec_ref[:, width : 2 * width] += fold_rows(grad * normed)
        vec_ref[:, 2 * width : 3 * width] += fold_rows(grad)
        dx_ref[r : r + chunk, :] = standard_back(grad, normed, rstd, norm_row(gains_ref, 2))
    turned = jnp.concatenate(parts).T
    acc_ref[:, width : 3 * width] += product(turned, dkv_ref[...])
    add_first_rows(dx_ref, cres_ref[...])

    @pl.when(step == count_ref[0] - 1)
    def _():
        acc_ref[:, :width] = inner_rows(
            ch_ref[...].astype(jnp.bfloat16), dqs_ref[...].astype(jnp.bfloat16)
        )
        acc_ref[:, 3 * width :] = inner_rows(co_ref[...].astype(jnp.bfloat16), da_ref[...].astype(jnp.bfloat16))
        unit_ref[...] = acc_ref[...].astype(jnp.bfloat16)
        finish_rows(vec_ref)


def mlp_back_kernel(
    count_ref, me_ref, unit_ref, gains_ref, shifts_ref, w_fc1_ref, w_fc2_ref, dx_ref, mid_ref, act_ref, slope_ref,
    dmid_ref, keep_ref, send_ref, vec_ref, vec1_ref,
    acc1_ref, acc2_ref, dz_ref, big_ref, normed_ref, rstd_ref,
):
    step = pl.program_id(0)
    rows, width = dx_ref.shape
    hidden = act_ref.shape[1]

    @pl.when(step == 0)
    def _():
        acc1_ref[...] = jnp.zeros_like(acc1_ref)
        acc2_ref[...] = jnp.zeros_like(acc2_ref)
        vec_ref[...] = jnp.zeros_like(vec_ref)
        vec1_ref[...] = jnp.zeros_like(vec1_ref)

    low = dx_ref[...].astype(jnp.bfloat16)
    vec_ref[:, :width] += fold_rows(low.astype(jnp.float32))
    low_turned = low.T
    chunk = PAIR
    parts = []
    for r in range(0, rows, chunk):
        normed, rstd = standardize(mid_ref[r : r + chunk, :])
        normed_ref[r : r + chunk, :] = normed
        rstd_ref[r : r + chunk, :] = rstd
        parts.append((normed * norm_row(gains_ref, 1) + norm_row(shifts_ref, 1)).astype(jnp.bfloat16))
    norm_turned = jnp.concatenate(parts).T
    for c in range(0, hidden, 768):
        cols = slice(c, c + 768)
        back = against(low, w_fc2_ref[cols, :])
        for r in range(0, rows, chunk):
            part = (back[r : r + chunk] * slope_ref[r : r + chunk, cols].astype(jnp.float32)).astype(jnp.bfloat16)
            dz_ref[r : r + chunk, cols] = part
            vec1_ref[:, cols] += fold_rows(part.astype(jnp.float32))
        acc1_ref[:, cols] += product(norm_turned, dz_ref[:, cols])
        acc2_ref[:, cols] += product(low_turned, act_ref[:, cols])
    mixed = against(dz_ref[...], w_fc1_ref[...])
    for r in range(0, rows, chunk):
        normed, rstd = normed_ref[r : r + chunk, :], rstd_ref[r : r + chunk, :]
        grad = mixed[r : r + chunk]
        vec_ref[:, width : 2 * width] += fold_rows(grad * normed)
        vec_ref[:, 2 * width : 3 * width] += fold_rows(grad)
        dmid_ref[r : r + chunk, :] = dx_ref[r : r + chunk, :] + standard_back(grad, normed, rstd, norm_row(gains_ref, 1))

    @pl.when(step == count_ref[0] - 1)
    def _():
        finish_rows(vec_ref)
        finish_rows(vec1_ref)
        me = me_ref[0]
        write_unit(me, keep_ref, send_ref, 0, from_square(unit_ref))
        write_unit(me, keep_ref, send_ref, 1, from_square(acc1_ref))
        big_ref[...] = acc2_ref[...].T
        write_unit(me, keep_ref, send_ref, 2, from_tall(big_ref))


def attend_back_kernel(
    count_ref, w_out_ref, dmid_ref, qkv_ref, o_ref,
    dqkv_ref, dwo_ref, vec_ref,
    do_ref,
):
    step = pl.program_id(0)
    rows, width = dmid_ref.shape

    @pl.when(step == 0)
    def _():
        dwo_ref[...] = jnp.zeros_like(dwo_ref)
        vec_ref[...] = jnp.zeros_like(vec_ref)

    low = dmid_ref[...].astype(jnp.bfloat16)
    vec_ref[:, :width] += fold_rows(low.astype(jnp.float32))
    do_ref[...] = against(low, w_out_ref[...]).astype(jnp.bfloat16)
    dwo_ref[...] += product(o_ref[...].T, low)
    mask = pair_mask(True, SEQ_LEN, 2)
    spots = [(r, c) for r in range(0, rows, PAIR) for c in range(0, width, 2 * HD)]
    for b in range(0, len(spots), 6):
        group = spots[b : b + 6]
        queries = [both_heads(qkv_ref[r : r + PAIR, c : c + 2 * HD]) for r, c in group]
        keys = [qkv_ref[r : r + PAIR, width + c : width + c + 2 * HD] for r, c in group]
        values = [qkv_ref[r : r + PAIR, 2 * width + c : 2 * width + c + 2 * HD] for r, c in group]
        grads = [both_heads(do_ref[r : r + PAIR, c : c + 2 * HD]) for r, c in group]
        scores = [against(key, query) + mask for key, query in zip(keys, queries)]
        backs = [against(value, grad) for value, grad in zip(values, grads)]
        probs = [soft_columns(score) for score in scores]
        inners = [
            (prob * (back - jnp.sum(back * prob, axis=0, keepdims=True))).astype(jnp.bfloat16)
            for prob, back in zip(probs, backs)
        ]
        grad_values = [product(prob.astype(jnp.bfloat16), grad) for prob, grad in zip(probs, grads)]
        grad_keys = [product(inner, query) for inner, query in zip(inners, queries)]
        grad_queries = [inner_rows(inner, key) for inner, key in zip(inners, keys)]
        for (r, c), grad in zip(group, grad_values):
            dqkv_ref[r : r + PAIR, 2 * width + c : 2 * width + c + 2 * HD] = grad.astype(jnp.bfloat16)
        for (r, c), grad in zip(group, grad_keys):
            dqkv_ref[r : r + PAIR, width + c : width + c + 2 * HD] = grad.astype(jnp.bfloat16)
        for (r, c), grad in zip(group, grad_queries):
            dqkv_ref[r : r + PAIR, c : c + 2 * HD] = (join_heads(grad) * HD ** -0.5).astype(jnp.bfloat16)
    for j in range(3):
        cols = slice(j * width, (j + 1) * width)
        vec_ref[:, (j + 1) * width : (j + 2) * width] += fold_rows(dqkv_ref[:, cols].astype(jnp.float32))

    @pl.when(step == count_ref[0] - 1)
    def _():
        finish_rows(vec_ref)


def weight_back_kernel(
    count_ref, me_ref, order_ref, tok_ref, gains_ref, shifts_ref, dwo_ref, dqkv_ref,
    keep_ref, send_ref,
    all_ref, x_ref, acc_ref,
):
    step = pl.program_id(0)
    seq_len, slots, width = tok_ref.shape
    rows = GROUP * PITCH

    @pl.when(step == 0)
    def _():
        widen_tokens(tok_ref, all_ref)
        x_ref[...] = jnp.zeros_like(x_ref)
        acc_ref[:, : 3 * width] = jnp.zeros((width, 3 * width), jnp.float32)
        acc_ref[:, 3 * width :] = dwo_ref[...]

    take_slots(order_ref, all_ref, x_ref, step, seq_len, slots)
    chunk = PAIR
    parts = []
    for r in range(0, rows, chunk):
        normed, _ = standardize(x_ref[r : r + chunk, :])
        parts.append((normed * norm_row(gains_ref, 0) + norm_row(shifts_ref, 0)).astype(jnp.bfloat16))
    turned = jnp.concatenate(parts).T
    acc_ref[:, : 3 * width] += product(turned, dqkv_ref[...])

    @pl.when(step == count_ref[0] - 1)
    def _():
        write_unit(me_ref[0], keep_ref, send_ref, 0, from_square(acc_ref))


def input_back_kernel(
    count_ref, order_ref, tok_ref, gains_ref, w_qkv_ref, vec1_ref, vec2_ref, vec3_ref, vec4_ref, vec5_ref, dmid_ref, dqkv_ref,
    dtok_ref, all_vec_ref,
    all_ref, out_ref, x_ref, vec_ref,
):
    step = pl.program_id(0)
    seq_len, slots, width = tok_ref.shape
    rows = GROUP * PITCH

    @pl.when(step == 0)
    def _():
        widen_tokens(tok_ref, all_ref)
        x_ref[...] = jnp.zeros_like(x_ref)
        out_ref[...] = jnp.zeros_like(out_ref)
        vec_ref[...] = jnp.zeros_like(vec_ref)

    take_slots(order_ref, all_ref, x_ref, step, seq_len, slots)
    chunk = PAIR
    mixed = against(dqkv_ref[...], w_qkv_ref[...])
    for r in range(0, rows, chunk):
        normed, rstd = standardize(x_ref[r : r + chunk, :])
        grad = mixed[r : r + chunk]
        vec_ref[:, :width] += fold_rows(grad * normed)
        vec_ref[:, width:] += fold_rows(grad)
        part = dmid_ref[r : r + chunk, :] + standard_back(grad, normed, rstd, norm_row(gains_ref, 0))
        for s in range(chunk // PITCH):
            for t in range(all_ref.shape[0]):
                out_ref[t, pl.ds(order_ref[step * GROUP + r // PITCH + s], seq_len, stride=slots), :] = part[
                    s * PITCH : s * PITCH + seq_len, t * 128 : (t + 1) * 128
                ]

    @pl.when(step == count_ref[0] - 1)
    def _():
        finish_rows(vec_ref)
        start = 0
        for ref in (vec_ref, vec1_ref, vec2_ref, vec3_ref, vec4_ref, vec5_ref):
            size = ref.shape[1]
            all_vec_ref[:, start : start + size] = ref[0:1, :]
            start += size
        for t in range(out_ref.shape[0]):
            dtok_ref[:, t * 128 : (t + 1) * 128] = out_ref[t]


def place_of(mask):
    return ((mask & 1) << 4) | (((mask >> 1) & 3) << 2) | ((mask >> 3) & 3)


def read_place(own_ref, got_ref, place, unit):
    inner = place & (BLOCKS // 2 - 1)
    block = jnp.where(place < BLOCKS // 2, own_ref[inner, unit], got_ref[inner, unit])
    return block.astype(jnp.float32)


def unpack_kernel(
    me_ref, own_ref, got_ref,
    qkv_ref, out_ref, fc1_ref, fc2_ref,
):
    step = pl.program_id(0)
    width, size = own_ref.shape[3], own_ref.shape[2]
    count = out_ref.shape[0] // size
    for r, c in [(r, c) for r in range(count) for c in range(4)]:
        place = place_of(((step * count + r) * 4 + c) ^ me_ref[0])
        cols, rows = slice(c * width, (c + 1) * width), slice(r * size, (r + 1) * size)
        tall = slice((r * 4 + c) * size, (r * 4 + c + 1) * size)
        upper = read_place(own_ref, got_ref, place, 0)
        if c < 3:
            qkv_ref[rows, cols] = upper
        else:
            out_ref[rows, :] = upper
        fc1_ref[0, rows, cols] = read_place(own_ref, got_ref, place, 1)
        fc2_ref[0, tall, :] = read_place(own_ref, got_ref, place, 2)
        fc1_ref[1, rows, cols] = read_place(own_ref, got_ref, place, 3)
        fc2_ref[1, tall, :] = read_place(own_ref, got_ref, place, 4)


def unpack_first_kernel(
    me_ref, own_ref, got_ref, vec_ref, qkv_in_ref, out_in_ref,
    qkv_ref, out_ref, gains_ref, shifts_ref, bqv_ref, bout_ref, bfc1_ref, bfc2_ref,
):
    step = pl.program_id(0)
    width = own_ref.shape[3]
    size = own_ref.shape[2]
    count = out_ref.shape[0] // size
    for r, c in [(r, c) for r in range(count) for c in range(4)]:
        block = read_place(own_ref, got_ref, place_of(((step * count + r) * 4 + c) ^ me_ref[0]), 0)
        rows = slice(r * size, (r + 1) * size)
        if c < 3:
            qkv_ref[rows, c * width : (c + 1) * width] = block
        else:
            out_ref[rows, :] = block

    @pl.when(step == 0)
    def _():
        hidden = bfc1_ref.shape[1]
        row_b, row_c, row_h = 2, 5, 9
        row_hidden = vec_ref.shape[1] // width - hidden // width
        row_a = row_hidden - 4

        def put(ref, place, row, count=1):
            ref[place] = vec_ref[:, row * width : (row + count) * width]

        for i, row in enumerate((0, row_b + 1, row_c + 1, row_h)):
            put(gains_ref, (i // 2, slice(i % 2, i % 2 + 1)), row)
            put(shifts_ref, (i // 2, slice(i % 2, i % 2 + 1)), row + 1)
        put(bqv_ref, (slice(0, 1), slice(0, width)), row_a + 1)
        put(bqv_ref, (slice(0, 1), slice(width, 2 * width)), row_a + 3)
        put(bqv_ref, (slice(1, 2), slice(0, width)), row_c + 3)
        put(bqv_ref, (slice(1, 2), slice(width, 2 * width)), row_c)
        put(bout_ref, slice(0, 1), row_a)
        put(bout_ref, slice(1, 2), row_h + 2)
        put(bfc1_ref, slice(0, 1), row_hidden, hidden // width)
        put(bfc1_ref, slice(1, 2), row_h + 6, hidden // width)
        put(bfc2_ref, slice(0, 1), row_b)
        put(bfc2_ref, slice(1, 2), row_h + 3)


def prepare_kernel(
    device_ref, counts_ref, proto_ref, teacher_ref,
    info_ref, live_ref, image_ref, unit_ref, turned_ref, inv_ref, teach_ref, expo_ref,
):
    slots = live_ref.shape[0]
    images_here = slots // MOST_CROPS
    counts = [counts_ref[device_ref[0] * images_here + i] for i in range(images_here)]
    total = functools.reduce(lambda a, b: a + b, counts)
    place = lax.broadcasted_iota(jnp.int32, (slots, 1), 0)
    live_ref[...] = (place < total).astype(jnp.float32)
    image = jnp.zeros((slots, 1), jnp.float32)
    live_before, dead_before = 0, total
    for i, amount in enumerate(counts):
        dead = MOST_CROPS - amount
        for k in range(MOST_CROPS):
            at = jnp.where(k < amount, live_before + k, dead_before + k - amount)
            info_ref[at + 2] = i * MOST_CROPS + k
        live_spot = (place >= live_before) & (place < live_before + amount)
        dead_spot = (place >= dead_before) & (place < dead_before + dead)
        image = jnp.where(live_spot | dead_spot, float(i), image)
        live_before = live_before + amount
        dead_before = dead_before + dead
    image_ref[...] = image
    info_ref[0] = (total + GROUP - 1) // GROUP
    info_ref[1] = device_ref[0] & (BLOCKS - 1)
    proto = proto_ref[...].astype(jnp.float32)
    inv = lax.rsqrt(jnp.sum(proto * proto, axis=0, keepdims=True) + EPS)
    inv_ref[...] = inv
    unit = (proto * inv).astype(jnp.bfloat16)
    unit_ref[...] = unit
    turned_ref[...] = unit.T
    bottle = proto.shape[0]
    images = teacher_ref.shape[0]
    for r in range(0, images, 64):
        expo = jnp.exp(teacher_ref[r : r + 64, :] * (1.0 / TEACHER_TEMP))
        expo_ref[r : r + 64, :] = expo
        teach_ref[r : r + 64, :bottle] = against(expo.astype(jnp.bfloat16), unit)
        teach_ref[r : r + 64, bottle:] = jnp.broadcast_to(jnp.sum(expo, axis=1, keepdims=True), (64, 128))


def repeat_rows(values, image):
    out = jnp.zeros((image.shape[0], values.shape[1]), values.dtype)
    for i in range(values.shape[0]):
        out = jnp.where(image == i, values[i : i + 1], out)
    return out


def three_parts(values):
    high = values.astype(jnp.bfloat16).astype(jnp.float32)
    middle = (values - high).astype(jnp.bfloat16).astype(jnp.float32)
    return [high, middle, values - high - middle]


def head_kernel(
    scale, own_columns, me_ref, live_ref, image_ref, teach_ref, co_ref, cx_ref, gains_ref, shifts_ref, final_ref,
    w_out_ref, b_out_ref, far_fc1_ref, b_fc1_ref, far_fc2_ref, b_fc2_ref,
    far_w1_ref, b1_ref, far_w2_ref, b2_ref, far_w3_ref, b3_ref, far_unit_ref,
    cg_ref, cres_ref, da_ref, common_ref, feats_ref, share0_ref, share1_ref, share2_ref, share3_ref, keep_ref, send_ref, vec_ref,
    act_ref, slope_ref, slope1_ref, slope2_ref, one_ref, two_ref, back_ref, up1_ref, up2_ref,
    w_fc1_ref, w_fc2_ref, w1_ref, w2_ref, w3_ref, unit_ref, done_ref,
):
    far = (far_fc1_ref.at[1], far_fc2_ref.at[1], far_w1_ref, far_w2_ref, far_w3_ref, far_unit_ref)
    near = (w_fc1_ref, w_fc2_ref, w1_ref, w2_ref, w3_ref, unit_ref)
    copies = [pltpu.make_async_copy(a, b, done_ref.at[i]) for i, (a, b) in enumerate(zip(far, near))]
    for copy in copies:
        copy.start()
    width = cx_ref.shape[1]
    hidden = w_fc1_ref.shape[1]
    hid, bottle = w3_ref.shape
    low = jnp.bfloat16
    middle = cx_ref[...] + product(co_ref[...].astype(low), w_out_ref[...]) + b_out_ref[1:2, :]
    normed_d, rstd_d = standardize(middle)
    low_d = (normed_d * norm_row(gains_ref, 3) + norm_row(shifts_ref, 3)).astype(low)
    copies[0].wait()
    for c in range(0, hidden, 256):
        cols = slice(c, c + 256)
        act, slope = smooth_both(product(low_d, w_fc1_ref[:, cols]) + b_fc1_ref[1:2, cols])
        act_ref[:, cols] = act.astype(low)
        slope_ref[:, cols] = slope
    def share(kind, c, values):
        for u in range(256 // (4 * own_columns)):
            start = kind * (hid // 4) + c // 4 + u * own_columns
            here = slice(start, start + own_columns)
            parts = [values[:, (u * 4 + j) * own_columns : (u * 4 + j + 1) * own_columns] for j in range(4)]
            for bit in (0, 1):
                flip = (me_ref[0] >> bit) & 1 == 1
                parts = [jnp.where(flip, parts[j ^ (1 << bit)], parts[j]) for j in range(4)]
            for ref, part in zip((share0_ref, share1_ref, share2_ref, share3_ref), parts):
                ref[:, here] = part

    copies[1].wait()
    out = middle + product(act_ref[...], w_fc2_ref[...]) + b_fc2_ref[1:2, :]
    normed_f, rstd_f = standardize(out)
    low_f = (normed_f * final_ref[0:1, :] + final_ref[1:2, :]).astype(low)
    common_ref[:, hid : hid + width] = low_f
    copies[2].wait()
    for c in range(0, hid, 256):
        cols = slice(c, c + 256)
        act, slope = smooth_both(product(low_f, w1_ref[:, cols]) + b1_ref[:, cols])
        one_ref[:, cols] = act.astype(low)
        share(0, c, act.astype(low))
        slope1_ref[:, cols] = slope
    first = one_ref[...]
    copies[3].wait()
    for c in range(0, hid, 256):
        cols = slice(c, c + 256)
        act, slope = smooth_both(product(first, w2_ref[:, cols]) + b2_ref[:, cols])
        two_ref[:, cols] = act.astype(low)
        share(1, c, act.astype(low))
        slope2_ref[:, cols] = slope
    copies[4].wait()
    embed = product(two_ref[...], w3_ref[...]) + b3_ref[...]
    inv = lax.rsqrt(jnp.sum(embed * embed, axis=1, keepdims=True) + EPS)
    feats = (embed * inv).astype(low)
    slots = feats.shape[0]
    total = jnp.zeros((slots, 1), jnp.float32)
    student = jnp.zeros((slots, bottle), jnp.float32)
    total_protos = unit_ref.shape[0]
    copies[5].wait()
    size = 512

    def some(i, carry):
        total, student = carry
        part = unit_ref[pl.ds(pl.multiple_of(i * size, size), size), :]
        expo = jnp.exp(against(feats, part) * (1.0 / STUDENT_TEMP) - SHIFT)
        return (
            total + jnp.sum(expo, axis=1, keepdims=True),
            student + product(expo.astype(low), part),
        )

    total, student = lax.fori_loop(0, total_protos // size, some, (total, student), unroll=4)
    teach_total = teach_ref[:, bottle : bottle + 128]
    teach = repeat_rows(teach_ref[:, :bottle] * (1.0 / teach_total[:, :1]), image_ref[...])
    grad_feat = live_ref[...] * (student * (1.0 / total) - teach) * scale
    logs = [live_ref[...]] + three_parts(SHIFT + jnp.log(total)) + three_parts(repeat_rows(jnp.log(teach_total), image_ref[...])[:, :1]) + [image_ref[...]]
    lane = lax.broadcasted_iota(jnp.int32, (slots, 128), 1)
    extra = jnp.zeros((slots, 128), jnp.float32)
    for i, part in enumerate(logs):
        extra = jnp.where(lane == i, part, extra)
    mark = hid + width + bottle
    feats_ref[:, :bottle] = feats
    feats_ref[:, bottle:] = extra.astype(low)
    grad_embed = inv * grad_feat - embed * (inv * inv * inv) * jnp.sum(embed * grad_feat, axis=1, keepdims=True)
    grad_embed = grad_embed.astype(low)
    common_ref[:, hid + width : mark] = grad_embed
    vec_ref[...] = jnp.zeros_like(vec_ref)
    vec_ref[:, 6 * width + hidden : 6 * width + hidden + bottle] = fold_rows(grad_embed.astype(jnp.float32))
    for c in range(0, hid, 256):
        cols = slice(c, c + 256)
        grad = (slope2_ref[:, cols] * against(grad_embed, w3_ref[cols, :])).astype(low)
        common_ref[:, cols] = grad
        vec_ref[:, 7 * width + hidden + hid + c : 7 * width + hidden + hid + c + 256] = fold_rows(grad.astype(jnp.float32))
    grad_two = common_ref[:, :hid]
    for c in range(0, hid, 256):
        cols = slice(c, c + 256)
        grad = (slope1_ref[:, cols] * against(grad_two, w2_ref[cols, :])).astype(low)
        back_ref[:, cols] = grad
        vec_ref[:, 7 * width + hidden + c : 7 * width + hidden + c + 256] = fold_rows(grad.astype(jnp.float32))
        share(2, c, grad)
    grad = against(back_ref[...], w1_ref[...])
    vec_ref[:, 4 * width : 5 * width] = fold_rows(grad * normed_f)
    vec_ref[:, 5 * width : 6 * width] = fold_rows(grad)
    grad_class = standard_back(grad, normed_f, rstd_f, final_ref[0:1, :])
    grad_low = grad_class.astype(low)
    vec_ref[:, 3 * width : 4 * width] = fold_rows(grad_low.astype(jnp.float32))
    up2_ref[...] = inner_rows(act_ref[...], grad_low).astype(low)
    for c in range(0, hidden, 256):
        cols = slice(c, c + 256)
        grad = (slope_ref[:, cols] * against(grad_low, w_fc2_ref[cols, :])).astype(low)
        act_ref[:, cols] = grad
        vec_ref[:, 6 * width + c : 6 * width + c + 256] = fold_rows(grad.astype(jnp.float32))
    grad_pre = act_ref[...]
    up1_ref[...] = inner_rows(low_d, grad_pre).astype(low)
    grad = against(grad_pre, w_fc1_ref[...])
    vec_ref[:, :width] = fold_rows(grad * normed_d)
    vec_ref[:, width : 2 * width] = fold_rows(grad)
    grad_middle = grad_class + standard_back(grad, normed_d, rstd_d, norm_row(gains_ref, 3))
    cres_ref[...] = grad_middle
    grad_low = grad_middle.astype(low)
    da_ref[...] = grad_low.astype(jnp.float32)
    vec_ref[:, 2 * width : 3 * width] = fold_rows(grad_low.astype(jnp.float32))
    cg_ref[...] = against(grad_low, w_out_ref[...]).astype(low).astype(jnp.float32)
    finish_rows(vec_ref)
    write_unit(me_ref[0], keep_ref, send_ref, 0, from_square(up1_ref), True)
    write_unit(me_ref[0], keep_ref, send_ref, 1, from_tall(up2_ref), True)


def head_sum_kernel(
    width, info_ref, common0_ref, common1_ref, common2_ref, common3_ref, share0_ref, share1_ref, share2_ref, share3_ref,
    kept_ref, sent_ref,
    parts_ref,
):
    quarter = share0_ref.shape[1] // 3
    full = quarter * 4
    share = jnp.concatenate([ref[...] for ref in (share0_ref, share1_ref, share2_ref, share3_ref)])
    common = jnp.concatenate([ref[...] for ref in (common0_ref, common1_ref, common2_ref, common3_ref)])
    low = jnp.bfloat16
    parts = [share[:, i * quarter : (i + 1) * quarter].T for i in range(3)]
    parts_ref[:, :width] = product(parts[2], common[:, full : full + width])
    for c in range(0, full, 512):
        parts_ref[:, width + c : width + c + 512] = product(parts[0], common[:, c : c + 512])
    mark = parts_ref.shape[1]
    parts_ref[:, width + full :] = product(parts[1], common[:, width + full : mark])
    size = kept_ref.shape[1]
    spot = (info_ref[1] >> 2) & 1
    for z in range(kept_ref.shape[0]):
        for ref, digit in ((kept_ref, spot), (sent_ref, 1 - spot)):
            ref[z] = parts_ref[pl.ds(pl.multiple_of((2 * z + digit) * size, 8), size), :].astype(jnp.bfloat16)


def proto_back_kernel(
    scale, owner_ref, unit_ref, proto_ref, inv_ref, thawed_ref, expo_ref, feats_ref,
    grad_ref,
    acc_ref, raw_ref,
):
    step = pl.program_id(0)
    bottle = unit_ref.shape[0]

    @pl.when(step == 0)
    def _():
        acc_ref[...] = jnp.zeros_like(acc_ref)

    rows = feats_ref.shape[0]
    slots = rows // 8
    images = slots // MOST_CROPS
    for l in range(8):
        here = slice(l * slots, (l + 1) * slots)
        extra = feats_ref[here, bottle:].astype(jnp.float32)
        lane = lax.broadcasted_iota(jnp.int32, extra.shape, 1)
        pick = lambda a, b: jnp.sum(jnp.where((lane >= a) & (lane < b), extra, 0.0), axis=1, keepdims=True)
        logits = product(feats_ref[here, :bottle], unit_ref[...]) * (1.0 / STUDENT_TEMP)
        target = repeat_rows(expo_ref[pl.ds(pl.multiple_of(owner_ref[step * 8 + l] * images, 8), images), :], pick(7, 8))
        raw = pick(0, 1) * (jnp.exp(logits - pick(1, 4)) - target * jnp.exp(-pick(4, 7))) * scale
        raw_ref[here, :] = raw.astype(jnp.bfloat16)
    acc_ref[...] += inner_rows(feats_ref[:, :bottle], raw_ref[...])

    @pl.when(step == pl.num_programs(0) - 1)
    def _():
        proto = proto_ref[...].astype(jnp.float32)
        inv = inv_ref[...]
        grad = acc_ref[...]
        inner = jnp.sum(proto * grad, axis=0, keepdims=True)
        grad_ref[...] = (inv * grad - proto * (inv * inv * inv * inner)) * thawed_ref[...]


def whole(array):
    return pl.BlockSpec(array.shape, lambda *i: (0,) * len(array.shape))


class Layer:
    def __init__(self, array, layer):
        self.array, self.layer = array, layer


class Far:
    def __init__(self, array):
        self.array = array


def spec_of(item):
    if isinstance(item, Far):
        return pl.BlockSpec(memory_space=pl.ANY)
    if isinstance(item, Layer):
        shape = item.array.shape[1:]
        return pl.BlockSpec((None,) + shape, lambda *i: (item.layer,) + (0,) * len(shape))
    return whole(item)


def array_of(item):
    return item.array if isinstance(item, (Layer, Far)) else item


class Shifted:
    def __init__(self, ref, first):
        self.ref, self.first = ref, first

    def __getitem__(self, index):
        return self.ref[self.first + index]


def run_kernel(body, steps, scalars, whole_in, step_in, outs, scratch, micros, info=None, limit=32):
    count = info
    if info is not None:
        inner, firsts = body, scalars
        scalars = [info]

        def body(info_ref, *refs):
            @pl.when(pl.program_id(0) < info_ref[0])
            def _():
                inner(info_ref, *[Shifted(info_ref, first) for first in firsts], *refs)

    def by_step(rows, width):
        if count is None:
            return pl.BlockSpec((rows, width), lambda i, *s: (i, 0))
        return pl.BlockSpec((rows, width), lambda i, c, *s: (jnp.minimum(i, c[0] - 1), 0))

    return pl.pallas_call(
        body,
        grid_spec=pltpu.PrefetchScalarGridSpec(
            num_scalar_prefetch=len(scalars),
            grid=(steps,),
            in_specs=[spec_of(a) for a in whole_in] + [by_step(rows, a.shape[1]) for a, rows in step_in],
            out_specs=[
                by_step(rows, shape[1])
                if rows
                else pl.BlockSpec(memory_space=pltpu.SMEM)
                if rows is None
                else pl.BlockSpec(shape, lambda *i, k=len(shape): (0,) * k)
                for shape, dtype, rows in outs
            ],
            scratch_shapes=scratch,
        ),
        out_shape=[jax.ShapeDtypeStruct(shape, dtype) for shape, dtype, rows in outs],
        compiler_params=pltpu.CompilerParams(
            dimension_semantics=("arbitrary",), vmem_limit_bytes=limit * 1024 * 1024
        ),
        cost_estimate=pl.CostEstimate(flops=micros * 10**9, bytes_accessed=2**20, transcendentals=0),
    )(*scalars, *[array_of(a) for a in whole_in], *[a for a, rows in step_in])


def axis_bits(n):
    bits = n.bit_length() - 1
    assert n == 1 << bits
    return bits


def swap(values, mask, n):
    return lax.ppermute(values, "dp", [(i, i ^ mask) for i in range(n)])


def group_masks(group):
    return [k << group[0] for k in range(1 << len(group))]


def own_digit(group):
    return (lax.axis_index("dp") >> group[0]) & ((1 << len(group)) - 1)


def upper_groups(n, first):
    bits = list(range(first, axis_bits(n)))
    return [bits[i : i + 2] for i in range(0, len(bits), 2)][::-1]


def gather_loose(block, group, n):
    return jnp.stack([swap(block, mask, n) if mask else block for mask in group_masks(group)])


def tree_sum(parts):
    while len(parts) > 1:
        parts = [parts[i] + parts[i + 1] for i in range(0, len(parts), 2)]
    return parts[0]


def scatter_send(parts, group):
    size = 1 << len(group)
    parts = parts.reshape((size, parts.shape[0] // size) + parts.shape[1:])
    digit = own_digit(group)
    return [lax.dynamic_index_in_dim(parts, digit ^ k, 0, keepdims=False) for k in range(size)]


def double(mine, got):
    return jnp.concatenate([mine, got])


def pick_send(parts, axis, group):
    digit = own_digit(group)
    return [lax.dynamic_index_in_dim(parts, digit ^ k, axis, keepdims=False) for k in range(2)]


def swap_parts(parts, group, n):
    return [swap(part, mask, n) if mask else part for part, mask in zip(parts, group_masks(group))]


def scatter_stage(parts, group, n):
    got = swap_parts(scatter_send(parts, group), group, n)
    return tree_sum([part.astype(jnp.float32) for part in got]).astype(parts.dtype)


def sum_stage(values, group, n):
    return tree_sum(swap_parts([values] * (1 << len(group)), group, n))


def fold_send(parts, group):
    size = 1 << len(group)
    parts = parts.reshape((size, parts.shape[0] // size) + parts.shape[1:])
    return [parts[k] for k in range(size)]


def fold_sum(parts):
    return tree_sum([part.astype(jnp.float32) for part in parts]).astype(parts[0].dtype)


def unfold_stage(parts, group, n):
    return jnp.concatenate([swap(parts, mask, n) if mask else parts for mask in group_masks(group)])


def extra_sum(values, n):
    for bit in range(5, axis_bits(n)):
        values = values + swap(values, 1 << bit, n)
    return values


def together(*values):
    return lax.optimization_barrier(values)


CORE, PLANE, LINE = [0], [1, 2], [3, 4]
UNPACK = 4


def per_device(
    tokens,
    layer_gains,
    layer_shifts,
    w_qkv,
    b_qv,
    w_out,
    b_out,
    w_fc1,
    b_fc1,
    w_fc2,
    b_fc2,
    final_gain,
    final_shift,
    head_w1,
    head_b1,
    head_w2,
    head_b2,
    head_w3,
    head_b3,
    prototypes,
    crop_counts,
    teacher_logits,
    first_epoch,
):
    low, wide = jnp.bfloat16, jnp.float32
    slot_count, seq_len, width = tokens.shape
    n = lax.axis_size("dp")
    device = lax.axis_index("dp")
    me = (device & (BLOCKS - 1)).reshape(1)
    bottle = prototypes.shape[0]
    hidden = w_fc1.shape[2]
    hid = head_w2.shape[0]
    rows = GROUP * PITCH
    steps = slot_count // GROUP
    padded = slot_count * PITCH
    row_count = slot_count * seq_len
    groups = upper_groups(n, 3)

    scale = 1.0 / (STUDENT_TEMP * n)
    images, protos = teacher_logits.shape
    info, own_live, image, unit_low, unit_turned, col_inv, teach_sum, teach_expo = run_kernel(
        prepare_kernel,
        1,
        [device.reshape(1), crop_counts],
        [prototypes, teacher_logits],
        [],
        [
            ((slot_count + 2,), jnp.int32, None),
            ((slot_count, 1), wide, 0),
            ((slot_count, 1), wide, 0),
            ((bottle, protos), low, 0),
            ((protos, bottle), low, 0),
            ((1, protos), wide, 0),
            ((images, bottle + 128), wide, 0),
            ((images, protos), wide, 0),
        ],
        [],
        4,
        limit=56,
    )
    unit_all = lax.all_gather(unit_turned, "dp", axis=0, tiled=True)
    teach_sum = teach_sum.reshape(n, -1, bottle + 128)
    for group in groups[:-1]:
        teach_sum = scatter_stage(teach_sum, group, n)

    gains, shifts = layer_gains, layer_shifts
    turned_tokens = tokens.transpose(1, 0, 2)
    all_rows = pltpu.VMEM((width // 128, row_count, 128), wide)
    teach_parts = scatter_send(teach_sum, groups[-1])
    turned_tokens, *teach_parts = together(turned_tokens, *teach_parts)
    teach_parts = swap_parts(teach_parts, groups[-1], n)
    qkv_a, attn_a, middle_a = run_kernel(
        attend_kernel,
        steps,
        [2],
        [turned_tokens, gains, shifts, Layer(w_qkv, 0), b_qv, Layer(w_out, 0), b_out],
        [],
        [((padded, 3 * width), low, rows), ((padded, width), low, rows), ((padded, width), wide, rows)],
        [all_rows, pltpu.VMEM((rows, width), wide), pltpu.VMEM((rows, width), low)],
        35,
        info,
        limit=56,
    )
    middle_a, *teach_parts = together(middle_a, *teach_parts)
    teach_sum = tree_sum(teach_parts)
    teach_parts = scatter_send(teach_sum, PLANE)
    middle_a, *teach_parts = together(middle_a, *teach_parts)
    teach_parts = swap_parts(teach_parts, PLANE, n)
    act_a, slope_a, lower_out, kv_c, query_c, attn_c, first_low, first_in = run_kernel(
        mlp_kernel,
        steps,
        [],
        [gains, shifts, Layer(w_fc1, 0), b_fc1, Layer(w_fc2, 0), b_fc2, Layer(w_qkv, 1), b_qv],
        [(middle_a, rows)],
        [
            ((padded, hidden), low, rows),
            ((padded, hidden), low, rows),
            ((padded, width), wide, rows),
            ((padded, 2 * width), low, rows),
            ((slot_count, width), wide, 0),
            ((slot_count, width), wide, 0),
            ((slot_count, width), wide, 0),
            ((slot_count, width), wide, 0),
        ],
        [pltpu.VMEM((rows, width), low), pltpu.VMEM((rows, width), wide), pltpu.VMEM((rows, HEADS * GROUP), wide)],
        40,
        info,
        limit=56,
    )
    first_in, *teach_parts = together(first_in, *teach_parts)
    teach_sum = scatter_stage(tree_sum(teach_parts), CORE, n)[0]

    finals = jnp.stack([final_gain, final_shift])
    vec_width = -(-(7 * width + hidden + 2 * hid) // width) * width
    grad_attended, grad_middle_c, grad_attn, common, feats, *shares, keep_u, send_u, vec_h = run_kernel(
        functools.partial(head_kernel, scale, hid // n),
        1,
        [me],
        [own_live, image, teach_sum, attn_c, first_in, gains, shifts, finals, Layer(w_out, 1), b_out, Far(w_fc1), b_fc1, Far(w_fc2), b_fc2,
         Far(head_w1), head_b1[None], Far(head_w2), head_b2[None], Far(head_w3), head_b3[None], Far(unit_all)],
        [],
        [
            ((slot_count, width), wide, 0),
            ((slot_count, width), wide, 0),
            ((slot_count, width), wide, 0),
            ((slot_count, hid + width + bottle), low, 0),
            ((slot_count, bottle + 128), low, 0),
            *[((slot_count, hid // 4 * 3), low, 0)] * 4,
            ((BLOCKS // 2, 2, width // 8, width), low, 0),
            ((BLOCKS // 2, 2, width // 8, width), low, 0),
            ((8, vec_width), wide, 0),
        ],
        [
            pltpu.VMEM((slot_count, hidden), low),
            pltpu.VMEM((slot_count, hidden), wide),
            pltpu.VMEM((slot_count, hid), wide),
            pltpu.VMEM((slot_count, hid), wide),
            pltpu.VMEM((slot_count, hid), low),
            pltpu.VMEM((slot_count, hid), low),
            pltpu.VMEM((slot_count, hid), low),
            pltpu.VMEM((width, hidden), low),
            pltpu.VMEM((hidden, width), low),
        ]
        + [pltpu.VMEM(v.shape, low) for v in (w_fc1[0], w_fc2[0], head_w1, head_w2, head_w3, unit_all)]
        + [pltpu.SemaphoreType.DMA((6,))],
        20,
        limit=min(56, 40 + unit_all.size // 2**19),
    )
    common_got = swap(common, 1, n)
    share0, share2 = shares[0], shares[2]
    share1, share3 = swap(shares[1], 1, n), swap(shares[3], 1, n)
    bits = list(range(5, axis_bits(n))) + [4, 3, 1, 2, 0]
    masks = [0]
    for bit in bits:
        masks = masks + [mask | (1 << bit) for mask in masks]
    for bit in bits[:-5]:
        feats = double(feats, swap(feats, 1 << bit, n))
    grad_attended, common, share2, share3, send_u, feats = together(grad_attended, common, share2, share3, send_u, feats)
    got_u = swap(send_u, 1, n)
    feats_got = swap(feats, 16, n)
    common2, share2, share3 = (swap(v, 2, n) for v in (common, share2, share3))
    grad_lower_out, unit_u, vec_c = run_kernel(
        upper_back_kernel,
        steps,
        [],
        [gains, shifts, Layer(w_qkv, 1), first_low, attn_c, grad_attn],
        [(lower_out, rows), (kv_c, rows), (query_c, GROUP), (grad_attended, GROUP), (grad_middle_c, GROUP)],
        [
            ((padded, width), wide, rows),
            ((width, 4 * width), low, 0),
            ((8, 4 * width), wide, 0),
        ],
        [
            pltpu.VMEM((width, 4 * width), wide),
            pltpu.VMEM((rows, width), wide),
            pltpu.VMEM((slot_count, width), wide),
            pltpu.VMEM((rows, HEADS * GROUP), wide),
            pltpu.VMEM((rows, 2 * width), low),
        ],
        20,
        info,
    )
    grad_lower_out, common2, share2, share3, got_u, feats_got = together(
        grad_lower_out, common2, share2, share3, got_u, feats_got
    )
    feats = double(feats, feats_got)
    common3 = swap(common2, 1, n)
    parts_u = fold_send(keep_u + got_u, LINE)
    head_keep, head_send = run_kernel(
        functools.partial(head_sum_kernel, width),
        1,
        [info],
        [common, common_got, common2, common3, share0, share1, share2, share3],
        [],
        [((n // 8, hid // n, width + hid + bottle), low, 0)] * 2,
        [pltpu.VMEM((hid // 4, width + hid + bottle), wide)],
        6,
    )
    grad_lower_out, head_send, feats, *parts_u = together(grad_lower_out, head_send, feats, *parts_u)
    head_got, feats_got = swap(head_send, 4, n), swap(feats, 8, n)
    parts_u = swap_parts(parts_u, LINE, n)
    grad_middle_a, keep_m, send_m, vec_b, vec_hidden = run_kernel(
        mlp_back_kernel,
        steps,
        [1],
        [unit_u, gains, shifts, Layer(w_fc1, 0), Layer(w_fc2, 0)],
        [(grad_lower_out, rows), (middle_a, rows), (act_a, rows), (slope_a, rows)],
        [
            ((padded, width), wide, rows),
            ((BLOCKS // 2, 3, width // 8, width), low, 0),
            ((BLOCKS // 2, 3, width // 8, width), low, 0),
            ((8, 3 * width), wide, 0),
            ((8, hidden), wide, 0),
        ],
        [
            pltpu.VMEM((width, hidden), wide),
            pltpu.VMEM((width, hidden), wide),
            pltpu.VMEM((rows, hidden), low),
            pltpu.VMEM((hidden, width), wide),
            pltpu.VMEM((rows, width), wide),
            pltpu.VMEM((rows, 1), wide),
        ],
        40,
        info,
        limit=44,
    )
    grad_middle_a, head_got, feats_got, send_m, *parts_u = together(grad_middle_a, head_got, feats_got, send_m, *parts_u)
    feats = double(feats, feats_got)
    head_parts = head_keep + head_got
    for bit in range(axis_bits(n) - 1, 4, -1):
        head_parts = scatter_stage(head_parts, [bit], n)
    head_keep, head_send = pick_send(head_parts.reshape((2, 2) + head_parts.shape[1:]), 1, [3])
    parts_m = [
        jnp.concatenate([a.reshape((-1,) + a.shape[2:]), b[0]])
        for a, b in zip(fold_send(keep_m + swap(send_m, 1, n), PLANE), fold_send(fold_sum(parts_u), PLANE))
    ]
    grad_middle_a, head_send, *parts_m = together(grad_middle_a, head_send, *parts_m)
    head_got = swap(head_send, 8, n)
    parts_m = swap_parts(parts_m, PLANE, n)
    grad_qkv, grad_wo, vec_a = run_kernel(
        attend_back_kernel,
        steps,
        [],
        [Layer(w_out, 0)],
        [(grad_middle_a, rows), (qkv_a, rows), (attn_a, rows)],
        [((padded, 3 * width), low, rows), ((width, width), wide, 0), ((8, 4 * width), wide, 0)],
        [pltpu.VMEM((rows, width), low)],
        40,
        info,
    )
    grad_qkv, head_got, *parts_m = together(grad_qkv, head_got, *parts_m)
    head_keep, head_send = pick_send(head_keep + head_got, 0, [4])
    sum_m = fold_sum(parts_m)
    sum_u = sum_m[None, 12:]
    parts_m = fold_send(sum_m[:12].reshape((4, 3) + sum_m.shape[1:]), LINE)
    grad_qkv, head_send, feats, *parts_m = together(grad_qkv, head_send, feats, *parts_m)
    feats_got = swap(feats, 2, n)
    parts_m = swap_parts(parts_m, LINE, n)
    keep_a, send_a = run_kernel(
        weight_back_kernel,
        steps,
        [1, 2],
        [turned_tokens, gains, shifts, grad_wo],
        [(grad_qkv, rows)],
        [
            ((BLOCKS // 2, 1, width // 8, width), low, 0),
            ((BLOCKS // 2, 1, width // 8, width), low, 0),
        ],
        [all_rows, pltpu.VMEM((rows, width), wide), pltpu.VMEM((width, 4 * width), wide)],
        10,
        info,
    )
    keep_a, send_a, feats_got, *parts_m = together(keep_a, send_a, feats_got, *parts_m)
    feats = double(feats, feats_got)
    sum_m = extra_sum(jnp.concatenate([fold_sum(parts_m), sum_u], axis=1), n)
    keep_a, send_a = fold_send(keep_a + swap(send_a, 1, n), [2])
    grad_qkv, sum_m, send_a, feats = together(grad_qkv, sum_m, send_a, feats)
    feats_got = swap(feats, 4, n)
    parts_m = swap_parts([sum_m] * 4, LINE, n)
    got_a = swap(send_a, 4, n)
    grad_tokens, vectors = run_kernel(
        input_back_kernel,
        steps,
        [2],
        [turned_tokens, gains, Layer(w_qkv, 0), vec_b, vec_c, vec_h, vec_a, vec_hidden],
        [(grad_middle_a, rows), (grad_qkv, rows)],
        [((row_count, width), wide, 0), ((1, 13 * width + hidden + vec_width), wide, 0)],
        [all_rows, all_rows, pltpu.VMEM((rows, width), wide), pltpu.VMEM((8, 2 * width), wide)],
        20,
        info,
    )
    tokens_grad = grad_tokens.reshape(seq_len, slot_count, width).transpose(1, 0, 2)
    vectors, got_a, feats_got, *parts_m = together(vectors, got_a, feats_got, *parts_m)
    feats = double(feats, feats_got)
    feats = double(feats, swap(feats, 1, n))

    keep_a, send_a = fold_send(keep_a + got_a, [1])
    send_a, vectors = together(send_a, vectors)
    got_a, got_v = swap(send_a, 2, n), swap(vectors, 1, n)
    vectors = vectors + got_v
    sum_m = jnp.concatenate(parts_m)
    half = sum_m.shape[0] // 2
    feats, vectors, sum_m = together(feats, vectors, sum_m)
    one, two = sum_m[:half], sum_m[half:]
    one, two = [one, swap(one, 2, n)], [two, swap(two, 4, n)]
    prototypes_grad = run_kernel(
        functools.partial(proto_back_kernel, scale),
        n // 8,
        [device ^ jnp.array(masks, jnp.int32)],
        [unit_low, prototypes, col_inv, (1 - first_epoch).astype(wide)[None], teach_expo],
        [(feats, 8 * slot_count)],
        [(prototypes.shape, wide, 0)],
        [pltpu.VMEM(prototypes.shape, wide), pltpu.VMEM((8 * slot_count, protos), low)],
        6,
    )[0]
    for bit in (4, 3):
        vectors = vectors + swap(vectors, 1 << bit, n)
    prototypes_grad, got_a, vectors, *parts_m = together(prototypes_grad, got_a, vectors, *one, *two)
    one, two = jnp.stack(parts_m[:2]), jnp.stack(parts_m[2:])
    sum_a = keep_a + got_a
    sum_a, vectors, one, two = together(sum_a, vectors, one, two)
    one, two = [one, swap(one, 4, n)], [two, swap(two, 2, n)]
    for bit in (4, 3):
        keep_a, send_a = fold_send(sum_a, [bit])
        sum_a = keep_a + swap(send_a, 1 << bit, n)
    sum_a = extra_sum(sum_a, n)
    vectors = extra_sum(vectors, n)
    for bit in (3, 4):
        sum_a = unfold_stage(sum_a, [bit], n)
    sum_a, vectors, head_send, *parts_m = together(sum_a, vectors, head_send, *one, *two)
    head_got = swap(head_send, 16, n)
    one = jnp.stack(parts_m[:2]).reshape((4,) + parts_m[0].shape[1:])
    two = jnp.stack(parts_m[2:], axis=1).reshape((4,) + parts_m[0].shape[1:])
    sum_m = jnp.concatenate([one, two], axis=1).reshape((BLOCKS // 2,) + one.shape[2:])
    got_m, got_a, got_v = swap(sum_m, 1, n), swap(sum_a, 2, n), swap(vectors, 2, n)
    got_m, got_a, got_v = together(got_m, got_a, got_v)
    sum_a, vectors = double(sum_a, got_a), vectors + got_v
    got_a, got_v = swap(sum_a, 4, n), swap(vectors, 4, n)
    specs = [
        pl.BlockSpec((None, width // UNPACK, 3 * width), lambda i: (1, i, 0)),
        pl.BlockSpec((None, width // UNPACK, width), lambda i: (1, i, 0)),
    ]
    shapes = [jax.ShapeDtypeStruct(s, wide) for s in ((2, width, 3 * width), (2, width, width))]
    params = pltpu.CompilerParams(dimension_semantics=("arbitrary",), vmem_limit_bytes=32 * 1024 * 1024)
    qkv_grad, out_grad, fc1_grad, fc2_grad = pl.pallas_call(
        unpack_kernel,
        grid=(UNPACK,),
        in_specs=[pl.BlockSpec(memory_space=pltpu.SMEM), whole(sum_m), whole(got_m)],
        out_specs=specs
        + [
            pl.BlockSpec((2, width // UNPACK, hidden), lambda i: (0, i, 0)),
            pl.BlockSpec((2, hidden // UNPACK, width), lambda i: (0, i, 0)),
        ],
        out_shape=shapes + [jax.ShapeDtypeStruct(s, wide) for s in ((2, width, hidden), (2, hidden, width))],
        compiler_params=params,
        cost_estimate=pl.CostEstimate(flops=8 * 10**9, bytes_accessed=2**20, transcendentals=0),
    )(me, sum_m, got_m)
    qkv_grad, out_grad, got_a, got_v, head_got = together(qkv_grad, out_grad, got_a, got_v, head_got)
    head_sum = (head_keep.astype(wide) + head_got.astype(wide)).reshape(hid // n, -1)
    w1_grad, w2_grad, w3_grad = head_sum[:, :width].T, head_sum[:, width : width + hid], head_sum[:, width + hid :]
    sum_a, vectors = double(sum_a, got_a), vectors + got_v
    got_a = swap(sum_a, 1, n)
    specs = [pl.BlockSpec(spec.block_shape, lambda i: (0, i, 0)) for spec in specs]
    small = [(2, 2, width), (2, 2, width), (2, 2 * width), (2, width), (2, hidden), (2, width)]
    qkv_grad, out_grad, gains_grad, shifts_grad, bqv_grad, bout_grad, bfc1_grad, bfc2_grad = pl.pallas_call(
        unpack_first_kernel,
        grid=(UNPACK,),
        in_specs=[pl.BlockSpec(memory_space=pltpu.SMEM), whole(sum_a), whole(got_a), whole(vectors)]
        + [pl.BlockSpec(memory_space=pl.ANY)] * 2,
        out_specs=specs + [pl.BlockSpec(shape, lambda i, k=len(shape): (0,) * k) for shape in small],
        out_shape=shapes + [jax.ShapeDtypeStruct(shape, wide) for shape in small],
        input_output_aliases={4: 0, 5: 1},
        compiler_params=params,
    )(me, sum_a, got_a, vectors, qkv_grad, out_grad)
    row_h = 9
    ends = vectors[0, (row_h + 7) * width + hidden : (row_h + 7) * width + hidden + 2 * hid]
    row_part = lambda row, size: vectors[0, row * width : row * width + size]
    own_part = lambda start: lax.dynamic_slice_in_dim(ends, start + device * (hid // n), hid // n)

    return (
        tokens_grad,
        gains_grad,
        shifts_grad,
        qkv_grad,
        bqv_grad,
        out_grad,
        bout_grad,
        fc1_grad,
        bfc1_grad,
        fc2_grad,
        bfc2_grad,
        row_part(row_h + 4, width),
        row_part(row_h + 5, width),
        w1_grad,
        own_part(0),
        w2_grad,
        own_part(hid),
        w3_grad,
        row_part(row_h + 6 + hidden // width, bottle),
        prototypes_grad,
    )


def solution(mesh):
    return jax.shard_map(
        per_device,
        mesh=mesh,
        in_specs=(
            P("dp", None, None),
            P(),
            P(),
            P(),
            P(),
            P(),
            P(),
            P(),
            P(),
            P(),
            P(),
            P(),
            P(),
            P(),
            P(),
            P(),
            P(),
            P(),
            P(),
            P(None, "dp"),
            P(),
            P(None, "dp"),
            P("dp"),
        ),
        out_specs=(
            P("dp", None, None),
            P(),
            P(),
            P(),
            P(),
            P(),
            P(),
            P(),
            P(),
            P(),
            P(),
            P(),
            P(),
            P(None, "dp"),
            P("dp"),
            P("dp", None),
            P("dp"),
            P("dp", None),
            P(),
            P(None, "dp"),
        ),
        check_vma=False,
    )
```
